32 devices in a mesh: gx: 4 (over z), gy: 4 (over y, x), gz: 2 (over core).
Axes of the slice: x: 2, y: 2, z: 4, core: 2. Of those that a mesh axis runs over, the one named last changes fastest.
Arguments:
- flow: float32 [4, 32, 64, 256], P(None, 'gx', 'gy', 'gz'), may hold values from -3 to 3
- basis: float32 [127, 3, 8192], P(None, None, ('gx', 'gy', 'gz')), may hold values from -1150 to 1150
- sample: int32 [8192], P(('gx', 'gy', 'gz')), may hold values from 0 to 16383
Outputs:
- flow_next: float32 [4, 32, 64, 256], P(None, 'gx', 'gy', 'gz')
- basis_next: float32 [128, 3, 8192], P(None, None, ('gx', 'gy', 'gz'))
- factor: float32 [128, 128], replicated
The draws below stay inside these ranges and needn't reach their ends.
All inputs are finite; a program needn't handle non-finite values.
Results may differ from the reference program's by a relative error of at most 0.000065.
Values sent between devices are 32-bit elements; how exact they have to be, the bound alone decides.
No kernel may reach another device: no remote copies, remote signals or barrier semaphores. Data moves between devices by JAX's collectives and lax.ppermute only.
A program may use at most 64 MiB of HBM per device.

```python
import math
import jax
import jax.numpy as jnp
from jax import lax

CX = 8
CY = 16
CZ = 128
PTS_DEV = 256
MODES = 127
NX = 32
NY = 64
NZ = 256
POINTS = 8192
N_GY = 4
N_GZ = 2


def draw_basis(key, part):
    first, second, third = jax.random.split(key, 3)
    base = jnp.clip(jax.random.normal(first, (MODES, 3, POINTS), jnp.float32), -6.0, 6.0)
    top = math.log(10.0)
    mixed = base + 0.3 * jnp.roll(base, 1, axis=0) + 0.2 * jnp.roll(base, 5, axis=0)
    column = jnp.exp(jax.random.uniform(second, (MODES, 1, 1), jnp.float32, 0.0, math.log(10.0)))
    blocks = POINTS // PTS_DEV
    rising = jnp.arange(blocks, dtype=jnp.float32) / max(blocks - 1, 1)
    spread = jax.random.uniform(third, (blocks,), jnp.float32)
    row_scale = jnp.repeat(jnp.exp(top * (0.5 * rising + 0.5 * spread)), PTS_DEV)
    return mixed * column * row_scale[None, None, :]


def set_ends(result, rng, smallest, high):
    longest = result.shape.index(max(result.shape))
    spots = []
    for shift in (0, 1):
        where = [jax.random.randint(jax.random.fold_in(rng, axis), (), 0, length) for axis, length in enumerate(result.shape)]
        where[longest] = (where[longest] + shift) % result.shape[longest]
        spots.append(tuple(where))
    return result.at[spots[0]].set(smallest).at[spots[1]].set(high)


def shard_levels(stream_key, shape, cuts, low, high):
    level = 1.0
    for dim, blocks in cuts:
        heights = jax.random.uniform(jax.random.fold_in(jax.random.fold_in(stream_key, 6), dim), (blocks,), jnp.float32, low / len(cuts), high / len(cuts))
        level = level * jnp.repeat(jnp.exp(heights), shape[dim] // blocks).reshape((-1,) + (1,) * (len(shape) - 1 - dim))
    return level


def scatter_about(stream_key, shape, width, bound, cuts=(), held_as=jnp.bfloat16):
    factor_of = shard_levels(stream_key, shape, cuts, -0.22, 0.18) if cuts else 1.0
    values = jax.random.normal(stream_key, shape, jnp.float32) * width * factor_of
    return jnp.minimum(jnp.maximum(values, -bound), bound).astype(held_as)


def setup_inputs(seed: int = 0) -> dict:
    seeds = jax.random.split(jax.random.key(seed), 4)
    flow = scatter_about(seeds[0], (4, NX, NY, NZ), 0.5, 3.0, ((1, 4), (2, 4), (3, 2)), jnp.float32)
    basis = draw_basis(jax.random.fold_in(seeds[3], 71), 0)
    sample = set_ends(jax.random.randint(seeds[2], (POINTS,), 0, CX * CY * CZ), jax.random.fold_in(seeds[2], 1), 0, (CX * CY * CZ) - 1).astype(jnp.int32)
    return dict(flow=flow, basis=basis, sample=sample)


DT_STEP = 0.35
VISCOSITY = 0.2
SOUND_SQ = 1.0
DRIVING = 0.5

def rates(ext):
    centre = ext[:, 1:-1, 1:-1, 1:-1]
    x_plus = ext[:, 2:, 1:-1, 1:-1]
    x_minus = ext[:, :-2, 1:-1, 1:-1]
    y_plus = ext[:, 1:-1, 2:, 1:-1]
    y_minus = ext[:, 1:-1, :-2, 1:-1]
    z_plus = ext[:, 1:-1, 1:-1, 2:]
    z_minus = ext[:, 1:-1, 1:-1, :-2]
    slope_x = 0.5 * (x_plus - x_minus)
    slope_y = 0.5 * (y_plus - y_minus)
    slope_z = 0.5 * (z_plus - z_minus)
    laplace = x_plus + x_minus + (y_plus + y_minus) + (z_plus + z_minus) - 6.0 * centre
    advect = centre[0] * slope_x[:3] + centre[1] * slope_y[:3] + centre[2] * slope_z[:3]
    pressure = jnp.stack([slope_x[3], slope_y[3], slope_z[3]])
    forcing = jnp.array([DRIVING, 0.0, 0.0], dtype=jnp.float32).reshape(3, 1, 1, 1)
    velocity = VISCOSITY * laplace[:3] - advect - pressure + forcing
    density = -SOUND_SQ * (slope_x[0] + slope_y[1] + slope_z[2])
    return jnp.concatenate([velocity, density[None]], axis=0)

def extend(fields):
    walled = jnp.pad(fields, ((0, 0), (0, 0), (1, 1), (0, 0)))
    return jnp.pad(walled, ((0, 0), (1, 1), (0, 0), (1, 1)), mode='wrap')

def reference(flow, basis, sample):
    section_one = flow + DT_STEP * rates(extend(flow))
    section_two = 0.75 * flow + 0.25 * (section_one + DT_STEP * rates(extend(section_one)))
    flow_next = 1.0 / 3.0 * flow + 2.0 / 3.0 * (section_two + DT_STEP * rates(extend(section_two)))
    rows = jnp.arange(POINTS, dtype=jnp.int32)
    brick = rows // PTS_DEV
    brick_x = brick // (N_GY * N_GZ)
    brick_y = brick // N_GZ % N_GY
    brick_z = brick % N_GZ
    cell_x = brick_x * CX + sample // (CY * CZ)
    cell_y = brick_y * CY + sample // CZ % CY
    cell_z = brick_z * CZ + sample % CZ
    snapshot = flow_next[:3, cell_x, cell_y, cell_z]
    stacked = jnp.concatenate([basis, snapshot[None]], axis=0).reshape(MODES + 1, 3 * POINTS)
    gram = jnp.dot(stacked.astype(jnp.float32), stacked.T.astype(jnp.float32), precision=lax.Precision.HIGHEST, preferred_element_type=jnp.float32) / (3.0 * POINTS)
    lower = jnp.linalg.cholesky(gram)
    basis_next = jax.scipy.linalg.solve_triangular(lower, stacked, lower=True).reshape(MODES + 1, 3, POINTS)
    return (flow_next, basis_next, lower.T)
```

```python
import functools

import jax
import jax.numpy as jnp
from jax import lax
from jax.experimental import pallas as pl
from jax.experimental.pallas import tpu as pltpu
from jax.sharding import PartitionSpec as P

DT_STEP = 0.35
VISCOSITY = 0.2
SOUND_SQ = 1.0
DRIVING = 0.5

ALL = ("gx", "gy", "gz")
DEPTH = 3
GAP = 2
EXACT = lax.Precision.HIGHEST
VMEM = pl.BlockSpec(memory_space=pltpu.VMEM)
PARAMS = pltpu.CompilerParams(vmem_limit_bytes=40 * 1024 * 1024)


def dot(a, b, dims):
    return lax.dot_general(
        a, b, (dims, ((), ())), precision=EXACT, preferred_element_type=jnp.float32
    )


def neighbours(block_low, block_high, axis, periodic):
    count = lax.axis_size(axis)
    forward = [(i, i + 1) for i in range(count - 1)]
    if periodic:
        forward.append((count - 1, 0))
    backward = [(target, source) for source, target in forward]
    return lax.ppermute(block_high, axis, forward), lax.ppermute(block_low, axis, backward)


def gram_kernel(basis_ref, gram_ref):
    modes = basis_ref.shape[1]
    total = jnp.zeros((modes, modes), jnp.float32)
    for c in range(basis_ref.shape[0]):
        rows = basis_ref[c]
        total = total + dot(rows, rows, ((1,), (1,)))
    gram_ref[...] = jnp.zeros_like(gram_ref)
    gram_ref[0:modes, 0:modes] = total


def slabs(fields, planes):
    return [(f, i) for f in range(fields) for i in range(planes)]


def spread(index, depth):
    per = 128 // (2 * depth)
    return index // per, 2 * depth * (index % per)


def edges_kernel(flow_ref, ylo_ref, yhi_ref, xlo_ref, xhi_ref, ext_ref, packed_ref):
    fields, nx, ny, nz = flow_ref.shape
    rows = ext_ref.shape[2]
    ext_ref[:, 0:DEPTH] = xlo_ref[...]
    ext_ref[:, DEPTH + nx : 2 * DEPTH + nx] = xhi_ref[...]
    gap = jnp.zeros((GAP, nz), jnp.float32)
    for f, i in slabs(fields, nx):
        plane = jnp.concatenate([flow_ref[f, i], yhi_ref[f, i], gap, ylo_ref[f, i]], axis=0)
        ext_ref[f, DEPTH + i] = plane
    lane = lax.broadcasted_iota(jnp.int32, (rows, nz), 1)
    parts = [jnp.zeros((rows, nz), jnp.float32) for _ in range(packed_ref.shape[0])]
    for s, (f, i) in enumerate(slabs(fields, nx + 2 * DEPTH)):
        part, start = spread(s, DEPTH)
        moved = pltpu.roll(ext_ref[f, i], (start + DEPTH) % nz, 1)
        parts[part] = jnp.where((lane >= start) & (lane < start + 2 * DEPTH), moved, parts[part])
    for k, value in enumerate(parts):
        packed_ref[k] = value


def plane_step(read, i, rows, lanes):
    def step(value, by, axis):
        size = value.shape[axis]
        return pltpu.roll(value, (size - by) % size, axis)

    centre = [read(f, i) for f in range(4)]
    x_plus = [read(f, i + 1)[:rows, :lanes] for f in range(4)]
    x_minus = [read(f, i - 1)[:rows, :lanes] for f in range(4)]
    y_plus = [step(v, 1, 0)[:rows, :lanes] for v in centre]
    y_minus = [step(v, -1, 0)[:rows, :lanes] for v in centre]
    z_plus = [step(v[:rows], 1, 1)[:, :lanes] for v in centre]
    z_minus = [step(v[:rows], -1, 1)[:, :lanes] for v in centre]
    centre = [v[:rows, :lanes] for v in centre]
    slope_x = [0.5 * (a - b) for a, b in zip(x_plus, x_minus)]
    slope_y = [0.5 * (a - b) for a, b in zip(y_plus, y_minus)]
    slope_z = [0.5 * (a - b) for a, b in zip(z_plus, z_minus)]
    pressure = [slope_x[3], slope_y[3], slope_z[3]]
    out = []
    for f in range(3):
        laplace = (
            x_plus[f] + x_minus[f] + (y_plus[f] + y_minus[f]) + (z_plus[f] + z_minus[f]) - 6.0 * centre[f]
        )
        advect = centre[0] * slope_x[f] + centre[1] * slope_y[f] + centre[2] * slope_z[f]
        value = VISCOSITY * laplace - advect - pressure[f]
        if f == 0:
            value = value + DRIVING
        out.append(value)
    out.append(-SOUND_SQ * (slope_x[0] + slope_y[1] + slope_z[2]))
    return centre, out


def step_kernel(
    walls_ref, ext_ref, low_ref, high_ref, basis_ref, sample_ref, summed_ref,
    flow_ref, snap_ref, send_ref,
    halo_ref, one_ref, two_ref,
):
    fields, nx, ny, nz = flow_ref.shape
    rows = ext_ref.shape[2]
    modes = basis_ref.shape[1]
    lane = lax.broadcasted_iota(jnp.int32, (rows, nz), 1)
    row = lax.broadcasted_iota(jnp.int32, (rows, 2 * nz), 0)
    below = (row >= ny + DEPTH + GAP) & (walls_ref[0] == 1)
    above = (row >= ny) & (row < ny + DEPTH) & (walls_ref[1] == 1)
    outside = below | above

    around = [
        jnp.where(lane < nz // 2, high_ref[k], low_ref[k]) for k in range(low_ref.shape[0])
    ]
    for s, (f, i) in enumerate(slabs(fields, nx + 2 * DEPTH)):
        part, start = spread(s, DEPTH)
        halo_ref[f, i] = pltpu.roll(around[part], (2 * nz - start - DEPTH) % nz, 1)

    def read_ext(f, i):
        return jnp.concatenate([ext_ref[f, i], halo_ref[f, i]], axis=1)

    def read_one(f, i):
        return one_ref[f, i]

    def read_two(f, i):
        return two_ref[f, i]

    def first(i, carry):
        centre, rate = plane_step(read_ext, i, rows, 2 * nz)
        for f in range(4):
            one_ref[f, i] = jnp.where(outside, 0.0, centre[f] + DT_STEP * rate[f])
        return carry

    def second(i, carry):
        centre, rate = plane_step(read_one, i, rows, 2 * nz)
        for f in range(4):
            value = 0.75 * read_ext(f, i) + 0.25 * (centre[f] + DT_STEP * rate[f])
            two_ref[f, i] = jnp.where(outside, 0.0, value)
        return carry

    def third(i, carry):
        centre, rate = plane_step(read_two, i, ny, nz)
        for f in range(4):
            start = ext_ref[f, i][:ny]
            flow_ref[f, i - DEPTH] = 1.0 / 3.0 * start + 2.0 / 3.0 * (centre[f] + DT_STEP * rate[f])
        return carry

    lax.fori_loop(1, nx + 2 * DEPTH - 1, first, 0)
    lax.fori_loop(2, nx + 2 * DEPTH - 2, second, 0)
    lax.fori_loop(3, nx + 2 * DEPTH - 3, third, 0)

    points = sample_ref.shape[1]
    spot = jnp.broadcast_to(sample_ref[...], (nz, points))
    place = lax.broadcasted_iota(jnp.int32, (nx * ny, points), 0)
    in_row = (place == jnp.broadcast_to(sample_ref[...] // nz, (nx * ny, points))).astype(jnp.bfloat16)
    in_lane = lax.broadcasted_iota(jnp.int32, (nz, points), 0) == spot % nz
    cross = jnp.zeros((8, modes + 1), jnp.float32)
    for c in range(3):
        field = flow_ref[c].reshape(nx * ny, nz)
        high = field.astype(jnp.bfloat16)
        rest = field - high.astype(jnp.float32)
        middle = rest.astype(jnp.bfloat16)
        low = (rest - middle.astype(jnp.float32)).astype(jnp.bfloat16)
        found = sum(
            lax.dot_general(p, in_row, (((0,), (0,)), ((), ())), preferred_element_type=jnp.float32)
            for p in (high, middle, low)
        )
        picked = jnp.sum(jnp.where(in_lane, found, 0.0), axis=0, keepdims=True)
        snap_ref[c] = picked
        stacked = jnp.concatenate([basis_ref[c], picked], axis=0)
        cross = cross + dot(jnp.broadcast_to(picked, (8, points)), stacked, ((1,), (1,)))

    per = send_ref.shape[1] - 4
    summed = jnp.zeros((8, modes + 1), jnp.float32)
    for k in range(summed_ref.shape[0] // 8):
        summed = summed + summed_ref[8 * k : 8 * k + 8]
    summed = summed + pltpu.roll(summed, 4, 0)
    sub = lax.broadcasted_iota(jnp.int32, summed.shape, 0)
    block = jnp.where(sub < per, summed, jnp.where(sub == per, cross, 0.0))
    for d in range(send_ref.shape[0]):
        send_ref[d] = block


def final_kernel(count, got_ref, basis_ref, snap_ref, basis_out_ref, factor_ref, work_ref):
    modes = basis_ref.shape[1]
    size = modes + 1
    per = got_ref.shape[1] - 4
    cross = jnp.zeros((8, size), jnp.float32)
    for d in range(got_ref.shape[0]):
        block = got_ref[d]
        if per * d < size:
            work_ref[per * d : per * d + per, 0:size] = block[0:per] / count
        cross = cross + block
    cross = cross[per : per + 1] / count
    col = lax.broadcasted_iota(jnp.int32, (size, size), 1)
    row = lax.broadcasted_iota(jnp.int32, (size, size), 0)
    work_ref[size - 1 : size, 0:size] = cross
    mark = (lax.broadcasted_iota(jnp.int32, (8, size), 1) == size - 1).astype(jnp.float32)
    top = lax.broadcasted_iota(jnp.int32, (8, size), 0) == 0
    side = dot(jnp.where(top, jnp.broadcast_to(cross, (8, size)), 0.0), mark, ((0,), (0,)))
    work_ref[:, 0:size] = jnp.where(col == size - 1, side, work_ref[:, 0:size])
    work_ref[:, size : 2 * size] = (row == col).astype(jnp.float32)

    tall = 8
    sub = lax.broadcasted_iota(jnp.int32, (tall, 1), 0)
    for p in range(size // tall):
        panel = work_ref[tall * p : tall * p + tall, :]
        for j in range(tall):
            c = tall * p + j
            scale = lax.rsqrt(panel[j : j + 1, c : c + 1])
            scaled = panel[j : j + 1, :] * scale
            times = jnp.where(sub > j, panel[:, c : c + 1] * scale, 0.0)
            panel = jnp.where(sub == j, scaled, panel - times * scaled)
        work_ref[tall * p : tall * p + tall, :] = panel
        if tall * (p + 1) < size:
            change = dot(panel[:, 0:size], panel, ((0,), (0,)))
            work_ref[tall * (p + 1) : size, :] = work_ref[tall * (p + 1) : size, :] - change[tall * (p + 1) : size]
    factor_ref[...] = jnp.where(col >= row, work_ref[:, 0:size], 0.0)
    inverse = work_ref[:, size : 2 * size]
    for c in range(basis_ref.shape[0]):
        stacked = jnp.concatenate([basis_ref[c], snap_ref[c]], axis=0)
        basis_out_ref[c] = dot(inverse, stacked, ((1,), (0,)))


def local(flow, basis, sample):
    fields, nx, ny, nz = flow.shape
    modes, comps, points = basis.shape
    size = modes + 1
    devices = lax.axis_size("gx") * lax.axis_size("gy") * lax.axis_size("gz")
    count = float(comps * points * devices)
    shape = functools.partial(jax.ShapeDtypeStruct, dtype=jnp.float32)
    call = functools.partial(pl.pallas_call, compiler_params=PARAMS)
    bricks = jnp.transpose(basis, (1, 0, 2))

    ylo, yhi = neighbours(flow[:, :, :DEPTH], flow[:, :, ny - DEPTH :], "gy", False)
    gram = call(gram_kernel, out_shape=shape((size, size)), in_specs=[VMEM], out_specs=VMEM)(bricks)

    gap = jnp.zeros((fields, DEPTH, GAP, nz), jnp.float32)

    def face(start):
        part = slice(start, start + DEPTH)
        return jnp.concatenate([flow[:, part], yhi[:, part], gap, ylo[:, part]], axis=2)

    xlo, xhi = neighbours(face(0), face(nx - DEPTH), "gx", True)

    per = 4
    sent = jnp.pad(gram, ((0, per * devices - size), (0, 0))) if per * devices > size else gram
    summed = lax.all_to_all(sent.reshape(devices, per, size), ALL, 0, 0).reshape(devices * per, size)

    rows = ny + 2 * DEPTH + GAP
    planes = nx + 2 * DEPTH
    parts = -(-fields * planes // (nz // (2 * DEPTH)))
    ext, packed = call(
        edges_kernel,
        out_shape=(shape((fields, planes, rows, nz)), shape((parts, rows, nz))),
        in_specs=[VMEM] * 5,
        out_specs=(VMEM, VMEM),
    )(flow, ylo, yhi, xlo, xhi)
    if lax.axis_size("gz") == 2:
        low = high = lax.ppermute(packed, "gz", [(0, 1), (1, 0)])
    else:
        low, high = neighbours(packed, packed, "gz", True)

    place = lax.axis_index("gy")
    walls = jnp.stack([place == 0, place == lax.axis_size("gy") - 1]).astype(jnp.int32)
    wide = pltpu.VMEM((fields, planes, rows, 2 * nz), jnp.float32)
    flow_next, snapshot, send = call(
        step_kernel,
        out_shape=(shape(flow.shape), shape((comps, 1, points)), shape((devices, per + 4, size))),
        in_specs=[pl.BlockSpec(memory_space=pltpu.SMEM)] + [VMEM] * 6,
        out_specs=(VMEM, VMEM, VMEM),
        scratch_shapes=[pltpu.VMEM((fields, planes, rows, nz), jnp.float32), wide, wide],
    )(walls, ext, low, high, bricks, sample.reshape(1, points), summed)

    got = lax.all_to_all(send, ALL, 0, 0)
    basis_next, factor = call(
        functools.partial(final_kernel, count),
        out_shape=(shape((comps, size, points)), shape((size, size))),
        in_specs=[VMEM] * 3,
        out_specs=(VMEM, VMEM),
        scratch_shapes=[pltpu.VMEM((size, 2 * size), jnp.float32)],
    )(got, bricks, snapshot)
    return flow_next, jnp.transpose(basis_next, (1, 0, 2)), factor


def solution(mesh):
    return jax.shard_map(
        local,
        mesh=mesh,
        in_specs=(
            P(None, "gx", "gy", "gz"),
            P(None, None, ("gx", "gy", "gz")),
            P(("gx", "gy", "gz")),
        ),
        out_specs=(P(None, "gx", "gy", "gz"), P(None, None, ("gx", "gy", "gz")), P()),
        check_vma=False,
    )
```

```python
import functools

import jax
import jax.numpy as jnp
from jax import lax
from jax.experimental import pallas as pl
from jax.experimental.pallas import tpu as pltpu
from jax.sharding import PartitionSpec as P

DT_STEP = 0.35
VISCOSITY = 0.2
SOUND_SQ = 1.0
DRIVING = 0.5

ALL = ("gx", "gy", "gz")
DEPTH = 3
GAP = 2
EXACT = lax.Precision.HIGHEST
VMEM = pl.BlockSpec(memory_space=pltpu.VMEM)
PARAMS = pltpu.CompilerParams(vmem_limit_bytes=40 * 1024 * 1024)


def dot(a, b, dims):
    return lax.dot_general(
        a, b, (dims, ((), ())), precision=EXACT, preferred_element_type=jnp.float32
    )


def neighbours(block_low, block_high, axis, periodic):
    count = lax.axis_size(axis)
    forward = [(i, i + 1) for i in range(count - 1)]
    if periodic:
        forward.append((count - 1, 0))
    backward = [(target, source) for source, target in forward]
    return lax.ppermute(block_high, axis, forward), lax.ppermute(block_low, axis, backward)


def first_kernel(basis_ref, flow_ref, sample_ref, gram_ref, bottom_ref, top_ref, cell_ref):
    modes = basis_ref.shape[1]
    ny = flow_ref.shape[2]
    bottom_ref[...] = flow_ref[:, :, 0:DEPTH]
    top_ref[...] = flow_ref[:, :, ny - DEPTH : ny]
    cell_ref[...] = sample_ref[...]
    total = jnp.zeros((modes, modes), jnp.float32)
    for c in range(basis_ref.shape[0]):
        rows = basis_ref[c]
        total = total + dot(rows, rows, ((1,), (1,)))
    gram_ref[...] = jnp.zeros_like(gram_ref)
    gram_ref[0:modes, 0:modes] = total


def slabs(fields, planes):
    return [(f, i) for f in range(fields) for i in range(planes)]


def spread(index, depth):
    per = 128 // (2 * depth)
    return index // per, 2 * depth * (index % per)


def edges_kernel(flow_ref, ylo_ref, yhi_ref, xlo_ref, xhi_ref, ext_ref, packed_ref):
    fields, nx, ny, nz = flow_ref.shape
    rows = ext_ref.shape[2]
    ext_ref[:, 0:DEPTH] = xlo_ref[...]
    ext_ref[:, DEPTH + nx : 2 * DEPTH + nx] = xhi_ref[...]
    gap = jnp.zeros((GAP, nz), jnp.float32)
    for f, i in slabs(fields, nx):
        plane = jnp.concatenate([flow_ref[f, i], yhi_ref[f, i], gap, ylo_ref[f, i]], axis=0)
        ext_ref[f, DEPTH + i] = plane
    lane = lax.broadcasted_iota(jnp.int32, (rows, nz), 1)
    parts = [jnp.zeros((rows, nz), jnp.float32) for _ in range(packed_ref.shape[0])]
    for s, (f, i) in enumerate(slabs(fields, nx + 2 * DEPTH)):
        part, start = spread(s, DEPTH)
        moved = pltpu.roll(ext_ref[f, i], (start + DEPTH) % nz, 1)
        parts[part] = jnp.where((lane >= start) & (lane < start + 2 * DEPTH), moved, parts[part])
    for k, value in enumerate(parts):
        packed_ref[k] = value


def plane_step(read, i, rows, lanes):
    def step(value, by, axis):
        size = value.shape[axis]
        return pltpu.roll(value, (size - by) % size, axis)

    centre = [read(f, i) for f in range(4)]
    x_plus = [read(f, i + 1)[:rows, :lanes] for f in range(4)]
    x_minus = [read(f, i - 1)[:rows, :lanes] for f in range(4)]
    y_plus = [step(v, 1, 0)[:rows, :lanes] for v in centre]
    y_minus = [step(v, -1, 0)[:rows, :lanes] for v in centre]
    z_plus = [step(v[:rows], 1, 1)[:, :lanes] for v in centre]
    z_minus = [step(v[:rows], -1, 1)[:, :lanes] for v in centre]
    centre = [v[:rows, :lanes] for v in centre]
    slope_x = [0.5 * (a - b) for a, b in zip(x_plus, x_minus)]
    slope_y = [0.5 * (a - b) for a, b in zip(y_plus, y_minus)]
    slope_z = [0.5 * (a - b) for a, b in zip(z_plus, z_minus)]
    pressure = [slope_x[3], slope_y[3], slope_z[3]]
    out = []
    for f in range(3):
        laplace = (
            x_plus[f] + x_minus[f] + (y_plus[f] + y_minus[f]) + (z_plus[f] + z_minus[f]) - 6.0 * centre[f]
        )
        advect = centre[0] * slope_x[f] + centre[1] * slope_y[f] + centre[2] * slope_z[f]
        value = VISCOSITY * laplace - advect - pressure[f]
        if f == 0:
            value = value + DRIVING
        out.append(value)
    out.append(-SOUND_SQ * (slope_x[0] + slope_y[1] + slope_z[2]))
    return centre, out


def step_kernel(
    walls_ref, ext_ref, low_ref, high_ref, basis_ref, sample_ref, summed_ref,
    flow_ref, snap_ref, send_ref,
    halo_ref, one_ref, two_ref,
):
    fields, nx, ny, nz = flow_ref.shape
    rows = ext_ref.shape[2]
    modes = basis_ref.shape[1]
    lane = lax.broadcasted_iota(jnp.int32, (rows, nz), 1)
    row = lax.broadcasted_iota(jnp.int32, (rows, 2 * nz), 0)
    below = (row >= ny + DEPTH + GAP) & (walls_ref[0] == 1)
    above = (row >= ny) & (row < ny + DEPTH) & (walls_ref[1] == 1)
    outside = below | above

    around = [
        jnp.where(lane < nz // 2, high_ref[k], low_ref[k]) for k in range(low_ref.shape[0])
    ]
    for s, (f, i) in enumerate(slabs(fields, nx + 2 * DEPTH)):
        part, start = spread(s, DEPTH)
        halo_ref[f, i] = pltpu.roll(around[part], (2 * nz - start - DEPTH) % nz, 1)

    def read_ext(f, i):
        return jnp.concatenate([ext_ref[f, i], halo_ref[f, i]], axis=1)

    def read_one(f, i):
        return one_ref[f, i]

    def read_two(f, i):
        return two_ref[f, i]

    def first(i, carry):
        centre, rate = plane_step(read_ext, i, rows, 2 * nz)
        for f in range(4):
            one_ref[f, i] = jnp.where(outside, 0.0, centre[f] + DT_STEP * rate[f])
        return carry

    def second(i, carry):
        centre, rate = plane_step(read_one, i, rows, 2 * nz)
        for f in range(4):
            value = 0.75 * read_ext(f, i) + 0.25 * (centre[f] + DT_STEP * rate[f])
            two_ref[f, i] = jnp.where(outside, 0.0, value)
        return carry

    def third(i, carry):
        centre, rate = plane_step(read_two, i, ny, nz)
        for f in range(4):
            start = ext_ref[f, i][:ny]
            flow_ref[f, i - DEPTH] = 1.0 / 3.0 * start + 2.0 / 3.0 * (centre[f] + DT_STEP * rate[f])
        return carry

    lax.fori_loop(1, nx + 2 * DEPTH - 1, first, 0)
    lax.fori_loop(2, nx + 2 * DEPTH - 2, second, 0)
    lax.fori_loop(3, nx + 2 * DEPTH - 3, third, 0)

    points = sample_ref.shape[1]
    spot = jnp.broadcast_to(sample_ref[...], (nz, points))
    place = lax.broadcasted_iota(jnp.int32, (nx * ny, points), 0)
    in_row = (place == jnp.broadcast_to(sample_ref[...] // nz, (nx * ny, points))).astype(jnp.bfloat16)
    in_lane = lax.broadcasted_iota(jnp.int32, (nz, points), 0) == spot % nz
    cross = jnp.zeros((8, modes + 1), jnp.float32)
    for c in range(3):
        field = flow_ref[c].reshape(nx * ny, nz)
        high = field.astype(jnp.bfloat16)
        rest = field - high.astype(jnp.float32)
        middle = rest.astype(jnp.bfloat16)
        low = (rest - middle.astype(jnp.float32)).astype(jnp.bfloat16)
        found = sum(
            lax.dot_general(p, in_row, (((0,), (0,)), ((), ())), preferred_element_type=jnp.float32)
            for p in (high, middle, low)
        )
        picked = jnp.sum(jnp.where(in_lane, found, 0.0), axis=0, keepdims=True)
        snap_ref[c] = picked
        stacked = jnp.concatenate([basis_ref[c], picked], axis=0)
        cross = cross + dot(jnp.broadcast_to(picked, (8, points)), stacked, ((1,), (1,)))

    per = send_ref.shape[1] - 4
    summed = jnp.zeros((8, modes + 1), jnp.float32)
    for k in range(summed_ref.shape[0] // 8):
        summed = summed + summed_ref[8 * k : 8 * k + 8]
    summed = summed + pltpu.roll(summed, 4, 0)
    sub = lax.broadcasted_iota(jnp.int32, summed.shape, 0)
    block = jnp.where(sub < per, summed, jnp.where(sub == per, cross, 0.0))
    for d in range(send_ref.shape[0]):
        send_ref[d] = block


def eliminate(work_ref, tall):
    size = work_ref.shape[0]
    blocks = tall // 8
    sub = lax.broadcasted_iota(jnp.int32, (8, 1), 0)
    for base in range(0, size, tall):
        panel = [work_ref[base + 8 * b : base + 8 * b + 8, :] for b in range(blocks)]
        column = [
            [jnp.broadcast_to(panel[b][:, base + k : base + k + 1], (8, 128)) for b in range(blocks)]
            for k in range(tall)
        ]
        for j in range(tall):
            mine, at = divmod(j, 8)
            scale = lax.rsqrt(column[j][mine][at : at + 1, :])
            times = {b: column[j][b] * scale for b in range(mine, blocks)}
            times[mine] = jnp.where(sub > at, times[mine], 0.0)
            scaled = panel[mine][at : at + 1, :] * jnp.concatenate([scale, scale], axis=1)
            for b in range(mine, blocks):
                value = panel[b] - jnp.concatenate([times[b], times[b]], axis=1) * scaled
                panel[b] = jnp.where(sub == at, scaled, value) if b == mine else value
            for k in range(j + 1, tall):
                other, place = divmod(k, 8)
                for b in range(other, blocks):
                    column[k][b] = column[k][b] - times[b] * times[other][place : place + 1, :]
        for b in range(blocks):
            work_ref[base + 8 * b : base + 8 * b + 8, :] = panel[b]
        if base + tall < size:
            done = work_ref[base : base + tall, :]
            change = dot(done[:, 0:size], done, ((0,), (0,)))
            work_ref[base + tall : size, :] = work_ref[base + tall : size, :] - change[base + tall : size]


def final_kernel(count, got_ref, basis_ref, snap_ref, basis_out_ref, factor_ref, work_ref):
    modes = basis_ref.shape[1]
    size = modes + 1
    per = got_ref.shape[1] - 4
    cross = jnp.zeros((8, size), jnp.float32)
    for d in range(got_ref.shape[0]):
        block = got_ref[d]
        if per * d < size:
            work_ref[per * d : per * d + per, 0:size] = block[0:per] / count
        cross = cross + block
    cross = cross[per : per + 1] / count
    col = lax.broadcasted_iota(jnp.int32, (size, size), 1)
    row = lax.broadcasted_iota(jnp.int32, (size, size), 0)
    work_ref[size - 1 : size, 0:size] = cross
    mark = (lax.broadcasted_iota(jnp.int32, (8, size), 1) == size - 1).astype(jnp.float32)
    top = lax.broadcasted_iota(jnp.int32, (8, size), 0) == 0
    side = dot(jnp.where(top, jnp.broadcast_to(cross, (8, size)), 0.0), mark, ((0,), (0,)))
    work_ref[:, 0:size] = jnp.where(col == size - 1, side, work_ref[:, 0:size])
    work_ref[:, size : 2 * size] = (row == col).astype(jnp.float32)

    eliminate(work_ref, 32)
    factor_ref[...] = jnp.where(col >= row, work_ref[:, 0:size], 0.0)
    inverse = work_ref[:, size : 2 * size]
    for c in range(basis_ref.shape[0]):
        stacked = jnp.concatenate([basis_ref[c], snap_ref[c]], axis=0)
        basis_out_ref[c] = dot(inverse, stacked, ((1,), (0,)))


def local(flow, basis, sample):
    fields, nx, ny, nz = flow.shape
    modes, comps, points = basis.shape
    size = modes + 1
    devices = lax.axis_size("gx") * lax.axis_size("gy") * lax.axis_size("gz")
    count = float(comps * points * devices)
    shape = functools.partial(jax.ShapeDtypeStruct, dtype=jnp.float32)
    call = functools.partial(pl.pallas_call, compiler_params=PARAMS)
    bricks = jnp.transpose(basis, (1, 0, 2))

    strip = shape((fields, nx, DEPTH, nz))
    gram, bottom, top, cells = call(
        first_kernel,
        out_shape=(shape((size, size)), strip, strip, jax.ShapeDtypeStruct((1, points), sample.dtype)),
        in_specs=[VMEM] * 3,
        out_specs=(VMEM,) * 4,
    )(bricks, flow, sample.reshape(1, points))
    ylo, yhi = neighbours(bottom, top, "gy", False)

    gap = jnp.zeros((fields, DEPTH, GAP, nz), jnp.float32)

    def face(start):
        part = slice(start, start + DEPTH)
        return jnp.concatenate([flow[:, part], yhi[:, part], gap, ylo[:, part]], axis=2)

    xlo, xhi = neighbours(face(0), face(nx - DEPTH), "gx", True)

    per = 4
    sent = jnp.pad(gram, ((0, per * devices - size), (0, 0))) if per * devices > size else gram
    summed = lax.all_to_all(sent.reshape(devices, per, size), ALL, 0, 0).reshape(devices * per, size)

    rows = ny + 2 * DEPTH + GAP
    planes = nx + 2 * DEPTH
    parts = -(-fields * planes // (nz // (2 * DEPTH)))
    ext, packed = call(
        edges_kernel,
        out_shape=(shape((fields, planes, rows, nz)), shape((parts, rows, nz))),
        in_specs=[VMEM] * 5,
        out_specs=(VMEM, VMEM),
    )(flow, ylo, yhi, xlo, xhi)
    if lax.axis_size("gz") == 2:
        low = high = lax.ppermute(packed, "gz", [(0, 1), (1, 0)])
    else:
        low, high = neighbours(packed, packed, "gz", True)

    place = lax.axis_index("gy")
    walls = jnp.stack([place == 0, place == lax.axis_size("gy") - 1]).astype(jnp.int32)
    wide = pltpu.VMEM((fields, planes, rows, 2 * nz), jnp.float32)
    flow_next, snapshot, send = call(
        step_kernel,
        out_shape=(shape(flow.shape), shape((comps, 1, points)), shape((devices, per + 4, size))),
        in_specs=[pl.BlockSpec(memory_space=pltpu.SMEM)] + [VMEM] * 6,
        out_specs=(VMEM, VMEM, VMEM),
        scratch_shapes=[pltpu.VMEM((fields, planes, rows, nz), jnp.float32), wide, wide],
    )(walls, ext, low, high, bricks, cells, summed)

    got = lax.all_to_all(send, ALL, 0, 0)
    basis_next, factor = call(
        functools.partial(final_kernel, count),
        out_shape=(shape((comps, size, points)), shape((size, size))),
        in_specs=[VMEM] * 3,
        out_specs=(VMEM, VMEM),
        scratch_shapes=[pltpu.VMEM((size, 2 * size), jnp.float32)],
    )(got, bricks, snapshot)
    return flow_next, jnp.transpose(basis_next, (1, 0, 2)), factor


def solution(mesh):
    return jax.shard_map(
        local,
        mesh=mesh,
        in_specs=(
            P(None, "gx", "gy", "gz"),
            P(None, None, ("gx", "gy", "gz")),
            P(("gx", "gy", "gz")),
        ),
        out_specs=(P(None, "gx", "gy", "gz"), P(None, None, ("gx", "gy", "gz")), P()),
        check_vma=False,
    )
```

```python
import functools

import jax
import jax.numpy as jnp
from jax import lax
from jax.experimental import pallas as pl
from jax.experimental.pallas import tpu as pltpu
from jax.sharding import PartitionSpec as P

DT_STEP = 0.35
VISCOSITY = 0.2
SOUND_SQ = 1.0
DRIVING = 0.5

ALL = ("gx", "gy", "gz")
DEPTH = 3
GAP = 2
EXACT = lax.Precision.HIGHEST
VMEM = pl.BlockSpec(memory_space=pltpu.VMEM)
PARAMS = pltpu.CompilerParams(vmem_limit_bytes=40 * 1024 * 1024)


def dot(a, b, dims):
    return lax.dot_general(
        a, b, (dims, ((), ())), precision=EXACT, preferred_element_type=jnp.float32
    )


def neighbours(block_low, block_high, axis, periodic):
    count = lax.axis_size(axis)
    forward = [(i, i + 1) for i in range(count - 1)]
    if periodic:
        forward.append((count - 1, 0))
    backward = [(target, source) for source, target in forward]
    return lax.ppermute(block_high, axis, forward), lax.ppermute(block_low, axis, backward)


def gram_kernel(basis_ref, gram_ref):
    modes = basis_ref.shape[1]
    total = jnp.zeros((modes, modes), jnp.float32)
    for c in range(basis_ref.shape[0]):
        rows = basis_ref[c]
        total = total + dot(rows, rows, ((1,), (1,)))
    gram_ref[...] = jnp.zeros_like(gram_ref)
    gram_ref[0:modes, 0:modes] = total


def strips_kernel(flow_hbm, bottom_ref, top_ref, flow_ref, sem):
    ny = flow_ref.shape[2]
    copy = pltpu.make_async_copy(flow_hbm, flow_ref, sem)
    copy.start()
    copy.wait()
    bottom_ref[...] = flow_ref[:, :, 0:DEPTH]
    top_ref[...] = flow_ref[:, :, ny - DEPTH : ny]


def slabs(fields, planes):
    return [(f, i) for f in range(fields) for i in range(planes)]


def spread(index, depth):
    per = 128 // (2 * depth)
    return index // per, 2 * depth * (index % per)


def edges_kernel(flow_ref, ylo_ref, yhi_ref, xlo_ref, xhi_ref, ext_ref, packed_ref):
    fields, nx, ny, nz = flow_ref.shape
    rows = ext_ref.shape[2]
    ext_ref[:, 0:DEPTH] = xlo_ref[...]
    ext_ref[:, DEPTH + nx : 2 * DEPTH + nx] = xhi_ref[...]
    gap = jnp.zeros((GAP, nz), jnp.float32)
    for f, i in slabs(fields, nx):
        plane = jnp.concatenate([flow_ref[f, i], yhi_ref[f, i], gap, ylo_ref[f, i]], axis=0)
        ext_ref[f, DEPTH + i] = plane
    lane = lax.broadcasted_iota(jnp.int32, (rows, nz), 1)
    parts = [jnp.zeros((rows, nz), jnp.float32) for _ in range(packed_ref.shape[0])]
    for s, (f, i) in enumerate(slabs(fields, nx + 2 * DEPTH)):
        part, start = spread(s, DEPTH)
        moved = pltpu.roll(ext_ref[f, i], (start + DEPTH) % nz, 1)
        parts[part] = jnp.where((lane >= start) & (lane < start + 2 * DEPTH), moved, parts[part])
    for k, value in enumerate(parts):
        packed_ref[k] = value


def plane_step(read, i, rows, lanes):
    def step(value, by, axis):
        size = value.shape[axis]
        return pltpu.roll(value, (size - by) % size, axis)

    centre = [read(f, i) for f in range(4)]
    x_plus = [read(f, i + 1)[:rows, :lanes] for f in range(4)]
    x_minus = [read(f, i - 1)[:rows, :lanes] for f in range(4)]
    y_plus = [step(v, 1, 0)[:rows, :lanes] for v in centre]
    y_minus = [step(v, -1, 0)[:rows, :lanes] for v in centre]
    z_plus = [step(v[:rows], 1, 1)[:, :lanes] for v in centre]
    z_minus = [step(v[:rows], -1, 1)[:, :lanes] for v in centre]
    centre = [v[:rows, :lanes] for v in centre]
    slope_x = [0.5 * (a - b) for a, b in zip(x_plus, x_minus)]
    slope_y = [0.5 * (a - b) for a, b in zip(y_plus, y_minus)]
    slope_z = [0.5 * (a - b) for a, b in zip(z_plus, z_minus)]
    pressure = [slope_x[3], slope_y[3], slope_z[3]]
    out = []
    for f in range(3):
        laplace = (
            x_plus[f] + x_minus[f] + (y_plus[f] + y_minus[f]) + (z_plus[f] + z_minus[f]) - 6.0 * centre[f]
        )
        advect = centre[0] * slope_x[f] + centre[1] * slope_y[f] + centre[2] * slope_z[f]
        value = VISCOSITY * laplace - advect - pressure[f]
        if f == 0:
            value = value + DRIVING
        out.append(value)
    out.append(-SOUND_SQ * (slope_x[0] + slope_y[1] + slope_z[2]))
    return centre, out


def step_kernel(
    walls_ref, ext_ref, low_ref, high_ref, basis_ref, sample_ref,
    flow_ref, snap_ref, cross_ref,
    halo_ref, one_ref, two_ref,
):
    fields, nx, ny, nz = flow_ref.shape
    rows = ext_ref.shape[2]
    modes = basis_ref.shape[1]
    lane = lax.broadcasted_iota(jnp.int32, (rows, nz), 1)
    row = lax.broadcasted_iota(jnp.int32, (rows, 2 * nz), 0)
    below = (row >= ny + DEPTH + GAP) & (walls_ref[0] == 1)
    above = (row >= ny) & (row < ny + DEPTH) & (walls_ref[1] == 1)
    outside = below | above

    around = [
        jnp.where(lane < nz // 2, high_ref[k], low_ref[k]) for k in range(low_ref.shape[0])
    ]
    for s, (f, i) in enumerate(slabs(fields, nx + 2 * DEPTH)):
        part, start = spread(s, DEPTH)
        halo_ref[f, i] = pltpu.roll(around[part], (2 * nz - start - DEPTH) % nz, 1)

    def read_ext(f, i):
        return jnp.concatenate([ext_ref[f, i], halo_ref[f, i]], axis=1)

    def read_one(f, i):
        return one_ref[f, i]

    def read_two(f, i):
        return two_ref[f, i]

    def first(i, carry):
        centre, rate = plane_step(read_ext, i, rows, 2 * nz)
        for f in range(4):
            one_ref[f, i] = jnp.where(outside, 0.0, centre[f] + DT_STEP * rate[f])
        return carry

    def second(i, carry):
        centre, rate = plane_step(read_one, i, rows, 2 * nz)
        for f in range(4):
            value = 0.75 * read_ext(f, i) + 0.25 * (centre[f] + DT_STEP * rate[f])
            two_ref[f, i] = jnp.where(outside, 0.0, value)
        return carry

    def third(i, carry):
        centre, rate = plane_step(read_two, i, ny, nz)
        for f in range(4):
            start = ext_ref[f, i][:ny]
            flow_ref[f, i - DEPTH] = 1.0 / 3.0 * start + 2.0 / 3.0 * (centre[f] + DT_STEP * rate[f])
        return carry

    lax.fori_loop(1, nx + 2 * DEPTH - 1, first, 0)
    lax.fori_loop(2, nx + 2 * DEPTH - 2, second, 0)
    lax.fori_loop(3, nx + 2 * DEPTH - 3, third, 0)

    points = sample_ref.shape[1]
    spot = jnp.broadcast_to(sample_ref[...], (nz, points))
    place = lax.broadcasted_iota(jnp.int32, (nx * ny, points), 0)
    in_row = (place == jnp.broadcast_to(sample_ref[...] // nz, (nx * ny, points))).astype(jnp.bfloat16)
    in_lane = lax.broadcasted_iota(jnp.int32, (nz, points), 0) == spot % nz
    cross = jnp.zeros((8, modes + 1), jnp.float32)
    for c in range(3):
        field = flow_ref[c].reshape(nx * ny, nz)
        high = field.astype(jnp.bfloat16)
        rest = field - high.astype(jnp.float32)
        middle = rest.astype(jnp.bfloat16)
        low = (rest - middle.astype(jnp.float32)).astype(jnp.bfloat16)
        found = sum(
            lax.dot_general(p, in_row, (((0,), (0,)), ((), ())), preferred_element_type=jnp.float32)
            for p in (high, middle, low)
        )
        picked = jnp.sum(jnp.where(in_lane, found, 0.0), axis=0, keepdims=True)
        snap_ref[c] = picked
        stacked = jnp.concatenate([basis_ref[c], picked], axis=0)
        cross = cross + dot(jnp.broadcast_to(picked, (8, points)), stacked, ((1,), (1,)))

    cross_ref[...] = cross


def merge_kernel(summed_ref, cross_ref, send_ref):
    per = send_ref.shape[1] - 4
    summed = jnp.zeros(cross_ref.shape, jnp.float32)
    for k in range(summed_ref.shape[0] // 8):
        summed = summed + summed_ref[8 * k : 8 * k + 8]
    summed = summed + pltpu.roll(summed, 4, 0)
    sub = lax.broadcasted_iota(jnp.int32, summed.shape, 0)
    block = jnp.where(sub < per, summed, jnp.where(sub == per, cross_ref[...], 0.0))
    for d in range(send_ref.shape[0]):
        send_ref[d] = block


def eliminate(work_ref, tall):
    size = work_ref.shape[0]
    blocks = tall // 8
    sub = lax.broadcasted_iota(jnp.int32, (8, 1), 0)
    for base in range(0, size, tall):
        panel = [work_ref[base + 8 * b : base + 8 * b + 8, :] for b in range(blocks)]
        column = [
            [jnp.broadcast_to(panel[b][:, base + k : base + k + 1], (8, 128)) for b in range(blocks)]
            for k in range(tall)
        ]
        for j in range(tall):
            mine, at = divmod(j, 8)
            scale = lax.rsqrt(column[j][mine][at : at + 1, :])
            times = {b: column[j][b] * scale for b in range(mine, blocks)}
            times[mine] = jnp.where(sub > at, times[mine], 0.0)
            scaled = panel[mine][at : at + 1, :] * jnp.concatenate([scale, scale], axis=1)
            for b in range(mine, blocks):
                value = panel[b] - jnp.concatenate([times[b], times[b]], axis=1) * scaled
                panel[b] = jnp.where(sub == at, scaled, value) if b == mine else value
            for k in range(j + 1, tall):
                other, place = divmod(k, 8)
                for b in range(other, blocks):
                    column[k][b] = column[k][b] - times[b] * times[other][place : place + 1, :]
        for b in range(blocks):
            work_ref[base + 8 * b : base + 8 * b + 8, :] = panel[b]
        if base + tall < size:
            done = work_ref[base : base + tall, :]
            change = dot(done[:, 0:size], done, ((0,), (0,)))
            work_ref[base + tall : size, :] = work_ref[base + tall : size, :] - change[base + tall : size]


def final_kernel(count, got_ref, basis_ref, snap_ref, basis_out_ref, factor_ref, work_ref):
    modes = basis_ref.shape[1]
    size = modes + 1
    per = got_ref.shape[1] - 4
    cross = jnp.zeros((8, size), jnp.float32)
    for d in range(got_ref.shape[0]):
        block = got_ref[d]
        if per * d < size:
            work_ref[per * d : per * d + per, 0:size] = block[0:per] / count
        cross = cross + block
    cross = cross[per : per + 1] / count
    col = lax.broadcasted_iota(jnp.int32, (size, size), 1)
    row = lax.broadcasted_iota(jnp.int32, (size, size), 0)
    work_ref[size - 1 : size, 0:size] = cross
    mark = (lax.broadcasted_iota(jnp.int32, (8, size), 1) == size - 1).astype(jnp.float32)
    top = lax.broadcasted_iota(jnp.int32, (8, size), 0) == 0
    side = dot(jnp.where(top, jnp.broadcast_to(cross, (8, size)), 0.0), mark, ((0,), (0,)))
    work_ref[:, 0:size] = jnp.where(col == size - 1, side, work_ref[:, 0:size])
    work_ref[:, size : 2 * size] = (row == col).astype(jnp.float32)

    eliminate(work_ref, 32)
    factor_ref[...] = jnp.where(col >= row, work_ref[:, 0:size], 0.0)
    inverse = work_ref[:, size : 2 * size]
    for c in range(basis_ref.shape[0]):
        stacked = jnp.concatenate([basis_ref[c], snap_ref[c]], axis=0)
        basis_out_ref[c] = dot(inverse, stacked, ((1,), (0,)))


def local(flow, basis, sample):
    fields, nx, ny, nz = flow.shape
    modes, comps, points = basis.shape
    size = modes + 1
    devices = lax.axis_size("gx") * lax.axis_size("gy") * lax.axis_size("gz")
    count = float(comps * points * devices)
    shape = functools.partial(jax.ShapeDtypeStruct, dtype=jnp.float32)
    call = functools.partial(pl.pallas_call, compiler_params=PARAMS)
    bricks = jnp.transpose(basis, (1, 0, 2))

    strip = shape((fields, nx, DEPTH, nz))
    bottom, top = call(
        strips_kernel,
        out_shape=(strip, strip),
        in_specs=[pl.BlockSpec(memory_space=pltpu.HBM)],
        out_specs=(VMEM, VMEM),
        scratch_shapes=[pltpu.VMEM(flow.shape, jnp.float32), pltpu.SemaphoreType.DMA],
    )(flow)
    ylo, yhi = neighbours(bottom, top, "gy", False)
    gram = call(gram_kernel, out_shape=shape((size, size)), in_specs=[VMEM], out_specs=VMEM)(bricks)
    ylo, yhi, gram = lax.optimization_barrier((ylo, yhi, gram))

    gap = jnp.zeros((fields, DEPTH, GAP, nz), jnp.float32)

    def face(start):
        part = slice(start, start + DEPTH)
        return jnp.concatenate([flow[:, part], yhi[:, part], gap, ylo[:, part]], axis=2)

    xlo, xhi = neighbours(face(0), face(nx - DEPTH), "gx", True)

    per = 4
    sent = jnp.pad(gram, ((0, per * devices - size), (0, 0))) if per * devices > size else gram
    summed = lax.all_to_all(sent.reshape(devices, per, size), ALL, 0, 0).reshape(devices * per, size)

    rows = ny + 2 * DEPTH + GAP
    planes = nx + 2 * DEPTH
    parts = -(-fields * planes // (nz // (2 * DEPTH)))
    ext, packed = call(
        edges_kernel,
        out_shape=(shape((fields, planes, rows, nz)), shape((parts, rows, nz))),
        in_specs=[VMEM] * 5,
        out_specs=(VMEM, VMEM),
    )(flow, ylo, yhi, xlo, xhi)
    if lax.axis_size("gz") == 2:
        low = high = lax.ppermute(packed, "gz", [(0, 1), (1, 0)])
    else:
        low, high = neighbours(packed, packed, "gz", True)

    place = lax.axis_index("gy")
    walls = jnp.stack([place == 0, place == lax.axis_size("gy") - 1]).astype(jnp.int32)
    wide = pltpu.VMEM((fields, planes, rows, 2 * nz), jnp.float32)
    flow_next, snapshot, cross = call(
        step_kernel,
        out_shape=(shape(flow.shape), shape((comps, 1, points)), shape((8, size))),
        in_specs=[pl.BlockSpec(memory_space=pltpu.SMEM)] + [VMEM] * 5,
        out_specs=(VMEM, VMEM, VMEM),
        scratch_shapes=[pltpu.VMEM((fields, planes, rows, nz), jnp.float32), wide, wide],
    )(walls, ext, low, high, bricks, sample.reshape(1, points))

    send = call(
        merge_kernel, out_shape=shape((devices, per + 4, size)), in_specs=[VMEM] * 2, out_specs=VMEM
    )(summed, cross)
    got = lax.all_to_all(send, ALL, 0, 0)
    basis_next, factor = call(
        functools.partial(final_kernel, count),
        out_shape=(shape((comps, size, points)), shape((size, size))),
        in_specs=[VMEM] * 3,
        out_specs=(VMEM, VMEM),
        scratch_shapes=[pltpu.VMEM((size, 2 * size), jnp.float32)],
    )(got, bricks, snapshot)
    return flow_next, jnp.transpose(basis_next, (1, 0, 2)), factor


def solution(mesh):
    return jax.shard_map(
        local,
        mesh=mesh,
        in_specs=(
            P(None, "gx", "gy", "gz"),
            P(None, None, ("gx", "gy", "gz")),
            P(("gx", "gy", "gz")),
        ),
        out_specs=(P(None, "gx", "gy", "gz"), P(None, None, ("gx", "gy", "gz")), P()),
        check_vma=False,
    )
```

```python
import functools

import jax
import jax.numpy as jnp
from jax import lax
from jax.experimental import pallas as pl
from jax.experimental.pallas import tpu as pltpu
from jax.sharding import PartitionSpec as P

DT_STEP = 0.35
VISCOSITY = 0.2
SOUND_SQ = 1.0
DRIVING = 0.5

ALL = ("gx", "gy", "gz")
DEPTH = 3
GAP = 2
EXACT = lax.Precision.HIGHEST
VMEM = pl.BlockSpec(memory_space=pltpu.VMEM)
PARAMS = pltpu.CompilerParams(vmem_limit_bytes=40 * 1024 * 1024)


def dot(a, b, dims):
    return lax.dot_general(
        a, b, (dims, ((), ())), precision=EXACT, preferred_element_type=jnp.float32
    )


def neighbours(block_low, block_high, axis):
    count = lax.axis_size(axis)
    forward = [(i, (i + 1) % count) for i in range(count)]
    backward = [(target, source) for source, target in forward]
    return lax.ppermute(block_high, axis, forward), lax.ppermute(block_low, axis, backward)


def gram_kernel(basis_ref, gram_ref):
    modes = basis_ref.shape[1]
    total = jnp.zeros((modes, modes), jnp.float32)
    for c in range(basis_ref.shape[0]):
        rows = basis_ref[c]
        total = total + dot(rows, rows, ((1,), (1,)))
    gram_ref[...] = jnp.zeros_like(gram_ref)
    gram_ref[0:modes, 0:modes] = total


def strips_kernel(flow_hbm, bottom_ref, top_ref, flow_ref, sem):
    ny = flow_ref.shape[2]
    copy = pltpu.make_async_copy(flow_hbm, flow_ref, sem)
    copy.start()
    copy.wait()
    bottom_ref[...] = flow_ref[:, :, 0:DEPTH]
    top_ref[...] = flow_ref[:, :, ny - DEPTH : ny]


def walls_kernel(walls_ref, flow_ref, ylo_ref, yhi_ref, mid_ref, first_ref, last_ref):
    fields, nx, ny, nz = flow_ref.shape
    gap = jnp.zeros((GAP, nz), jnp.float32)
    for f in range(fields):
        for i in range(nx):
            below = jnp.where(walls_ref[0] == 1, 0.0, ylo_ref[f, i])
            above = jnp.where(walls_ref[1] == 1, 0.0, yhi_ref[f, i])
            plane = jnp.concatenate([flow_ref[f, i], above, gap, below], axis=0)
            mid_ref[f, i] = plane
            if i < DEPTH:
                first_ref[f, i] = plane
            if i >= nx - DEPTH:
                last_ref[f, i - nx + DEPTH] = plane


def plane_of(mid_ref, xlo_ref, xhi_ref, f, i):
    nx = mid_ref.shape[1]
    if i < DEPTH:
        return xlo_ref[f, i]
    if i < DEPTH + nx:
        return mid_ref[f, i - DEPTH]
    return xhi_ref[f, i - DEPTH - nx]


GROUP = 8


def pack_kernel(mid_ref, xlo_ref, xhi_ref, packed_ref):
    fields, nx, rows, nz = mid_ref.shape
    lane = lax.broadcasted_iota(jnp.int32, (rows, nz), 1)
    for f in range(fields):
        value = jnp.zeros((rows, nz), jnp.float32)
        for i in range(nx + 2 * DEPTH):
            start = GROUP * i
            moved = pltpu.roll(plane_of(mid_ref, xlo_ref, xhi_ref, f, i), (start + DEPTH) % nz, 1)
            value = jnp.where((lane >= start) & (lane < start + 2 * DEPTH), moved, value)
        packed_ref[f] = value


def step(value, by, axis):
    size = value.shape[axis]
    return pltpu.roll(value, (size - by) % size, axis)


def rates(centre, x_plus, x_minus, y_plus, y_minus, z_plus, z_minus):
    slope_x = [0.5 * (a - b) for a, b in zip(x_plus, x_minus)]
    slope_y = [0.5 * (a - b) for a, b in zip(y_plus, y_minus)]
    slope_z = [0.5 * (a - b) for a, b in zip(z_plus, z_minus)]
    pressure = [slope_x[3], slope_y[3], slope_z[3]]
    out = []
    for f in range(3):
        laplace = (
            x_plus[f] + x_minus[f] + (y_plus[f] + y_minus[f]) + (z_plus[f] + z_minus[f]) - 6.0 * centre[f]
        )
        advect = centre[0] * slope_x[f] + centre[1] * slope_y[f] + centre[2] * slope_z[f]
        value = VISCOSITY * laplace - advect - pressure[f]
        if f == 0:
            value = value + DRIVING
        out.append(value)
    out.append(-SOUND_SQ * (slope_x[0] + slope_y[1] + slope_z[2]))
    return out


def step_kernel(
    walls_ref, mid_ref, xlo_ref, xhi_ref, own_ref, low_ref, high_ref, basis_ref, sample_ref,
    flow_ref, snap_ref, cross_ref,
    one_ref, two_ref,
):
    fields, nx, ny, nz = flow_ref.shape
    rows = mid_ref.shape[2]
    modes = basis_ref.shape[1]
    lane = lax.broadcasted_iota(jnp.int32, (rows, nz), 1)
    row = lax.broadcasted_iota(jnp.int32, (rows, nz), 0)
    below = (row >= ny + DEPTH + GAP) & (walls_ref[0] == 1)
    above = (row >= ny) & (row < ny + DEPTH) & (walls_ref[1] == 1)
    outside = below | above
    every = range(4)

    def start(f, i):
        return plane_of(mid_ref, xlo_ref, xhi_ref, f, i)

    def after_one(value, rate):
        return jnp.where(outside, 0.0, value + DT_STEP * rate)

    def after_two(begin, value, rate):
        return jnp.where(outside, 0.0, 0.75 * begin + 0.25 * (value + DT_STEP * rate))

    left = lane % GROUP < DEPTH

    def window_rates(q):
        return rates(
            q, [step(v, GROUP, 1) for v in q], [step(v, -GROUP, 1) for v in q],
            [step(v, 1, 0) for v in q], [step(v, -1, 0) for v in q],
            [step(v, 1, 1) for v in q], [step(v, -1, 1) for v in q],
        )

    own = [own_ref[f] for f in every]
    other = [jnp.where(left, low_ref[f], high_ref[f]) for f in every]
    ends = [other]
    windows = []
    for parts in ((other, own), (own, other)):
        q0 = [jnp.where(left, a, b) for a, b in zip(*parts)]
        q1 = [after_one(v, r) for v, r in zip(q0, window_rates(q0))]
        q2 = [after_two(s, v, r) for s, v, r in zip(q0, q1, window_rates(q1))]
        windows.append((q1, q2))
    for stage in (0, 1):
        ends.append([jnp.where(left, a, b) for a, b in zip(windows[0][stage], windows[1][stage])])

    def plane_rates(read, beyond, i, rows):
        centre = [read(f, i) for f in every]
        z_plus, z_minus = [], []
        for f in every:
            end = pltpu.roll(beyond[f], (2 * nz - GROUP * i - DEPTH) % nz, 1)[:rows]
            z_plus.append(step(jnp.where(lane[:rows] == 0, end, centre[f][:rows]), 1, 1))
            z_minus.append(step(jnp.where(lane[:rows] == nz - 1, end, centre[f][:rows]), -1, 1))
        y_plus = [step(v, 1, 0)[:rows] for v in centre]
        y_minus = [step(v, -1, 0)[:rows] for v in centre]
        centre = [v[:rows] for v in centre]
        x_plus = [read(f, i + 1)[:rows] for f in every]
        x_minus = [read(f, i - 1)[:rows] for f in every]
        return centre, rates(centre, x_plus, x_minus, y_plus, y_minus, z_plus, z_minus)

    planes = nx + 2 * DEPTH
    for i in range(1, planes - 1):
        centre, rate = plane_rates(start, ends[0], i, rows)
        for f in every:
            one_ref[f, i] = after_one(centre[f], rate[f])
    for i in range(2, planes - 2):
        centre, rate = plane_rates(lambda f, i: one_ref[f, i], ends[1], i, rows)
        for f in every:
            two_ref[f, i] = after_two(start(f, i), centre[f], rate[f])
    for i in range(3, planes - 3):
        centre, rate = plane_rates(lambda f, i: two_ref[f, i], ends[2], i, ny)
        for f in every:
            value = 1.0 / 3.0 * start(f, i)[:ny] + 2.0 / 3.0 * (centre[f] + DT_STEP * rate[f])
            flow_ref[f, i - DEPTH] = value

    points = sample_ref.shape[1]
    spot = jnp.broadcast_to(sample_ref[...], (nz, points))
    place = lax.broadcasted_iota(jnp.int32, (nx * ny, points), 0)
    in_row = (place == jnp.broadcast_to(sample_ref[...] // nz, (nx * ny, points))).astype(jnp.bfloat16)
    in_lane = lax.broadcasted_iota(jnp.int32, (nz, points), 0) == spot % nz
    cross = jnp.zeros((8, modes + 1), jnp.float32)
    for c in range(3):
        field = flow_ref[c].reshape(nx * ny, nz).T
        high = field.astype(jnp.bfloat16)
        rest = field - high.astype(jnp.float32)
        middle = rest.astype(jnp.bfloat16)
        low = (rest - middle.astype(jnp.float32)).astype(jnp.bfloat16)
        found = sum(
            lax.dot_general(p, in_row, (((1,), (0,)), ((), ())), preferred_element_type=jnp.float32)
            for p in (high, middle, low)
        )
        picked = jnp.sum(jnp.where(in_lane, found, 0.0), axis=0, keepdims=True)
        snap_ref[c] = picked
        stacked = jnp.concatenate([basis_ref[c], picked], axis=0)
        cross = cross + dot(jnp.broadcast_to(picked, (8, points)), stacked, ((1,), (1,)))
    cross_ref[...] = cross


def merge_kernel(summed_ref, cross_ref, send_ref):
    per = send_ref.shape[1] - 4
    summed = jnp.zeros(cross_ref.shape, jnp.float32)
    for k in range(summed_ref.shape[0] // 8):
        summed = summed + summed_ref[8 * k : 8 * k + 8]
    summed = summed + pltpu.roll(summed, 4, 0)
    sub = lax.broadcasted_iota(jnp.int32, summed.shape, 0)
    block = jnp.where(sub < per, summed, jnp.where(sub == per, cross_ref[...], 0.0))
    for d in range(send_ref.shape[0]):
        send_ref[d] = block


def eliminate(work_ref, tall):
    size = work_ref.shape[0]
    blocks = tall // 8
    sub = lax.broadcasted_iota(jnp.int32, (8, 1), 0)
    for base in range(0, size, tall):
        panel = [work_ref[base + 8 * b : base + 8 * b + 8, :] for b in range(blocks)]
        column = [
            [jnp.broadcast_to(panel[b][:, base + k : base + k + 1], (8, 128)) for b in range(blocks)]
            for k in range(tall)
        ]
        for j in range(tall):
            mine, at = divmod(j, 8)
            scale = lax.rsqrt(column[j][mine][at : at + 1, :])
            times = {b: column[j][b] * scale for b in range(mine, blocks)}
            times[mine] = jnp.where(sub > at, times[mine], 0.0)
            scaled = panel[mine][at : at + 1, :] * jnp.concatenate([scale, scale], axis=1)
            for b in range(mine, blocks):
                value = panel[b] - jnp.concatenate([times[b], times[b]], axis=1) * scaled
                panel[b] = jnp.where(sub == at, scaled, value) if b == mine else value
            for k in range(j + 1, tall):
                other, place = divmod(k, 8)
                for b in range(other, blocks):
                    column[k][b] = column[k][b] - times[b] * times[other][place : place + 1, :]
        for b in range(blocks):
            work_ref[base + 8 * b : base + 8 * b + 8, :] = panel[b]
        if base + tall < size:
            done = work_ref[base : base + tall, :]
            change = dot(done[:, 0:size], done, ((0,), (0,)))
            work_ref[base + tall : size, :] = work_ref[base + tall : size, :] - change[base + tall : size]


def final_kernel(
    count, got_ref, basis_ref, snap_ref, flow_ref,
    basis_hbm, factor_hbm, flow_hbm,
    work_ref, basis_out_ref, factor_ref, sems,
):
    modes = basis_ref.shape[1]
    size = modes + 1
    per = got_ref.shape[1] - 4
    copies = [pltpu.make_async_copy(flow_ref, flow_hbm, sems.at[0])]
    copies[0].start()
    cross = jnp.zeros((8, size), jnp.float32)
    for d in range(got_ref.shape[0]):
        block = got_ref[d]
        if per * d < size:
            work_ref[per * d : per * d + per, 0:size] = block[0:per] / count
        cross = cross + block
    cross = cross[per : per + 1] / count
    col = lax.broadcasted_iota(jnp.int32, (size, size), 1)
    row = lax.broadcasted_iota(jnp.int32, (size, size), 0)
    work_ref[size - 1 : size, 0:size] = cross
    mark = (lax.broadcasted_iota(jnp.int32, (8, size), 1) == size - 1).astype(jnp.float32)
    top = lax.broadcasted_iota(jnp.int32, (8, size), 0) == 0
    side = dot(jnp.where(top, jnp.broadcast_to(cross, (8, size)), 0.0), mark, ((0,), (0,)))
    work_ref[:, 0:size] = jnp.where(col == size - 1, side, work_ref[:, 0:size])
    work_ref[:, size : 2 * size] = (row == col).astype(jnp.float32)
    eliminate(work_ref, 32)
    factor_ref[...] = jnp.where(col >= row, work_ref[:, 0:size], 0.0)
    copies.append(pltpu.make_async_copy(factor_ref, factor_hbm, sems.at[1]))
    copies[1].start()
    inverse = work_ref[:, size : 2 * size]
    for c in range(basis_ref.shape[0]):
        stacked = jnp.concatenate([basis_ref[c], snap_ref[c]], axis=0)
        basis_out_ref[c] = dot(inverse, stacked, ((1,), (0,)))
        copies.append(pltpu.make_async_copy(basis_out_ref.at[c], basis_hbm.at[c], sems.at[2 + c]))
        copies[-1].start()
    for copy in copies:
        copy.wait()


def local(flow, basis, sample):
    fields, nx, ny, nz = flow.shape
    modes, comps, points = basis.shape
    size = modes + 1
    devices = lax.axis_size("gx") * lax.axis_size("gy") * lax.axis_size("gz")
    count = float(comps * points * devices)
    shape = functools.partial(jax.ShapeDtypeStruct, dtype=jnp.float32)
    call = functools.partial(pl.pallas_call, compiler_params=PARAMS)
    bricks = jnp.transpose(basis, (1, 0, 2))

    strip = shape((fields, nx, DEPTH, nz))
    bottom, top = call(
        strips_kernel,
        out_shape=(strip, strip),
        in_specs=[pl.BlockSpec(memory_space=pltpu.HBM)],
        out_specs=(VMEM, VMEM),
        scratch_shapes=[pltpu.VMEM(flow.shape, jnp.float32), pltpu.SemaphoreType.DMA],
    )(flow)
    ylo, yhi = neighbours(bottom, top, "gy")
    gram = call(gram_kernel, out_shape=shape((size, size)), in_specs=[VMEM], out_specs=VMEM)(bricks)
    ylo, yhi, gram = lax.optimization_barrier((ylo, yhi, gram))

    rows = ny + 2 * DEPTH + GAP
    place = lax.axis_index("gy")
    walls = jnp.stack([place == 0, place == lax.axis_size("gy") - 1]).astype(jnp.int32)
    face = shape((fields, DEPTH, rows, nz))
    mid, first, last = call(
        walls_kernel,
        out_shape=(shape((fields, nx, rows, nz)), face, face),
        in_specs=[pl.BlockSpec(memory_space=pltpu.SMEM)] + [VMEM] * 3,
        out_specs=(VMEM,) * 3,
    )(walls, flow, ylo, yhi)
    xlo, xhi = neighbours(first, last, "gx")

    per = 4
    sent = jnp.pad(gram, ((0, per * devices - size), (0, 0))) if per * devices > size else gram
    summed = lax.all_to_all(sent.reshape(devices, per, size), ALL, 0, 0).reshape(devices * per, size)

    packed = call(
        pack_kernel, out_shape=shape((fields, rows, nz)), in_specs=[VMEM] * 3, out_specs=VMEM
    )(mid, xlo, xhi)
    if lax.axis_size("gz") == 2:
        low = high = lax.ppermute(packed, "gz", [(0, 1), (1, 0)])
    else:
        low, high = neighbours(packed, packed, "gz")

    between = pltpu.VMEM((fields, nx + 2 * DEPTH, rows, nz), jnp.float32)
    flow_new, snapshot, cross = call(
        step_kernel,
        out_shape=(shape(flow.shape), shape((comps, 1, points)), shape((8, size))),
        in_specs=[pl.BlockSpec(memory_space=pltpu.SMEM)] + [VMEM] * 8,
        out_specs=(VMEM, VMEM, VMEM),
        scratch_shapes=[between, between],
    )(walls, mid, xlo, xhi, packed, low, high, bricks, sample.reshape(1, points))

    send = call(
        merge_kernel, out_shape=shape((devices, per + 4, size)), in_specs=[VMEM] * 2, out_specs=VMEM
    )(summed, cross)
    got = lax.all_to_all(send, ALL, 0, 0)
    whole = pl.BlockSpec(memory_space=pltpu.HBM)
    basis_next, factor, flow_next = call(
        functools.partial(final_kernel, count),
        out_shape=(shape((comps, size, points)), shape((size, size)), shape(flow.shape)),
        in_specs=[VMEM] * 4,
        out_specs=(whole,) * 3,
        scratch_shapes=[
            pltpu.VMEM((size, 2 * size), jnp.float32),
            pltpu.VMEM((comps, size, points), jnp.float32),
            pltpu.VMEM((size, size), jnp.float32),
            pltpu.SemaphoreType.DMA((2 + comps,)),
        ],
    )(got, bricks, snapshot, flow_new)
    return flow_next, jnp.transpose(basis_next, (1, 0, 2)), factor


def solution(mesh):
    return jax.shard_map(
        local,
        mesh=mesh,
        in_specs=(
            P(None, "gx", "gy", "gz"),
            P(None, None, ("gx", "gy", "gz")),
            P(("gx", "gy", "gz")),
        ),
        out_specs=(P(None, "gx", "gy", "gz"), P(None, None, ("gx", "gy", "gz")), P()),
        check_vma=False,
    )
```

```python
import functools

import jax
import jax.numpy as jnp
from jax import lax
from jax.experimental import pallas as pl
from jax.experimental.pallas import tpu as pltpu
from jax.sharding import PartitionSpec as P

DT_STEP = 0.35
VISCOSITY = 0.2
SOUND_SQ = 1.0
DRIVING = 0.5

ALL = ("gx", "gy", "gz")
DEPTH = 3
EXACT = lax.Precision.HIGHEST
VMEM = pl.BlockSpec(memory_space=pltpu.VMEM)
PARAMS = pltpu.CompilerParams(vmem_limit_bytes=40 * 1024 * 1024)


def dot(a, b, dims):
    return lax.dot_general(
        a, b, (dims, ((), ())), precision=EXACT, preferred_element_type=jnp.float32
    )


def neighbours(block_low, block_high, axis):
    count = lax.axis_size(axis)
    forward = [(i, (i + 1) % count) for i in range(count)]
    backward = [(target, source) for source, target in forward]
    return lax.ppermute(block_high, axis, forward), lax.ppermute(block_low, axis, backward)


def pack_upper(rows, tall):
    size = rows.shape[1]
    lane = lax.broadcasted_iota(jnp.int32, (tall, size), 1)
    part = [rows[tall * k : tall * k + tall] for k in range(4)]
    return [part[0], jnp.where(lane >= tall, part[1], pltpu.roll(part[3], tall, 1)), part[2]]


def unpack_upper(packed, tall):
    return [packed[0], packed[1], packed[2], pltpu.roll(packed[1], packed[1].shape[1] - tall, 1)]


def gram_kernel(basis_ref, send_ref, gram_ref, packed_ref):
    modes = basis_ref.shape[1]
    tall = gram_ref.shape[0] // 4
    total = jnp.zeros((modes, modes), jnp.float32)
    for c in range(basis_ref.shape[0]):
        rows = basis_ref[c]
        total = total + dot(rows, rows, ((1,), (1,)))
    gram_ref[...] = jnp.zeros_like(gram_ref)
    gram_ref[0:modes, 0:modes] = total
    packed_ref[...] = jnp.zeros_like(packed_ref)
    for k, value in enumerate(pack_upper(gram_ref[...], tall)):
        packed_ref[tall * k : tall * k + tall] = value
    per = send_ref.shape[1]
    for d in range(send_ref.shape[0]):
        send_ref[d] = packed_ref[per * d : per * d + per]


STRIP = 4


def strips_kernel(flow_ref, bottom_ref, top_ref):
    ny = flow_ref.shape[2]
    bottom_ref[...] = flow_ref[:, :, 0:STRIP]
    top_ref[...] = flow_ref[:, :, ny - STRIP : ny]


def walls_kernel(walls_ref, flow_ref, ylo_ref, yhi_ref, mid_ref, first_ref, last_ref):
    fields, nx, ny, nz = flow_ref.shape
    sub = lax.broadcasted_iota(jnp.int32, (2 * STRIP, nz), 0)
    outside = ((sub >= STRIP) & (walls_ref[0] == 1)) | ((sub < STRIP) & (walls_ref[1] == 1))
    for f in range(fields):
        halo = []
        for i in range(nx):
            strips = jnp.concatenate([yhi_ref[f, i], ylo_ref[f, i]], axis=0)
            halo.append(jnp.where(outside, 0.0, strips))
            mid_ref[f, i, 0:ny] = flow_ref[f, i]
            mid_ref[f, i, ny : ny + 2 * STRIP] = halo[i]
        for face_ref, begin, near, next_one in ((first_ref, 0, 0, 1), (last_ref, nx - DEPTH, nx - 1, nx - 2)):
            for k in range(DEPTH):
                face_ref[f, ny * k : ny * k + ny] = flow_ref[f, begin + k]
            face_ref[f, ny * DEPTH : ny * DEPTH + 2 * STRIP] = corner_rows(halo[near], halo[next_one], sub)


def corner_rows(near, next_one, sub):
    tile = jnp.where(sub == 2, pltpu.roll(next_one, 2, 0), pltpu.roll(next_one, 6, 0))
    tile = jnp.where((sub == 2) | (sub == 5), tile, 0.0)
    return jnp.where((sub < 2) | (sub >= 6), near, tile)


def corner_planes(tile, sub):
    near = jnp.where((sub < 2) | (sub >= 6), tile, 0.0)
    next_one = jnp.where(sub == 0, pltpu.roll(tile, 6, 0), pltpu.roll(tile, 2, 0))
    return [near, jnp.where((sub == 0) | (sub == 7), next_one, 0.0), jnp.zeros_like(tile)]


def plane_of(mid_ref, xlo_ref, xhi_ref, f, i):
    nx = mid_ref.shape[1]
    if i < DEPTH:
        return xlo_ref[f, i]
    if i < DEPTH + nx:
        return mid_ref[f, i - DEPTH]
    return xhi_ref[f, i - DEPTH - nx]


GROUP = 8


def pack_kernel(mid_ref, low_face_ref, high_face_ref, packed_ref, xlo_ref, xhi_ref):
    fields, nx, rows, nz = mid_ref.shape
    ny = rows - 2 * STRIP
    lane = lax.broadcasted_iota(jnp.int32, (rows, nz), 1)
    sub = lax.broadcasted_iota(jnp.int32, (2 * STRIP, nz), 0)
    for f in range(fields):
        for face_ref, out_ref, order in ((low_face_ref, xlo_ref, (2, 1, 0)), (high_face_ref, xhi_ref, (0, 1, 2))):
            halo = corner_planes(face_ref[f, ny * DEPTH : ny * DEPTH + 2 * STRIP], sub)
            for k in range(DEPTH):
                out_ref[f, k, 0:ny] = face_ref[f, ny * k : ny * k + ny]
                out_ref[f, k, ny:rows] = halo[order[k]]
        value = jnp.zeros((rows, nz), jnp.float32)
        for i in range(nx + 2 * DEPTH):
            start = GROUP * i
            moved = pltpu.roll(plane_of(mid_ref, xlo_ref, xhi_ref, f, i), (start + DEPTH) % nz, 1)
            value = jnp.where((lane >= start) & (lane < start + 2 * DEPTH), moved, value)
        packed_ref[f] = value


def step(value, by, axis):
    size = value.shape[axis]
    return pltpu.roll(value, (size - by) % size, axis)


def rates(centre, x_plus, x_minus, y_plus, y_minus, z_plus, z_minus):
    slope_x = [0.5 * (a - b) for a, b in zip(x_plus, x_minus)]
    slope_y = [0.5 * (a - b) for a, b in zip(y_plus, y_minus)]
    slope_z = [0.5 * (a - b) for a, b in zip(z_plus, z_minus)]
    pressure = [slope_x[3], slope_y[3], slope_z[3]]
    out = []
    for f in range(3):
        laplace = (
            x_plus[f] + x_minus[f] + (y_plus[f] + y_minus[f]) + (z_plus[f] + z_minus[f]) - 6.0 * centre[f]
        )
        advect = centre[0] * slope_x[f] + centre[1] * slope_y[f] + centre[2] * slope_z[f]
        value = VISCOSITY * laplace - advect - pressure[f]
        if f == 0:
            value = value + DRIVING
        out.append(value)
    out.append(-SOUND_SQ * (slope_x[0] + slope_y[1] + slope_z[2]))
    return out


def beyond_walls(walls_ref, ny, shape):
    row = lax.broadcasted_iota(jnp.int32, shape, 0)
    below = (row >= ny + STRIP) & (walls_ref[0] == 1)
    above = (row >= ny) & (row < ny + STRIP) & (walls_ref[1] == 1)
    return below | above


def plane_rates(read, i, rows, ends=None):
    every = range(4)
    centre = [read(f, i) for f in every]
    x_plus = [read(f, i + 1)[:rows] for f in every]
    x_minus = [read(f, i - 1)[:rows] for f in every]
    y_plus = [step(v, 1, 0)[:rows] for v in centre]
    y_minus = [step(v, -1, 0)[:rows] for v in centre]
    centre = [v[:rows] for v in centre]
    upward, downward = centre, centre
    if ends is not None:
        lane = lax.broadcasted_iota(jnp.int32, centre[0].shape, 1)
        upward = [jnp.where(lane == 0, e[:rows], v) for e, v in zip(ends, centre)]
        downward = [jnp.where(lane == lane.shape[1] - 1, e[:rows], v) for e, v in zip(ends, centre)]
    z_plus = [step(v, 1, 1) for v in upward]
    z_minus = [step(v, -1, 1) for v in downward]
    return centre, rates(centre, x_plus, x_minus, y_plus, y_minus, z_plus, z_minus)


def stage_one(outside, value, rate):
    return jnp.where(outside, 0.0, value + DT_STEP * rate)


def stage_two(outside, begin, value, rate):
    return jnp.where(outside, 0.0, 0.75 * begin + 0.25 * (value + DT_STEP * rate))


def first_kernel(walls_ref, mid_ref, xlo_ref, xhi_ref, one_ref):
    fields, nx, rows, nz = mid_ref.shape
    outside = beyond_walls(walls_ref, rows - 2 * STRIP, (rows, nz))
    for i in range(1, nx + 2 * DEPTH - 1):
        centre, rate = plane_rates(functools.partial(plane_of, mid_ref, xlo_ref, xhi_ref), i, rows)
        for f in range(4):
            one_ref[f, i - 1] = stage_one(outside, centre[f], rate[f])


def step_kernel(
    walls_ref, mid_ref, xlo_ref, xhi_ref, first_ref, own_ref, low_ref, high_ref, basis_ref, sample_ref,
    flow_ref, snap_ref, cross_ref,
    one_ref, two_ref,
):
    fields, nx, ny, nz = flow_ref.shape
    rows = mid_ref.shape[2]
    modes = basis_ref.shape[1]
    planes = nx + 2 * DEPTH
    lane = lax.broadcasted_iota(jnp.int32, (rows, nz), 1)
    outside = beyond_walls(walls_ref, ny, (rows, nz))
    every = range(4)
    start = functools.partial(plane_of, mid_ref, xlo_ref, xhi_ref)

    left = lane % GROUP < DEPTH

    def window_rates(q):
        return rates(
            q, [step(v, GROUP, 1) for v in q], [step(v, -GROUP, 1) for v in q],
            [step(v, 1, 0) for v in q], [step(v, -1, 0) for v in q],
            [step(v, 1, 1) for v in q], [step(v, -1, 1) for v in q],
        )

    own = [own_ref[f] for f in every]
    other = [jnp.where(left, low_ref[f], high_ref[f]) for f in every]
    windows = []
    for parts in ((other, own), (own, other)):
        q0 = [jnp.where(left, a, b) for a, b in zip(*parts)]
        q1 = [stage_one(outside, v, r) for v, r in zip(q0, window_rates(q0))]
        q2 = [stage_two(outside, s, v, r) for s, v, r in zip(q0, q1, window_rates(q1))]
        windows.append((q1, q2))
    (low_one, low_two), (high_one, high_two) = windows
    ends_one = [jnp.where(left, a, b) for a, b in zip(low_one, high_one)]
    ends_two = [jnp.where(left, a, b) for a, b in zip(low_two, high_two)]
    rim_one = [jnp.where(left, b, a) for a, b in zip(low_one, high_one)]

    def at_plane(values, i):
        return [pltpu.roll(v, (2 * nz - GROUP * i - DEPTH) % nz, 1) for v in values]

    rim = (lane == 0) | (lane == nz - 1)
    for i in range(1, planes - 1):
        for f, value in enumerate(at_plane(rim_one, i)):
            one_ref[f, i - 1] = jnp.where(rim, value, first_ref[f, i - 1])
    for i in range(2, planes - 2):
        centre, rate = plane_rates(lambda f, i: one_ref[f, i - 1], i, rows, at_plane(ends_one, i))
        for f in every:
            two_ref[f, i - 2] = stage_two(outside, start(f, i), centre[f], rate[f])
    for i in range(3, planes - 3):
        centre, rate = plane_rates(lambda f, i: two_ref[f, i - 2], i, ny, at_plane(ends_two, i))
        for f in every:
            value = 1.0 / 3.0 * start(f, i)[:ny] + 2.0 / 3.0 * (centre[f] + DT_STEP * rate[f])
            flow_ref[f, i - DEPTH] = value

    points = sample_ref.shape[1]
    spot = jnp.broadcast_to(sample_ref[...], (nz, points))
    place = lax.broadcasted_iota(jnp.int32, (nx * ny, points), 0)
    in_row = (place == jnp.broadcast_to(sample_ref[...] // nz, (nx * ny, points))).astype(jnp.bfloat16)
    in_lane = lax.broadcasted_iota(jnp.int32, (nz, points), 0) == spot % nz
    product = jnp.zeros((modes + 1, points), jnp.float32)
    for c in range(3):
        field = flow_ref[c].reshape(nx * ny, nz).T
        high = field.astype(jnp.bfloat16)
        rest = field - high.astype(jnp.float32)
        middle = rest.astype(jnp.bfloat16)
        low = (rest - middle.astype(jnp.float32)).astype(jnp.bfloat16)
        found = sum(
            lax.dot_general(p, in_row, (((1,), (0,)), ((), ())), preferred_element_type=jnp.float32)
            for p in (high, middle, low)
        )
        picked = jnp.sum(jnp.where(in_lane, found, 0.0), axis=0, keepdims=True)
        snap_ref[c] = picked
        product = product + jnp.concatenate([basis_ref[c], picked], axis=0) * picked
    total = jnp.sum(product, axis=1, keepdims=True)
    size = modes + 1
    diagonal = lax.broadcasted_iota(jnp.int32, (size, size), 0) == lax.broadcasted_iota(jnp.int32, (size, size), 1)
    cross_ref[...] = jnp.sum(jnp.where(diagonal, total, 0.0), axis=0, keepdims=True)


def merge_kernel(parts_ref, cross_ref, send_ref):
    total = parts_ref[0]
    for d in range(1, parts_ref.shape[0]):
        total = total + parts_ref[d]
    block = jnp.concatenate([total, cross_ref[...]], axis=0)
    for d in range(send_ref.shape[0]):
        send_ref[d] = block


def final_kernel(
    count, got_ref, basis_ref, snap_ref, flow_ref,
    basis_hbm, factor_hbm, flow_hbm,
    packed_ref, work_ref, basis_out_ref, factor_ref, sems,
):
    comps, modes, points = basis_ref.shape
    size = modes + 1
    tall = size // 4
    per = got_ref.shape[1] - 1
    copies = [pltpu.make_async_copy(flow_ref, flow_hbm, sems.at[0])]
    copies[0].start()

    total = jnp.zeros((per + 1, size), jnp.float32)
    for d in range(got_ref.shape[0]):
        block = got_ref[d]
        if per * d < packed_ref.shape[0]:
            packed_ref[per * d : per * d + per] = block[0:per]
        total = total + block
    cross = total[per : per + 1] / count
    mark = (lax.broadcasted_iota(jnp.int32, (8, size), 1) == size - 1).astype(jnp.float32)
    top = lax.broadcasted_iota(jnp.int32, (8, size), 0) == 0
    side = dot(jnp.where(top, jnp.broadcast_to(cross, (8, size)), 0.0), mark, ((0,), (0,)))
    lane = lax.broadcasted_iota(jnp.int32, (tall, size), 1)
    row = lax.broadcasted_iota(jnp.int32, (tall, size), 0)
    old = unpack_upper([packed_ref[tall * k : tall * k + tall] / count for k in range(3)], tall)
    for k in range(4):
        value = jnp.where(lane == size - 1, side[tall * k : tall * k + tall], old[k])
        if k == 3:
            value = jnp.where(row == tall - 1, jnp.broadcast_to(cross, value.shape), value)
        work_ref[tall * k : tall * k + tall, 0:size] = value
        work_ref[tall * k : tall * k + tall, size : 2 * size] = (lane == row + tall * k).astype(jnp.float32)

    stacked = [jnp.concatenate([basis_ref[c], snap_ref[c]], axis=0) for c in range(comps)]
    for k in range(4):
        base = tall * k
        eliminate(work_ref, base, tall)
        done = work_ref[base : base + tall, :]
        if k < 3:
            change = dot(done[:, 0:size], done, ((0,), (0,)))
            work_ref[base + tall : size, :] = work_ref[base + tall : size, :] - change[base + tall : size]
        factor_ref[base : base + tall, :] = jnp.where(lane >= row + base, done[:, 0:size], 0.0)
        for c in range(comps):
            basis_out_ref[c, base : base + tall, :] = dot(done[:, size : 2 * size], stacked[c], ((1,), (0,)))
        rows = (slice(None), pl.ds(base, tall), slice(None))
        copies.append(pltpu.make_async_copy(basis_out_ref.at[rows], basis_hbm.at[rows], sems.at[2 + k]))
        copies[-1].start()
    copies.append(pltpu.make_async_copy(factor_ref, factor_hbm, sems.at[1]))
    copies[-1].start()
    for copy in copies:
        copy.wait()


def eliminate(work_ref, base, tall):
    blocks = tall // 8
    sub = lax.broadcasted_iota(jnp.int32, (8, 128), 0)
    panel = [work_ref[base + 8 * b : base + 8 * b + 8, :] for b in range(blocks)]
    column = [
        [jnp.broadcast_to(panel[b][:, base + k : base + k + 1], (8, 128)) for b in range(blocks)] for k in range(tall)
    ]
    scale = [jnp.zeros((8, 128), jnp.float32) for _ in range(blocks)]
    for j in range(tall):
        mine, at = divmod(j, 8)
        pivot = column[j][mine][at : at + 1, :]
        inverse = 1.0 / pivot
        for k in range(j + 1, tall):
            other, place = divmod(k, 8)
            times = column[j][other][place : place + 1, :]
            for b in range(other, blocks):
                if k == j + 1:
                    column[k][b] = column[k][b] - (column[j][b] * times) * inverse
                else:
                    column[k][b] = column[k][b] - column[j][b] * (times * inverse)
        scale[mine] = jnp.where(sub == at, lax.rsqrt(pivot), scale[mine])
        pivot_row = panel[mine][at : at + 1, :] * jnp.concatenate([inverse, inverse], axis=1)
        for b in range(mine, blocks):
            times = jnp.where(sub > at, column[j][b], 0.0) if b == mine else column[j][b]
            panel[b] = panel[b] - jnp.concatenate([times, times], axis=1) * pivot_row
    for b in range(blocks):
        work_ref[base + 8 * b : base + 8 * b + 8, :] = panel[b] * jnp.concatenate([scale[b], scale[b]], axis=1)


def local(flow, basis, sample):
    fields, nx, ny, nz = flow.shape
    modes, comps, points = basis.shape
    size = modes + 1
    devices = lax.axis_size("gx") * lax.axis_size("gy") * lax.axis_size("gz")
    count = float(comps * points * devices)
    shape = functools.partial(jax.ShapeDtypeStruct, dtype=jnp.float32)
    call = functools.partial(pl.pallas_call, compiler_params=PARAMS)
    bricks = jnp.transpose(basis, (1, 0, 2))

    smem = pl.BlockSpec(memory_space=pltpu.SMEM)
    quarter = size // 4
    per = -(-3 * quarter // devices)

    strip = shape((fields, nx, STRIP, nz))
    bottom, top = call(strips_kernel, out_shape=(strip, strip), in_specs=[VMEM], out_specs=(VMEM, VMEM))(flow)
    ylo, yhi = neighbours(bottom, top, "gy")
    gram = call(
        gram_kernel,
        out_shape=shape((devices, per, size)),
        in_specs=[VMEM],
        out_specs=VMEM,
        scratch_shapes=[pltpu.VMEM((size, size), jnp.float32), pltpu.VMEM((devices * per, size), jnp.float32)],
    )(bricks)
    ylo, yhi, gram = lax.optimization_barrier((ylo, yhi, gram))

    rows = ny + 2 * STRIP
    place = lax.axis_index("gy")
    walls = jnp.stack([place == 0, place == lax.axis_size("gy") - 1]).astype(jnp.int32)
    face = shape((fields, DEPTH * ny + 2 * STRIP, nz))
    mid, first, last = call(
        walls_kernel,
        out_shape=(shape((fields, nx, rows, nz)), face, face),
        in_specs=[smem] + [VMEM] * 3,
        out_specs=(VMEM,) * 3,
    )(walls, flow, ylo, yhi)
    low_face, high_face = neighbours(first, last, "gx")
    parts = lax.all_to_all(gram, ALL, 0, 0)

    beside = shape((fields, DEPTH, rows, nz))
    packed, xlo, xhi = call(
        pack_kernel,
        out_shape=(shape((fields, rows, nz)), beside, beside),
        in_specs=[VMEM] * 3,
        out_specs=(VMEM,) * 3,
    )(mid, low_face, high_face)
    if lax.axis_size("gz") == 2:
        low = high = lax.ppermute(packed, "gz", [(0, 1), (1, 0)])
    else:
        low, high = neighbours(packed, packed, "gz")
    begun = call(
        first_kernel,
        out_shape=shape((fields, nx + 2 * DEPTH - 2, rows, nz)),
        in_specs=[smem] + [VMEM] * 3,
        out_specs=VMEM,
    )(walls, mid, xlo, xhi)
    flow_new, snapshot, cross = call(
        step_kernel,
        out_shape=(shape(flow.shape), shape((comps, 1, points)), shape((1, size))),
        in_specs=[smem] + [VMEM] * 9,
        out_specs=(VMEM, VMEM, VMEM),
        scratch_shapes=[
            pltpu.VMEM((fields, nx + 2 * DEPTH - 2, rows, nz), jnp.float32),
            pltpu.VMEM((fields, nx + 2 * DEPTH - 4, rows, nz), jnp.float32),
        ],
    )(walls, mid, xlo, xhi, begun, packed, low, high, bricks, sample.reshape(1, points))

    send = call(
        merge_kernel, out_shape=shape((devices, per + 1, size)), in_specs=[VMEM] * 2, out_specs=VMEM
    )(parts, cross)
    got = lax.all_to_all(send, ALL, 0, 0)
    whole = pl.BlockSpec(memory_space=pltpu.HBM)
    basis_next, factor, flow_next = call(
        functools.partial(final_kernel, count),
        out_shape=(shape((comps, size, points)), shape((size, size)), shape(flow.shape)),
        in_specs=[VMEM] * 4,
        out_specs=(whole,) * 3,
        scratch_shapes=[
            pltpu.VMEM((3 * quarter, size), jnp.float32),
            pltpu.VMEM((size, 2 * size), jnp.float32),
            pltpu.VMEM((comps, size, points), jnp.float32),
            pltpu.VMEM((size, size), jnp.float32),
            pltpu.SemaphoreType.DMA((6,)),
        ],
    )(got, bricks, snapshot, flow_new)
    return flow_next, jnp.transpose(basis_next, (1, 0, 2)), factor


def solution(mesh):
    return jax.shard_map(
        local,
        mesh=mesh,
        in_specs=(
            P(None, "gx", "gy", "gz"),
            P(None, None, ("gx", "gy", "gz")),
            P(("gx", "gy", "gz")),
        ),
        out_specs=(P(None, "gx", "gy", "gz"), P(None, None, ("gx", "gy", "gz")), P()),
        check_vma=False,
    )
```

```python
import functools

import jax
import jax.numpy as jnp
from jax import lax
from jax.experimental import pallas as pl
from jax.experimental.pallas import tpu as pltpu
from jax.sharding import PartitionSpec as P

DT_STEP = 0.35
VISCOSITY = 0.2
SOUND_SQ = 1.0
DRIVING = 0.5

ALL = ("gx", "gy", "gz")
DEPTH = 3
EXACT = lax.Precision.HIGHEST
VMEM = pl.BlockSpec(memory_space=pltpu.VMEM)
PARAMS = pltpu.CompilerParams(vmem_limit_bytes=40 * 1024 * 1024)


def dot(a, b, dims):
    return lax.dot_general(
        a, b, (dims, ((), ())), precision=EXACT, preferred_element_type=jnp.float32
    )


def neighbours(block_low, block_high, axis):
    count = lax.axis_size(axis)
    forward = [(i, (i + 1) % count) for i in range(count)]
    backward = [(target, source) for source, target in forward]
    return lax.ppermute(block_high, axis, forward), lax.ppermute(block_low, axis, backward)


def pack_upper(rows, tall):
    size = rows.shape[1]
    lane = lax.broadcasted_iota(jnp.int32, (tall, size), 1)
    part = [rows[tall * k : tall * k + tall] for k in range(4)]
    return [part[0], jnp.where(lane >= tall, part[1], pltpu.roll(part[3], tall, 1)), part[2]]


def unpack_upper(packed, tall):
    return [packed[0], packed[1], packed[2], pltpu.roll(packed[1], packed[1].shape[1] - tall, 1)]


def gram_kernel(basis_ref, send_ref, gram_ref, packed_ref):
    modes = basis_ref.shape[1]
    tall = gram_ref.shape[0] // 4
    total = jnp.zeros((modes, modes), jnp.float32)
    for c in range(basis_ref.shape[0]):
        rows = basis_ref[c]
        total = total + dot(rows, rows, ((1,), (1,)))
    gram_ref[...] = jnp.zeros_like(gram_ref)
    gram_ref[0:modes, 0:modes] = total
    packed_ref[...] = jnp.zeros_like(packed_ref)
    for k, value in enumerate(pack_upper(gram_ref[...], tall)):
        packed_ref[tall * k : tall * k + tall] = value
    per = send_ref.shape[1]
    for d in range(send_ref.shape[0]):
        send_ref[d] = packed_ref[per * d : per * d + per]


GAP = 2
HALO = 2 * DEPTH + GAP


def strips_kernel(planes, flow_ref, bottom_ref, top_ref):
    ny = flow_ref.shape[1] // planes
    for f in range(flow_ref.shape[0]):
        for j in range(DEPTH):
            bottom_ref[f, planes * j : planes * j + planes] = flow_ref[f, pl.ds(j, planes, stride=ny), :]
            top_ref[f, planes * j : planes * j + planes] = flow_ref[f, pl.ds(ny - DEPTH + j, planes, stride=ny), :]


def walls_kernel(planes, walls_ref, flow_ref, ylo_ref, yhi_ref, mid_ref, first_ref, last_ref):
    fields, cells, nz = flow_ref.shape
    ny = cells // planes
    rows = ny + HALO
    sub = lax.broadcasted_iota(jnp.int32, (HALO, nz), 0)
    empty = jnp.zeros((planes, nz), jnp.float32)
    for f in range(fields):
        for i in range(planes):
            mid_ref[f, rows * i : rows * i + ny] = flow_ref[f, ny * i : ny * i + ny]
        for j in range(HALO):
            if j < DEPTH:
                value = jnp.where(walls_ref[1] == 1, 0.0, yhi_ref[f, planes * j : planes * j + planes])
            elif j < DEPTH + GAP:
                value = empty
            else:
                k = j - DEPTH - GAP
                value = jnp.where(walls_ref[0] == 1, 0.0, ylo_ref[f, planes * k : planes * k + planes])
            mid_ref[f, pl.ds(ny + j, planes, stride=rows), :] = value
        for face_ref, begin, near, next_one in (
            (first_ref, 0, 0, 1), (last_ref, planes - DEPTH, planes - 1, planes - 2)
        ):
            for k in range(DEPTH):
                face_ref[f, ny * k : ny * k + ny] = flow_ref[f, ny * (begin + k) : ny * (begin + k) + ny]
            halos = [mid_ref[f, rows * i + ny : rows * i + rows] for i in (near, next_one)]
            face_ref[f, ny * DEPTH : ny * DEPTH + HALO] = corner_rows(*halos, sub)


def corner_rows(near, next_one, sub):
    tile = jnp.where(sub == 2, pltpu.roll(next_one, 2, 0), pltpu.roll(next_one, 6, 0))
    tile = jnp.where((sub == 2) | (sub == 5), tile, 0.0)
    return jnp.where((sub < 2) | (sub >= 6), near, tile)


def corner_planes(tile, sub):
    near = jnp.where((sub < 2) | (sub >= 6), tile, 0.0)
    next_one = jnp.where(sub == 0, pltpu.roll(tile, 6, 0), pltpu.roll(tile, 2, 0))
    return [near, jnp.where((sub == 0) | (sub == 7), next_one, 0.0), jnp.zeros_like(tile)]


def plane_of(mid_ref, xlo_ref, xhi_ref, f, i):
    nx = mid_ref.shape[1]
    if i < DEPTH:
        return xlo_ref[f, i]
    if i < DEPTH + nx:
        return mid_ref[f, i - DEPTH]
    return xhi_ref[f, i - DEPTH - nx]


GROUP = 8


def pack_kernel(mid_ref, low_face_ref, high_face_ref, packed_ref, xlo_ref, xhi_ref):
    fields, nx, rows, nz = mid_ref.shape
    ny = rows - HALO
    lane = lax.broadcasted_iota(jnp.int32, (rows, nz), 1)
    sub = lax.broadcasted_iota(jnp.int32, (HALO, nz), 0)
    for f in range(fields):
        for face_ref, out_ref, order in ((low_face_ref, xlo_ref, (2, 1, 0)), (high_face_ref, xhi_ref, (0, 1, 2))):
            halo = corner_planes(face_ref[f, ny * DEPTH : ny * DEPTH + HALO], sub)
            for k in range(DEPTH):
                out_ref[f, k, 0:ny] = face_ref[f, ny * k : ny * k + ny]
                out_ref[f, k, ny:rows] = halo[order[k]]
        value = jnp.zeros((rows, nz), jnp.float32)
        for i in range(nx + 2 * DEPTH):
            start = GROUP * i
            moved = pltpu.roll(plane_of(mid_ref, xlo_ref, xhi_ref, f, i), (start + DEPTH) % nz, 1)
            value = jnp.where((lane >= start) & (lane < start + 2 * DEPTH), moved, value)
        packed_ref[f] = value


def step(value, by, axis):
    size = value.shape[axis]
    return pltpu.roll(value, (size - by) % size, axis)


def rates(centre, x_plus, x_minus, y_plus, y_minus, z_plus, z_minus):
    slope_x = [0.5 * (a - b) for a, b in zip(x_plus, x_minus)]
    slope_y = [0.5 * (a - b) for a, b in zip(y_plus, y_minus)]
    slope_z = [0.5 * (a - b) for a, b in zip(z_plus, z_minus)]
    pressure = [slope_x[3], slope_y[3], slope_z[3]]
    out = []
    for f in range(3):
        laplace = (
            x_plus[f] + x_minus[f] + (y_plus[f] + y_minus[f]) + (z_plus[f] + z_minus[f]) - 6.0 * centre[f]
        )
        advect = centre[0] * slope_x[f] + centre[1] * slope_y[f] + centre[2] * slope_z[f]
        value = VISCOSITY * laplace - advect - pressure[f]
        if f == 0:
            value = value + DRIVING
        out.append(value)
    out.append(-SOUND_SQ * (slope_x[0] + slope_y[1] + slope_z[2]))
    return out


def beyond_walls(walls_ref, ny, shape):
    row = lax.broadcasted_iota(jnp.int32, shape, 0)
    below = (row >= ny + DEPTH + GAP) & (walls_ref[0] == 1)
    above = (row >= ny) & (row < ny + DEPTH) & (walls_ref[1] == 1)
    return below | above


def plane_rates(read, i, rows, ends=None):
    every = range(4)
    centre = [read(f, i) for f in every]
    x_plus = [read(f, i + 1)[:rows] for f in every]
    x_minus = [read(f, i - 1)[:rows] for f in every]
    y_plus = [step(v, 1, 0)[:rows] for v in centre]
    y_minus = [step(v, -1, 0)[:rows] for v in centre]
    centre = [v[:rows] for v in centre]
    upward, downward = centre, centre
    if ends is not None:
        lane = lax.broadcasted_iota(jnp.int32, centre[0].shape, 1)
        upward = [jnp.where(lane == 0, e[:rows], v) for e, v in zip(ends, centre)]
        downward = [jnp.where(lane == lane.shape[1] - 1, e[:rows], v) for e, v in zip(ends, centre)]
    z_plus = [step(v, 1, 1) for v in upward]
    z_minus = [step(v, -1, 1) for v in downward]
    return centre, rates(centre, x_plus, x_minus, y_plus, y_minus, z_plus, z_minus)


def stage_one(outside, value, rate):
    return jnp.where(outside, 0.0, value + DT_STEP * rate)


def stage_two(outside, begin, value, rate):
    return jnp.where(outside, 0.0, 0.75 * begin + 0.25 * (value + DT_STEP * rate))


def first_kernel(walls_ref, sample_hbm, mid_ref, xlo_ref, xhi_ref, one_ref, sample_ref, sem):
    copy = pltpu.make_async_copy(sample_hbm, sample_ref, sem)
    copy.start()
    fields, nx, rows, nz = mid_ref.shape
    outside = beyond_walls(walls_ref, rows - HALO, (rows, nz))
    for i in range(1, nx + 2 * DEPTH - 1):
        centre, rate = plane_rates(functools.partial(plane_of, mid_ref, xlo_ref, xhi_ref), i, rows)
        for f in range(4):
            one_ref[f, i - 1] = stage_one(outside, centre[f], rate[f])
    copy.wait()


def step_kernel(
    walls_ref, mid_ref, xlo_ref, xhi_ref, first_ref, own_ref, low_ref, high_ref, basis_ref, sample_ref,
    flow_ref, snap_ref, cross_ref,
    one_ref, two_ref,
):
    fields, nx, ny, nz = flow_ref.shape
    rows = mid_ref.shape[2]
    modes = basis_ref.shape[1]
    planes = nx + 2 * DEPTH
    lane = lax.broadcasted_iota(jnp.int32, (rows, nz), 1)
    outside = beyond_walls(walls_ref, ny, (rows, nz))
    every = range(4)
    start = functools.partial(plane_of, mid_ref, xlo_ref, xhi_ref)

    left = lane % GROUP < DEPTH

    def window_rates(q):
        return rates(
            q, [step(v, GROUP, 1) for v in q], [step(v, -GROUP, 1) for v in q],
            [step(v, 1, 0) for v in q], [step(v, -1, 0) for v in q],
            [step(v, 1, 1) for v in q], [step(v, -1, 1) for v in q],
        )

    own = [own_ref[f] for f in every]
    other = [jnp.where(left, low_ref[f], high_ref[f]) for f in every]
    windows = []
    for parts in ((other, own), (own, other)):
        q0 = [jnp.where(left, a, b) for a, b in zip(*parts)]
        q1 = [stage_one(outside, v, r) for v, r in zip(q0, window_rates(q0))]
        q2 = [stage_two(outside, s, v, r) for s, v, r in zip(q0, q1, window_rates(q1))]
        windows.append((q1, q2))
    (low_one, low_two), (high_one, high_two) = windows
    ends_one = [jnp.where(left, a, b) for a, b in zip(low_one, high_one)]
    ends_two = [jnp.where(left, a, b) for a, b in zip(low_two, high_two)]
    rim_one = [jnp.where(left, b, a) for a, b in zip(low_one, high_one)]

    def at_plane(values, i):
        return [pltpu.roll(v, (2 * nz - GROUP * i - DEPTH) % nz, 1) for v in values]

    rim = (lane == 0) | (lane == nz - 1)
    for i in range(1, planes - 1):
        for f, value in enumerate(at_plane(rim_one, i)):
            one_ref[f, i - 1] = jnp.where(rim, value, first_ref[f, i - 1])
    for i in range(2, planes - 2):
        centre, rate = plane_rates(lambda f, i: one_ref[f, i - 1], i, rows, at_plane(ends_one, i))
        for f in every:
            two_ref[f, i - 2] = stage_two(outside, start(f, i), centre[f], rate[f])
    for i in range(3, planes - 3):
        centre, rate = plane_rates(lambda f, i: two_ref[f, i - 2], i, ny, at_plane(ends_two, i))
        for f in every:
            value = 1.0 / 3.0 * start(f, i)[:ny] + 2.0 / 3.0 * (centre[f] + DT_STEP * rate[f])
            flow_ref[f, i - DEPTH] = value

    points = sample_ref.shape[1]
    spot = jnp.broadcast_to(sample_ref[...], (nz, points))
    place = lax.broadcasted_iota(jnp.int32, (nx * ny, points), 0)
    in_row = (place == jnp.broadcast_to(sample_ref[...] // nz, (nx * ny, points))).astype(jnp.bfloat16)
    in_lane = lax.broadcasted_iota(jnp.int32, (nz, points), 0) == spot % nz
    product = jnp.zeros((modes + 1, points), jnp.float32)
    for c in range(3):
        field = flow_ref[c].reshape(nx * ny, nz).T
        high = field.astype(jnp.bfloat16)
        rest = field - high.astype(jnp.float32)
        middle = rest.astype(jnp.bfloat16)
        low = (rest - middle.astype(jnp.float32)).astype(jnp.bfloat16)
        found = sum(
            lax.dot_general(p, in_row, (((1,), (0,)), ((), ())), preferred_element_type=jnp.float32)
            for p in (high, middle, low)
        )
        picked = jnp.sum(jnp.where(in_lane, found, 0.0), axis=0, keepdims=True)
        snap_ref[c] = picked
        product = product + jnp.concatenate([basis_ref[c], picked], axis=0) * picked
    total = jnp.sum(product, axis=1, keepdims=True)
    size = modes + 1
    diagonal = lax.broadcasted_iota(jnp.int32, (size, size), 0) == lax.broadcasted_iota(jnp.int32, (size, size), 1)
    cross_ref[...] = jnp.sum(jnp.where(diagonal, total, 0.0), axis=0, keepdims=True)


def merge_kernel(parts_ref, cross_ref, send_ref):
    total = parts_ref[0]
    for d in range(1, parts_ref.shape[0]):
        total = total + parts_ref[d]
    block = jnp.concatenate([total, cross_ref[...]], axis=0)
    for d in range(send_ref.shape[0]):
        send_ref[d] = block


def final_kernel(
    count, got_ref, basis_ref, snap_ref, flow_ref,
    basis_hbm, factor_hbm, flow_hbm,
    packed_ref, work_ref, basis_out_ref, factor_ref, sems,
):
    comps, modes, points = basis_ref.shape
    size = modes + 1
    tall = size // 4
    per = got_ref.shape[1] - 1
    copies = [pltpu.make_async_copy(flow_ref, flow_hbm, sems.at[0])]
    copies[0].start()

    total = jnp.zeros((per + 1, size), jnp.float32)
    for d in range(got_ref.shape[0]):
        block = got_ref[d]
        if per * d < packed_ref.shape[0]:
            packed_ref[per * d : per * d + per] = block[0:per]
        total = total + block
    cross = total[per : per + 1] / count
    lane = lax.broadcasted_iota(jnp.int32, (tall, size), 1)
    row = lax.broadcasted_iota(jnp.int32, (tall, size), 0)
    old = unpack_upper([packed_ref[tall * k : tall * k + tall] / count for k in range(3)], tall)
    for k in range(4):
        side = jnp.sum(jnp.where(lane == row + tall * k, cross, 0.0), axis=1, keepdims=True)
        value = jnp.where(lane == size - 1, side, old[k])
        if k == 3:
            value = jnp.where(row == tall - 1, jnp.broadcast_to(cross, value.shape), value)
        work_ref[tall * k : tall * k + tall, 0:size] = value
        work_ref[tall * k : tall * k + tall, size : 2 * size] = (lane == row + tall * k).astype(jnp.float32)

    stacked = [jnp.concatenate([basis_ref[c], snap_ref[c]], axis=0) for c in range(comps)]
    for k in range(4):
        base = tall * k
        eliminate(work_ref, base, tall)
        done = work_ref[base : base + tall, :]
        if k < 3:
            change = dot(done[:, 0:size], done, ((0,), (0,)))
            work_ref[base + tall : size, :] = work_ref[base + tall : size, :] - change[base + tall : size]
        factor_ref[base : base + tall, :] = jnp.where(lane >= row + base, done[:, 0:size], 0.0)
        for c in range(comps):
            basis_out_ref[c, base : base + tall, :] = dot(done[:, size : 2 * size], stacked[c], ((1,), (0,)))
        rows = (slice(None), pl.ds(base, tall), slice(None))
        copies.append(pltpu.make_async_copy(basis_out_ref.at[rows], basis_hbm.at[rows], sems.at[2 + k]))
        copies[-1].start()
    copies.append(pltpu.make_async_copy(factor_ref, factor_hbm, sems.at[1]))
    copies[-1].start()
    for copy in copies:
        copy.wait()


def eliminate(work_ref, base, tall):
    blocks = tall // 8
    sub = lax.broadcasted_iota(jnp.int32, (8, 128), 0)
    panel = [work_ref[base + 8 * b : base + 8 * b + 8, :] for b in range(blocks)]
    column = [
        [jnp.broadcast_to(panel[b][:, base + k : base + k + 1], (8, 128)) for b in range(blocks)] for k in range(tall)
    ]
    scale = [jnp.zeros((8, 128), jnp.float32) for _ in range(blocks)]
    for j in range(tall):
        mine, at = divmod(j, 8)
        pivot = column[j][mine][at : at + 1, :]
        inverse = 1.0 / pivot
        for k in range(j + 1, tall):
            other, place = divmod(k, 8)
            times = column[j][other][place : place + 1, :]
            for b in range(other, blocks):
                if k == j + 1:
                    column[k][b] = column[k][b] - (column[j][b] * times) * inverse
                else:
                    column[k][b] = column[k][b] - column[j][b] * (times * inverse)
        scale[mine] = jnp.where(sub == at, lax.rsqrt(pivot), scale[mine])
        pivot_row = panel[mine][at : at + 1, :] * jnp.concatenate([inverse, inverse], axis=1)
        for b in range(mine, blocks):
            times = jnp.where(sub > at, column[j][b], 0.0) if b == mine else column[j][b]
            panel[b] = panel[b] - jnp.concatenate([times, times], axis=1) * pivot_row
    for b in range(blocks):
        work_ref[base + 8 * b : base + 8 * b + 8, :] = panel[b] * jnp.concatenate([scale[b], scale[b]], axis=1)


def local(flow, basis, sample):
    fields, nx, ny, nz = flow.shape
    modes, comps, points = basis.shape
    size = modes + 1
    devices = lax.axis_size("gx") * lax.axis_size("gy") * lax.axis_size("gz")
    count = float(comps * points * devices)
    shape = functools.partial(jax.ShapeDtypeStruct, dtype=jnp.float32)
    call = functools.partial(pl.pallas_call, compiler_params=PARAMS)
    bricks = jnp.transpose(basis, (1, 0, 2))

    smem = pl.BlockSpec(memory_space=pltpu.SMEM)
    whole = pl.BlockSpec(memory_space=pltpu.HBM)
    flat = flow.reshape(fields, nx * ny, nz)
    quarter = size // 4
    per = -(-3 * quarter // devices)

    strip = shape((fields, nx * DEPTH, nz))
    bottom, top = call(
        functools.partial(strips_kernel, nx), out_shape=(strip, strip), in_specs=[VMEM], out_specs=(VMEM, VMEM)
    )(flat)
    ylo, yhi = neighbours(bottom, top, "gy")
    gram = call(
        gram_kernel,
        out_shape=shape((devices, per, size)),
        in_specs=[VMEM],
        out_specs=VMEM,
        scratch_shapes=[pltpu.VMEM((size, size), jnp.float32), pltpu.VMEM((devices * per, size), jnp.float32)],
    )(bricks)
    ylo, yhi, gram = lax.optimization_barrier((ylo, yhi, gram))

    rows = ny + HALO
    place = lax.axis_index("gy")
    walls = jnp.stack([place == 0, place == lax.axis_size("gy") - 1]).astype(jnp.int32)
    face = shape((fields, DEPTH * ny + HALO, nz))
    mid, first, last = call(
        functools.partial(walls_kernel, nx),
        out_shape=(shape((fields, nx * rows, nz)), face, face),
        in_specs=[smem] + [VMEM] * 3,
        out_specs=(VMEM,) * 3,
    )(walls, flat, ylo, yhi)
    mid = mid.reshape(fields, nx, rows, nz)
    low_face, high_face = neighbours(first, last, "gx")
    parts = lax.all_to_all(gram, ALL, 0, 0)

    beside = shape((fields, DEPTH, rows, nz))
    packed, xlo, xhi = call(
        pack_kernel,
        out_shape=(shape((fields, rows, nz)), beside, beside),
        in_specs=[VMEM] * 3,
        out_specs=(VMEM,) * 3,
    )(mid, low_face, high_face)
    if lax.axis_size("gz") == 2:
        low = high = lax.ppermute(packed, "gz", [(0, 1), (1, 0)])
    else:
        low, high = neighbours(packed, packed, "gz")
    begun, cells = call(
        first_kernel,
        out_shape=(
            shape((fields, nx + 2 * DEPTH - 2, rows, nz)),
            jax.ShapeDtypeStruct((1, points), sample.dtype),
        ),
        in_specs=[smem, whole] + [VMEM] * 3,
        out_specs=(VMEM, VMEM),
        scratch_shapes=[pltpu.SemaphoreType.DMA],
    )(walls, sample.reshape(1, points), mid, xlo, xhi)
    flow_new, snapshot, cross = call(
        step_kernel,
        out_shape=(shape(flow.shape), shape((comps, 1, points)), shape((1, size))),
        in_specs=[smem] + [VMEM] * 9,
        out_specs=(VMEM, VMEM, VMEM),
        scratch_shapes=[
            pltpu.VMEM((fields, nx + 2 * DEPTH - 2, rows, nz), jnp.float32),
            pltpu.VMEM((fields, nx + 2 * DEPTH - 4, rows, nz), jnp.float32),
        ],
    )(walls, mid, xlo, xhi, begun, packed, low, high, bricks, cells)

    send = call(
        merge_kernel, out_shape=shape((devices, per + 1, size)), in_specs=[VMEM] * 2, out_specs=VMEM
    )(parts, cross)
    got = lax.all_to_all(send, ALL, 0, 0)
    basis_next, factor, flow_next = call(
        functools.partial(final_kernel, count),
        out_shape=(shape((comps, size, points)), shape((size, size)), shape(flow.shape)),
        in_specs=[VMEM] * 4,
        out_specs=(whole,) * 3,
        scratch_shapes=[
            pltpu.VMEM((3 * quarter, size), jnp.float32),
            pltpu.VMEM((size, 2 * size), jnp.float32),
            pltpu.VMEM((comps, size, points), jnp.float32),
            pltpu.VMEM((size, size), jnp.float32),
            pltpu.SemaphoreType.DMA((6,)),
        ],
    )(got, bricks, snapshot, flow_new)
    return flow_next, jnp.transpose(basis_next, (1, 0, 2)), factor


def solution(mesh):
    return jax.shard_map(
        local,
        mesh=mesh,
        in_specs=(
            P(None, "gx", "gy", "gz"),
            P(None, None, ("gx", "gy", "gz")),
            P(("gx", "gy", "gz")),
        ),
        out_specs=(P(None, "gx", "gy", "gz"), P(None, None, ("gx", "gy", "gz")), P()),
        check_vma=False,
    )
```

```python
import functools

import jax
import jax.numpy as jnp
from jax import lax
from jax.experimental import pallas as pl
from jax.experimental.pallas import tpu as pltpu
from jax.sharding import PartitionSpec as P

DT_STEP = 0.35
VISCOSITY = 0.2
SOUND_SQ = 1.0
DRIVING = 0.5

ALL = ("gx", "gy", "gz")
DEPTH = 3
EXACT = lax.Precision.HIGHEST
VMEM = pl.BlockSpec(memory_space=pltpu.VMEM)
PARAMS = pltpu.CompilerParams(vmem_limit_bytes=40 * 1024 * 1024)


def dot(a, b, dims):
    return lax.dot_general(
        a, b, (dims, ((), ())), precision=EXACT, preferred_element_type=jnp.float32
    )


def neighbours(block_low, block_high, axis):
    count = lax.axis_size(axis)
    forward = [(i, (i + 1) % count) for i in range(count)]
    backward = [(target, source) for source, target in forward]
    return lax.ppermute(block_high, axis, forward), lax.ppermute(block_low, axis, backward)


def pack_upper(rows, tall):
    size = rows.shape[1]
    lane = lax.broadcasted_iota(jnp.int32, (tall, size), 1)
    part = [rows[tall * k : tall * k + tall] for k in range(4)]
    return [part[0], jnp.where(lane >= tall, part[1], pltpu.roll(part[3], tall, 1)), part[2]]


def unpack_upper(packed, tall):
    return [packed[0], packed[1], packed[2], pltpu.roll(packed[1], packed[1].shape[1] - tall, 1)]


def gram_kernel(basis_ref, send_ref, gram_ref, packed_ref):
    modes = basis_ref.shape[1]
    tall = gram_ref.shape[0] // 4
    total = jnp.zeros((modes, modes), jnp.float32)
    for c in range(basis_ref.shape[0]):
        rows = basis_ref[c]
        total = total + dot(rows, rows, ((1,), (1,)))
    gram_ref[...] = jnp.zeros_like(gram_ref)
    gram_ref[0:modes, 0:modes] = total
    packed_ref[...] = jnp.zeros_like(packed_ref)
    for k, value in enumerate(pack_upper(gram_ref[...], tall)):
        packed_ref[tall * k : tall * k + tall] = value
    per = send_ref.shape[1]
    for d in range(send_ref.shape[0]):
        send_ref[d] = packed_ref[per * d : per * d + per]


GAP = 2
HALO = 2 * DEPTH + GAP


def strips_kernel(planes, flow_ref, bottom_ref, top_ref):
    ny = flow_ref.shape[1] // planes
    for f in range(flow_ref.shape[0]):
        for j in range(DEPTH):
            bottom_ref[f, planes * j : planes * j + planes] = flow_ref[f, pl.ds(j, planes, stride=ny), :]
            top_ref[f, planes * j : planes * j + planes] = flow_ref[f, pl.ds(ny - DEPTH + j, planes, stride=ny), :]


def walls_kernel(planes, walls_ref, flow_ref, ylo_ref, yhi_ref, mid_ref, first_ref, last_ref):
    fields, cells, nz = flow_ref.shape
    ny = cells // planes
    rows = ny + HALO
    sub = lax.broadcasted_iota(jnp.int32, (HALO, nz), 0)
    empty = jnp.zeros((planes, nz), jnp.float32)
    for f in range(fields):
        for i in range(planes):
            mid_ref[f, rows * i : rows * i + ny] = flow_ref[f, ny * i : ny * i + ny]
        for j in range(HALO):
            if j < DEPTH:
                value = jnp.where(walls_ref[1:2] == 1, 0.0, yhi_ref[f, planes * j : planes * j + planes])
            elif j < DEPTH + GAP:
                value = empty
            else:
                k = j - DEPTH - GAP
                value = jnp.where(walls_ref[0:1] == 1, 0.0, ylo_ref[f, planes * k : planes * k + planes])
            mid_ref[f, pl.ds(ny + j, planes, stride=rows), :] = value
        for face_ref, begin, near, next_one in (
            (first_ref, 0, 0, 1), (last_ref, planes - DEPTH, planes - 1, planes - 2)
        ):
            for k in range(DEPTH):
                face_ref[f, ny * k : ny * k + ny] = flow_ref[f, ny * (begin + k) : ny * (begin + k) + ny]
            halos = [mid_ref[f, rows * i + ny : rows * i + rows] for i in (near, next_one)]
            face_ref[f, ny * DEPTH : ny * DEPTH + HALO] = corner_rows(*halos, sub)


def corner_rows(near, next_one, sub):
    tile = jnp.where(sub == 2, pltpu.roll(next_one, 2, 0), pltpu.roll(next_one, 6, 0))
    tile = jnp.where((sub == 2) | (sub == 5), tile, 0.0)
    return jnp.where((sub < 2) | (sub >= 6), near, tile)


def corner_planes(tile, sub):
    near = jnp.where((sub < 2) | (sub >= 6), tile, 0.0)
    next_one = jnp.where(sub == 0, pltpu.roll(tile, 6, 0), pltpu.roll(tile, 2, 0))
    return [near, jnp.where((sub == 0) | (sub == 7), next_one, 0.0), jnp.zeros_like(tile)]


def plane_of(mid_ref, xlo_ref, xhi_ref, f, i):
    nx = mid_ref.shape[1]
    if i < DEPTH:
        return xlo_ref[f, i]
    if i < DEPTH + nx:
        return mid_ref[f, i - DEPTH]
    return xhi_ref[f, i - DEPTH - nx]


GROUP = 8


def pack_kernel(mid_ref, low_face_ref, high_face_ref, packed_ref, xlo_ref, xhi_ref):
    fields, nx, rows, nz = mid_ref.shape
    ny = rows - HALO
    lane = lax.broadcasted_iota(jnp.int32, (rows, nz), 1)
    sub = lax.broadcasted_iota(jnp.int32, (HALO, nz), 0)
    for f in range(fields):
        for face_ref, out_ref, order in ((low_face_ref, xlo_ref, (2, 1, 0)), (high_face_ref, xhi_ref, (0, 1, 2))):
            halo = corner_planes(face_ref[f, ny * DEPTH : ny * DEPTH + HALO], sub)
            for k in range(DEPTH):
                out_ref[f, k, 0:ny] = face_ref[f, ny * k : ny * k + ny]
                out_ref[f, k, ny:rows] = halo[order[k]]
        value = jnp.zeros((rows, nz), jnp.float32)
        for i in range(nx + 2 * DEPTH):
            start = GROUP * i
            moved = pltpu.roll(plane_of(mid_ref, xlo_ref, xhi_ref, f, i), (start + DEPTH) % nz, 1)
            value = jnp.where((lane >= start) & (lane < start + 2 * DEPTH), moved, value)
        packed_ref[f] = value


def step(value, by, axis):
    size = value.shape[axis]
    return pltpu.roll(value, (size - by) % size, axis)


def rates(centre, x_plus, x_minus, y_plus, y_minus, z_plus, z_minus):
    slope_x = [0.5 * (a - b) for a, b in zip(x_plus, x_minus)]
    slope_y = [0.5 * (a - b) for a, b in zip(y_plus, y_minus)]
    slope_z = [0.5 * (a - b) for a, b in zip(z_plus, z_minus)]
    pressure = [slope_x[3], slope_y[3], slope_z[3]]
    out = []
    for f in range(3):
        laplace = (
            x_plus[f] + x_minus[f] + (y_plus[f] + y_minus[f]) + (z_plus[f] + z_minus[f]) - 6.0 * centre[f]
        )
        advect = centre[0] * slope_x[f] + centre[1] * slope_y[f] + centre[2] * slope_z[f]
        value = VISCOSITY * laplace - advect - pressure[f]
        if f == 0:
            value = value + DRIVING
        out.append(value)
    out.append(-SOUND_SQ * (slope_x[0] + slope_y[1] + slope_z[2]))
    return out


def beyond_walls(walls_ref, ny, shape):
    row = lax.broadcasted_iota(jnp.int32, shape, 0)
    below = (row >= ny + DEPTH + GAP) & (walls_ref[0:1] == 1)
    above = (row >= ny) & (row < ny + DEPTH) & (walls_ref[1:2] == 1)
    return below | above


def plane_rates(read, i, rows, ends=None):
    every = range(4)
    centre = [read(f, i) for f in every]
    x_plus = [read(f, i + 1)[:rows] for f in every]
    x_minus = [read(f, i - 1)[:rows] for f in every]
    y_plus = [step(v, 1, 0)[:rows] for v in centre]
    y_minus = [step(v, -1, 0)[:rows] for v in centre]
    centre = [v[:rows] for v in centre]
    upward, downward = centre, centre
    if ends is not None:
        lane = lax.broadcasted_iota(jnp.int32, centre[0].shape, 1)
        upward = [jnp.where(lane == 0, e[:rows], v) for e, v in zip(ends, centre)]
        downward = [jnp.where(lane == lane.shape[1] - 1, e[:rows], v) for e, v in zip(ends, centre)]
    z_plus = [step(v, 1, 1) for v in upward]
    z_minus = [step(v, -1, 1) for v in downward]
    return centre, rates(centre, x_plus, x_minus, y_plus, y_minus, z_plus, z_minus)


def stage_one(outside, value, rate):
    return jnp.where(outside, 0.0, value + DT_STEP * rate)


def stage_two(outside, begin, value, rate):
    return jnp.where(outside, 0.0, 0.75 * begin + 0.25 * (value + DT_STEP * rate))


def first_kernel(walls_ref, sample_hbm, mid_ref, xlo_ref, xhi_ref, one_ref, sample_ref, sem):
    copy = pltpu.make_async_copy(sample_hbm, sample_ref, sem)
    copy.start()
    fields, nx, rows, nz = mid_ref.shape
    outside = beyond_walls(walls_ref, rows - HALO, (rows, nz))
    for i in range(1, nx + 2 * DEPTH - 1):
        centre, rate = plane_rates(functools.partial(plane_of, mid_ref, xlo_ref, xhi_ref), i, rows)
        for f in range(4):
            one_ref[f, i - 1] = stage_one(outside, centre[f], rate[f])
    copy.wait()


def step_kernel(
    walls_ref, mid_ref, xlo_ref, xhi_ref, first_ref, own_ref, low_ref, high_ref, basis_ref, sample_ref,
    flow_ref, snap_ref, cross_ref,
    one_ref, two_ref,
):
    fields, nx, ny, nz = flow_ref.shape
    rows = mid_ref.shape[2]
    modes = basis_ref.shape[1]
    planes = nx + 2 * DEPTH
    lane = lax.broadcasted_iota(jnp.int32, (rows, nz), 1)
    outside = beyond_walls(walls_ref, ny, (rows, nz))
    every = range(4)
    start = functools.partial(plane_of, mid_ref, xlo_ref, xhi_ref)

    left = lane % GROUP < DEPTH

    def window_rates(q):
        return rates(
            q, [step(v, GROUP, 1) for v in q], [step(v, -GROUP, 1) for v in q],
            [step(v, 1, 0) for v in q], [step(v, -1, 0) for v in q],
            [step(v, 1, 1) for v in q], [step(v, -1, 1) for v in q],
        )

    own = [own_ref[f] for f in every]
    other = [jnp.where(left, low_ref[f], high_ref[f]) for f in every]
    windows = []
    for parts in ((other, own), (own, other)):
        q0 = [jnp.where(left, a, b) for a, b in zip(*parts)]
        q1 = [stage_one(outside, v, r) for v, r in zip(q0, window_rates(q0))]
        q2 = [stage_two(outside, s, v, r) for s, v, r in zip(q0, q1, window_rates(q1))]
        windows.append((q1, q2))
    (low_one, low_two), (high_one, high_two) = windows
    ends_one = [jnp.where(left, a, b) for a, b in zip(low_one, high_one)]
    ends_two = [jnp.where(left, a, b) for a, b in zip(low_two, high_two)]
    rim_one = [jnp.where(left, b, a) for a, b in zip(low_one, high_one)]

    def at_plane(values, i):
        return [pltpu.roll(v, (2 * nz - GROUP * i - DEPTH) % nz, 1) for v in values]

    rim = (lane == 0) | (lane == nz - 1)
    for i in range(1, planes - 1):
        for f, value in enumerate(at_plane(rim_one, i)):
            one_ref[f, i - 1] = jnp.where(rim, value, first_ref[f, i - 1])
    for i in range(2, planes - 2):
        centre, rate = plane_rates(lambda f, i: one_ref[f, i - 1], i, rows, at_plane(ends_one, i))
        for f in every:
            two_ref[f, i - 2] = stage_two(outside, start(f, i), centre[f], rate[f])
    for i in range(3, planes - 3):
        centre, rate = plane_rates(lambda f, i: two_ref[f, i - 2], i, ny, at_plane(ends_two, i))
        for f in every:
            value = 1.0 / 3.0 * start(f, i)[:ny] + 2.0 / 3.0 * (centre[f] + DT_STEP * rate[f])
            flow_ref[f, i - DEPTH] = value

    points = sample_ref.shape[1]
    spot = jnp.broadcast_to(sample_ref[...], (nz, points))
    place = lax.broadcasted_iota(jnp.int32, (nx * ny, points), 0)
    in_row = (place == jnp.broadcast_to(sample_ref[...] // nz, (nx * ny, points))).astype(jnp.bfloat16)
    in_lane = lax.broadcasted_iota(jnp.int32, (nz, points), 0) == spot % nz
    product = jnp.zeros((modes + 1, points), jnp.float32)
    for c in range(3):
        field = flow_ref[c].reshape(nx * ny, nz).T
        high = field.astype(jnp.bfloat16)
        rest = field - high.astype(jnp.float32)
        middle = rest.astype(jnp.bfloat16)
        low = (rest - middle.astype(jnp.float32)).astype(jnp.bfloat16)
        found = sum(
            lax.dot_general(p, in_row, (((1,), (0,)), ((), ())), preferred_element_type=jnp.float32)
            for p in (high, middle, low)
        )
        picked = jnp.sum(jnp.where(in_lane, found, 0.0), axis=0, keepdims=True)
        snap_ref[c] = picked
        product = product + jnp.concatenate([basis_ref[c], picked], axis=0) * picked
    total = jnp.sum(product, axis=1, keepdims=True)
    size = modes + 1
    diagonal = lax.broadcasted_iota(jnp.int32, (size, size), 0) == lax.broadcasted_iota(jnp.int32, (size, size), 1)
    cross_ref[...] = jnp.sum(jnp.where(diagonal, total, 0.0), axis=0, keepdims=True)


def merge_kernel(parts_ref, cross_ref, send_ref):
    total = parts_ref[0]
    for d in range(1, parts_ref.shape[0]):
        total = total + parts_ref[d]
    block = jnp.concatenate([total, cross_ref[...]], axis=0)
    for d in range(send_ref.shape[0]):
        send_ref[d] = block


def final_kernel(
    count, got_ref, basis_ref, snap_ref, flow_ref,
    basis_hbm, factor_hbm, flow_hbm,
    packed_ref, work_ref, basis_out_ref, factor_ref, sems,
):
    comps, modes, points = basis_ref.shape
    size = modes + 1
    tall = size // 4
    per = got_ref.shape[1] - 1
    copies = [pltpu.make_async_copy(flow_ref, flow_hbm, sems.at[0])]
    copies[0].start()

    total = jnp.zeros((per + 1, size), jnp.float32)
    for d in range(got_ref.shape[0]):
        block = got_ref[d]
        if per * d < packed_ref.shape[0]:
            packed_ref[per * d : per * d + per] = block[0:per]
        total = total + block
    cross = total[per : per + 1] / count
    lane = lax.broadcasted_iota(jnp.int32, (tall, size), 1)
    row = lax.broadcasted_iota(jnp.int32, (tall, size), 0)
    old = unpack_upper([packed_ref[tall * k : tall * k + tall] / count for k in range(3)], tall)
    for k in range(4):
        side = jnp.sum(jnp.where(lane == row + tall * k, cross, 0.0), axis=1, keepdims=True)
        value = jnp.where(lane == size - 1, side, old[k])
        if k == 3:
            value = jnp.where(row == tall - 1, jnp.broadcast_to(cross, value.shape), value)
        work_ref[tall * k : tall * k + tall, 0:size] = value
        work_ref[tall * k : tall * k + tall, size : 2 * size] = (lane == row + tall * k).astype(jnp.float32)

    stacked = [jnp.concatenate([basis_ref[c], snap_ref[c]], axis=0) for c in range(comps)]
    for k in range(4):
        base = tall * k
        eliminate(work_ref, base, tall)
        done = work_ref[base : base + tall, :]
        if k < 3:
            change = dot(done[:, 0:size], done, ((0,), (0,)))
            work_ref[base + tall : size, :] = work_ref[base + tall : size, :] - change[base + tall : size]
        factor_ref[base : base + tall, :] = jnp.where(lane >= row + base, done[:, 0:size], 0.0)
        for c in range(comps):
            basis_out_ref[c, base : base + tall, :] = dot(done[:, size : 2 * size], stacked[c], ((1,), (0,)))
        rows = (slice(None), pl.ds(base, tall), slice(None))
        copies.append(pltpu.make_async_copy(basis_out_ref.at[rows], basis_hbm.at[rows], sems.at[2 + k]))
        copies[-1].start()
    copies.append(pltpu.make_async_copy(factor_ref, factor_hbm, sems.at[1]))
    copies[-1].start()
    for copy in copies:
        copy.wait()


def eliminate(work_ref, base, tall):
    blocks = tall // 8
    sub = lax.broadcasted_iota(jnp.int32, (8, 128), 0)
    panel = [work_ref[base + 8 * b : base + 8 * b + 8, :] for b in range(blocks)]
    column = [
        [jnp.broadcast_to(panel[b][:, base + k : base + k + 1], (8, 128)) for b in range(blocks)] for k in range(tall)
    ]
    scale = [jnp.zeros((8, 128), jnp.float32) for _ in range(blocks)]
    for j in range(tall):
        mine, at = divmod(j, 8)
        pivot = column[j][mine][at : at + 1, :]
        inverse = 1.0 / pivot
        for k in range(j + 1, tall):
            other, place = divmod(k, 8)
            times = column[j][other][place : place + 1, :]
            for b in range(other, blocks):
                if k == j + 1:
                    column[k][b] = column[k][b] - (column[j][b] * times) * inverse
                else:
                    column[k][b] = column[k][b] - column[j][b] * (times * inverse)
        scale[mine] = jnp.where(sub == at, lax.rsqrt(pivot), scale[mine])
        pivot_row = panel[mine][at : at + 1, :] * jnp.concatenate([inverse, inverse], axis=1)
        for b in range(mine, blocks):
            times = jnp.where(sub > at, column[j][b], 0.0) if b == mine else column[j][b]
            panel[b] = panel[b] - jnp.concatenate([times, times], axis=1) * pivot_row
    for b in range(blocks):
        work_ref[base + 8 * b : base + 8 * b + 8, :] = panel[b] * jnp.concatenate([scale[b], scale[b]], axis=1)


def local(flow, basis, sample):
    fields, nx, ny, nz = flow.shape
    modes, comps, points = basis.shape
    size = modes + 1
    devices = lax.axis_size("gx") * lax.axis_size("gy") * lax.axis_size("gz")
    count = float(comps * points * devices)
    shape = functools.partial(jax.ShapeDtypeStruct, dtype=jnp.float32)
    call = functools.partial(pl.pallas_call, compiler_params=PARAMS)
    bricks = jnp.transpose(basis, (1, 0, 2))

    whole = pl.BlockSpec(memory_space=pltpu.HBM)
    flat = flow.reshape(fields, nx * ny, nz)
    quarter = size // 4
    per = -(-3 * quarter // devices)

    strip = shape((fields, nx * DEPTH, nz))
    bottom, top = call(
        functools.partial(strips_kernel, nx), out_shape=(strip, strip), in_specs=[VMEM], out_specs=(VMEM, VMEM)
    )(flat)
    ylo, yhi = neighbours(bottom, top, "gy")
    gram = call(
        gram_kernel,
        out_shape=shape((devices, per, size)),
        in_specs=[VMEM],
        out_specs=VMEM,
        scratch_shapes=[pltpu.VMEM((size, size), jnp.float32), pltpu.VMEM((devices * per, size), jnp.float32)],
    )(bricks)
    ylo, yhi, gram = lax.optimization_barrier((ylo, yhi, gram))

    rows = ny + HALO
    place = lax.axis_index("gy")
    walls = jnp.stack([place == 0, place == lax.axis_size("gy") - 1]).astype(jnp.int32)
    walls = jnp.broadcast_to(walls[:, None], (2, nz))
    face = shape((fields, DEPTH * ny + HALO, nz))
    mid, first, last = call(
        functools.partial(walls_kernel, nx),
        out_shape=(shape((fields, nx * rows, nz)), face, face),
        in_specs=[VMEM] * 4,
        out_specs=(VMEM,) * 3,
    )(walls, flat, ylo, yhi)
    mid = mid.reshape(fields, nx, rows, nz)
    low_face, high_face = neighbours(first, last, "gx")
    parts = lax.all_to_all(gram, ALL, 0, 0)

    beside = shape((fields, DEPTH, rows, nz))
    packed, xlo, xhi = call(
        pack_kernel,
        out_shape=(shape((fields, rows, nz)), beside, beside),
        in_specs=[VMEM] * 3,
        out_specs=(VMEM,) * 3,
    )(mid, low_face, high_face)
    if lax.axis_size("gz") == 2:
        low = high = lax.ppermute(packed, "gz", [(0, 1), (1, 0)])
    else:
        low, high = neighbours(packed, packed, "gz")
    begun, cells = call(
        first_kernel,
        out_shape=(
            shape((fields, nx + 2 * DEPTH - 2, rows, nz)),
            jax.ShapeDtypeStruct((1, points), sample.dtype),
        ),
        in_specs=[VMEM, whole] + [VMEM] * 3,
        out_specs=(VMEM, VMEM),
        scratch_shapes=[pltpu.SemaphoreType.DMA],
    )(walls, sample.reshape(1, points), mid, xlo, xhi)
    flow_new, snapshot, cross = call(
        step_kernel,
        out_shape=(shape(flow.shape), shape((comps, 1, points)), shape((1, size))),
        in_specs=[VMEM] * 10,
        out_specs=(VMEM, VMEM, VMEM),
        scratch_shapes=[
            pltpu.VMEM((fields, nx + 2 * DEPTH - 2, rows, nz), jnp.float32),
            pltpu.VMEM((fields, nx + 2 * DEPTH - 4, rows, nz), jnp.float32),
        ],
    )(walls, mid, xlo, xhi, begun, packed, low, high, bricks, cells)

    send = call(
        merge_kernel, out_shape=shape((devices, per + 1, size)), in_specs=[VMEM] * 2, out_specs=VMEM
    )(parts, cross)
    got = lax.all_to_all(send, ALL, 0, 0)
    basis_next, factor, flow_next = call(
        functools.partial(final_kernel, count),
        out_shape=(shape((comps, size, points)), shape((size, size)), shape(flow.shape)),
        in_specs=[VMEM] * 4,
        out_specs=(whole,) * 3,
        scratch_shapes=[
            pltpu.VMEM((3 * quarter, size), jnp.float32),
            pltpu.VMEM((size, 2 * size), jnp.float32),
            pltpu.VMEM((comps, size, points), jnp.float32),
            pltpu.VMEM((size, size), jnp.float32),
            pltpu.SemaphoreType.DMA((6,)),
        ],
    )(got, bricks, snapshot, flow_new)
    return flow_next, jnp.transpose(basis_next, (1, 0, 2)), factor


def solution(mesh):
    return jax.shard_map(
        local,
        mesh=mesh,
        in_specs=(
            P(None, "gx", "gy", "gz"),
            P(None, None, ("gx", "gy", "gz")),
            P(("gx", "gy", "gz")),
        ),
        out_specs=(P(None, "gx", "gy", "gz"), P(None, None, ("gx", "gy", "gz")), P()),
        check_vma=False,
    )
```

```python
import functools

import jax
import jax.numpy as jnp
from jax import lax
from jax.experimental import pallas as pl
from jax.experimental.pallas import tpu as pltpu
from jax.sharding import PartitionSpec as P

DT_STEP = 0.35
VISCOSITY = 0.2
SOUND_SQ = 1.0
DRIVING = 0.5

ALL = ("gx", "gy", "gz")
DEPTH = 3
EXACT = lax.Precision.HIGHEST
VMEM = pl.BlockSpec(memory_space=pltpu.VMEM)
PARAMS = pltpu.CompilerParams(vmem_limit_bytes=40 * 1024 * 1024)


def dot(a, b, dims):
    return lax.dot_general(
        a, b, (dims, ((), ())), precision=EXACT, preferred_element_type=jnp.float32
    )


def neighbours(block_low, block_high, axis):
    count = lax.axis_size(axis)
    forward = [(i, (i + 1) % count) for i in range(count)]
    backward = [(target, source) for source, target in forward]
    return lax.ppermute(block_high, axis, forward), lax.ppermute(block_low, axis, backward)


def pairs(block_even, block_odd, axis):
    count = lax.axis_size(axis)
    even = [(i, i + 1 - 2 * (i % 2)) for i in range(count)]
    odd = [(i, (i - 1 + 2 * (i % 2)) % count) for i in range(count)]
    return lax.ppermute(block_even, axis, even), lax.ppermute(block_odd, axis, odd)


LOWER_WALL, UPPER_WALL, ODD_Y, ODD_X = range(4)


def flag(flags_ref, which):
    return flags_ref[which : which + 1] == 1


def pack_upper(rows, tall):
    size = rows.shape[1]
    lane = lax.broadcasted_iota(jnp.int32, (tall, size), 1)
    part = [rows[tall * k : tall * k + tall] for k in range(4)]
    return [part[0], jnp.where(lane >= tall, part[1], pltpu.roll(part[3], tall, 1)), part[2]]


def unpack_upper(packed, tall):
    return [packed[0], packed[1], packed[2], pltpu.roll(packed[1], packed[1].shape[1] - tall, 1)]


def gram_kernel(basis_ref, send_ref, gram_ref, packed_ref):
    modes = basis_ref.shape[1]
    tall = gram_ref.shape[0] // 4
    total = jnp.zeros((modes, modes), jnp.float32)
    for c in range(basis_ref.shape[0]):
        rows = basis_ref[c]
        total = total + dot(rows, rows, ((1,), (1,)))
    gram_ref[...] = jnp.zeros_like(gram_ref)
    gram_ref[0:modes, 0:modes] = total
    packed_ref[...] = jnp.zeros_like(packed_ref)
    for k, value in enumerate(pack_upper(gram_ref[...], tall)):
        packed_ref[tall * k : tall * k + tall] = value
    per = send_ref.shape[1]
    for d in range(send_ref.shape[0]):
        send_ref[d] = packed_ref[per * d : per * d + per]


GAP = 2
HALO = 2 * DEPTH + GAP


def strips_kernel(planes, flags_ref, flow_ref, even_ref, odd_ref):
    ny = flow_ref.shape[1] // planes
    odd = flag(flags_ref, ODD_Y)
    for f in range(flow_ref.shape[0]):
        for j in range(DEPTH):
            bottom = flow_ref[f, pl.ds(j, planes, stride=ny), :]
            top = flow_ref[f, pl.ds(ny - DEPTH + j, planes, stride=ny), :]
            even_ref[f, planes * j : planes * j + planes] = jnp.where(odd, bottom, top)
            odd_ref[f, planes * j : planes * j + planes] = jnp.where(odd, top, bottom)


def walls_kernel(planes, flags_ref, flow_ref, even_ref, odd_ref, mid_ref, face_even_ref, face_odd_ref):
    fields, cells, nz = flow_ref.shape
    odd_y, odd_x = flag(flags_ref, ODD_Y), flag(flags_ref, ODD_X)
    ny = cells // planes
    rows = ny + HALO
    sub = lax.broadcasted_iota(jnp.int32, (HALO, nz), 0)
    empty = jnp.zeros((planes, nz), jnp.float32)
    for f in range(fields):
        for i in range(planes):
            mid_ref[f, rows * i : rows * i + ny] = flow_ref[f, ny * i : ny * i + ny]
        for j in range(HALO):
            k = j if j < DEPTH else j - DEPTH - GAP
            part = slice(planes * k, planes * k + planes)
            if j < DEPTH:
                value = jnp.where(odd_y, odd_ref[f, part], even_ref[f, part])
                value = jnp.where(flag(flags_ref, UPPER_WALL), 0.0, value)
            elif j < DEPTH + GAP:
                value = empty
            else:
                value = jnp.where(odd_y, even_ref[f, part], odd_ref[f, part])
                value = jnp.where(flag(flags_ref, LOWER_WALL), 0.0, value)
            mid_ref[f, pl.ds(ny + j, planes, stride=rows), :] = value
        faces = []
        for begin, near, next_one in ((0, 0, 1), (planes - DEPTH, planes - 1, planes - 2)):
            halos = [mid_ref[f, rows * i + ny : rows * i + rows] for i in (near, next_one)]
            faces.append([flow_ref[f, ny * i : ny * i + ny] for i in range(begin, begin + DEPTH)] + [corner_rows(*halos, sub)])
        for k, (first, last) in enumerate(zip(*faces)):
            part = slice(ny * k, ny * k + first.shape[0])
            face_even_ref[f, part] = jnp.where(odd_x, first, last)
            face_odd_ref[f, part] = jnp.where(odd_x, last, first)


def corner_rows(near, next_one, sub):
    tile = jnp.where(sub == 2, pltpu.roll(next_one, 2, 0), pltpu.roll(next_one, 6, 0))
    tile = jnp.where((sub == 2) | (sub == 5), tile, 0.0)
    return jnp.where((sub < 2) | (sub >= 6), near, tile)


def corner_planes(tile, sub):
    near = jnp.where((sub < 2) | (sub >= 6), tile, 0.0)
    next_one = jnp.where(sub == 0, pltpu.roll(tile, 6, 0), pltpu.roll(tile, 2, 0))
    return [near, jnp.where((sub == 0) | (sub == 7), next_one, 0.0), jnp.zeros_like(tile)]


def plane_of(mid_ref, xlo_ref, xhi_ref, f, i):
    nx = mid_ref.shape[1]
    if i < DEPTH:
        return xlo_ref[f, i]
    if i < DEPTH + nx:
        return mid_ref[f, i - DEPTH]
    return xhi_ref[f, i - DEPTH - nx]


GROUP = 8


def pack_kernel(flags_ref, mid_ref, even_ref, odd_ref, packed_ref, xlo_ref, xhi_ref):
    fields, nx, rows, nz = mid_ref.shape
    ny = rows - HALO
    odd = flag(flags_ref, ODD_X)
    lane = lax.broadcasted_iota(jnp.int32, (rows, nz), 1)
    sub = lax.broadcasted_iota(jnp.int32, (HALO, nz), 0)
    for f in range(fields):
        for one_ref, other_ref, out_ref, order in (
            (even_ref, odd_ref, xlo_ref, (2, 1, 0)), (odd_ref, even_ref, xhi_ref, (0, 1, 2))
        ):
            face = jnp.where(odd, one_ref[f], other_ref[f])
            halo = corner_planes(face[ny * DEPTH :], sub)
            for k in range(DEPTH):
                out_ref[f, k, 0:ny] = face[ny * k : ny * k + ny]
                out_ref[f, k, ny:rows] = halo[order[k]]
        value = jnp.zeros((rows, nz), jnp.float32)
        for i in range(nx + 2 * DEPTH):
            start = GROUP * i
            moved = pltpu.roll(plane_of(mid_ref, xlo_ref, xhi_ref, f, i), (start + DEPTH) % nz, 1)
            value = jnp.where((lane >= start) & (lane < start + 2 * DEPTH), moved, value)
        packed_ref[f] = value


def step(value, by, axis):
    size = value.shape[axis]
    return pltpu.roll(value, (size - by) % size, axis)


def rates(centre, x_plus, x_minus, y_plus, y_minus, z_plus, z_minus):
    slope_x = [0.5 * (a - b) for a, b in zip(x_plus, x_minus)]
    slope_y = [0.5 * (a - b) for a, b in zip(y_plus, y_minus)]
    slope_z = [0.5 * (a - b) for a, b in zip(z_plus, z_minus)]
    pressure = [slope_x[3], slope_y[3], slope_z[3]]
    out = []
    for f in range(3):
        laplace = (
            x_plus[f] + x_minus[f] + (y_plus[f] + y_minus[f]) + (z_plus[f] + z_minus[f]) - 6.0 * centre[f]
        )
        advect = centre[0] * slope_x[f] + centre[1] * slope_y[f] + centre[2] * slope_z[f]
        value = VISCOSITY * laplace - advect - pressure[f]
        if f == 0:
            value = value + DRIVING
        out.append(value)
    out.append(-SOUND_SQ * (slope_x[0] + slope_y[1] + slope_z[2]))
    return out


def beyond_walls(flags_ref, ny, shape):
    row = lax.broadcasted_iota(jnp.int32, shape, 0)
    below = (row >= ny + DEPTH + GAP) & flag(flags_ref, LOWER_WALL)
    above = (row >= ny) & (row < ny + DEPTH) & flag(flags_ref, UPPER_WALL)
    return below | above


def plane_rates(read, i, rows, ends=None):
    every = range(4)
    centre = [read(f, i) for f in every]
    x_plus = [read(f, i + 1)[:rows] for f in every]
    x_minus = [read(f, i - 1)[:rows] for f in every]
    y_plus = [step(v, 1, 0)[:rows] for v in centre]
    y_minus = [step(v, -1, 0)[:rows] for v in centre]
    centre = [v[:rows] for v in centre]
    upward, downward = centre, centre
    if ends is not None:
        lane = lax.broadcasted_iota(jnp.int32, centre[0].shape, 1)
        upward = [jnp.where(lane == 0, e[:rows], v) for e, v in zip(ends, centre)]
        downward = [jnp.where(lane == lane.shape[1] - 1, e[:rows], v) for e, v in zip(ends, centre)]
    z_plus = [step(v, 1, 1) for v in upward]
    z_minus = [step(v, -1, 1) for v in downward]
    return centre, rates(centre, x_plus, x_minus, y_plus, y_minus, z_plus, z_minus)


def stage_one(outside, value, rate):
    return jnp.where(outside, 0.0, value + DT_STEP * rate)


def stage_two(outside, begin, value, rate):
    return jnp.where(outside, 0.0, 0.75 * begin + 0.25 * (value + DT_STEP * rate))


def first_kernel(flags_ref, sample_hbm, mid_ref, xlo_ref, xhi_ref, one_ref, sample_ref, sem):
    copy = pltpu.make_async_copy(sample_hbm, sample_ref, sem)
    copy.start()
    fields, nx, rows, nz = mid_ref.shape
    outside = beyond_walls(flags_ref, rows - HALO, (rows, nz))
    for i in range(1, nx + 2 * DEPTH - 1):
        centre, rate = plane_rates(functools.partial(plane_of, mid_ref, xlo_ref, xhi_ref), i, rows)
        for f in range(4):
            one_ref[f, i - 1] = stage_one(outside, centre[f], rate[f])
    copy.wait()


def step_kernel(
    flags_ref, mid_ref, xlo_ref, xhi_ref, first_ref, own_ref, low_ref, high_ref, basis_ref, sample_ref,
    flow_ref, snap_ref, cross_ref,
    one_ref, two_ref,
):
    fields, nx, ny, nz = flow_ref.shape
    rows = mid_ref.shape[2]
    modes = basis_ref.shape[1]
    planes = nx + 2 * DEPTH
    lane = lax.broadcasted_iota(jnp.int32, (rows, nz), 1)
    outside = beyond_walls(flags_ref, ny, (rows, nz))
    every = range(4)
    start = functools.partial(plane_of, mid_ref, xlo_ref, xhi_ref)

    left = lane % GROUP < DEPTH

    def window_rates(q):
        return rates(
            q, [step(v, GROUP, 1) for v in q], [step(v, -GROUP, 1) for v in q],
            [step(v, 1, 0) for v in q], [step(v, -1, 0) for v in q],
            [step(v, 1, 1) for v in q], [step(v, -1, 1) for v in q],
        )

    own = [own_ref[f] for f in every]
    other = [jnp.where(left, low_ref[f], high_ref[f]) for f in every]
    windows = []
    for parts in ((other, own), (own, other)):
        q0 = [jnp.where(left, a, b) for a, b in zip(*parts)]
        q1 = [stage_one(outside, v, r) for v, r in zip(q0, window_rates(q0))]
        q2 = [stage_two(outside, s, v, r) for s, v, r in zip(q0, q1, window_rates(q1))]
        windows.append((q1, q2))
    (low_one, low_two), (high_one, high_two) = windows
    ends_one = [jnp.where(left, a, b) for a, b in zip(low_one, high_one)]
    ends_two = [jnp.where(left, a, b) for a, b in zip(low_two, high_two)]
    rim_one = [jnp.where(left, b, a) for a, b in zip(low_one, high_one)]

    def at_plane(values, i):
        return [pltpu.roll(v, (2 * nz - GROUP * i - DEPTH) % nz, 1) for v in values]

    rim = (lane == 0) | (lane == nz - 1)
    for i in range(1, planes - 1):
        for f, value in enumerate(at_plane(rim_one, i)):
            one_ref[f, i - 1] = jnp.where(rim, value, first_ref[f, i - 1])
    for i in range(2, planes - 2):
        centre, rate = plane_rates(lambda f, i: one_ref[f, i - 1], i, rows, at_plane(ends_one, i))
        for f in every:
            two_ref[f, i - 2] = stage_two(outside, start(f, i), centre[f], rate[f])
    for i in range(3, planes - 3):
        centre, rate = plane_rates(lambda f, i: two_ref[f, i - 2], i, ny, at_plane(ends_two, i))
        for f in every:
            value = 1.0 / 3.0 * start(f, i)[:ny] + 2.0 / 3.0 * (centre[f] + DT_STEP * rate[f])
            flow_ref[f, i - DEPTH] = value

    points = sample_ref.shape[1]
    spot = jnp.broadcast_to(sample_ref[...], (nz, points))
    place = lax.broadcasted_iota(jnp.int32, (nx * ny, points), 0)
    in_row = (place == jnp.broadcast_to(sample_ref[...] // nz, (nx * ny, points))).astype(jnp.bfloat16)
    in_lane = lax.broadcasted_iota(jnp.int32, (nz, points), 0) == spot % nz
    product = jnp.zeros((modes + 1, points), jnp.float32)
    for c in range(3):
        field = flow_ref[c].reshape(nx * ny, nz).T
        high = field.astype(jnp.bfloat16)
        rest = field - high.astype(jnp.float32)
        middle = rest.astype(jnp.bfloat16)
        low = (rest - middle.astype(jnp.float32)).astype(jnp.bfloat16)
        found = sum(
            lax.dot_general(p, in_row, (((1,), (0,)), ((), ())), preferred_element_type=jnp.float32)
            for p in (high, middle, low)
        )
        picked = jnp.sum(jnp.where(in_lane, found, 0.0), axis=0, keepdims=True)
        snap_ref[c] = picked
        product = product + jnp.concatenate([basis_ref[c], picked], axis=0) * picked
    total = jnp.sum(product, axis=1, keepdims=True)
    size = modes + 1
    diagonal = lax.broadcasted_iota(jnp.int32, (size, size), 0) == lax.broadcasted_iota(jnp.int32, (size, size), 1)
    cross_ref[...] = jnp.sum(jnp.where(diagonal, total, 0.0), axis=0, keepdims=True)


def merge_kernel(parts_ref, cross_ref, send_ref):
    total = parts_ref[0]
    for d in range(1, parts_ref.shape[0]):
        total = total + parts_ref[d]
    block = jnp.concatenate([total, cross_ref[...]], axis=0)
    for d in range(send_ref.shape[0]):
        send_ref[d] = block


def final_kernel(
    count, got_ref, basis_ref, snap_ref, flow_ref,
    basis_hbm, factor_hbm, flow_hbm,
    packed_ref, work_ref, basis_out_ref, factor_ref, sems,
):
    comps, modes, points = basis_ref.shape
    size = modes + 1
    tall = size // 4
    per = got_ref.shape[1] - 1
    copies = [pltpu.make_async_copy(flow_ref, flow_hbm, sems.at[0])]
    copies[0].start()

    total = jnp.zeros((per + 1, size), jnp.float32)
    for d in range(got_ref.shape[0]):
        block = got_ref[d]
        if per * d < packed_ref.shape[0]:
            packed_ref[per * d : per * d + per] = block[0:per]
        total = total + block
    cross = total[per : per + 1] / count
    mark = (lax.broadcasted_iota(jnp.int32, (8, size), 1) == size - 1).astype(jnp.float32)
    top = lax.broadcasted_iota(jnp.int32, (8, size), 0) == 0
    side = dot(jnp.where(top, jnp.broadcast_to(cross, (8, size)), 0.0), mark, ((0,), (0,)))
    lane = lax.broadcasted_iota(jnp.int32, (tall, size), 1)
    row = lax.broadcasted_iota(jnp.int32, (tall, size), 0)
    old = unpack_upper([packed_ref[tall * k : tall * k + tall] / count for k in range(3)], tall)
    for k in range(4):
        value = jnp.where(lane == size - 1, side[tall * k : tall * k + tall], old[k])
        if k == 3:
            value = jnp.where(row == tall - 1, jnp.broadcast_to(cross, value.shape), value)
        work_ref[tall * k : tall * k + tall, 0:size] = value
        work_ref[tall * k : tall * k + tall, size : 2 * size] = (lane == row + tall * k).astype(jnp.float32)

    stacked = [jnp.concatenate([basis_ref[c], snap_ref[c]], axis=0) for c in range(comps)]
    for k in range(4):
        base = tall * k
        eliminate(work_ref, base, tall)
        done = work_ref[base : base + tall, :]
        if k < 3:
            change = dot(done[:, 0:size], done, ((0,), (0,)))
            work_ref[base + tall : size, :] = work_ref[base + tall : size, :] - change[base + tall : size]
        factor_ref[base : base + tall, :] = jnp.where(lane >= row + base, done[:, 0:size], 0.0)
        for c in range(comps):
            basis_out_ref[c, base : base + tall, :] = dot(done[:, size : 2 * size], stacked[c], ((1,), (0,)))
        rows = (slice(None), pl.ds(base, tall), slice(None))
        copies.append(pltpu.make_async_copy(basis_out_ref.at[rows], basis_hbm.at[rows], sems.at[2 + k]))
        copies[-1].start()
    copies.append(pltpu.make_async_copy(factor_ref, factor_hbm, sems.at[1]))
    copies[-1].start()
    for copy in copies:
        copy.wait()


def eliminate(work_ref, base, tall):
    blocks = tall // 8
    sub = lax.broadcasted_iota(jnp.int32, (8, 128), 0)
    panel = [work_ref[base + 8 * b : base + 8 * b + 8, :] for b in range(blocks)]
    column = [
        [jnp.broadcast_to(panel[b][:, base + k : base + k + 1], (8, 128)) for b in range(blocks)] for k in range(tall)
    ]
    scale = [jnp.zeros((8, 128), jnp.float32) for _ in range(blocks)]
    for j in range(tall):
        mine, at = divmod(j, 8)
        pivot = column[j][mine][at : at + 1, :]
        inverse = 1.0 / pivot
        scaled = {b: column[j][b] * inverse for b in range(mine, blocks)}
        for k in range(j + 1, tall):
            other, place = divmod(k, 8)
            times = scaled[other][place : place + 1, :]
            for b in range(other, blocks):
                column[k][b] = column[k][b] - column[j][b] * times
        scale[mine] = jnp.where(sub == at, lax.rsqrt(pivot), scale[mine])
        pivot_row = panel[mine][at : at + 1, :] * jnp.concatenate([inverse, inverse], axis=1)
        for b in range(mine, blocks):
            times = jnp.where(sub > at, column[j][b], 0.0) if b == mine else column[j][b]
            panel[b] = panel[b] - jnp.concatenate([times, times], axis=1) * pivot_row
    for b in range(blocks):
        work_ref[base + 8 * b : base + 8 * b + 8, :] = panel[b] * jnp.concatenate([scale[b], scale[b]], axis=1)


def local(flow, basis, sample):
    fields, nx, ny, nz = flow.shape
    modes, comps, points = basis.shape
    size = modes + 1
    devices = lax.axis_size("gx") * lax.axis_size("gy") * lax.axis_size("gz")
    count = float(comps * points * devices)
    shape = functools.partial(jax.ShapeDtypeStruct, dtype=jnp.float32)
    call = functools.partial(pl.pallas_call, compiler_params=PARAMS)
    bricks = jnp.transpose(basis, (1, 0, 2))

    whole = pl.BlockSpec(memory_space=pltpu.HBM)
    flat = flow.reshape(fields, nx * ny, nz)
    quarter = size // 4
    per = -(-3 * quarter // devices)

    place = lax.axis_index("gy")
    flags = [place == 0, place == lax.axis_size("gy") - 1, place % 2 == 1, lax.axis_index("gx") % 2 == 1]
    flags = jnp.broadcast_to(jnp.stack(flags).astype(jnp.int32)[:, None], (len(flags), nz))
    strip = shape((fields, nx * DEPTH, nz))
    strips = call(
        functools.partial(strips_kernel, nx), out_shape=(strip, strip), in_specs=[VMEM] * 2, out_specs=(VMEM, VMEM)
    )(flags, flat)
    y_even, y_odd = pairs(*strips, "gy")
    gram = call(
        gram_kernel,
        out_shape=shape((devices, per, size)),
        in_specs=[VMEM],
        out_specs=VMEM,
        scratch_shapes=[pltpu.VMEM((size, size), jnp.float32), pltpu.VMEM((devices * per, size), jnp.float32)],
    )(bricks)
    y_even, y_odd, gram = lax.optimization_barrier((y_even, y_odd, gram))

    rows = ny + HALO
    face = shape((fields, DEPTH * ny + HALO, nz))
    mid, *faces = call(
        functools.partial(walls_kernel, nx),
        out_shape=(shape((fields, nx * rows, nz)), face, face),
        in_specs=[VMEM] * 4,
        out_specs=(VMEM,) * 3,
    )(flags, flat, y_even, y_odd)
    mid = mid.reshape(fields, nx, rows, nz)
    x_even, x_odd = pairs(*faces, "gx")
    parts = lax.all_to_all(gram, ALL, 0, 0)

    beside = shape((fields, DEPTH, rows, nz))
    packed, xlo, xhi = call(
        pack_kernel,
        out_shape=(shape((fields, rows, nz)), beside, beside),
        in_specs=[VMEM] * 4,
        out_specs=(VMEM,) * 3,
    )(flags, mid, x_even, x_odd)
    if lax.axis_size("gz") == 2:
        low = high = lax.ppermute(packed, "gz", [(0, 1), (1, 0)])
    else:
        low, high = neighbours(packed, packed, "gz")
    begun, cells = call(
        first_kernel,
        out_shape=(
            shape((fields, nx + 2 * DEPTH - 2, rows, nz)),
            jax.ShapeDtypeStruct((1, points), sample.dtype),
        ),
        in_specs=[VMEM, whole] + [VMEM] * 3,
        out_specs=(VMEM, VMEM),
        scratch_shapes=[pltpu.SemaphoreType.DMA],
    )(flags, sample.reshape(1, points), mid, xlo, xhi)
    flow_new, snapshot, cross = call(
        step_kernel,
        out_shape=(shape(flow.shape), shape((comps, 1, points)), shape((1, size))),
        in_specs=[VMEM] * 10,
        out_specs=(VMEM, VMEM, VMEM),
        scratch_shapes=[
            pltpu.VMEM((fields, nx + 2 * DEPTH - 2, rows, nz), jnp.float32),
            pltpu.VMEM((fields, nx + 2 * DEPTH - 4, rows, nz), jnp.float32),
        ],
    )(flags, mid, xlo, xhi, begun, packed, low, high, bricks, cells)

    send = call(
        merge_kernel, out_shape=shape((devices, per + 1, size)), in_specs=[VMEM] * 2, out_specs=VMEM
    )(parts, cross)
    got = lax.all_to_all(send, ALL, 0, 0)
    basis_next, factor, flow_next = call(
        functools.partial(final_kernel, count),
        out_shape=(shape((comps, size, points)), shape((size, size)), shape(flow.shape)),
        in_specs=[VMEM] * 4,
        out_specs=(whole,) * 3,
        scratch_shapes=[
            pltpu.VMEM((3 * quarter, size), jnp.float32),
            pltpu.VMEM((size, 2 * size), jnp.float32),
            pltpu.VMEM((comps, size, points), jnp.float32),
            pltpu.VMEM((size, size), jnp.float32),
            pltpu.SemaphoreType.DMA((6,)),
        ],
    )(got, bricks, snapshot, flow_new)
    return flow_next, jnp.transpose(basis_next, (1, 0, 2)), factor


def solution(mesh):
    return jax.shard_map(
        local,
        mesh=mesh,
        in_specs=(
            P(None, "gx", "gy", "gz"),
            P(None, None, ("gx", "gy", "gz")),
            P(("gx", "gy", "gz")),
        ),
        out_specs=(P(None, "gx", "gy", "gz"), P(None, None, ("gx", "gy", "gz")), P()),
        check_vma=False,
    )
```

```python
import functools

import jax
import jax.numpy as jnp
from jax import lax
from jax.experimental import pallas as pl
from jax.experimental.pallas import tpu as pltpu
from jax.sharding import PartitionSpec as P

DT_STEP = 0.35
VISCOSITY = 0.2
SOUND_SQ = 1.0
DRIVING = 0.5

ALL = ("gx", "gy", "gz")
DEPTH = 3
EXACT = lax.Precision.HIGHEST
VMEM = pl.BlockSpec(memory_space=pltpu.VMEM)
PARAMS = pltpu.CompilerParams(vmem_limit_bytes=40 * 1024 * 1024)


def dot(a, b, dims):
    return lax.dot_general(
        a, b, (dims, ((), ())), precision=EXACT, preferred_element_type=jnp.float32
    )


def neighbours(block_low, block_high, axis):
    count = lax.axis_size(axis)
    forward = [(i, (i + 1) % count) for i in range(count)]
    backward = [(target, source) for source, target in forward]
    return lax.ppermute(block_high, axis, forward), lax.ppermute(block_low, axis, backward)


def pairs(block_even, block_odd, axis, periodic):
    count = lax.axis_size(axis)
    even = [(i, i + 1 - 2 * (i % 2)) for i in range(count)]
    odd = [(i, (i - 1 + 2 * (i % 2)) % count) for i in range(count)]
    if not periodic:
        odd[0], odd[-1] = (0, 0), (count - 1, count - 1)
    from_odd = lax.ppermute(block_odd, axis, odd)
    return lax.ppermute(block_even, axis, even), from_odd


LOWER_WALL, UPPER_WALL, ODD_Y, ODD_X = range(4)


def flag(flags_ref, which):
    return flags_ref[which : which + 1] == 1


def pack_upper(rows, tall):
    size = rows.shape[1]
    lane = lax.broadcasted_iota(jnp.int32, (tall, size), 1)
    part = [rows[tall * k : tall * k + tall] for k in range(4)]
    return [part[0], jnp.where(lane >= tall, part[1], pltpu.roll(part[3], tall, 1)), part[2]]


def unpack_upper(packed, tall):
    return [packed[0], packed[1], packed[2], pltpu.roll(packed[1], packed[1].shape[1] - tall, 1)]


def gram_kernel(basis_ref, send_ref, gram_ref, packed_ref):
    modes = basis_ref.shape[1]
    tall = gram_ref.shape[0] // 4
    total = jnp.zeros((modes, modes), jnp.float32)
    for c in range(basis_ref.shape[0]):
        rows = basis_ref[c]
        total = total + dot(rows, rows, ((1,), (1,)))
    gram_ref[...] = jnp.zeros_like(gram_ref)
    gram_ref[0:modes, 0:modes] = total
    packed_ref[...] = jnp.zeros_like(packed_ref)
    for k, value in enumerate(pack_upper(gram_ref[...], tall)):
        packed_ref[tall * k : tall * k + tall] = value
    per = send_ref.shape[1]
    for d in range(send_ref.shape[0]):
        send_ref[d] = packed_ref[per * d : per * d + per]


GAP = 2
HALO = 2 * DEPTH + GAP


def strips_kernel(planes, flags_ref, flow_ref, even_ref, odd_ref):
    ny = flow_ref.shape[1] // planes
    odd = flag(flags_ref, ODD_Y)
    for f in range(flow_ref.shape[0]):
        for j in range(DEPTH):
            bottom = flow_ref[f, pl.ds(j, planes, stride=ny), :]
            top = flow_ref[f, pl.ds(ny - DEPTH + j, planes, stride=ny), :]
            even_ref[f, planes * j : planes * j + planes] = jnp.where(odd, bottom, top)
            odd_ref[f, planes * j : planes * j + planes] = jnp.where(odd, top, bottom)


def walls_kernel(planes, flags_ref, flow_ref, even_ref, odd_ref, mid_ref, face_even_ref, face_odd_ref):
    fields, cells, nz = flow_ref.shape
    odd_y, odd_x = flag(flags_ref, ODD_Y), flag(flags_ref, ODD_X)
    ny = cells // planes
    rows = ny + HALO
    sub = lax.broadcasted_iota(jnp.int32, (HALO, nz), 0)
    empty = jnp.zeros((planes, nz), jnp.float32)
    for f in range(fields):
        for i in range(planes):
            mid_ref[f, rows * i : rows * i + ny] = flow_ref[f, ny * i : ny * i + ny]
        for j in range(HALO):
            k = j if j < DEPTH else j - DEPTH - GAP
            part = slice(planes * k, planes * k + planes)
            if j < DEPTH:
                value = jnp.where(odd_y, odd_ref[f, part], even_ref[f, part])
                value = jnp.where(flag(flags_ref, UPPER_WALL), 0.0, value)
            elif j < DEPTH + GAP:
                value = empty
            else:
                value = jnp.where(odd_y, even_ref[f, part], odd_ref[f, part])
                value = jnp.where(flag(flags_ref, LOWER_WALL), 0.0, value)
            mid_ref[f, pl.ds(ny + j, planes, stride=rows), :] = value
        faces = []
        for begin, near, next_one in ((0, 0, 1), (planes - DEPTH, planes - 1, planes - 2)):
            halos = [mid_ref[f, rows * i + ny : rows * i + rows] for i in (near, next_one)]
            faces.append([flow_ref[f, ny * i : ny * i + ny] for i in range(begin, begin + DEPTH)] + [corner_rows(*halos, sub)])
        for k, (first, last) in enumerate(zip(*faces)):
            part = slice(ny * k, ny * k + first.shape[0])
            face_even_ref[f, part] = jnp.where(odd_x, first, last)
            face_odd_ref[f, part] = jnp.where(odd_x, last, first)


def corner_rows(near, next_one, sub):
    tile = jnp.where(sub == 2, pltpu.roll(next_one, 2, 0), pltpu.roll(next_one, 6, 0))
    tile = jnp.where((sub == 2) | (sub == 5), tile, 0.0)
    return jnp.where((sub < 2) | (sub >= 6), near, tile)


def corner_planes(tile, sub):
    near = jnp.where((sub < 2) | (sub >= 6), tile, 0.0)
    next_one = jnp.where(sub == 0, pltpu.roll(tile, 6, 0), pltpu.roll(tile, 2, 0))
    return [near, jnp.where((sub == 0) | (sub == 7), next_one, 0.0), jnp.zeros_like(tile)]


def plane_of(mid_ref, xlo_ref, xhi_ref, f, i):
    nx = mid_ref.shape[1]
    if i < DEPTH:
        return xlo_ref[f, i]
    if i < DEPTH + nx:
        return mid_ref[f, i - DEPTH]
    return xhi_ref[f, i - DEPTH - nx]


GROUP = 8


def pack_kernel(flags_ref, mid_ref, even_ref, odd_ref, packed_ref, xlo_ref, xhi_ref):
    fields, nx, rows, nz = mid_ref.shape
    ny = rows - HALO
    odd = flag(flags_ref, ODD_X)
    lane = lax.broadcasted_iota(jnp.int32, (rows, nz), 1)
    sub = lax.broadcasted_iota(jnp.int32, (HALO, nz), 0)
    for f in range(fields):
        for one_ref, other_ref, out_ref, order in (
            (even_ref, odd_ref, xlo_ref, (2, 1, 0)), (odd_ref, even_ref, xhi_ref, (0, 1, 2))
        ):
            face = jnp.where(odd, one_ref[f], other_ref[f])
            halo = corner_planes(face[ny * DEPTH :], sub)
            for k in range(DEPTH):
                out_ref[f, k, 0:ny] = face[ny * k : ny * k + ny]
                out_ref[f, k, ny:rows] = halo[order[k]]
        value = jnp.zeros((rows, nz), jnp.float32)
        for i in range(nx + 2 * DEPTH):
            start = GROUP * i
            moved = pltpu.roll(plane_of(mid_ref, xlo_ref, xhi_ref, f, i), (start + DEPTH) % nz, 1)
            value = jnp.where((lane >= start) & (lane < start + 2 * DEPTH), moved, value)
        packed_ref[f] = value


def step(value, by, axis):
    size = value.shape[axis]
    return pltpu.roll(value, (size - by) % size, axis)


def rates(centre, x_plus, x_minus, y_plus, y_minus, z_plus, z_minus):
    slope_x = [0.5 * (a - b) for a, b in zip(x_plus, x_minus)]
    slope_y = [0.5 * (a - b) for a, b in zip(y_plus, y_minus)]
    slope_z = [0.5 * (a - b) for a, b in zip(z_plus, z_minus)]
    pressure = [slope_x[3], slope_y[3], slope_z[3]]
    out = []
    for f in range(3):
        laplace = (
            x_plus[f] + x_minus[f] + (y_plus[f] + y_minus[f]) + (z_plus[f] + z_minus[f]) - 6.0 * centre[f]
        )
        advect = centre[0] * slope_x[f] + centre[1] * slope_y[f] + centre[2] * slope_z[f]
        value = VISCOSITY * laplace - advect - pressure[f]
        if f == 0:
            value = value + DRIVING
        out.append(value)
    out.append(-SOUND_SQ * (slope_x[0] + slope_y[1] + slope_z[2]))
    return out


def beyond_walls(flags_ref, ny, shape):
    row = lax.broadcasted_iota(jnp.int32, shape, 0)
    below = (row >= ny + DEPTH + GAP) & flag(flags_ref, LOWER_WALL)
    above = (row >= ny) & (row < ny + DEPTH) & flag(flags_ref, UPPER_WALL)
    return below | above


def plane_rates(read, i, rows, ends=None):
    every = range(4)
    centre = [read(f, i) for f in every]
    x_plus = [read(f, i + 1)[:rows] for f in every]
    x_minus = [read(f, i - 1)[:rows] for f in every]
    y_plus = [step(v, 1, 0)[:rows] for v in centre]
    y_minus = [step(v, -1, 0)[:rows] for v in centre]
    centre = [v[:rows] for v in centre]
    upward, downward = centre, centre
    if ends is not None:
        lane = lax.broadcasted_iota(jnp.int32, centre[0].shape, 1)
        upward = [jnp.where(lane == 0, e[:rows], v) for e, v in zip(ends, centre)]
        downward = [jnp.where(lane == lane.shape[1] - 1, e[:rows], v) for e, v in zip(ends, centre)]
    z_plus = [step(v, 1, 1) for v in upward]
    z_minus = [step(v, -1, 1) for v in downward]
    return centre, rates(centre, x_plus, x_minus, y_plus, y_minus, z_plus, z_minus)


def stage_one(outside, value, rate):
    return jnp.where(outside, 0.0, value + DT_STEP * rate)


def stage_two(outside, begin, value, rate):
    return jnp.where(outside, 0.0, 0.75 * begin + 0.25 * (value + DT_STEP * rate))


def first_kernel(flags_ref, sample_hbm, mid_ref, xlo_ref, xhi_ref, one_ref, sample_ref, sem):
    copy = pltpu.make_async_copy(sample_hbm, sample_ref, sem)
    copy.start()
    fields, nx, rows, nz = mid_ref.shape
    outside = beyond_walls(flags_ref, rows - HALO, (rows, nz))
    for i in range(1, nx + 2 * DEPTH - 1):
        centre, rate = plane_rates(functools.partial(plane_of, mid_ref, xlo_ref, xhi_ref), i, rows)
        for f in range(4):
            one_ref[f, i - 1] = stage_one(outside, centre[f], rate[f])
    copy.wait()


def step_kernel(
    flags_ref, mid_ref, xlo_ref, xhi_ref, first_ref, own_ref, low_ref, high_ref, basis_ref, sample_ref,
    flow_ref, snap_ref, cross_ref,
    one_ref, two_ref,
):
    fields, nx, ny, nz = flow_ref.shape
    rows = mid_ref.shape[2]
    modes = basis_ref.shape[1]
    planes = nx + 2 * DEPTH
    lane = lax.broadcasted_iota(jnp.int32, (rows, nz), 1)
    outside = beyond_walls(flags_ref, ny, (rows, nz))
    every = range(4)
    start = functools.partial(plane_of, mid_ref, xlo_ref, xhi_ref)

    left = lane % GROUP < DEPTH

    def window_rates(q):
        return rates(
            q, [step(v, GROUP, 1) for v in q], [step(v, -GROUP, 1) for v in q],
            [step(v, 1, 0) for v in q], [step(v, -1, 0) for v in q],
            [step(v, 1, 1) for v in q], [step(v, -1, 1) for v in q],
        )

    own = [own_ref[f] for f in every]
    other = [jnp.where(left, low_ref[f], high_ref[f]) for f in every]
    windows = []
    for parts in ((other, own), (own, other)):
        q0 = [jnp.where(left, a, b) for a, b in zip(*parts)]
        q1 = [stage_one(outside, v, r) for v, r in zip(q0, window_rates(q0))]
        q2 = [stage_two(outside, s, v, r) for s, v, r in zip(q0, q1, window_rates(q1))]
        windows.append((q1, q2))
    (low_one, low_two), (high_one, high_two) = windows
    ends_one = [jnp.where(left, a, b) for a, b in zip(low_one, high_one)]
    ends_two = [jnp.where(left, a, b) for a, b in zip(low_two, high_two)]
    rim_one = [jnp.where(left, b, a) for a, b in zip(low_one, high_one)]

    def at_plane(values, i):
        return [pltpu.roll(v, (2 * nz - GROUP * i - DEPTH) % nz, 1) for v in values]

    rim = (lane == 0) | (lane == nz - 1)
    for i in range(1, planes - 1):
        for f, value in enumerate(at_plane(rim_one, i)):
            one_ref[f, i - 1] = jnp.where(rim, value, first_ref[f, i - 1])
    for i in range(2, planes - 2):
        centre, rate = plane_rates(lambda f, i: one_ref[f, i - 1], i, rows, at_plane(ends_one, i))
        for f in every:
            two_ref[f, i - 2] = stage_two(outside, start(f, i), centre[f], rate[f])
    for i in range(3, planes - 3):
        centre, rate = plane_rates(lambda f, i: two_ref[f, i - 2], i, ny, at_plane(ends_two, i))
        for f in every:
            value = 1.0 / 3.0 * start(f, i)[:ny] + 2.0 / 3.0 * (centre[f] + DT_STEP * rate[f])
            flow_ref[f, i - DEPTH] = value

    points = sample_ref.shape[1]
    spot = jnp.broadcast_to(sample_ref[...], (nz, points))
    place = lax.broadcasted_iota(jnp.int32, (nx * ny, points), 0)
    in_row = (place == jnp.broadcast_to(sample_ref[...] // nz, (nx * ny, points))).astype(jnp.bfloat16)
    in_lane = lax.broadcasted_iota(jnp.int32, (nz, points), 0) == spot % nz
    product = jnp.zeros((modes + 1, points), jnp.float32)
    for c in range(3):
        field = flow_ref[c].reshape(nx * ny, nz).T
        high = field.astype(jnp.bfloat16)
        rest = field - high.astype(jnp.float32)
        middle = rest.astype(jnp.bfloat16)
        low = (rest - middle.astype(jnp.float32)).astype(jnp.bfloat16)
        found = sum(
            lax.dot_general(p, in_row, (((1,), (0,)), ((), ())), preferred_element_type=jnp.float32)
            for p in (high, middle, low)
        )
        picked = jnp.sum(jnp.where(in_lane, found, 0.0), axis=0, keepdims=True)
        snap_ref[c] = picked
        product = product + jnp.concatenate([basis_ref[c], picked], axis=0) * picked
    total = jnp.sum(product, axis=1, keepdims=True)
    size = modes + 1
    diagonal = lax.broadcasted_iota(jnp.int32, (size, size), 0) == lax.broadcasted_iota(jnp.int32, (size, size), 1)
    cross_ref[...] = jnp.sum(jnp.where(diagonal, total, 0.0), axis=0, keepdims=True)


def merge_kernel(parts_ref, cross_ref, send_ref):
    total = parts_ref[0]
    for d in range(1, parts_ref.shape[0]):
        total = total + parts_ref[d]
    block = jnp.concatenate([total, cross_ref[...]], axis=0)
    for d in range(send_ref.shape[0]):
        send_ref[d] = block


def final_kernel(
    count, got_ref, basis_ref, snap_ref, flow_ref,
    basis_hbm, factor_hbm, flow_hbm,
    packed_ref, work_ref, basis_out_ref, factor_ref, sems,
):
    comps, modes, points = basis_ref.shape
    size = modes + 1
    tall = size // 4
    per = got_ref.shape[1] - 1
    copies = [pltpu.make_async_copy(flow_ref, flow_hbm, sems.at[0])]
    copies[0].start()

    total = jnp.zeros((per + 1, size), jnp.float32)
    for d in range(got_ref.shape[0]):
        block = got_ref[d]
        if per * d < packed_ref.shape[0]:
            packed_ref[per * d : per * d + per] = block[0:per]
        total = total + block
    cross = total[per : per + 1] / count
    mark = (lax.broadcasted_iota(jnp.int32, (8, size), 1) == size - 1).astype(jnp.float32)
    top = lax.broadcasted_iota(jnp.int32, (8, size), 0) == 0
    side = dot(jnp.where(top, jnp.broadcast_to(cross, (8, size)), 0.0), mark, ((0,), (0,)))
    lane = lax.broadcasted_iota(jnp.int32, (tall, size), 1)
    row = lax.broadcasted_iota(jnp.int32, (tall, size), 0)
    old = unpack_upper([packed_ref[tall * k : tall * k + tall] / count for k in range(3)], tall)
    for k in range(4):
        value = jnp.where(lane == size - 1, side[tall * k : tall * k + tall], old[k])
        if k == 3:
            value = jnp.where(row == tall - 1, jnp.broadcast_to(cross, value.shape), value)
        work_ref[tall * k : tall * k + tall, 0:size] = value
        work_ref[tall * k : tall * k + tall, size : 2 * size] = (lane == row + tall * k).astype(jnp.float32)

    stacked = [jnp.concatenate([basis_ref[c], snap_ref[c]], axis=0) for c in range(comps)]
    for k in range(4):
        base = tall * k
        eliminate(work_ref, base, tall)
        done = work_ref[base : base + tall, :]
        if k < 3:
            change = dot(done[:, 0:size], done, ((0,), (0,)))
            work_ref[base + tall : size, :] = work_ref[base + tall : size, :] - change[base + tall : size]
        factor_ref[base : base + tall, :] = jnp.where(lane >= row + base, done[:, 0:size], 0.0)
        for c in range(comps):
            basis_out_ref[c, base : base + tall, :] = dot(done[:, size : 2 * size], stacked[c], ((1,), (0,)))
        rows = (slice(None), pl.ds(base, tall), slice(None))
        copies.append(pltpu.make_async_copy(basis_out_ref.at[rows], basis_hbm.at[rows], sems.at[2 + k]))
        copies[-1].start()
    copies.append(pltpu.make_async_copy(factor_ref, factor_hbm, sems.at[1]))
    copies[-1].start()
    for copy in copies:
        copy.wait()


def eliminate(work_ref, base, tall):
    blocks = tall // 8
    sub = lax.broadcasted_iota(jnp.int32, (8, 128), 0)
    panel = [work_ref[base + 8 * b : base + 8 * b + 8, :] for b in range(blocks)]
    column = [
        [jnp.broadcast_to(panel[b][:, base + k : base + k + 1], (8, 128)) for b in range(blocks)] for k in range(tall)
    ]
    scale = [jnp.zeros((8, 128), jnp.float32) for _ in range(blocks)]
    for j in range(tall):
        mine, at = divmod(j, 8)
        pivot = column[j][mine][at : at + 1, :]
        inverse = 1.0 / pivot
        scaled = {b: column[j][b] * inverse for b in range(mine, blocks)}
        for k in range(j + 1, tall):
            other, place = divmod(k, 8)
            times = scaled[other][place : place + 1, :]
            for b in range(other, blocks):
                column[k][b] = column[k][b] - column[j][b] * times
        scale[mine] = jnp.where(sub == at, lax.rsqrt(pivot), scale[mine])
        pivot_row = panel[mine][at : at + 1, :] * jnp.concatenate([inverse, inverse], axis=1)
        for b in range(mine, blocks):
            times = jnp.where(sub > at, column[j][b], 0.0) if b == mine else column[j][b]
            panel[b] = panel[b] - jnp.concatenate([times, times], axis=1) * pivot_row
    for b in range(blocks):
        work_ref[base + 8 * b : base + 8 * b + 8, :] = panel[b] * jnp.concatenate([scale[b], scale[b]], axis=1)


def local(flow, basis, sample):
    fields, nx, ny, nz = flow.shape
    modes, comps, points = basis.shape
    size = modes + 1
    devices = lax.axis_size("gx") * lax.axis_size("gy") * lax.axis_size("gz")
    count = float(comps * points * devices)
    shape = functools.partial(jax.ShapeDtypeStruct, dtype=jnp.float32)
    call = functools.partial(pl.pallas_call, compiler_params=PARAMS)
    bricks = jnp.transpose(basis, (1, 0, 2))

    whole = pl.BlockSpec(memory_space=pltpu.HBM)
    flat = flow.reshape(fields, nx * ny, nz)
    quarter = size // 4
    per = -(-3 * quarter // devices)

    place = lax.axis_index("gy")
    flags = [place == 0, place == lax.axis_size("gy") - 1, place % 2 == 1, lax.axis_index("gx") % 2 == 1]
    flags = jnp.broadcast_to(jnp.stack(flags).astype(jnp.int32)[:, None], (len(flags), nz))
    strip = shape((fields, nx * DEPTH, nz))
    strips = call(
        functools.partial(strips_kernel, nx), out_shape=(strip, strip), in_specs=[VMEM] * 2, out_specs=(VMEM, VMEM)
    )(flags, flat)
    y_even, y_odd = pairs(*strips, "gy", False)
    gram = call(
        gram_kernel,
        out_shape=shape((devices, per, size)),
        in_specs=[VMEM],
        out_specs=VMEM,
        scratch_shapes=[pltpu.VMEM((size, size), jnp.float32), pltpu.VMEM((devices * per, size), jnp.float32)],
    )(bricks)
    y_even, y_odd, gram = lax.optimization_barrier((y_even, y_odd, gram))

    rows = ny + HALO
    face = shape((fields, DEPTH * ny + HALO, nz))
    mid, *faces = call(
        functools.partial(walls_kernel, nx),
        out_shape=(shape((fields, nx * rows, nz)), face, face),
        in_specs=[VMEM] * 4,
        out_specs=(VMEM,) * 3,
    )(flags, flat, y_even, y_odd)
    mid = mid.reshape(fields, nx, rows, nz)
    x_even, x_odd = pairs(*faces, "gx", True)
    parts = lax.all_to_all(gram, ALL, 0, 0)

    beside = shape((fields, DEPTH, rows, nz))
    packed, xlo, xhi = call(
        pack_kernel,
        out_shape=(shape((fields, rows, nz)), beside, beside),
        in_specs=[VMEM] * 4,
        out_specs=(VMEM,) * 3,
    )(flags, mid, x_even, x_odd)
    if lax.axis_size("gz") == 2:
        low = high = lax.ppermute(packed, "gz", [(0, 1), (1, 0)])
    else:
        low, high = neighbours(packed, packed, "gz")
    begun, cells = call(
        first_kernel,
        out_shape=(
            shape((fields, nx + 2 * DEPTH - 2, rows, nz)),
            jax.ShapeDtypeStruct((1, points), sample.dtype),
        ),
        in_specs=[VMEM, whole] + [VMEM] * 3,
        out_specs=(VMEM, VMEM),
        scratch_shapes=[pltpu.SemaphoreType.DMA],
    )(flags, sample.reshape(1, points), mid, xlo, xhi)
    flow_new, snapshot, cross = call(
        step_kernel,
        out_shape=(shape(flow.shape), shape((comps, 1, points)), shape((1, size))),
        in_specs=[VMEM] * 10,
        out_specs=(VMEM, VMEM, VMEM),
        scratch_shapes=[
            pltpu.VMEM((fields, nx + 2 * DEPTH - 2, rows, nz), jnp.float32),
            pltpu.VMEM((fields, nx + 2 * DEPTH - 4, rows, nz), jnp.float32),
        ],
    )(flags, mid, xlo, xhi, begun, packed, low, high, bricks, cells)

    send = call(
        merge_kernel, out_shape=shape((devices, per + 1, size)), in_specs=[VMEM] * 2, out_specs=VMEM
    )(parts, cross)
    got = lax.all_to_all(send, ALL, 0, 0)
    basis_next, factor, flow_next = call(
        functools.partial(final_kernel, count),
        out_shape=(shape((comps, size, points)), shape((size, size)), shape(flow.shape)),
        in_specs=[VMEM] * 4,
        out_specs=(whole,) * 3,
        scratch_shapes=[
            pltpu.VMEM((3 * quarter, size), jnp.float32),
            pltpu.VMEM((size, 2 * size), jnp.float32),
            pltpu.VMEM((comps, size, points), jnp.float32),
            pltpu.VMEM((size, size), jnp.float32),
            pltpu.SemaphoreType.DMA((6,)),
        ],
    )(got, bricks, snapshot, flow_new)
    return flow_next, jnp.transpose(basis_next, (1, 0, 2)), factor


def solution(mesh):
    return jax.shard_map(
        local,
        mesh=mesh,
        in_specs=(
            P(None, "gx", "gy", "gz"),
            P(None, None, ("gx", "gy", "gz")),
            P(("gx", "gy", "gz")),
        ),
        out_specs=(P(None, "gx", "gy", "gz"), P(None, None, ("gx", "gy", "gz")), P()),
        check_vma=False,
    )
```

```python
import functools

import jax
import jax.numpy as jnp
from jax import lax
from jax.experimental import pallas as pl
from jax.experimental.pallas import tpu as pltpu
from jax.sharding import PartitionSpec as P

DT_STEP = 0.35
VISCOSITY = 0.2
SOUND_SQ = 1.0
DRIVING = 0.5

ALL = ("gx", "gy", "gz")
DEPTH = 3
EXACT = lax.Precision.HIGHEST
VMEM = pl.BlockSpec(memory_space=pltpu.VMEM)
PARAMS = pltpu.CompilerParams(vmem_limit_bytes=40 * 1024 * 1024)


def dot(a, b, dims):
    return lax.dot_general(
        a, b, (dims, ((), ())), precision=EXACT, preferred_element_type=jnp.float32
    )


def three_parts(value):
    high = value.astype(jnp.bfloat16)
    rest = value - high.astype(jnp.float32)
    middle = rest.astype(jnp.bfloat16)
    return high, middle, (rest - middle.astype(jnp.float32)).astype(jnp.bfloat16)


def dot_parts(a, b, dims):
    return lax.dot_general(a, b, (dims, ((), ())), preferred_element_type=jnp.float32)


def dot_stacked(a, b):
    (a1, a2, a3), (b1, b2, b3) = three_parts(a), three_parts(b)
    first = jnp.concatenate([a1, a1, a2, a2, a1, a3], axis=0)
    second = jnp.concatenate([b1, b2, b1, b2, b3, b1], axis=0)
    return dot_parts(first, second, ((0,), (0,)))


def neighbours(block_low, block_high, axis):
    count = lax.axis_size(axis)
    forward = [(i, (i + 1) % count) for i in range(count)]
    backward = [(target, source) for source, target in forward]
    return lax.ppermute(block_high, axis, forward), lax.ppermute(block_low, axis, backward)


def pairs(block_even, block_odd, axis):
    count = lax.axis_size(axis)
    even = [(i, i + 1 - 2 * (i % 2)) for i in range(count)]
    odd = [(i, (i - 1 + 2 * (i % 2)) % count) for i in range(count)]
    return lax.ppermute(block_even, axis, even), lax.ppermute(block_odd, axis, odd)


LOWER_WALL, UPPER_WALL, ODD_Y, ODD_X = range(4)


def flag(flags_ref, which):
    return flags_ref[which : which + 1] == 1


def pack_upper(rows, tall):
    size = rows.shape[1]
    lane = lax.broadcasted_iota(jnp.int32, (tall, size), 1)
    part = [rows[tall * k : tall * k + tall] for k in range(4)]
    return [part[0], jnp.where(lane >= tall, part[1], pltpu.roll(part[3], tall, 1)), part[2]]


def unpack_upper(packed, tall):
    return [packed[0], packed[1], packed[2], pltpu.roll(packed[1], packed[1].shape[1] - tall, 1)]


def gram_kernel(basis_ref, send_ref, parts_ref, gram_ref, packed_ref):
    modes = basis_ref.shape[1]
    tall = gram_ref.shape[0] // 4
    total = jnp.zeros((modes, modes), jnp.float32)
    for c in range(basis_ref.shape[0]):
        rows = basis_ref[c]
        total = total + dot(rows, rows, ((1,), (1,)))
        filled = jnp.concatenate([rows, jnp.zeros((1, rows.shape[1]), jnp.float32)], axis=0)
        for k, part in enumerate(three_parts(filled)):
            parts_ref[k, c] = part
    gram_ref[...] = jnp.zeros_like(gram_ref)
    gram_ref[0:modes, 0:modes] = total
    packed_ref[...] = jnp.zeros_like(packed_ref)
    for k, value in enumerate(pack_upper(gram_ref[...], tall)):
        packed_ref[tall * k : tall * k + tall] = value
    per = send_ref.shape[1]
    for d in range(send_ref.shape[0]):
        send_ref[d] = packed_ref[per * d : per * d + per]


GAP = 2
HALO = 2 * DEPTH + GAP


def strips_kernel(planes, flags_ref, flow_ref, even_ref, odd_ref):
    ny = flow_ref.shape[1] // planes
    odd = flag(flags_ref, ODD_Y)
    for f in range(flow_ref.shape[0]):
        for j in range(DEPTH):
            bottom = flow_ref[f, pl.ds(j, planes, stride=ny), :]
            top = flow_ref[f, pl.ds(ny - DEPTH + j, planes, stride=ny), :]
            even_ref[f, planes * j : planes * j + planes] = jnp.where(odd, bottom, top)
            odd_ref[f, planes * j : planes * j + planes] = jnp.where(odd, top, bottom)


def walls_kernel(planes, flags_ref, flow_ref, even_ref, odd_ref, mid_ref, face_even_ref, face_odd_ref):
    fields, cells, nz = flow_ref.shape
    odd_y, odd_x = flag(flags_ref, ODD_Y), flag(flags_ref, ODD_X)
    ny = cells // planes
    rows = ny + HALO
    sub = lax.broadcasted_iota(jnp.int32, (HALO, nz), 0)
    empty = jnp.zeros((planes, nz), jnp.float32)
    for f in range(fields):
        for i in range(planes):
            mid_ref[f, rows * i : rows * i + ny] = flow_ref[f, ny * i : ny * i + ny]
        for j in range(HALO):
            k = j if j < DEPTH else j - DEPTH - GAP
            part = slice(planes * k, planes * k + planes)
            if j < DEPTH:
                value = jnp.where(odd_y, odd_ref[f, part], even_ref[f, part])
                value = jnp.where(flag(flags_ref, UPPER_WALL), 0.0, value)
            elif j < DEPTH + GAP:
                value = empty
            else:
                value = jnp.where(odd_y, even_ref[f, part], odd_ref[f, part])
                value = jnp.where(flag(flags_ref, LOWER_WALL), 0.0, value)
            mid_ref[f, pl.ds(ny + j, planes, stride=rows), :] = value
        faces = []
        for begin, near, next_one in ((0, 0, 1), (planes - DEPTH, planes - 1, planes - 2)):
            halos = [mid_ref[f, rows * i + ny : rows * i + rows] for i in (near, next_one)]
            faces.append([flow_ref[f, ny * i : ny * i + ny] for i in range(begin, begin + DEPTH)] + [corner_rows(*halos, sub)])
        for k, (first, last) in enumerate(zip(*faces)):
            part = slice(ny * k, ny * k + first.shape[0])
            face_even_ref[f, part] = jnp.where(odd_x, first, last)
            face_odd_ref[f, part] = jnp.where(odd_x, last, first)


def corner_rows(near, next_one, sub):
    tile = jnp.where(sub == 2, pltpu.roll(next_one, 2, 0), pltpu.roll(next_one, 6, 0))
    tile = jnp.where((sub == 2) | (sub == 5), tile, 0.0)
    return jnp.where((sub < 2) | (sub >= 6), near, tile)


def corner_planes(tile, sub):
    near = jnp.where((sub < 2) | (sub >= 6), tile, 0.0)
    next_one = jnp.where(sub == 0, pltpu.roll(tile, 6, 0), pltpu.roll(tile, 2, 0))
    return [near, jnp.where((sub == 0) | (sub == 7), next_one, 0.0), jnp.zeros_like(tile)]


def plane_of(mid_ref, xlo_ref, xhi_ref, f, i):
    nx = mid_ref.shape[1]
    if i < DEPTH:
        return xlo_ref[f, i]
    if i < DEPTH + nx:
        return mid_ref[f, i - DEPTH]
    return xhi_ref[f, i - DEPTH - nx]


GROUP = 8


def pack_kernel(flags_ref, mid_ref, even_ref, odd_ref, packed_ref, xlo_ref, xhi_ref):
    fields, nx, rows, nz = mid_ref.shape
    ny = rows - HALO
    odd = flag(flags_ref, ODD_X)
    lane = lax.broadcasted_iota(jnp.int32, (rows, nz), 1)
    sub = lax.broadcasted_iota(jnp.int32, (HALO, nz), 0)
    for f in range(fields):
        for one_ref, other_ref, out_ref, order in (
            (even_ref, odd_ref, xlo_ref, (2, 1, 0)), (odd_ref, even_ref, xhi_ref, (0, 1, 2))
        ):
            face = jnp.where(odd, one_ref[f], other_ref[f])
            halo = corner_planes(face[ny * DEPTH :], sub)
            for k in range(DEPTH):
                out_ref[f, k, 0:ny] = face[ny * k : ny * k + ny]
                out_ref[f, k, ny:rows] = halo[order[k]]
        value = jnp.zeros((rows, nz), jnp.float32)
        for i in range(nx + 2 * DEPTH):
            start = GROUP * i
            moved = pltpu.roll(plane_of(mid_ref, xlo_ref, xhi_ref, f, i), (start + DEPTH) % nz, 1)
            value = jnp.where((lane >= start) & (lane < start + 2 * DEPTH), moved, value)
        packed_ref[f] = value


def step(value, by, axis):
    size = value.shape[axis]
    return pltpu.roll(value, (size - by) % size, axis)


def rates(centre, x_plus, x_minus, y_plus, y_minus, z_plus, z_minus):
    slope_x = [0.5 * (a - b) for a, b in zip(x_plus, x_minus)]
    slope_y = [0.5 * (a - b) for a, b in zip(y_plus, y_minus)]
    slope_z = [0.5 * (a - b) for a, b in zip(z_plus, z_minus)]
    pressure = [slope_x[3], slope_y[3], slope_z[3]]
    out = []
    for f in range(3):
        laplace = (
            x_plus[f] + x_minus[f] + (y_plus[f] + y_minus[f]) + (z_plus[f] + z_minus[f]) - 6.0 * centre[f]
        )
        advect = centre[0] * slope_x[f] + centre[1] * slope_y[f] + centre[2] * slope_z[f]
        value = VISCOSITY * laplace - advect - pressure[f]
        if f == 0:
            value = value + DRIVING
        out.append(value)
    out.append(-SOUND_SQ * (slope_x[0] + slope_y[1] + slope_z[2]))
    return out


def beyond_walls(flags_ref, ny, shape):
    row = lax.broadcasted_iota(jnp.int32, shape, 0)
    below = (row >= ny + DEPTH + GAP) & flag(flags_ref, LOWER_WALL)
    above = (row >= ny) & (row < ny + DEPTH) & flag(flags_ref, UPPER_WALL)
    return below | above


def plane_rates(read, i, rows, ends=None):
    every = range(4)
    centre = [read(f, i) for f in every]
    x_plus = [read(f, i + 1)[:rows] for f in every]
    x_minus = [read(f, i - 1)[:rows] for f in every]
    y_plus = [step(v, 1, 0)[:rows] for v in centre]
    y_minus = [step(v, -1, 0)[:rows] for v in centre]
    centre = [v[:rows] for v in centre]
    upward, downward = centre, centre
    if ends is not None:
        lane = lax.broadcasted_iota(jnp.int32, centre[0].shape, 1)
        upward = [jnp.where(lane == 0, e[:rows], v) for e, v in zip(ends, centre)]
        downward = [jnp.where(lane == lane.shape[1] - 1, e[:rows], v) for e, v in zip(ends, centre)]
    z_plus = [step(v, 1, 1) for v in upward]
    z_minus = [step(v, -1, 1) for v in downward]
    return centre, rates(centre, x_plus, x_minus, y_plus, y_minus, z_plus, z_minus)


def stage_one(outside, value, rate):
    return jnp.where(outside, 0.0, value + DT_STEP * rate)


def stage_two(outside, begin, value, rate):
    return jnp.where(outside, 0.0, 0.75 * begin + 0.25 * (value + DT_STEP * rate))


def first_kernel(flags_ref, sample_hbm, mid_ref, xlo_ref, xhi_ref, one_ref, sample_ref, sem):
    copy = pltpu.make_async_copy(sample_hbm, sample_ref, sem)
    copy.start()
    fields, nx, rows, nz = mid_ref.shape
    outside = beyond_walls(flags_ref, rows - HALO, (rows, nz))
    for i in range(1, nx + 2 * DEPTH - 1):
        centre, rate = plane_rates(functools.partial(plane_of, mid_ref, xlo_ref, xhi_ref), i, rows)
        for f in range(4):
            one_ref[f, i - 1] = stage_one(outside, centre[f], rate[f])
    copy.wait()


def step_kernel(
    flags_ref, mid_ref, xlo_ref, xhi_ref, first_ref, own_ref, low_ref, high_ref, basis_ref, sample_ref,
    flow_ref, snap_ref, cross_ref,
    one_ref, two_ref,
):
    fields, nx, ny, nz = flow_ref.shape
    rows = mid_ref.shape[2]
    modes = basis_ref.shape[1]
    planes = nx + 2 * DEPTH
    lane = lax.broadcasted_iota(jnp.int32, (rows, nz), 1)
    outside = beyond_walls(flags_ref, ny, (rows, nz))
    every = range(4)
    start = functools.partial(plane_of, mid_ref, xlo_ref, xhi_ref)

    left = lane % GROUP < DEPTH

    def window_rates(q):
        return rates(
            q, [step(v, GROUP, 1) for v in q], [step(v, -GROUP, 1) for v in q],
            [step(v, 1, 0) for v in q], [step(v, -1, 0) for v in q],
            [step(v, 1, 1) for v in q], [step(v, -1, 1) for v in q],
        )

    own = [own_ref[f] for f in every]
    other = [jnp.where(left, low_ref[f], high_ref[f]) for f in every]
    windows = []
    for parts in ((other, own), (own, other)):
        q0 = [jnp.where(left, a, b) for a, b in zip(*parts)]
        q1 = [stage_one(outside, v, r) for v, r in zip(q0, window_rates(q0))]
        q2 = [stage_two(outside, s, v, r) for s, v, r in zip(q0, q1, window_rates(q1))]
        windows.append((q1, q2))
    (low_one, low_two), (high_one, high_two) = windows
    ends_one = [jnp.where(left, a, b) for a, b in zip(low_one, high_one)]
    ends_two = [jnp.where(left, a, b) for a, b in zip(low_two, high_two)]
    rim_one = [jnp.where(left, b, a) for a, b in zip(low_one, high_one)]

    def at_plane(values, i):
        return [pltpu.roll(v, (2 * nz - GROUP * i - DEPTH) % nz, 1) for v in values]

    rim = (lane == 0) | (lane == nz - 1)
    for i in range(1, planes - 1):
        for f, value in enumerate(at_plane(rim_one, i)):
            one_ref[f, i - 1] = jnp.where(rim, value, first_ref[f, i - 1])
    for i in range(2, planes - 2):
        centre, rate = plane_rates(lambda f, i: one_ref[f, i - 1], i, rows, at_plane(ends_one, i))
        for f in every:
            two_ref[f, i - 2] = stage_two(outside, start(f, i), centre[f], rate[f])
    for i in range(3, planes - 3):
        centre, rate = plane_rates(lambda f, i: two_ref[f, i - 2], i, ny, at_plane(ends_two, i))
        for f in every:
            value = 1.0 / 3.0 * start(f, i)[:ny] + 2.0 / 3.0 * (centre[f] + DT_STEP * rate[f])
            flow_ref[f, i - DEPTH] = value

    points = sample_ref.shape[1]
    spot = jnp.broadcast_to(sample_ref[...], (nz, points))
    place = lax.broadcasted_iota(jnp.int32, (nx * ny, points), 0)
    in_row = (place == jnp.broadcast_to(sample_ref[...] // nz, (nx * ny, points))).astype(jnp.bfloat16)
    in_lane = lax.broadcasted_iota(jnp.int32, (nz, points), 0) == spot % nz
    product = jnp.zeros((modes + 1, points), jnp.float32)
    for c in range(3):
        field = flow_ref[c].reshape(nx * ny, nz).T
        found = sum(dot_parts(part, in_row, ((1,), (0,))) for part in three_parts(field))
        picked = jnp.sum(jnp.where(in_lane, found, 0.0), axis=0, keepdims=True)
        snap_ref[c] = picked
        product = product + jnp.concatenate([basis_ref[c], picked], axis=0) * picked
    total = jnp.sum(product, axis=1, keepdims=True)
    size = modes + 1
    diagonal = lax.broadcasted_iota(jnp.int32, (size, size), 0) == lax.broadcasted_iota(jnp.int32, (size, size), 1)
    cross_ref[...] = jnp.sum(jnp.where(diagonal, total, 0.0), axis=0, keepdims=True)


def merge_kernel(parts_ref, cross_ref, send_ref):
    total = parts_ref[0]
    for d in range(1, parts_ref.shape[0]):
        total = total + parts_ref[d]
    block = jnp.concatenate([total, cross_ref[...]], axis=0)
    for d in range(send_ref.shape[0]):
        send_ref[d] = block


def final_kernel(
    count, got_ref, parts_ref, snap_ref, flow_ref,
    basis_hbm, factor_hbm, flow_hbm,
    packed_ref, work_ref, basis_out_ref, factor_ref, sems,
):
    _, comps, size, points = parts_ref.shape
    tall = size // 4
    per = got_ref.shape[1] - 1
    copies = [pltpu.make_async_copy(flow_ref, flow_hbm, sems.at[0])]
    copies[0].start()

    total = jnp.zeros((per + 1, size), jnp.float32)
    for d in range(got_ref.shape[0]):
        block = got_ref[d]
        if per * d < packed_ref.shape[0]:
            packed_ref[per * d : per * d + per] = block[0:per]
        total = total + block
    cross = total[per : per + 1] / count
    top = lax.broadcasted_iota(jnp.int32, (16, size), 0)
    mark = (lax.broadcasted_iota(jnp.int32, (16, size), 1) == size - 1) & (top < 3)
    thirds = jnp.zeros((16, size), jnp.float32)
    for k, part in enumerate(three_parts(cross)):
        thirds = jnp.where(top == k, part.astype(jnp.float32), thirds)
    side = dot_parts(thirds.astype(jnp.bfloat16), mark.astype(jnp.bfloat16), ((0,), (0,)))
    lane = lax.broadcasted_iota(jnp.int32, (tall, size), 1)
    row = lax.broadcasted_iota(jnp.int32, (tall, size), 0)
    old = unpack_upper([packed_ref[tall * k : tall * k + tall] / count for k in range(3)], tall)
    for k in range(4):
        value = jnp.where(lane == size - 1, side[tall * k : tall * k + tall], old[k])
        if k == 3:
            value = jnp.where(row == tall - 1, jnp.broadcast_to(cross, value.shape), value)
        work_ref[tall * k : tall * k + tall, 0:size] = value
        work_ref[tall * k : tall * k + tall, size : 2 * size] = (lane == row + tall * k).astype(jnp.float32)

    for k in range(4):
        base = tall * k
        eliminate(work_ref, base, tall)
        done = work_ref[base : base + tall, :]
        if k < 3:
            change = dot_stacked(done[:, 0:size], done)
            work_ref[base + tall : size, :] = work_ref[base + tall : size, :] - change[base + tall : size]
        factor_ref[base : base + tall, :] = jnp.where(lane >= row + base, done[:, 0:size], 0.0)
        if k < 2:
            continue
        begin, count_rows = (0, base + tall) if k == 2 else (base, tall)
        inverse = work_ref[begin : base + tall, size : 2 * size]
        pieces = jnp.concatenate(three_parts(inverse), axis=0)
        for c in range(comps):
            value = jnp.zeros((count_rows, points), jnp.float32)
            for n in (2, 1, 0):
                products = dot_parts(pieces[: count_rows * (3 - n)], parts_ref[n, c], ((1,), (0,)))
                for m in range(2 - n, -1, -1):
                    value = value + products[count_rows * m : count_rows * m + count_rows]
            if k == 3:
                value = value + inverse[:, size - 1 : size] * snap_ref[c]
            basis_out_ref[c, begin : base + tall, :] = value
        rows = (slice(None), pl.ds(begin, count_rows), slice(None))
        copies.append(pltpu.make_async_copy(basis_out_ref.at[rows], basis_hbm.at[rows], sems.at[k]))
        copies[-1].start()
    copies.append(pltpu.make_async_copy(factor_ref, factor_hbm, sems.at[1]))
    copies[-1].start()
    for copy in copies:
        copy.wait()


def eliminate(work_ref, base, tall):
    blocks = tall // 8
    sub = lax.broadcasted_iota(jnp.int32, (8, 128), 0)
    panel = [work_ref[base + 8 * b : base + 8 * b + 8, :] for b in range(blocks)]
    column = [
        [jnp.broadcast_to(panel[b][:, base + k : base + k + 1], (8, 128)) for b in range(blocks)] for k in range(tall)
    ]
    scale = [jnp.zeros((8, 128), jnp.float32) for _ in range(blocks)]
    for j in range(tall):
        mine, at = divmod(j, 8)
        pivot = column[j][mine][at : at + 1, :]
        inverse = 1.0 / pivot
        scaled = {b: column[j][b] * inverse for b in range(mine, blocks)}
        for k in range(j + 1, tall):
            other, place = divmod(k, 8)
            times = scaled[other][place : place + 1, :]
            for b in range(other, blocks):
                column[k][b] = column[k][b] - column[j][b] * times
        scale[mine] = jnp.where(sub == at, lax.rsqrt(pivot), scale[mine])
        pivot_row = panel[mine][at : at + 1, :] * jnp.concatenate([inverse, inverse], axis=1)
        for b in range(mine, blocks):
            times = jnp.where(sub > at, column[j][b], 0.0) if b == mine else column[j][b]
            panel[b] = panel[b] - jnp.concatenate([times, times], axis=1) * pivot_row
    for b in range(blocks):
        work_ref[base + 8 * b : base + 8 * b + 8, :] = panel[b] * jnp.concatenate([scale[b], scale[b]], axis=1)


def local(flow, basis, sample):
    fields, nx, ny, nz = flow.shape
    modes, comps, points = basis.shape
    size = modes + 1
    devices = lax.axis_size("gx") * lax.axis_size("gy") * lax.axis_size("gz")
    count = float(comps * points * devices)
    shape = functools.partial(jax.ShapeDtypeStruct, dtype=jnp.float32)
    call = functools.partial(pl.pallas_call, compiler_params=PARAMS)
    bricks = jnp.transpose(basis, (1, 0, 2))

    whole = pl.BlockSpec(memory_space=pltpu.HBM)
    flat = flow.reshape(fields, nx * ny, nz)
    quarter = size // 4
    per = -(-3 * quarter // devices)

    place = lax.axis_index("gy")
    flags = [place == 0, place == lax.axis_size("gy") - 1, place % 2 == 1, lax.axis_index("gx") % 2 == 1]
    flags = jnp.broadcast_to(jnp.stack(flags).astype(jnp.int32)[:, None], (len(flags), nz))
    strip = shape((fields, nx * DEPTH, nz))
    strips = call(
        functools.partial(strips_kernel, nx), out_shape=(strip, strip), in_specs=[VMEM] * 2, out_specs=(VMEM, VMEM)
    )(flags, flat)
    y_even, y_odd = pairs(*strips, "gy")
    gram, basis_parts = call(
        gram_kernel,
        out_shape=(shape((devices, per, size)), jax.ShapeDtypeStruct((3, comps, size, points), jnp.bfloat16)),
        in_specs=[VMEM],
        out_specs=(VMEM, VMEM),
        scratch_shapes=[pltpu.VMEM((size, size), jnp.float32), pltpu.VMEM((devices * per, size), jnp.float32)],
    )(bricks)
    y_even, y_odd, gram = lax.optimization_barrier((y_even, y_odd, gram))

    rows = ny + HALO
    face = shape((fields, DEPTH * ny + HALO, nz))
    mid, *faces = call(
        functools.partial(walls_kernel, nx),
        out_shape=(shape((fields, nx * rows, nz)), face, face),
        in_specs=[VMEM] * 4,
        out_specs=(VMEM,) * 3,
    )(flags, flat, y_even, y_odd)
    mid = mid.reshape(fields, nx, rows, nz)
    x_even, x_odd = pairs(*faces, "gx")
    parts = lax.all_to_all(gram, ALL, 0, 0)

    beside = shape((fields, DEPTH, rows, nz))
    packed, xlo, xhi = call(
        pack_kernel,
        out_shape=(shape((fields, rows, nz)), beside, beside),
        in_specs=[VMEM] * 4,
        out_specs=(VMEM,) * 3,
    )(flags, mid, x_even, x_odd)
    if lax.axis_size("gz") == 2:
        low = high = lax.ppermute(packed, "gz", [(0, 1), (1, 0)])
    else:
        low, high = neighbours(packed, packed, "gz")
    begun, cells = call(
        first_kernel,
        out_shape=(
            shape((fields, nx + 2 * DEPTH - 2, rows, nz)),
            jax.ShapeDtypeStruct((1, points), sample.dtype),
        ),
        in_specs=[VMEM, whole] + [VMEM] * 3,
        out_specs=(VMEM, VMEM),
        scratch_shapes=[pltpu.SemaphoreType.DMA],
    )(flags, sample.reshape(1, points), mid, xlo, xhi)
    flow_new, snapshot, cross = call(
        step_kernel,
        out_shape=(shape(flow.shape), shape((comps, 1, points)), shape((1, size))),
        in_specs=[VMEM] * 10,
        out_specs=(VMEM, VMEM, VMEM),
        scratch_shapes=[
            pltpu.VMEM((fields, nx + 2 * DEPTH - 2, rows, nz), jnp.float32),
            pltpu.VMEM((fields, nx + 2 * DEPTH - 4, rows, nz), jnp.float32),
        ],
    )(flags, mid, xlo, xhi, begun, packed, low, high, bricks, cells)

    send = call(
        merge_kernel, out_shape=shape((devices, per + 1, size)), in_specs=[VMEM] * 2, out_specs=VMEM
    )(parts, cross)
    got = lax.all_to_all(send, ALL, 0, 0)
    basis_next, factor, flow_next = call(
        functools.partial(final_kernel, count),
        out_shape=(shape((comps, size, points)), shape((size, size)), shape(flow.shape)),
        in_specs=[VMEM] * 4,
        out_specs=(whole,) * 3,
        scratch_shapes=[
            pltpu.VMEM((3 * quarter, size), jnp.float32),
            pltpu.VMEM((size, 2 * size), jnp.float32),
            pltpu.VMEM((comps, size, points), jnp.float32),
            pltpu.VMEM((size, size), jnp.float32),
            pltpu.SemaphoreType.DMA((4,)),
        ],
    )(got, basis_parts, snapshot, flow_new)
    return flow_next, jnp.transpose(basis_next, (1, 0, 2)), factor


def solution(mesh):
    return jax.shard_map(
        local,
        mesh=mesh,
        in_specs=(
            P(None, "gx", "gy", "gz"),
            P(None, None, ("gx", "gy", "gz")),
            P(("gx", "gy", "gz")),
        ),
        out_specs=(P(None, "gx", "gy", "gz"), P(None, None, ("gx", "gy", "gz")), P()),
        check_vma=False,
    )
```

```python
import functools

import jax
import jax.numpy as jnp
from jax import lax
from jax.experimental import pallas as pl
from jax.experimental.pallas import tpu as pltpu
from jax.sharding import PartitionSpec as P

DT_STEP = 0.35
VISCOSITY = 0.2
SOUND_SQ = 1.0
DRIVING = 0.5

ALL = ("gx", "gy", "gz")
DEPTH = 3
EXACT = lax.Precision.HIGHEST
VMEM = pl.BlockSpec(memory_space=pltpu.VMEM)
PARAMS = pltpu.CompilerParams(vmem_limit_bytes=40 * 1024 * 1024)


def dot(a, b, dims):
    return lax.dot_general(
        a, b, (dims, ((), ())), precision=EXACT, preferred_element_type=jnp.float32
    )


def three_parts(value):
    high = value.astype(jnp.bfloat16)
    rest = value - high.astype(jnp.float32)
    middle = rest.astype(jnp.bfloat16)
    return high, middle, (rest - middle.astype(jnp.float32)).astype(jnp.bfloat16)


def dot_parts(a, b, dims):
    return lax.dot_general(a, b, (dims, ((), ())), preferred_element_type=jnp.float32)


def dot_stacked(a, b):
    (a1, a2, a3), (b1, b2, b3) = three_parts(a), three_parts(b)
    first = jnp.concatenate([a1, a1, a2, a2, a1, a3], axis=0)
    second = jnp.concatenate([b1, b2, b1, b2, b3, b1], axis=0)
    return dot_parts(first, second, ((0,), (0,)))


def neighbours(block_low, block_high, axis):
    count = lax.axis_size(axis)
    forward = [(i, (i + 1) % count) for i in range(count)]
    backward = [(target, source) for source, target in forward]
    return lax.ppermute(block_high, axis, forward), lax.ppermute(block_low, axis, backward)


def pairs(block_even, block_odd, axis):
    count = lax.axis_size(axis)
    even = [(i, i + 1 - 2 * (i % 2)) for i in range(count)]
    odd = [(i, (i - 1 + 2 * (i % 2)) % count) for i in range(count)]
    return lax.ppermute(block_even, axis, even), lax.ppermute(block_odd, axis, odd)


LOWER_WALL, UPPER_WALL, ODD_Y = range(3)


def flag(flags_ref, which):
    return flags_ref[which : which + 1] == 1


def pack_upper(rows, tall):
    size = rows.shape[1]
    lane = lax.broadcasted_iota(jnp.int32, (tall, size), 1)
    part = [rows[tall * k : tall * k + tall] for k in range(4)]
    return [part[0], jnp.where(lane >= tall, part[1], pltpu.roll(part[3], tall, 1)), part[2]]


def unpack_upper(packed, tall):
    return [packed[0], packed[1], packed[2], pltpu.roll(packed[1], packed[1].shape[1] - tall, 1)]


def gram_kernel(basis_ref, send_ref, parts_ref, gram_ref, packed_ref):
    modes = basis_ref.shape[1]
    tall = gram_ref.shape[0] // 4
    total = jnp.zeros((modes, modes), jnp.float32)
    for c in range(basis_ref.shape[0]):
        rows = basis_ref[c]
        total = total + dot(rows, rows, ((1,), (1,)))
        filled = jnp.concatenate([rows, jnp.zeros((1, rows.shape[1]), jnp.float32)], axis=0)
        for k, part in enumerate(three_parts(filled)):
            parts_ref[k, c] = part
    gram_ref[...] = jnp.zeros_like(gram_ref)
    gram_ref[0:modes, 0:modes] = total
    packed_ref[...] = jnp.zeros_like(packed_ref)
    for k, value in enumerate(pack_upper(gram_ref[...], tall)):
        packed_ref[tall * k : tall * k + tall] = value
    per = send_ref.shape[1]
    for d in range(send_ref.shape[0]):
        send_ref[d] = packed_ref[per * d : per * d + per]


GAP = 2
HALO = 2 * DEPTH + GAP


def strips_kernel(planes, flags_ref, flow_ref, even_ref, odd_ref):
    ny = flow_ref.shape[1] // planes
    odd = flag(flags_ref, ODD_Y)
    for f in range(flow_ref.shape[0]):
        for j in range(DEPTH):
            bottom = flow_ref[f, pl.ds(j, planes, stride=ny), :]
            top = flow_ref[f, pl.ds(ny - DEPTH + j, planes, stride=ny), :]
            even_ref[f, planes * j : planes * j + planes] = jnp.where(odd, bottom, top)
            odd_ref[f, planes * j : planes * j + planes] = jnp.where(odd, top, bottom)


def walls_kernel(planes, flags_ref, flow_ref, even_ref, odd_ref, mid_ref, first_ref, last_ref):
    fields, cells, nz = flow_ref.shape
    odd_y = flag(flags_ref, ODD_Y)
    ny = cells // planes
    rows = ny + HALO
    sub = lax.broadcasted_iota(jnp.int32, (HALO, nz), 0)
    empty = jnp.zeros((planes, nz), jnp.float32)
    for f in range(fields):
        for i in range(planes):
            mid_ref[f, rows * i : rows * i + ny] = flow_ref[f, ny * i : ny * i + ny]
        for j in range(HALO):
            k = j if j < DEPTH else j - DEPTH - GAP
            part = slice(planes * k, planes * k + planes)
            if j < DEPTH:
                value = jnp.where(odd_y, odd_ref[f, part], even_ref[f, part])
                value = jnp.where(flag(flags_ref, UPPER_WALL), 0.0, value)
            elif j < DEPTH + GAP:
                value = empty
            else:
                value = jnp.where(odd_y, even_ref[f, part], odd_ref[f, part])
                value = jnp.where(flag(flags_ref, LOWER_WALL), 0.0, value)
            mid_ref[f, pl.ds(ny + j, planes, stride=rows), :] = value
        for face_ref, begin, near, next_one in (
            (first_ref, 0, 0, 1), (last_ref, planes - DEPTH, planes - 1, planes - 2)
        ):
            for k in range(DEPTH):
                face_ref[f, ny * k : ny * k + ny] = flow_ref[f, ny * (begin + k) : ny * (begin + k) + ny]
            halos = [mid_ref[f, rows * i + ny : rows * i + rows] for i in (near, next_one)]
            face_ref[f, ny * DEPTH : ny * DEPTH + HALO] = corner_rows(*halos, sub)


def corner_rows(near, next_one, sub):
    tile = jnp.where(sub == 2, pltpu.roll(next_one, 2, 0), pltpu.roll(next_one, 6, 0))
    tile = jnp.where((sub == 2) | (sub == 5), tile, 0.0)
    return jnp.where((sub < 2) | (sub >= 6), near, tile)


def corner_planes(tile, sub):
    near = jnp.where((sub < 2) | (sub >= 6), tile, 0.0)
    next_one = jnp.where(sub == 0, pltpu.roll(tile, 6, 0), pltpu.roll(tile, 2, 0))
    return [near, jnp.where((sub == 0) | (sub == 7), next_one, 0.0), jnp.zeros_like(tile)]


def plane_of(mid_ref, xlo_ref, xhi_ref, f, i):
    nx = mid_ref.shape[1]
    if i < DEPTH:
        return xlo_ref[f, i]
    if i < DEPTH + nx:
        return mid_ref[f, i - DEPTH]
    return xhi_ref[f, i - DEPTH - nx]


GROUP = 8


def pack_kernel(mid_ref, low_ref, high_ref, packed_ref, xlo_ref, xhi_ref):
    fields, nx, rows, nz = mid_ref.shape
    ny = rows - HALO
    lane = lax.broadcasted_iota(jnp.int32, (rows, nz), 1)
    sub = lax.broadcasted_iota(jnp.int32, (HALO, nz), 0)
    for f in range(fields):
        for face_ref, out_ref, order in ((low_ref, xlo_ref, (2, 1, 0)), (high_ref, xhi_ref, (0, 1, 2))):
            face = face_ref[f]
            halo = corner_planes(face[ny * DEPTH :], sub)
            for k in range(DEPTH):
                out_ref[f, k, 0:ny] = face[ny * k : ny * k + ny]
                out_ref[f, k, ny:rows] = halo[order[k]]
        value = jnp.zeros((rows, nz), jnp.float32)
        for i in range(nx + 2 * DEPTH):
            start = GROUP * i
            moved = pltpu.roll(plane_of(mid_ref, xlo_ref, xhi_ref, f, i), (start + DEPTH) % nz, 1)
            value = jnp.where((lane >= start) & (lane < start + 2 * DEPTH), moved, value)
        packed_ref[f] = value


def step(value, by, axis):
    size = value.shape[axis]
    return pltpu.roll(value, (size - by) % size, axis)


def rates(centre, x_plus, x_minus, y_plus, y_minus, z_plus, z_minus):
    slope_x = [0.5 * (a - b) for a, b in zip(x_plus, x_minus)]
    slope_y = [0.5 * (a - b) for a, b in zip(y_plus, y_minus)]
    slope_z = [0.5 * (a - b) for a, b in zip(z_plus, z_minus)]
    pressure = [slope_x[3], slope_y[3], slope_z[3]]
    out = []
    for f in range(3):
        laplace = (
            x_plus[f] + x_minus[f] + (y_plus[f] + y_minus[f]) + (z_plus[f] + z_minus[f]) - 6.0 * centre[f]
        )
        advect = centre[0] * slope_x[f] + centre[1] * slope_y[f] + centre[2] * slope_z[f]
        value = VISCOSITY * laplace - advect - pressure[f]
        if f == 0:
            value = value + DRIVING
        out.append(value)
    out.append(-SOUND_SQ * (slope_x[0] + slope_y[1] + slope_z[2]))
    return out


def beyond_walls(flags_ref, ny, shape):
    row = lax.broadcasted_iota(jnp.int32, shape, 0)
    below = (row >= ny + DEPTH + GAP) & flag(flags_ref, LOWER_WALL)
    above = (row >= ny) & (row < ny + DEPTH) & flag(flags_ref, UPPER_WALL)
    return below | above


def plane_rates(read, i, rows, ends=None):
    every = range(4)
    centre = [read(f, i) for f in every]
    x_plus = [read(f, i + 1)[:rows] for f in every]
    x_minus = [read(f, i - 1)[:rows] for f in every]
    y_plus = [step(v, 1, 0)[:rows] for v in centre]
    y_minus = [step(v, -1, 0)[:rows] for v in centre]
    centre = [v[:rows] for v in centre]
    upward, downward = centre, centre
    if ends is not None:
        lane = lax.broadcasted_iota(jnp.int32, centre[0].shape, 1)
        upward = [jnp.where(lane == 0, e[:rows], v) for e, v in zip(ends, centre)]
        downward = [jnp.where(lane == lane.shape[1] - 1, e[:rows], v) for e, v in zip(ends, centre)]
    z_plus = [step(v, 1, 1) for v in upward]
    z_minus = [step(v, -1, 1) for v in downward]
    return centre, rates(centre, x_plus, x_minus, y_plus, y_minus, z_plus, z_minus)


def stage_one(outside, value, rate):
    return jnp.where(outside, 0.0, value + DT_STEP * rate)


def stage_two(outside, begin, value, rate):
    return jnp.where(outside, 0.0, 0.75 * begin + 0.25 * (value + DT_STEP * rate))


def first_kernel(flags_ref, sample_hbm, mid_ref, xlo_ref, xhi_ref, one_ref, sample_ref, sem):
    copy = pltpu.make_async_copy(sample_hbm, sample_ref, sem)
    copy.start()
    fields, nx, rows, nz = mid_ref.shape
    outside = beyond_walls(flags_ref, rows - HALO, (rows, nz))
    for i in range(1, nx + 2 * DEPTH - 1):
        centre, rate = plane_rates(functools.partial(plane_of, mid_ref, xlo_ref, xhi_ref), i, rows)
        for f in range(4):
            one_ref[f, i - 1] = stage_one(outside, centre[f], rate[f])
    copy.wait()


def step_kernel(
    flags_ref, mid_ref, xlo_ref, xhi_ref, first_ref, own_ref, low_ref, high_ref, basis_ref, sample_ref,
    flow_ref, snap_ref, cross_ref,
    one_ref, two_ref,
):
    fields, nx, ny, nz = flow_ref.shape
    rows = mid_ref.shape[2]
    modes = basis_ref.shape[1]
    planes = nx + 2 * DEPTH
    lane = lax.broadcasted_iota(jnp.int32, (rows, nz), 1)
    outside = beyond_walls(flags_ref, ny, (rows, nz))
    every = range(4)
    start = functools.partial(plane_of, mid_ref, xlo_ref, xhi_ref)

    left = lane % GROUP < DEPTH

    def window_rates(q):
        return rates(
            q, [step(v, GROUP, 1) for v in q], [step(v, -GROUP, 1) for v in q],
            [step(v, 1, 0) for v in q], [step(v, -1, 0) for v in q],
            [step(v, 1, 1) for v in q], [step(v, -1, 1) for v in q],
        )

    own = [own_ref[f] for f in every]
    other = [jnp.where(left, low_ref[f], high_ref[f]) for f in every]
    windows = []
    for parts in ((other, own), (own, other)):
        q0 = [jnp.where(left, a, b) for a, b in zip(*parts)]
        q1 = [stage_one(outside, v, r) for v, r in zip(q0, window_rates(q0))]
        q2 = [stage_two(outside, s, v, r) for s, v, r in zip(q0, q1, window_rates(q1))]
        windows.append((q1, q2))
    (low_one, low_two), (high_one, high_two) = windows
    ends_one = [jnp.where(left, a, b) for a, b in zip(low_one, high_one)]
    ends_two = [jnp.where(left, a, b) for a, b in zip(low_two, high_two)]
    rim_one = [jnp.where(left, b, a) for a, b in zip(low_one, high_one)]

    def at_plane(values, i):
        return [pltpu.roll(v, (2 * nz - GROUP * i - DEPTH) % nz, 1) for v in values]

    rim = (lane == 0) | (lane == nz - 1)
    for i in range(1, planes - 1):
        for f, value in enumerate(at_plane(rim_one, i)):
            one_ref[f, i - 1] = jnp.where(rim, value, first_ref[f, i - 1])
    for i in range(2, planes - 2):
        centre, rate = plane_rates(lambda f, i: one_ref[f, i - 1], i, rows, at_plane(ends_one, i))
        for f in every:
            two_ref[f, i - 2] = stage_two(outside, start(f, i), centre[f], rate[f])
    for i in range(3, planes - 3):
        centre, rate = plane_rates(lambda f, i: two_ref[f, i - 2], i, ny, at_plane(ends_two, i))
        for f in every:
            value = 1.0 / 3.0 * start(f, i)[:ny] + 2.0 / 3.0 * (centre[f] + DT_STEP * rate[f])
            flow_ref[f, i - DEPTH] = value

    points = sample_ref.shape[1]
    spot = jnp.broadcast_to(sample_ref[...], (nz, points))
    place = lax.broadcasted_iota(jnp.int32, (nx * ny, points), 0)
    in_row = (place == jnp.broadcast_to(sample_ref[...] // nz, (nx * ny, points))).astype(jnp.bfloat16)
    in_lane = lax.broadcasted_iota(jnp.int32, (nz, points), 0) == spot % nz
    product = jnp.zeros((modes + 1, points), jnp.float32)
    for c in range(3):
        field = flow_ref[c].reshape(nx * ny, nz).T
        found = sum(dot_parts(part, in_row, ((1,), (0,))) for part in three_parts(field))
        picked = jnp.sum(jnp.where(in_lane, found, 0.0), axis=0, keepdims=True)
        snap_ref[c] = picked
        product = product + jnp.concatenate([basis_ref[c], picked], axis=0) * picked
    total = jnp.sum(product, axis=1, keepdims=True)
    size = modes + 1
    diagonal = lax.broadcasted_iota(jnp.int32, (size, size), 0) == lax.broadcasted_iota(jnp.int32, (size, size), 1)
    cross_ref[...] = jnp.sum(jnp.where(diagonal, total, 0.0), axis=0, keepdims=True)


def merge_kernel(parts_ref, cross_ref, send_ref):
    total = parts_ref[0]
    for d in range(1, parts_ref.shape[0]):
        total = total + parts_ref[d]
    block = jnp.concatenate([total, cross_ref[...]], axis=0)
    for d in range(send_ref.shape[0]):
        send_ref[d] = block


def final_kernel(
    count, got_ref, parts_ref, snap_ref, flow_ref,
    basis_hbm, factor_hbm, flow_hbm,
    packed_ref, work_ref, basis_out_ref, factor_ref, sems,
):
    _, comps, size, points = parts_ref.shape
    tall = size // 4
    per = got_ref.shape[1] - 1
    copies = [pltpu.make_async_copy(flow_ref, flow_hbm, sems.at[0])]
    copies[0].start()

    total = jnp.zeros((per + 1, size), jnp.float32)
    for d in range(got_ref.shape[0]):
        block = got_ref[d]
        if per * d < packed_ref.shape[0]:
            packed_ref[per * d : per * d + per] = block[0:per]
        total = total + block
    cross = total[per : per + 1] / count
    top = lax.broadcasted_iota(jnp.int32, (16, size), 0)
    mark = (lax.broadcasted_iota(jnp.int32, (16, size), 1) == size - 1) & (top < 3)
    thirds = jnp.zeros((16, size), jnp.float32)
    for k, part in enumerate(three_parts(cross)):
        thirds = jnp.where(top == k, part.astype(jnp.float32), thirds)
    side = dot_parts(thirds.astype(jnp.bfloat16), mark.astype(jnp.bfloat16), ((0,), (0,)))
    lane = lax.broadcasted_iota(jnp.int32, (tall, size), 1)
    row = lax.broadcasted_iota(jnp.int32, (tall, size), 0)
    old = unpack_upper([packed_ref[tall * k : tall * k + tall] / count for k in range(3)], tall)
    for k in range(4):
        value = jnp.where(lane == size - 1, side[tall * k : tall * k + tall], old[k])
        if k == 3:
            value = jnp.where(row == tall - 1, jnp.broadcast_to(cross, value.shape), value)
        work_ref[tall * k : tall * k + tall, 0:size] = value
        work_ref[tall * k : tall * k + tall, size : 2 * size] = (lane == row + tall * k).astype(jnp.float32)

    for k in range(4):
        base = tall * k
        eliminate(work_ref, base, tall)
        done = work_ref[base : base + tall, :]
        if k < 3:
            change = dot_stacked(done[:, 0:size], done)
            work_ref[base + tall : size, :] = work_ref[base + tall : size, :] - change[base + tall : size]
        factor_ref[base : base + tall, :] = jnp.where(lane >= row + base, done[:, 0:size], 0.0)
        if k < 2:
            continue
        begin, count_rows = (0, base + tall) if k == 2 else (base, tall)
        inverse = work_ref[begin : base + tall, size : 2 * size]
        pieces = jnp.concatenate(three_parts(inverse), axis=0)
        for c in range(comps):
            value = jnp.zeros((count_rows, points), jnp.float32)
            for n in (2, 1, 0):
                products = dot_parts(pieces[: count_rows * (3 - n)], parts_ref[n, c], ((1,), (0,)))
                for m in range(2 - n, -1, -1):
                    value = value + products[count_rows * m : count_rows * m + count_rows]
            if k == 3:
                value = value + inverse[:, size - 1 : size] * snap_ref[c]
            basis_out_ref[c, begin : base + tall, :] = value
        rows = (slice(None), pl.ds(begin, count_rows), slice(None))
        copies.append(pltpu.make_async_copy(basis_out_ref.at[rows], basis_hbm.at[rows], sems.at[k]))
        copies[-1].start()
    copies.append(pltpu.make_async_copy(factor_ref, factor_hbm, sems.at[1]))
    copies[-1].start()
    for copy in copies:
        copy.wait()


def eliminate(work_ref, base, tall):
    blocks = tall // 8
    sub = lax.broadcasted_iota(jnp.int32, (8, 128), 0)
    panel = [work_ref[base + 8 * b : base + 8 * b + 8, :] for b in range(blocks)]
    scale = [jnp.zeros((8, 128), jnp.float32) for _ in range(blocks)]
    half = tall // 2
    for low in (0, half):
        high = low + half
        column = {
            k: {b: jnp.broadcast_to(panel[b][:, base + k : base + k + 1], (8, 128)) for b in range(k // 8, blocks)}
            for k in range(low, high)
        }
        for j in range(low, high):
            mine, at = divmod(j, 8)
            pivot = column[j][mine][at : at + 1, :]
            inverse = 1.0 / pivot
            scaled = {b: column[j][b] * inverse for b in range(mine, blocks)}
            for k in range(j + 1, high):
                other, place = divmod(k, 8)
                times = scaled[other][place : place + 1, :]
                for b in range(other, blocks):
                    column[k][b] = column[k][b] - column[j][b] * times
            scale[mine] = jnp.where(sub == at, lax.rsqrt(pivot), scale[mine])
            pivot_row = panel[mine][at : at + 1, :]
            for b in range(mine, blocks):
                times = jnp.where(sub > at, scaled[b], 0.0) if b == mine else scaled[b]
                panel[b] = panel[b] - jnp.concatenate([times, times], axis=1) * pivot_row
    for b in range(blocks):
        work_ref[base + 8 * b : base + 8 * b + 8, :] = panel[b] * jnp.concatenate([scale[b], scale[b]], axis=1)


def local(flow, basis, sample):
    fields, nx, ny, nz = flow.shape
    modes, comps, points = basis.shape
    size = modes + 1
    devices = lax.axis_size("gx") * lax.axis_size("gy") * lax.axis_size("gz")
    count = float(comps * points * devices)
    shape = functools.partial(jax.ShapeDtypeStruct, dtype=jnp.float32)
    call = functools.partial(pl.pallas_call, compiler_params=PARAMS)
    bricks = jnp.transpose(basis, (1, 0, 2))

    whole = pl.BlockSpec(memory_space=pltpu.HBM)
    flat = flow.reshape(fields, nx * ny, nz)
    quarter = size // 4
    per = -(-3 * quarter // devices)

    place = lax.axis_index("gy")
    flags = [place == 0, place == lax.axis_size("gy") - 1, place % 2 == 1]
    flags = jnp.broadcast_to(jnp.stack(flags).astype(jnp.int32)[:, None], (len(flags), nz))
    strip = shape((fields, nx * DEPTH, nz))
    strips = call(
        functools.partial(strips_kernel, nx), out_shape=(strip, strip), in_specs=[VMEM] * 2, out_specs=(VMEM, VMEM)
    )(flags, flat)
    y_even, y_odd = pairs(*strips, "gy")
    gram, basis_parts = call(
        gram_kernel,
        out_shape=(shape((devices, per, size)), jax.ShapeDtypeStruct((3, comps, size, points), jnp.bfloat16)),
        in_specs=[VMEM],
        out_specs=(VMEM, VMEM),
        scratch_shapes=[pltpu.VMEM((size, size), jnp.float32), pltpu.VMEM((devices * per, size), jnp.float32)],
    )(bricks)
    y_even, y_odd, gram = lax.optimization_barrier((y_even, y_odd, gram))

    rows = ny + HALO
    face = shape((fields, DEPTH * ny + HALO, nz))
    mid, first, last = call(
        functools.partial(walls_kernel, nx),
        out_shape=(shape((fields, nx * rows, nz)), face, face),
        in_specs=[VMEM] * 4,
        out_specs=(VMEM,) * 3,
    )(flags, flat, y_even, y_odd)
    mid = mid.reshape(fields, nx, rows, nz)
    low_face, high_face = neighbours(first, last, "gx")
    parts = lax.all_to_all(gram, ALL, 0, 0)

    beside = shape((fields, DEPTH, rows, nz))
    packed, xlo, xhi = call(
        pack_kernel,
        out_shape=(shape((fields, rows, nz)), beside, beside),
        in_specs=[VMEM] * 3,
        out_specs=(VMEM,) * 3,
    )(mid, low_face, high_face)
    if lax.axis_size("gz") == 2:
        low = high = lax.ppermute(packed, "gz", [(0, 1), (1, 0)])
    else:
        low, high = neighbours(packed, packed, "gz")
    begun, cells = call(
        first_kernel,
        out_shape=(
            shape((fields, nx + 2 * DEPTH - 2, rows, nz)),
            jax.ShapeDtypeStruct((1, points), sample.dtype),
        ),
        in_specs=[VMEM, whole] + [VMEM] * 3,
        out_specs=(VMEM, VMEM),
        scratch_shapes=[pltpu.SemaphoreType.DMA],
    )(flags, sample.reshape(1, points), mid, xlo, xhi)
    flow_new, snapshot, cross = call(
        step_kernel,
        out_shape=(shape(flow.shape), shape((comps, 1, points)), shape((1, size))),
        in_specs=[VMEM] * 10,
        out_specs=(VMEM, VMEM, VMEM),
        scratch_shapes=[
            pltpu.VMEM((fields, nx + 2 * DEPTH - 2, rows, nz), jnp.float32),
            pltpu.VMEM((fields, nx + 2 * DEPTH - 4, rows, nz), jnp.float32),
        ],
    )(flags, mid, xlo, xhi, begun, packed, low, high, bricks, cells)

    send = call(
        merge_kernel, out_shape=shape((devices, per + 1, size)), in_specs=[VMEM] * 2, out_specs=VMEM
    )(parts, cross)
    got = lax.all_to_all(send, ALL, 0, 0)
    basis_next, factor, flow_next = call(
        functools.partial(final_kernel, count),
        out_shape=(shape((comps, size, points)), shape((size, size)), shape(flow.shape)),
        in_specs=[VMEM] * 4,
        out_specs=(whole,) * 3,
        scratch_shapes=[
            pltpu.VMEM((3 * quarter, size), jnp.float32),
            pltpu.VMEM((size, 2 * size), jnp.float32),
            pltpu.VMEM((comps, size, points), jnp.float32),
            pltpu.VMEM((size, size), jnp.float32),
            pltpu.SemaphoreType.DMA((4,)),
        ],
    )(got, basis_parts, snapshot, flow_new)
    return flow_next, jnp.transpose(basis_next, (1, 0, 2)), factor


def solution(mesh):
    return jax.shard_map(
        local,
        mesh=mesh,
        in_specs=(
            P(None, "gx", "gy", "gz"),
            P(None, None, ("gx", "gy", "gz")),
            P(("gx", "gy", "gz")),
        ),
        out_specs=(P(None, "gx", "gy", "gz"), P(None, None, ("gx", "gy", "gz")), P()),
        check_vma=False,
    )
```

```python
import functools

import jax
import jax.numpy as jnp
from jax import lax
from jax.experimental import pallas as pl
from jax.experimental.pallas import tpu as pltpu
from jax.sharding import PartitionSpec as P

DT_STEP = 0.35
VISCOSITY = 0.2
SOUND_SQ = 1.0
DRIVING = 0.5

ALL = ("gx", "gy", "gz")
DEPTH = 3
EXACT = lax.Precision.HIGHEST
VMEM = pl.BlockSpec(memory_space=pltpu.VMEM)
PARAMS = pltpu.CompilerParams(vmem_limit_bytes=40 * 1024 * 1024)


def dot(a, b, dims):
    return lax.dot_general(
        a, b, (dims, ((), ())), precision=EXACT, preferred_element_type=jnp.float32
    )


def three_parts(value):
    high = value.astype(jnp.bfloat16)
    rest = value - high.astype(jnp.float32)
    middle = rest.astype(jnp.bfloat16)
    return high, middle, (rest - middle.astype(jnp.float32)).astype(jnp.bfloat16)


def dot_parts(a, b, dims):
    return lax.dot_general(a, b, (dims, ((), ())), preferred_element_type=jnp.float32)


def dot_stacked(a, b):
    (a1, a2, a3), (b1, b2, b3) = three_parts(a), three_parts(b)
    first = jnp.concatenate([a1, a1, a2, a2, a1, a3], axis=0)
    second = jnp.concatenate([b1, b2, b1, b2, b3, b1], axis=0)
    return dot_parts(first, second, ((0,), (0,)))


def neighbours(block_low, block_high, axis):
    count = lax.axis_size(axis)
    forward = [(i, (i + 1) % count) for i in range(count)]
    backward = [(target, source) for source, target in forward]
    return lax.ppermute(block_high, axis, forward), lax.ppermute(block_low, axis, backward)


def pairs(block_odd, block_even, axis):
    count = lax.axis_size(axis)
    even = [(i, i + 1 - 2 * (i % 2)) for i in range(count)]
    odd = [(i, (i - 1 + 2 * (i % 2)) % count) for i in range(count)]
    from_odd = lax.ppermute(block_odd, axis, odd)
    return lax.ppermute(block_even, axis, even), from_odd


LOWER_WALL, UPPER_WALL, ODD_Y = range(3)


def flag(flags_ref, which):
    return flags_ref[which : which + 1] == 1


def pack_upper(rows, tall):
    size = rows.shape[1]
    lane = lax.broadcasted_iota(jnp.int32, (tall, size), 1)
    part = [rows[tall * k : tall * k + tall] for k in range(4)]
    return [part[0], jnp.where(lane >= tall, part[1], pltpu.roll(part[3], tall, 1)), part[2]]


def unpack_upper(packed, tall):
    return [packed[0], packed[1], packed[2], pltpu.roll(packed[1], packed[1].shape[1] - tall, 1)]


def gram_kernel(basis_ref, send_ref, parts_ref, gram_ref, packed_ref):
    modes = basis_ref.shape[1]
    tall = gram_ref.shape[0] // 4
    total = jnp.zeros((modes, modes), jnp.float32)
    for c in range(basis_ref.shape[0]):
        rows = basis_ref[c]
        total = total + dot(rows, rows, ((1,), (1,)))
        filled = jnp.concatenate([rows, jnp.zeros((1, rows.shape[1]), jnp.float32)], axis=0)
        for k, part in enumerate(three_parts(filled)):
            parts_ref[k, c] = part
    gram_ref[...] = jnp.zeros_like(gram_ref)
    gram_ref[0:modes, 0:modes] = total
    packed_ref[...] = jnp.zeros_like(packed_ref)
    for k, value in enumerate(pack_upper(gram_ref[...], tall)):
        packed_ref[tall * k : tall * k + tall] = value
    per = send_ref.shape[1]
    for d in range(send_ref.shape[0]):
        send_ref[d] = packed_ref[per * d : per * d + per]


GAP = 2
HALO = 2 * DEPTH + GAP


def strips_kernel(planes, flags_ref, flow_ref, odd_ref, even_ref):
    ny = flow_ref.shape[1] // planes
    odd = flag(flags_ref, ODD_Y)
    for f in range(flow_ref.shape[0]):
        for j in range(DEPTH):
            bottom = flow_ref[f, pl.ds(j, planes, stride=ny), :]
            top = flow_ref[f, pl.ds(ny - DEPTH + j, planes, stride=ny), :]
            even_ref[f, planes * j : planes * j + planes] = jnp.where(odd, bottom, top)
            odd_ref[f, planes * j : planes * j + planes] = jnp.where(odd, top, bottom)


def walls_kernel(planes, flags_ref, flow_ref, odd_ref, even_ref, mid_ref, first_ref, last_ref):
    fields, cells, nz = flow_ref.shape
    odd_y = flag(flags_ref, ODD_Y)
    ny = cells // planes
    rows = ny + HALO
    sub = lax.broadcasted_iota(jnp.int32, (HALO, nz), 0)
    empty = jnp.zeros((planes, nz), jnp.float32)
    for f in range(fields):
        for i in range(planes):
            mid_ref[f, rows * i : rows * i + ny] = flow_ref[f, ny * i : ny * i + ny]
        for j in range(HALO):
            k = j if j < DEPTH else j - DEPTH - GAP
            part = slice(planes * k, planes * k + planes)
            if j < DEPTH:
                value = jnp.where(odd_y, odd_ref[f, part], even_ref[f, part])
                value = jnp.where(flag(flags_ref, UPPER_WALL), 0.0, value)
            elif j < DEPTH + GAP:
                value = empty
            else:
                value = jnp.where(odd_y, even_ref[f, part], odd_ref[f, part])
                value = jnp.where(flag(flags_ref, LOWER_WALL), 0.0, value)
            mid_ref[f, pl.ds(ny + j, planes, stride=rows), :] = value
        for face_ref, begin, near, next_one in (
            (first_ref, 0, 0, 1), (last_ref, planes - DEPTH, planes - 1, planes - 2)
        ):
            for k in range(DEPTH):
                face_ref[f, ny * k : ny * k + ny] = flow_ref[f, ny * (begin + k) : ny * (begin + k) + ny]
            halos = [mid_ref[f, rows * i + ny : rows * i + rows] for i in (near, next_one)]
            face_ref[f, ny * DEPTH : ny * DEPTH + HALO] = corner_rows(*halos, sub)


def corner_rows(near, next_one, sub):
    tile = jnp.where(sub == 2, pltpu.roll(next_one, 2, 0), pltpu.roll(next_one, 6, 0))
    tile = jnp.where((sub == 2) | (sub == 5), tile, 0.0)
    return jnp.where((sub < 2) | (sub >= 6), near, tile)


def corner_planes(tile, sub):
    near = jnp.where((sub < 2) | (sub >= 6), tile, 0.0)
    next_one = jnp.where(sub == 0, pltpu.roll(tile, 6, 0), pltpu.roll(tile, 2, 0))
    return [near, jnp.where((sub == 0) | (sub == 7), next_one, 0.0), jnp.zeros_like(tile)]


def plane_of(mid_ref, xlo_ref, xhi_ref, f, i):
    nx = mid_ref.shape[1]
    if i < DEPTH:
        return xlo_ref[f, i]
    if i < DEPTH + nx:
        return mid_ref[f, i - DEPTH]
    return xhi_ref[f, i - DEPTH - nx]


GROUP = 8


def pack_kernel(mid_ref, low_ref, high_ref, packed_ref, xlo_ref, xhi_ref):
    fields, nx, rows, nz = mid_ref.shape
    ny = rows - HALO
    lane = lax.broadcasted_iota(jnp.int32, (rows, nz), 1)
    sub = lax.broadcasted_iota(jnp.int32, (HALO, nz), 0)
    for f in range(fields):
        for face_ref, out_ref, order in ((low_ref, xlo_ref, (2, 1, 0)), (high_ref, xhi_ref, (0, 1, 2))):
            face = face_ref[f]
            halo = corner_planes(face[ny * DEPTH :], sub)
            for k in range(DEPTH):
                out_ref[f, k, 0:ny] = face[ny * k : ny * k + ny]
                out_ref[f, k, ny:rows] = halo[order[k]]
        value = jnp.zeros((rows, nz), jnp.float32)
        for i in range(nx + 2 * DEPTH):
            start = GROUP * i
            moved = pltpu.roll(plane_of(mid_ref, xlo_ref, xhi_ref, f, i), (start + DEPTH) % nz, 1)
            value = jnp.where((lane >= start) & (lane < start + 2 * DEPTH), moved, value)
        packed_ref[f] = value


def step(value, by, axis):
    size = value.shape[axis]
    return pltpu.roll(value, (size - by) % size, axis)


def rates(centre, x_plus, x_minus, y_plus, y_minus, z_plus, z_minus):
    slope_x = [0.5 * (a - b) for a, b in zip(x_plus, x_minus)]
    slope_y = [0.5 * (a - b) for a, b in zip(y_plus, y_minus)]
    slope_z = [0.5 * (a - b) for a, b in zip(z_plus, z_minus)]
    pressure = [slope_x[3], slope_y[3], slope_z[3]]
    out = []
    for f in range(3):
        laplace = (
            x_plus[f] + x_minus[f] + (y_plus[f] + y_minus[f]) + (z_plus[f] + z_minus[f]) - 6.0 * centre[f]
        )
        advect = centre[0] * slope_x[f] + centre[1] * slope_y[f] + centre[2] * slope_z[f]
        value = VISCOSITY * laplace - advect - pressure[f]
        if f == 0:
            value = value + DRIVING
        out.append(value)
    out.append(-SOUND_SQ * (slope_x[0] + slope_y[1] + slope_z[2]))
    return out


def beyond_walls(flags_ref, ny, shape):
    row = lax.broadcasted_iota(jnp.int32, shape, 0)
    below = (row >= ny + DEPTH + GAP) & flag(flags_ref, LOWER_WALL)
    above = (row >= ny) & (row < ny + DEPTH) & flag(flags_ref, UPPER_WALL)
    return below | above


def plane_rates(read, i, rows, ends=None):
    every = range(4)
    centre = [read(f, i) for f in every]
    x_plus = [read(f, i + 1)[:rows] for f in every]
    x_minus = [read(f, i - 1)[:rows] for f in every]
    y_plus = [step(v, 1, 0)[:rows] for v in centre]
    y_minus = [step(v, -1, 0)[:rows] for v in centre]
    centre = [v[:rows] for v in centre]
    upward, downward = centre, centre
    if ends is not None:
        lane = lax.broadcasted_iota(jnp.int32, centre[0].shape, 1)
        upward = [jnp.where(lane == 0, e[:rows], v) for e, v in zip(ends, centre)]
        downward = [jnp.where(lane == lane.shape[1] - 1, e[:rows], v) for e, v in zip(ends, centre)]
    z_plus = [step(v, 1, 1) for v in upward]
    z_minus = [step(v, -1, 1) for v in downward]
    return centre, rates(centre, x_plus, x_minus, y_plus, y_minus, z_plus, z_minus)


def stage_one(outside, value, rate):
    return jnp.where(outside, 0.0, value + DT_STEP * rate)


def stage_two(outside, begin, value, rate):
    return jnp.where(outside, 0.0, 0.75 * begin + 0.25 * (value + DT_STEP * rate))


def first_kernel(flags_ref, sample_hbm, mid_ref, xlo_ref, xhi_ref, one_ref, sample_ref, sem):
    copy = pltpu.make_async_copy(sample_hbm, sample_ref, sem)
    copy.start()
    fields, nx, rows, nz = mid_ref.shape
    outside = beyond_walls(flags_ref, rows - HALO, (rows, nz))
    for i in range(1, nx + 2 * DEPTH - 1):
        centre, rate = plane_rates(functools.partial(plane_of, mid_ref, xlo_ref, xhi_ref), i, rows)
        for f in range(4):
            one_ref[f, i - 1] = stage_one(outside, centre[f], rate[f])
    copy.wait()


def step_kernel(
    flags_ref, mid_ref, xlo_ref, xhi_ref, first_ref, own_ref, low_ref, high_ref, basis_ref, sample_ref,
    flow_ref, snap_ref, cross_ref,
    one_ref, two_ref,
):
    fields, nx, ny, nz = flow_ref.shape
    rows = mid_ref.shape[2]
    modes = basis_ref.shape[1]
    planes = nx + 2 * DEPTH
    lane = lax.broadcasted_iota(jnp.int32, (rows, nz), 1)
    outside = beyond_walls(flags_ref, ny, (rows, nz))
    every = range(4)
    start = functools.partial(plane_of, mid_ref, xlo_ref, xhi_ref)

    left = lane % GROUP < DEPTH

    def window_rates(q):
        return rates(
            q, [step(v, GROUP, 1) for v in q], [step(v, -GROUP, 1) for v in q],
            [step(v, 1, 0) for v in q], [step(v, -1, 0) for v in q],
            [step(v, 1, 1) for v in q], [step(v, -1, 1) for v in q],
        )

    own = [own_ref[f] for f in every]
    other = [jnp.where(left, low_ref[f], high_ref[f]) for f in every]
    windows = []
    for parts in ((other, own), (own, other)):
        q0 = [jnp.where(left, a, b) for a, b in zip(*parts)]
        q1 = [stage_one(outside, v, r) for v, r in zip(q0, window_rates(q0))]
        q2 = [stage_two(outside, s, v, r) for s, v, r in zip(q0, q1, window_rates(q1))]
        windows.append((q1, q2))
    (low_one, low_two), (high_one, high_two) = windows
    ends_one = [jnp.where(left, a, b) for a, b in zip(low_one, high_one)]
    ends_two = [jnp.where(left, a, b) for a, b in zip(low_two, high_two)]
    rim_one = [jnp.where(left, b, a) for a, b in zip(low_one, high_one)]

    def at_plane(values, i):
        return [pltpu.roll(v, (2 * nz - GROUP * i - DEPTH) % nz, 1) for v in values]

    rim = (lane == 0) | (lane == nz - 1)
    for i in range(1, planes - 1):
        for f, value in enumerate(at_plane(rim_one, i)):
            one_ref[f, i - 1] = jnp.where(rim, value, first_ref[f, i - 1])
    for i in range(2, planes - 2):
        centre, rate = plane_rates(lambda f, i: one_ref[f, i - 1], i, rows, at_plane(ends_one, i))
        for f in every:
            two_ref[f, i - 2] = stage_two(outside, start(f, i), centre[f], rate[f])
    for i in range(3, planes - 3):
        centre, rate = plane_rates(lambda f, i: two_ref[f, i - 2], i, ny, at_plane(ends_two, i))
        for f in every:
            value = 1.0 / 3.0 * start(f, i)[:ny] + 2.0 / 3.0 * (centre[f] + DT_STEP * rate[f])
            flow_ref[f, i - DEPTH] = value

    points = sample_ref.shape[1]
    spot = jnp.broadcast_to(sample_ref[...], (nz, points))
    place = lax.broadcasted_iota(jnp.int32, (nx * ny, points), 0)
    in_row = (place == jnp.broadcast_to(sample_ref[...] // nz, (nx * ny, points))).astype(jnp.bfloat16)
    in_lane = lax.broadcasted_iota(jnp.int32, (nz, points), 0) == spot % nz
    product = jnp.zeros((modes + 1, points), jnp.float32)
    for c in range(3):
        field = flow_ref[c].reshape(nx * ny, nz).T
        found = sum(dot_parts(part, in_row, ((1,), (0,))) for part in three_parts(field))
        picked = jnp.sum(jnp.where(in_lane, found, 0.0), axis=0, keepdims=True)
        snap_ref[c] = picked
        product = product + jnp.concatenate([basis_ref[c], picked], axis=0) * picked
    total = jnp.sum(product, axis=1, keepdims=True)
    size = modes + 1
    diagonal = lax.broadcasted_iota(jnp.int32, (size, size), 0) == lax.broadcasted_iota(jnp.int32, (size, size), 1)
    cross_ref[...] = jnp.sum(jnp.where(diagonal, total, 0.0), axis=0, keepdims=True)


def merge_kernel(parts_ref, cross_ref, send_ref):
    total = parts_ref[0]
    for d in range(1, parts_ref.shape[0]):
        total = total + parts_ref[d]
    block = jnp.concatenate([total, cross_ref[...]], axis=0)
    for d in range(send_ref.shape[0]):
        send_ref[d] = block


def final_kernel(
    count, got_ref, parts_ref, snap_ref, flow_ref,
    basis_hbm, factor_hbm, flow_hbm,
    packed_ref, work_ref, basis_out_ref, factor_ref, sems,
):
    _, comps, size, points = parts_ref.shape
    tall = size // 4
    per = got_ref.shape[1] - 1
    copies = [pltpu.make_async_copy(flow_ref, flow_hbm, sems.at[0])]
    copies[0].start()

    total = jnp.zeros((per + 1, size), jnp.float32)
    for d in range(got_ref.shape[0]):
        block = got_ref[d]
        if per * d < packed_ref.shape[0]:
            packed_ref[per * d : per * d + per] = block[0:per]
        total = total + block
    cross = total[per : per + 1] / count
    top = lax.broadcasted_iota(jnp.int32, (16, size), 0)
    mark = (lax.broadcasted_iota(jnp.int32, (16, size), 1) == size - 1) & (top < 3)
    thirds = jnp.zeros((16, size), jnp.float32)
    for k, part in enumerate(three_parts(cross)):
        thirds = jnp.where(top == k, part.astype(jnp.float32), thirds)
    side = dot_parts(thirds.astype(jnp.bfloat16), mark.astype(jnp.bfloat16), ((0,), (0,)))
    lane = lax.broadcasted_iota(jnp.int32, (tall, size), 1)
    row = lax.broadcasted_iota(jnp.int32, (tall, size), 0)
    old = unpack_upper([packed_ref[tall * k : tall * k + tall] / count for k in range(3)], tall)
    for k in range(4):
        value = jnp.where(lane == size - 1, side[tall * k : tall * k + tall], old[k])
        if k == 3:
            value = jnp.where(row == tall - 1, jnp.broadcast_to(cross, value.shape), value)
        work_ref[tall * k : tall * k + tall, 0:size] = value
        work_ref[tall * k : tall * k + tall, size : 2 * size] = (lane == row + tall * k).astype(jnp.float32)

    for k in range(4):
        base = tall * k
        eliminate(work_ref, base, tall)
        done = work_ref[base : base + tall, :]
        if k < 3:
            change = dot_stacked(done[:, 0:size], done)
            work_ref[base + tall : size, :] = work_ref[base + tall : size, :] - change[base + tall : size]
        factor_ref[base : base + tall, :] = jnp.where(lane >= row + base, done[:, 0:size], 0.0)
        if k < 2:
            continue
        begin, count_rows = (0, base + tall) if k == 2 else (base, tall)
        inverse = work_ref[begin : base + tall, size : 2 * size]
        pieces = jnp.concatenate(three_parts(inverse), axis=0)
        for c in range(comps):
            value = jnp.zeros((count_rows, points), jnp.float32)
            for n in (2, 1, 0):
                products = dot_parts(pieces[: count_rows * (3 - n)], parts_ref[n, c], ((1,), (0,)))
                for m in range(2 - n, -1, -1):
                    value = value + products[count_rows * m : count_rows * m + count_rows]
            if k == 3:
                value = value + inverse[:, size - 1 : size] * snap_ref[c]
            basis_out_ref[c, begin : base + tall, :] = value
        rows = (slice(None), pl.ds(begin, count_rows), slice(None))
        copies.append(pltpu.make_async_copy(basis_out_ref.at[rows], basis_hbm.at[rows], sems.at[k]))
        copies[-1].start()
    copies.append(pltpu.make_async_copy(factor_ref, factor_hbm, sems.at[1]))
    copies[-1].start()
    for copy in copies:
        copy.wait()


def eliminate(work_ref, base, tall):
    blocks = tall // 8
    sub = lax.broadcasted_iota(jnp.int32, (8, 128), 0)
    panel = [work_ref[base + 8 * b : base + 8 * b + 8, :] for b in range(blocks)]
    scale = [jnp.zeros((8, 128), jnp.float32) for _ in range(blocks)]
    half = tall // 2
    for low in (0, half):
        high = low + half
        column = {
            k: {b: jnp.broadcast_to(panel[b][:, base + k : base + k + 1], (8, 128)) for b in range(k // 8, blocks)}
            for k in range(low, high)
        }
        for j in range(low, high):
            mine, at = divmod(j, 8)
            pivot = column[j][mine][at : at + 1, :]
            inverse = 1.0 / pivot
            scaled = {b: column[j][b] * inverse for b in range(mine, blocks)}
            for k in range(j + 1, high):
                other, place = divmod(k, 8)
                times = scaled[other][place : place + 1, :]
                for b in range(other, blocks):
                    column[k][b] = column[k][b] - column[j][b] * times
            scale[mine] = jnp.where(sub == at, lax.rsqrt(pivot), scale[mine])
            pivot_row = panel[mine][at : at + 1, :]
            for b in range(mine, blocks):
                times = jnp.where(sub > at, scaled[b], 0.0) if b == mine else scaled[b]
                panel[b] = panel[b] - jnp.concatenate([times, times], axis=1) * pivot_row
    for b in range(blocks):
        work_ref[base + 8 * b : base + 8 * b + 8, :] = panel[b] * jnp.concatenate([scale[b], scale[b]], axis=1)


def local(flow, basis, sample):
    fields, nx, ny, nz = flow.shape
    modes, comps, points = basis.shape
    size = modes + 1
    devices = lax.axis_size("gx") * lax.axis_size("gy") * lax.axis_size("gz")
    count = float(comps * points * devices)
    shape = functools.partial(jax.ShapeDtypeStruct, dtype=jnp.float32)
    call = functools.partial(pl.pallas_call, compiler_params=PARAMS)
    bricks = jnp.transpose(basis, (1, 0, 2))

    whole = pl.BlockSpec(memory_space=pltpu.HBM)
    flat = flow.reshape(fields, nx * ny, nz)
    quarter = size // 4
    per = -(-3 * quarter // devices)

    place = lax.axis_index("gy")
    flags = [place == 0, place == lax.axis_size("gy") - 1, place % 2 == 1]
    flags = jnp.broadcast_to(jnp.stack(flags).astype(jnp.int32)[:, None], (len(flags), nz))
    strip = shape((fields, nx * DEPTH, nz))
    strips = call(
        functools.partial(strips_kernel, nx), out_shape=(strip, strip), in_specs=[VMEM] * 2, out_specs=(VMEM, VMEM)
    )(flags, flat)
    y_even, y_odd = pairs(*strips, "gy")
    gram, basis_parts = call(
        gram_kernel,
        out_shape=(shape((devices, per, size)), jax.ShapeDtypeStruct((3, comps, size, points), jnp.bfloat16)),
        in_specs=[VMEM],
        out_specs=(VMEM, VMEM),
        scratch_shapes=[pltpu.VMEM((size, size), jnp.float32), pltpu.VMEM((devices * per, size), jnp.float32)],
    )(bricks)
    y_odd, y_even, gram = lax.optimization_barrier((y_odd, y_even, gram))

    rows = ny + HALO
    face = shape((fields, DEPTH * ny + HALO, nz))
    mid, first, last = call(
        functools.partial(walls_kernel, nx),
        out_shape=(shape((fields, nx * rows, nz)), face, face),
        in_specs=[VMEM] * 4,
        out_specs=(VMEM,) * 3,
    )(flags, flat, y_odd, y_even)
    mid = mid.reshape(fields, nx, rows, nz)
    low_face, high_face = neighbours(first, last, "gx")
    parts = lax.all_to_all(gram, ALL, 0, 0)

    beside = shape((fields, DEPTH, rows, nz))
    packed, xlo, xhi = call(
        pack_kernel,
        out_shape=(shape((fields, rows, nz)), beside, beside),
        in_specs=[VMEM] * 3,
        out_specs=(VMEM,) * 3,
    )(mid, low_face, high_face)
    if lax.axis_size("gz") == 2:
        low = high = lax.ppermute(packed, "gz", [(0, 1), (1, 0)])
    else:
        low, high = neighbours(packed, packed, "gz")
    begun, cells = call(
        first_kernel,
        out_shape=(
            shape((fields, nx + 2 * DEPTH - 2, rows, nz)),
            jax.ShapeDtypeStruct((1, points), sample.dtype),
        ),
        in_specs=[VMEM, whole] + [VMEM] * 3,
        out_specs=(VMEM, VMEM),
        scratch_shapes=[pltpu.SemaphoreType.DMA],
    )(flags, sample.reshape(1, points), mid, xlo, xhi)
    flow_new, snapshot, cross = call(
        step_kernel,
        out_shape=(shape(flow.shape), shape((comps, 1, points)), shape((1, size))),
        in_specs=[VMEM] * 10,
        out_specs=(VMEM, VMEM, VMEM),
        scratch_shapes=[
            pltpu.VMEM((fields, nx + 2 * DEPTH - 2, rows, nz), jnp.float32),
            pltpu.VMEM((fields, nx + 2 * DEPTH - 4, rows, nz), jnp.float32),
        ],
    )(flags, mid, xlo, xhi, begun, packed, low, high, bricks, cells)

    send = call(
        merge_kernel, out_shape=shape((devices, per + 1, size)), in_specs=[VMEM] * 2, out_specs=VMEM
    )(parts, cross)
    got = lax.all_to_all(send, ALL, 0, 0)
    basis_next, factor, flow_next = call(
        functools.partial(final_kernel, count),
        out_shape=(shape((comps, size, points)), shape((size, size)), shape(flow.shape)),
        in_specs=[VMEM] * 4,
        out_specs=(whole,) * 3,
        scratch_shapes=[
            pltpu.VMEM((3 * quarter, size), jnp.float32),
            pltpu.VMEM((size, 2 * size), jnp.float32),
            pltpu.VMEM((comps, size, points), jnp.float32),
            pltpu.VMEM((size, size), jnp.float32),
            pltpu.SemaphoreType.DMA((4,)),
        ],
    )(got, basis_parts, snapshot, flow_new)
    return flow_next, jnp.transpose(basis_next, (1, 0, 2)), factor


def solution(mesh):
    return jax.shard_map(
        local,
        mesh=mesh,
        in_specs=(
            P(None, "gx", "gy", "gz"),
            P(None, None, ("gx", "gy", "gz")),
            P(("gx", "gy", "gz")),
        ),
        out_specs=(P(None, "gx", "gy", "gz"), P(None, None, ("gx", "gy", "gz")), P()),
        check_vma=False,
    )
```

```python
import functools

import jax
import jax.numpy as jnp
from jax import lax
from jax.experimental import pallas as pl
from jax.experimental.pallas import tpu as pltpu
from jax.sharding import PartitionSpec as P

DT_STEP = 0.35
VISCOSITY = 0.2
SOUND_SQ = 1.0
DRIVING = 0.5

ALL = ("gz", "gy", "gx")
DEPTH = 3
EXACT = lax.Precision.HIGHEST
VMEM = pl.BlockSpec(memory_space=pltpu.VMEM)
PARAMS = pltpu.CompilerParams(vmem_limit_bytes=40 * 1024 * 1024)


def dot(a, b, dims):
    return lax.dot_general(
        a, b, (dims, ((), ())), precision=EXACT, preferred_element_type=jnp.float32
    )


def three_parts(value):
    high = value.astype(jnp.bfloat16)
    rest = value - high.astype(jnp.float32)
    middle = rest.astype(jnp.bfloat16)
    return high, middle, (rest - middle.astype(jnp.float32)).astype(jnp.bfloat16)


def dot_parts(a, b, dims):
    return lax.dot_general(a, b, (dims, ((), ())), preferred_element_type=jnp.float32)


def dot_stacked(a, b):
    (a1, a2, a3), (b1, b2, b3) = three_parts(a), three_parts(b)
    first = jnp.concatenate([a1, a1, a2, a2, a1, a3], axis=0)
    second = jnp.concatenate([b1, b2, b1, b2, b3, b1], axis=0)
    return dot_parts(first, second, ((0,), (0,)))


def neighbours(block_low, block_high, axis):
    count = lax.axis_size(axis)
    forward = [(i, (i + 1) % count) for i in range(count)]
    backward = [(target, source) for source, target in forward]
    return lax.ppermute(block_high, axis, forward), lax.ppermute(block_low, axis, backward)


def pairs(block_odd, block_even, axis):
    count = lax.axis_size(axis)
    even = [(i, i + 1 - 2 * (i % 2)) for i in range(count)]
    odd = [(i, (i - 1 + 2 * (i % 2)) % count) for i in range(count)]
    from_odd = lax.ppermute(block_odd, axis, odd)
    return lax.ppermute(block_even, axis, even), from_odd


LOWER_WALL, UPPER_WALL, ODD_Y = range(3)


def flag(flags_ref, which):
    return flags_ref[which : which + 1] == 1


def pack_upper(rows, tall):
    size = rows.shape[1]
    lane = lax.broadcasted_iota(jnp.int32, (tall, size), 1)
    part = [rows[tall * k : tall * k + tall] for k in range(4)]
    return [part[0], jnp.where(lane >= tall, part[1], pltpu.roll(part[3], tall, 1)), part[2]]


def unpack_upper(packed, tall):
    return [packed[0], packed[1], packed[2], pltpu.roll(packed[1], packed[1].shape[1] - tall, 1)]


def gram_kernel(basis_ref, send_ref, parts_ref, gram_ref, packed_ref):
    modes = basis_ref.shape[1]
    tall = gram_ref.shape[0] // 4
    total = jnp.zeros((modes, modes), jnp.float32)
    for c in range(basis_ref.shape[0]):
        rows = basis_ref[c]
        total = total + dot(rows, rows, ((1,), (1,)))
        filled = jnp.concatenate([rows, jnp.zeros((1, rows.shape[1]), jnp.float32)], axis=0)
        for k, part in enumerate(three_parts(filled)):
            parts_ref[k, c] = part
    gram_ref[...] = jnp.zeros_like(gram_ref)
    gram_ref[0:modes, 0:modes] = total
    packed_ref[...] = jnp.zeros_like(packed_ref)
    for k, value in enumerate(pack_upper(gram_ref[...], tall)):
        packed_ref[tall * k : tall * k + tall] = value
    per = send_ref.shape[1] - 1
    empty = jnp.zeros((1, send_ref.shape[2]), jnp.float32)
    for d in range(send_ref.shape[0]):
        send_ref[d] = jnp.concatenate([packed_ref[per * d : per * d + per], empty], axis=0)


GAP = 2
HALO = 2 * DEPTH + GAP


def strips_kernel(planes, flags_ref, flow_ref, odd_ref, even_ref):
    ny = flow_ref.shape[1] // planes
    odd = flag(flags_ref, ODD_Y)
    for f in range(flow_ref.shape[0]):
        for j in range(DEPTH):
            bottom = flow_ref[f, pl.ds(j, planes, stride=ny), :]
            top = flow_ref[f, pl.ds(ny - DEPTH + j, planes, stride=ny), :]
            even_ref[f, planes * j : planes * j + planes] = jnp.where(odd, bottom, top)
            odd_ref[f, planes * j : planes * j + planes] = jnp.where(odd, top, bottom)


def walls_kernel(planes, flags_ref, flow_ref, odd_ref, even_ref, mid_ref, first_ref, last_ref):
    fields, cells, nz = flow_ref.shape
    odd_y = flag(flags_ref, ODD_Y)
    ny = cells // planes
    rows = ny + HALO
    sub = lax.broadcasted_iota(jnp.int32, (HALO, nz), 0)
    empty = jnp.zeros((planes, nz), jnp.float32)
    for f in range(fields):
        for i in range(planes):
            mid_ref[f, rows * i : rows * i + ny] = flow_ref[f, ny * i : ny * i + ny]
        for j in range(HALO):
            k = j if j < DEPTH else j - DEPTH - GAP
            part = slice(planes * k, planes * k + planes)
            if j < DEPTH:
                value = jnp.where(odd_y, odd_ref[f, part], even_ref[f, part])
                value = jnp.where(flag(flags_ref, UPPER_WALL), 0.0, value)
            elif j < DEPTH + GAP:
                value = empty
            else:
                value = jnp.where(odd_y, even_ref[f, part], odd_ref[f, part])
                value = jnp.where(flag(flags_ref, LOWER_WALL), 0.0, value)
            mid_ref[f, pl.ds(ny + j, planes, stride=rows), :] = value
        for face_ref, begin, near, next_one in (
            (first_ref, 0, 0, 1), (last_ref, planes - DEPTH, planes - 1, planes - 2)
        ):
            for k in range(DEPTH):
                face_ref[f, ny * k : ny * k + ny] = flow_ref[f, ny * (begin + k) : ny * (begin + k) + ny]
            halos = [mid_ref[f, rows * i + ny : rows * i + rows] for i in (near, next_one)]
            face_ref[f, ny * DEPTH : ny * DEPTH + HALO] = corner_rows(*halos, sub)


def corner_rows(near, next_one, sub):
    tile = jnp.where(sub == 2, pltpu.roll(next_one, 2, 0), pltpu.roll(next_one, 6, 0))
    tile = jnp.where((sub == 2) | (sub == 5), tile, 0.0)
    return jnp.where((sub < 2) | (sub >= 6), near, tile)


def corner_planes(tile, sub):
    near = jnp.where((sub < 2) | (sub >= 6), tile, 0.0)
    next_one = jnp.where(sub == 0, pltpu.roll(tile, 6, 0), pltpu.roll(tile, 2, 0))
    return [near, jnp.where((sub == 0) | (sub == 7), next_one, 0.0), jnp.zeros_like(tile)]


def plane_of(mid_ref, xlo_ref, xhi_ref, f, i):
    nx = mid_ref.shape[1]
    if i < DEPTH:
        return xlo_ref[f, i]
    if i < DEPTH + nx:
        return mid_ref[f, i - DEPTH]
    return xhi_ref[f, i - DEPTH - nx]


GROUP = 8


def pack_kernel(mid_ref, low_ref, high_ref, packed_ref, xlo_ref, xhi_ref):
    fields, nx, rows, nz = mid_ref.shape
    ny = rows - HALO
    lane = lax.broadcasted_iota(jnp.int32, (rows, nz), 1)
    sub = lax.broadcasted_iota(jnp.int32, (HALO, nz), 0)
    for f in range(fields):
        for face_ref, out_ref, order in ((low_ref, xlo_ref, (2, 1, 0)), (high_ref, xhi_ref, (0, 1, 2))):
            face = face_ref[f]
            halo = corner_planes(face[ny * DEPTH :], sub)
            for k in range(DEPTH):
                out_ref[f, k, 0:ny] = face[ny * k : ny * k + ny]
                out_ref[f, k, ny:rows] = halo[order[k]]
        value = jnp.zeros((rows, nz), jnp.float32)
        for i in range(nx + 2 * DEPTH):
            start = GROUP * i
            moved = pltpu.roll(plane_of(mid_ref, xlo_ref, xhi_ref, f, i), (start + DEPTH) % nz, 1)
            value = jnp.where((lane >= start) & (lane < start + 2 * DEPTH), moved, value)
        packed_ref[f] = value


def step(value, by, axis):
    size = value.shape[axis]
    return pltpu.roll(value, (size - by) % size, axis)


def rates(centre, x_plus, x_minus, y_plus, y_minus, z_plus, z_minus):
    slope_x = [0.5 * (a - b) for a, b in zip(x_plus, x_minus)]
    slope_y = [0.5 * (a - b) for a, b in zip(y_plus, y_minus)]
    slope_z = [0.5 * (a - b) for a, b in zip(z_plus, z_minus)]
    pressure = [slope_x[3], slope_y[3], slope_z[3]]
    out = []
    for f in range(3):
        laplace = (
            x_plus[f] + x_minus[f] + (y_plus[f] + y_minus[f]) + (z_plus[f] + z_minus[f]) - 6.0 * centre[f]
        )
        advect = centre[0] * slope_x[f] + centre[1] * slope_y[f] + centre[2] * slope_z[f]
        value = VISCOSITY * laplace - advect - pressure[f]
        if f == 0:
            value = value + DRIVING
        out.append(value)
    out.append(-SOUND_SQ * (slope_x[0] + slope_y[1] + slope_z[2]))
    return out


def beyond_walls(flags_ref, ny, shape):
    row = lax.broadcasted_iota(jnp.int32, shape, 0)
    below = (row >= ny + DEPTH + GAP) & flag(flags_ref, LOWER_WALL)
    above = (row >= ny) & (row < ny + DEPTH) & flag(flags_ref, UPPER_WALL)
    return below | above


def plane_rates(read, i, rows, ends=None):
    every = range(4)
    centre = [read(f, i) for f in every]
    x_plus = [read(f, i + 1)[:rows] for f in every]
    x_minus = [read(f, i - 1)[:rows] for f in every]
    y_plus = [step(v, 1, 0)[:rows] for v in centre]
    y_minus = [step(v, -1, 0)[:rows] for v in centre]
    centre = [v[:rows] for v in centre]
    upward, downward = centre, centre
    if ends is not None:
        lane = lax.broadcasted_iota(jnp.int32, centre[0].shape, 1)
        upward = [jnp.where(lane == 0, e[:rows], v) for e, v in zip(ends, centre)]
        downward = [jnp.where(lane == lane.shape[1] - 1, e[:rows], v) for e, v in zip(ends, centre)]
    z_plus = [step(v, 1, 1) for v in upward]
    z_minus = [step(v, -1, 1) for v in downward]
    return centre, rates(centre, x_plus, x_minus, y_plus, y_minus, z_plus, z_minus)


def stage_one(outside, value, rate):
    return jnp.where(outside, 0.0, value + DT_STEP * rate)


def stage_two(outside, begin, value, rate):
    return jnp.where(outside, 0.0, 0.75 * begin + 0.25 * (value + DT_STEP * rate))


def first_kernel(flags_ref, sample_hbm, mid_ref, xlo_ref, xhi_ref, one_ref, sample_ref, sem):
    copy = pltpu.make_async_copy(sample_hbm, sample_ref, sem)
    copy.start()
    fields, nx, rows, nz = mid_ref.shape
    outside = beyond_walls(flags_ref, rows - HALO, (rows, nz))
    for i in range(1, nx + 2 * DEPTH - 1):
        centre, rate = plane_rates(functools.partial(plane_of, mid_ref, xlo_ref, xhi_ref), i, rows)
        for f in range(4):
            one_ref[f, i - 1] = stage_one(outside, centre[f], rate[f])
    copy.wait()


def step_kernel(
    flags_ref, mid_ref, xlo_ref, xhi_ref, first_ref, own_ref, low_ref, high_ref, basis_ref, sample_ref,
    flow_ref, snap_ref, cross_ref,
    one_ref, two_ref,
):
    fields, nx, ny, nz = flow_ref.shape
    rows = mid_ref.shape[2]
    modes = basis_ref.shape[1]
    planes = nx + 2 * DEPTH
    lane = lax.broadcasted_iota(jnp.int32, (rows, nz), 1)
    outside = beyond_walls(flags_ref, ny, (rows, nz))
    every = range(4)
    start = functools.partial(plane_of, mid_ref, xlo_ref, xhi_ref)

    left = lane % GROUP < DEPTH

    def window_rates(q):
        return rates(
            q, [step(v, GROUP, 1) for v in q], [step(v, -GROUP, 1) for v in q],
            [step(v, 1, 0) for v in q], [step(v, -1, 0) for v in q],
            [step(v, 1, 1) for v in q], [step(v, -1, 1) for v in q],
        )

    own = [own_ref[f] for f in every]
    other = [jnp.where(left, low_ref[f], high_ref[f]) for f in every]
    windows = []
    for parts in ((other, own), (own, other)):
        q0 = [jnp.where(left, a, b) for a, b in zip(*parts)]
        q1 = [stage_one(outside, v, r) for v, r in zip(q0, window_rates(q0))]
        q2 = [stage_two(outside, s, v, r) for s, v, r in zip(q0, q1, window_rates(q1))]
        windows.append((q1, q2))
    (low_one, low_two), (high_one, high_two) = windows
    ends_one = [jnp.where(left, a, b) for a, b in zip(low_one, high_one)]
    ends_two = [jnp.where(left, a, b) for a, b in zip(low_two, high_two)]
    rim_one = [jnp.where(left, b, a) for a, b in zip(low_one, high_one)]

    def at_plane(values, i):
        return [pltpu.roll(v, (2 * nz - GROUP * i - DEPTH) % nz, 1) for v in values]

    rim = (lane == 0) | (lane == nz - 1)
    for i in range(1, planes - 1):
        for f, value in enumerate(at_plane(rim_one, i)):
            one_ref[f, i - 1] = jnp.where(rim, value, first_ref[f, i - 1])
    for i in range(2, planes - 2):
        centre, rate = plane_rates(lambda f, i: one_ref[f, i - 1], i, rows, at_plane(ends_one, i))
        for f in every:
            two_ref[f, i - 2] = stage_two(outside, start(f, i), centre[f], rate[f])
    for i in range(3, planes - 3):
        centre, rate = plane_rates(lambda f, i: two_ref[f, i - 2], i, ny, at_plane(ends_two, i))
        for f in every:
            value = 1.0 / 3.0 * start(f, i)[:ny] + 2.0 / 3.0 * (centre[f] + DT_STEP * rate[f])
            flow_ref[f, i - DEPTH] = value

    points = sample_ref.shape[1]
    spot = jnp.broadcast_to(sample_ref[...], (nz, points))
    place = lax.broadcasted_iota(jnp.int32, (nx * ny, points), 0)
    in_row = (place == jnp.broadcast_to(sample_ref[...] // nz, (nx * ny, points))).astype(jnp.bfloat16)
    in_lane = lax.broadcasted_iota(jnp.int32, (nz, points), 0) == spot % nz
    product = jnp.zeros((modes + 1, points), jnp.float32)
    for c in range(3):
        field = flow_ref[c].reshape(nx * ny, nz).T
        found = sum(dot_parts(part, in_row, ((1,), (0,))) for part in three_parts(field))
        picked = jnp.sum(jnp.where(in_lane, found, 0.0), axis=0, keepdims=True)
        snap_ref[c] = picked
        product = product + jnp.concatenate([basis_ref[c], picked], axis=0) * picked
    total = jnp.sum(product, axis=1, keepdims=True)
    size = modes + 1
    diagonal = lax.broadcasted_iota(jnp.int32, (size, size), 0) == lax.broadcasted_iota(jnp.int32, (size, size), 1)
    cross_ref[...] = jnp.sum(jnp.where(diagonal, total, 0.0), axis=0, keepdims=True)


def merge_kernel(parts_ref, cross_ref, send_ref):
    total = parts_ref[0]
    for d in range(1, parts_ref.shape[0]):
        total = total + parts_ref[d]
    block = jnp.concatenate([total[: total.shape[0] - 1], cross_ref[...]], axis=0)
    for d in range(send_ref.shape[0]):
        send_ref[d] = block


def final_kernel(
    count, got_ref, parts_ref, snap_ref, flow_ref,
    basis_hbm, factor_hbm, flow_hbm,
    packed_ref, work_ref, basis_out_ref, factor_ref, sems,
):
    _, comps, size, points = parts_ref.shape
    tall = size // 4
    per = got_ref.shape[1] - 1
    copies = [pltpu.make_async_copy(flow_ref, flow_hbm, sems.at[0])]
    copies[0].start()

    total = jnp.zeros((per + 1, size), jnp.float32)
    for d in range(got_ref.shape[0]):
        block = got_ref[d]
        if per * d < packed_ref.shape[0]:
            packed_ref[per * d : per * d + per] = block[0:per]
        total = total + block
    cross = total[per : per + 1] / count
    top = lax.broadcasted_iota(jnp.int32, (16, size), 0)
    mark = (lax.broadcasted_iota(jnp.int32, (16, size), 1) == size - 1) & (top < 3)
    thirds = jnp.zeros((16, size), jnp.float32)
    for k, part in enumerate(three_parts(cross)):
        thirds = jnp.where(top == k, part.astype(jnp.float32), thirds)
    side = dot_parts(thirds.astype(jnp.bfloat16), mark.astype(jnp.bfloat16), ((0,), (0,)))
    lane = lax.broadcasted_iota(jnp.int32, (tall, size), 1)
    row = lax.broadcasted_iota(jnp.int32, (tall, size), 0)
    old = unpack_upper([packed_ref[tall * k : tall * k + tall] / count for k in range(3)], tall)
    for k in range(4):
        value = jnp.where(lane == size - 1, side[tall * k : tall * k + tall], old[k])
        if k == 3:
            value = jnp.where(row == tall - 1, jnp.broadcast_to(cross, value.shape), value)
        work_ref[tall * k : tall * k + tall, 0:size] = value
        work_ref[tall * k : tall * k + tall, size : 2 * size] = (lane == row + tall * k).astype(jnp.float32)

    for k in range(4):
        base = tall * k
        eliminate(work_ref, base, tall)
        done = work_ref[base : base + tall, :]
        if k < 3:
            change = dot_stacked(done[:, 0:size], done)
            work_ref[base + tall : size, :] = work_ref[base + tall : size, :] - change[base + tall : size]
        factor_ref[base : base + tall, :] = jnp.where(lane >= row + base, done[:, 0:size], 0.0)
        if k < 2:
            continue
        begin, count_rows = (0, base + tall) if k == 2 else (base, tall)
        inverse = work_ref[begin : base + tall, size : 2 * size]
        pieces = jnp.concatenate(three_parts(inverse), axis=0)
        for c in range(comps):
            value = jnp.zeros((count_rows, points), jnp.float32)
            for n in (2, 1, 0):
                products = dot_parts(pieces[: count_rows * (3 - n)], parts_ref[n, c], ((1,), (0,)))
                for m in range(2 - n, -1, -1):
                    value = value + products[count_rows * m : count_rows * m + count_rows]
            if k == 3:
                value = value + inverse[:, size - 1 : size] * snap_ref[c]
            basis_out_ref[c, begin : base + tall, :] = value
        rows = (slice(None), pl.ds(begin, count_rows), slice(None))
        copies.append(pltpu.make_async_copy(basis_out_ref.at[rows], basis_hbm.at[rows], sems.at[k]))
        copies[-1].start()
    copies.append(pltpu.make_async_copy(factor_ref, factor_hbm, sems.at[1]))
    copies[-1].start()
    for copy in copies:
        copy.wait()


def eliminate(work_ref, base, tall):
    blocks = tall // 8
    sub = lax.broadcasted_iota(jnp.int32, (8, 128), 0)
    panel = [work_ref[base + 8 * b : base + 8 * b + 8, :] for b in range(blocks)]
    scale = [jnp.zeros((8, 128), jnp.float32) for _ in range(blocks)]
    half = tall // 2
    for low in (0, half):
        high = low + half
        column = {
            k: {b: jnp.broadcast_to(panel[b][:, base + k : base + k + 1], (8, 128)) for b in range(k // 8, blocks)}
            for k in range(low, high)
        }
        for j in range(low, high):
            mine, at = divmod(j, 8)
            pivot = column[j][mine][at : at + 1, :]
            inverse = 1.0 / pivot
            scaled = {b: column[j][b] * inverse for b in range(mine, blocks)}
            for k in range(j + 1, high):
                other, place = divmod(k, 8)
                times = scaled[other][place : place + 1, :]
                for b in range(other, blocks):
                    column[k][b] = column[k][b] - column[j][b] * times
            scale[mine] = jnp.where(sub == at, lax.rsqrt(pivot), scale[mine])
            pivot_row = panel[mine][at : at + 1, :]
            for b in range(mine, blocks):
                times = jnp.where(sub > at, scaled[b], 0.0) if b == mine else scaled[b]
                panel[b] = panel[b] - jnp.concatenate([times, times], axis=1) * pivot_row
    for b in range(blocks):
        work_ref[base + 8 * b : base + 8 * b + 8, :] = panel[b] * jnp.concatenate([scale[b], scale[b]], axis=1)


def local(flow, basis, sample):
    fields, nx, ny, nz = flow.shape
    modes, comps, points = basis.shape
    size = modes + 1
    devices = lax.axis_size("gx") * lax.axis_size("gy") * lax.axis_size("gz")
    count = float(comps * points * devices)
    shape = functools.partial(jax.ShapeDtypeStruct, dtype=jnp.float32)
    call = functools.partial(pl.pallas_call, compiler_params=PARAMS)
    bricks = jnp.transpose(basis, (1, 0, 2))

    whole = pl.BlockSpec(memory_space=pltpu.HBM)
    flat = flow.reshape(fields, nx * ny, nz)
    quarter = size // 4
    per = -(-3 * quarter // devices)

    place = lax.axis_index("gy")
    flags = [place == 0, place == lax.axis_size("gy") - 1, place % 2 == 1]
    flags = jnp.broadcast_to(jnp.stack(flags).astype(jnp.int32)[:, None], (len(flags), nz))
    strip = shape((fields, nx * DEPTH, nz))
    strips = call(
        functools.partial(strips_kernel, nx), out_shape=(strip, strip), in_specs=[VMEM] * 2, out_specs=(VMEM, VMEM)
    )(flags, flat)
    y_even, y_odd = pairs(*strips, "gy")
    gram, basis_parts = call(
        gram_kernel,
        out_shape=(shape((devices, per + 1, size)), jax.ShapeDtypeStruct((3, comps, size, points), jnp.bfloat16)),
        in_specs=[VMEM],
        out_specs=(VMEM, VMEM),
        scratch_shapes=[pltpu.VMEM((size, size), jnp.float32), pltpu.VMEM((devices * per, size), jnp.float32)],
    )(bricks)
    y_odd, y_even, gram = lax.optimization_barrier((y_odd, y_even, gram))

    rows = ny + HALO
    face = shape((fields, DEPTH * ny + HALO, nz))
    mid, first, last = call(
        functools.partial(walls_kernel, nx),
        out_shape=(shape((fields, nx * rows, nz)), face, face),
        in_specs=[VMEM] * 4,
        out_specs=(VMEM,) * 3,
    )(flags, flat, y_odd, y_even)
    mid = mid.reshape(fields, nx, rows, nz)
    low_face, high_face = neighbours(first, last, "gx")
    parts = lax.all_to_all(gram, ALL, 0, 0)

    beside = shape((fields, DEPTH, rows, nz))
    packed, xlo, xhi = call(
        pack_kernel,
        out_shape=(shape((fields, rows, nz)), beside, beside),
        in_specs=[VMEM] * 3,
        out_specs=(VMEM,) * 3,
    )(mid, low_face, high_face)
    if lax.axis_size("gz") == 2:
        low = high = lax.ppermute(packed, "gz", [(0, 1), (1, 0)])
    else:
        low, high = neighbours(packed, packed, "gz")
    begun, cells = call(
        first_kernel,
        out_shape=(
            shape((fields, nx + 2 * DEPTH - 2, rows, nz)),
            jax.ShapeDtypeStruct((1, points), sample.dtype),
        ),
        in_specs=[VMEM, whole] + [VMEM] * 3,
        out_specs=(VMEM, VMEM),
        scratch_shapes=[pltpu.SemaphoreType.DMA],
    )(flags, sample.reshape(1, points), mid, xlo, xhi)
    flow_new, snapshot, cross = call(
        step_kernel,
        out_shape=(shape(flow.shape), shape((comps, 1, points)), shape((1, size))),
        in_specs=[VMEM] * 10,
        out_specs=(VMEM, VMEM, VMEM),
        scratch_shapes=[
            pltpu.VMEM((fields, nx + 2 * DEPTH - 2, rows, nz), jnp.float32),
            pltpu.VMEM((fields, nx + 2 * DEPTH - 4, rows, nz), jnp.float32),
        ],
    )(flags, mid, xlo, xhi, begun, packed, low, high, bricks, cells)

    send = call(
        merge_kernel, out_shape=shape((devices, per + 1, size)), in_specs=[VMEM] * 2, out_specs=VMEM
    )(parts, cross)
    got = lax.all_to_all(send, ALL, 0, 0)
    basis_next, factor, flow_next = call(
        functools.partial(final_kernel, count),
        out_shape=(shape((comps, size, points)), shape((size, size)), shape(flow.shape)),
        in_specs=[VMEM] * 4,
        out_specs=(whole,) * 3,
        scratch_shapes=[
            pltpu.VMEM((3 * quarter, size), jnp.float32),
            pltpu.VMEM((size, 2 * size), jnp.float32),
            pltpu.VMEM((comps, size, points), jnp.float32),
            pltpu.VMEM((size, size), jnp.float32),
            pltpu.SemaphoreType.DMA((4,)),
        ],
    )(got, basis_parts, snapshot, flow_new)
    return flow_next, jnp.transpose(basis_next, (1, 0, 2)), factor


def solution(mesh):
    return jax.shard_map(
        local,
        mesh=mesh,
        in_specs=(
            P(None, "gx", "gy", "gz"),
            P(None, None, ("gx", "gy", "gz")),
            P(("gx", "gy", "gz")),
        ),
        out_specs=(P(None, "gx", "gy", "gz"), P(None, None, ("gx", "gy", "gz")), P()),
        check_vma=False,
    )
```

```python
import functools

import jax
import jax.numpy as jnp
from jax import lax
from jax.experimental import pallas as pl
from jax.experimental.pallas import tpu as pltpu
from jax.sharding import PartitionSpec as P

DT_STEP = 0.35
VISCOSITY = 0.2
SOUND_SQ = 1.0
DRIVING = 0.5

ALL = ("gz", "gy", "gx")
DEPTH = 3
EXACT = lax.Precision.HIGHEST
VMEM = pl.BlockSpec(memory_space=pltpu.VMEM)
PARAMS = pltpu.CompilerParams(vmem_limit_bytes=40 * 1024 * 1024)


def dot(a, b, dims):
    return lax.dot_general(
        a, b, (dims, ((), ())), precision=EXACT, preferred_element_type=jnp.float32
    )


def three_parts(value):
    high = value.astype(jnp.bfloat16)
    rest = value - high.astype(jnp.float32)
    middle = rest.astype(jnp.bfloat16)
    return high, middle, (rest - middle.astype(jnp.float32)).astype(jnp.bfloat16)


def dot_parts(a, b, dims):
    return lax.dot_general(a, b, (dims, ((), ())), preferred_element_type=jnp.float32)


def dot_stacked(a, b):
    (a1, a2, a3), (b1, b2, b3) = three_parts(a), three_parts(b)
    first = jnp.concatenate([a1, a1, a2, a2, a1, a3], axis=0)
    second = jnp.concatenate([b1, b2, b1, b2, b3, b1], axis=0)
    return dot_parts(first, second, ((0,), (0,)))


def neighbours(block_low, block_high, axis):
    count = lax.axis_size(axis)
    forward = [(i, (i + 1) % count) for i in range(count)]
    backward = [(target, source) for source, target in forward]
    return lax.ppermute(block_high, axis, forward), lax.ppermute(block_low, axis, backward)


def pairs(block_odd, block_even, axis):
    count = lax.axis_size(axis)
    even = [(i, i + 1 - 2 * (i % 2)) for i in range(count)]
    odd = [(i, (i - 1 + 2 * (i % 2)) % count) for i in range(count)]
    from_odd = lax.ppermute(block_odd, axis, odd)
    return lax.ppermute(block_even, axis, even), from_odd


LOWER_WALL, UPPER_WALL, ODD_Y = range(3)


def flag(flags_ref, which):
    return flags_ref[which : which + 1] == 1


def pack_upper(rows, tall):
    size = rows.shape[1]
    lane = lax.broadcasted_iota(jnp.int32, (tall, size), 1)
    part = [rows[tall * k : tall * k + tall] for k in range(4)]
    return [part[0], jnp.where(lane >= tall, part[1], pltpu.roll(part[3], tall, 1)), part[2]]


def unpack_upper(packed, tall):
    return [packed[0], packed[1], packed[2], pltpu.roll(packed[1], packed[1].shape[1] - tall, 1)]


def gram_kernel(basis_ref, send_ref, parts_ref, gram_ref, packed_ref):
    modes = basis_ref.shape[1]
    tall = gram_ref.shape[0] // 4
    total = jnp.zeros((modes, modes), jnp.float32)
    for c in range(basis_ref.shape[0]):
        rows = basis_ref[c]
        total = total + dot(rows, rows, ((1,), (1,)))
        filled = jnp.concatenate([rows, jnp.zeros((1, rows.shape[1]), jnp.float32)], axis=0)
        for k, part in enumerate(three_parts(filled)):
            parts_ref[k, c] = part
    gram_ref[...] = jnp.zeros_like(gram_ref)
    gram_ref[0:modes, 0:modes] = total
    packed_ref[...] = jnp.zeros_like(packed_ref)
    for k, value in enumerate(pack_upper(gram_ref[...], tall)):
        packed_ref[tall * k : tall * k + tall] = value
    per = send_ref.shape[1] - 1
    empty = jnp.zeros((1, send_ref.shape[2]), jnp.float32)
    for d in range(send_ref.shape[0]):
        send_ref[d] = jnp.concatenate([packed_ref[per * d : per * d + per], empty], axis=0)


GAP = 2
HALO = 2 * DEPTH + GAP


def strips_kernel(planes, flags_ref, flow_ref, odd_ref, even_ref):
    ny = flow_ref.shape[1] // planes
    odd = flag(flags_ref, ODD_Y)
    for f in range(flow_ref.shape[0]):
        for j in range(DEPTH):
            bottom = flow_ref[f, pl.ds(j, planes, stride=ny), :]
            top = flow_ref[f, pl.ds(ny - DEPTH + j, planes, stride=ny), :]
            even_ref[f, planes * j : planes * j + planes] = jnp.where(odd, bottom, top)
            odd_ref[f, planes * j : planes * j + planes] = jnp.where(odd, top, bottom)


def walls_kernel(planes, flags_ref, flow_ref, odd_ref, even_ref, mid_ref, first_ref, last_ref):
    fields, cells, nz = flow_ref.shape
    odd_y = flag(flags_ref, ODD_Y)
    ny = cells // planes
    rows = ny + HALO
    sub = lax.broadcasted_iota(jnp.int32, (HALO, nz), 0)
    empty = jnp.zeros((planes, nz), jnp.float32)
    for f in range(fields):
        for i in range(planes):
            mid_ref[f, rows * i : rows * i + ny] = flow_ref[f, ny * i : ny * i + ny]
        for j in range(HALO):
            k = j if j < DEPTH else j - DEPTH - GAP
            part = slice(planes * k, planes * k + planes)
            if j < DEPTH:
                value = jnp.where(odd_y, odd_ref[f, part], even_ref[f, part])
                value = jnp.where(flag(flags_ref, UPPER_WALL), 0.0, value)
            elif j < DEPTH + GAP:
                value = empty
            else:
                value = jnp.where(odd_y, even_ref[f, part], odd_ref[f, part])
                value = jnp.where(flag(flags_ref, LOWER_WALL), 0.0, value)
            mid_ref[f, pl.ds(ny + j, planes, stride=rows), :] = value
        for face_ref, begin, near, next_one in (
            (first_ref, 0, 0, 1), (last_ref, planes - DEPTH, planes - 1, planes - 2)
        ):
            for k in range(DEPTH):
                face_ref[f, ny * k : ny * k + ny] = flow_ref[f, ny * (begin + k) : ny * (begin + k) + ny]
            halos = [mid_ref[f, rows * i + ny : rows * i + rows] for i in (near, next_one)]
            face_ref[f, ny * DEPTH : ny * DEPTH + HALO] = corner_rows(*halos, sub)


def corner_rows(near, next_one, sub):
    tile = jnp.where(sub == 2, pltpu.roll(next_one, 2, 0), pltpu.roll(next_one, 6, 0))
    tile = jnp.where((sub == 2) | (sub == 5), tile, 0.0)
    return jnp.where((sub < 2) | (sub >= 6), near, tile)


def corner_planes(tile, sub):
    near = jnp.where((sub < 2) | (sub >= 6), tile, 0.0)
    next_one = jnp.where(sub == 0, pltpu.roll(tile, 6, 0), pltpu.roll(tile, 2, 0))
    return [near, jnp.where((sub == 0) | (sub == 7), next_one, 0.0), jnp.zeros_like(tile)]


def plane_of(mid_ref, xlo_ref, xhi_ref, f, i):
    nx = mid_ref.shape[1]
    if i < DEPTH:
        return xlo_ref[f, i]
    if i < DEPTH + nx:
        return mid_ref[f, i - DEPTH]
    return xhi_ref[f, i - DEPTH - nx]


GROUP = 8


def pack_kernel(mid_ref, low_ref, high_ref, packed_ref, xlo_ref, xhi_ref):
    fields, nx, rows, nz = mid_ref.shape
    ny = rows - HALO
    lane = lax.broadcasted_iota(jnp.int32, (rows, nz), 1)
    sub = lax.broadcasted_iota(jnp.int32, (HALO, nz), 0)
    for f in range(fields):
        for face_ref, out_ref, order in ((low_ref, xlo_ref, (2, 1, 0)), (high_ref, xhi_ref, (0, 1, 2))):
            face = face_ref[f]
            halo = corner_planes(face[ny * DEPTH :], sub)
            for k in range(DEPTH):
                out_ref[f, k, 0:ny] = face[ny * k : ny * k + ny]
                out_ref[f, k, ny:rows] = halo[order[k]]
        value = jnp.zeros((rows, nz), jnp.float32)
        for i in range(nx + 2 * DEPTH):
            start = GROUP * i
            moved = pltpu.roll(plane_of(mid_ref, xlo_ref, xhi_ref, f, i), (start + DEPTH) % nz, 1)
            value = jnp.where((lane >= start) & (lane < start + 2 * DEPTH), moved, value)
        packed_ref[f] = value


def step(value, by, axis):
    size = value.shape[axis]
    return pltpu.roll(value, (size - by) % size, axis)


def rates(centre, x_plus, x_minus, y_plus, y_minus, z_plus, z_minus):
    slope_x = [0.5 * (a - b) for a, b in zip(x_plus, x_minus)]
    slope_y = [0.5 * (a - b) for a, b in zip(y_plus, y_minus)]
    slope_z = [0.5 * (a - b) for a, b in zip(z_plus, z_minus)]
    pressure = [slope_x[3], slope_y[3], slope_z[3]]
    out = []
    for f in range(3):
        laplace = (
            x_plus[f] + x_minus[f] + (y_plus[f] + y_minus[f]) + (z_plus[f] + z_minus[f]) - 6.0 * centre[f]
        )
        advect = centre[0] * slope_x[f] + centre[1] * slope_y[f] + centre[2] * slope_z[f]
        value = VISCOSITY * laplace - advect - pressure[f]
        if f == 0:
            value = value + DRIVING
        out.append(value)
    out.append(-SOUND_SQ * (slope_x[0] + slope_y[1] + slope_z[2]))
    return out


def beyond_walls(flags_ref, ny, shape):
    row = lax.broadcasted_iota(jnp.int32, shape, 0)
    below = (row >= ny + DEPTH + GAP) & flag(flags_ref, LOWER_WALL)
    above = (row >= ny) & (row < ny + DEPTH) & flag(flags_ref, UPPER_WALL)
    return below | above


def plane_rates(read, i, rows, ends=None):
    every = range(4)
    centre = [read(f, i) for f in every]
    x_plus = [read(f, i + 1)[:rows] for f in every]
    x_minus = [read(f, i - 1)[:rows] for f in every]
    y_plus = [step(v, 1, 0)[:rows] for v in centre]
    y_minus = [step(v, -1, 0)[:rows] for v in centre]
    centre = [v[:rows] for v in centre]
    upward, downward = centre, centre
    if ends is not None:
        lane = lax.broadcasted_iota(jnp.int32, centre[0].shape, 1)
        upward = [jnp.where(lane == 0, e[:rows], v) for e, v in zip(ends, centre)]
        downward = [jnp.where(lane == lane.shape[1] - 1, e[:rows], v) for e, v in zip(ends, centre)]
    z_plus = [step(v, 1, 1) for v in upward]
    z_minus = [step(v, -1, 1) for v in downward]
    return centre, rates(centre, x_plus, x_minus, y_plus, y_minus, z_plus, z_minus)


def stage_one(outside, value, rate):
    return jnp.where(outside, 0.0, value + DT_STEP * rate)


def stage_two(outside, begin, value, rate):
    return jnp.where(outside, 0.0, 0.75 * begin + 0.25 * (value + DT_STEP * rate))


def first_kernel(flags_ref, sample_hbm, mid_ref, xlo_ref, xhi_ref, one_ref, sample_ref, sem):
    copy = pltpu.make_async_copy(sample_hbm, sample_ref, sem)
    copy.start()
    fields, nx, rows, nz = mid_ref.shape
    outside = beyond_walls(flags_ref, rows - HALO, (rows, nz))
    for i in range(1, nx + 2 * DEPTH - 1):
        centre, rate = plane_rates(functools.partial(plane_of, mid_ref, xlo_ref, xhi_ref), i, rows)
        for f in range(4):
            one_ref[f, i - 1] = stage_one(outside, centre[f], rate[f])
    copy.wait()


def step_kernel(
    flags_ref, mid_ref, xlo_ref, xhi_ref, first_ref, own_ref, low_ref, high_ref, basis_ref, sample_ref,
    flow_ref, snap_ref, cross_ref,
    one_ref, two_ref,
):
    fields, nx, ny, nz = flow_ref.shape
    rows = mid_ref.shape[2]
    modes = basis_ref.shape[1]
    planes = nx + 2 * DEPTH
    lane = lax.broadcasted_iota(jnp.int32, (rows, nz), 1)
    outside = beyond_walls(flags_ref, ny, (rows, nz))
    every = range(4)
    start = functools.partial(plane_of, mid_ref, xlo_ref, xhi_ref)

    left = lane % GROUP < DEPTH

    def window_rates(q):
        return rates(
            q, [step(v, GROUP, 1) for v in q], [step(v, -GROUP, 1) for v in q],
            [step(v, 1, 0) for v in q], [step(v, -1, 0) for v in q],
            [step(v, 1, 1) for v in q], [step(v, -1, 1) for v in q],
        )

    own = [own_ref[f] for f in every]
    other = [jnp.where(left, low_ref[f], high_ref[f]) for f in every]
    windows = []
    for parts in ((other, own), (own, other)):
        q0 = [jnp.where(left, a, b) for a, b in zip(*parts)]
        q1 = [stage_one(outside, v, r) for v, r in zip(q0, window_rates(q0))]
        q2 = [stage_two(outside, s, v, r) for s, v, r in zip(q0, q1, window_rates(q1))]
        windows.append((q1, q2))
    (low_one, low_two), (high_one, high_two) = windows
    ends_one = [jnp.where(left, a, b) for a, b in zip(low_one, high_one)]
    ends_two = [jnp.where(left, a, b) for a, b in zip(low_two, high_two)]
    rim_one = [jnp.where(left, b, a) for a, b in zip(low_one, high_one)]

    def at_plane(values, i):
        return [pltpu.roll(v, (2 * nz - GROUP * i - DEPTH) % nz, 1) for v in values]

    rim = (lane == 0) | (lane == nz - 1)
    for i in range(1, planes - 1):
        for f, value in enumerate(at_plane(rim_one, i)):
            one_ref[f, i - 1] = jnp.where(rim, value, first_ref[f, i - 1])
    for i in range(2, planes - 2):
        centre, rate = plane_rates(lambda f, i: one_ref[f, i - 1], i, rows, at_plane(ends_one, i))
        for f in every:
            two_ref[f, i - 2] = stage_two(outside, start(f, i), centre[f], rate[f])
    for i in range(3, planes - 3):
        centre, rate = plane_rates(lambda f, i: two_ref[f, i - 2], i, ny, at_plane(ends_two, i))
        for f in every:
            value = 1.0 / 3.0 * start(f, i)[:ny] + 2.0 / 3.0 * (centre[f] + DT_STEP * rate[f])
            flow_ref[f, i - DEPTH] = value

    points = sample_ref.shape[1]
    spot = jnp.broadcast_to(sample_ref[...], (nz, points))
    place = lax.broadcasted_iota(jnp.int32, (nx * ny, points), 0)
    in_row = (place == jnp.broadcast_to(sample_ref[...] // nz, (nx * ny, points))).astype(jnp.bfloat16)
    in_lane = lax.broadcasted_iota(jnp.int32, (nz, points), 0) == spot % nz
    product = jnp.zeros((modes + 1, points), jnp.float32)
    for c in range(3):
        field = flow_ref[c].reshape(nx * ny, nz).T
        found = sum(dot_parts(part, in_row, ((1,), (0,))) for part in three_parts(field))
        picked = jnp.sum(jnp.where(in_lane, found, 0.0), axis=0, keepdims=True)
        snap_ref[c] = picked
        product = product + jnp.concatenate([basis_ref[c], picked], axis=0) * picked
    total = jnp.sum(product, axis=1, keepdims=True)
    size = modes + 1
    diagonal = lax.broadcasted_iota(jnp.int32, (size, size), 0) == lax.broadcasted_iota(jnp.int32, (size, size), 1)
    cross_ref[...] = jnp.sum(jnp.where(diagonal, total, 0.0), axis=0, keepdims=True)


def merge_kernel(parts_ref, cross_ref, send_ref):
    total = parts_ref[0]
    for d in range(1, parts_ref.shape[0]):
        total = total + parts_ref[d]
    block = jnp.concatenate([total[: total.shape[0] - 1], cross_ref[...]], axis=0)
    for d in range(send_ref.shape[0]):
        send_ref[d] = block


def final_kernel(
    count, got_ref, parts_ref, snap_ref, flow_ref,
    basis_hbm, factor_hbm, flow_hbm,
    packed_ref, work_ref, basis_out_ref, factor_ref, sems,
):
    _, comps, size, points = parts_ref.shape
    tall = size // 4
    per = got_ref.shape[1] - 1
    copies = [pltpu.make_async_copy(flow_ref, flow_hbm, sems.at[0])]
    copies[0].start()

    total = jnp.zeros((per + 1, size), jnp.float32)
    for d in range(got_ref.shape[0]):
        block = got_ref[d]
        if per * d < packed_ref.shape[0]:
            packed_ref[per * d : per * d + per] = block[0:per]
        total = total + block
    cross = total[per : per + 1] / count
    top = lax.broadcasted_iota(jnp.int32, (16, size), 0)
    mark = (lax.broadcasted_iota(jnp.int32, (16, size), 1) == size - 1) & (top < 3)
    thirds = jnp.zeros((16, size), jnp.float32)
    for k, part in enumerate(three_parts(cross)):
        thirds = jnp.where(top == k, part.astype(jnp.float32), thirds)
    side = dot_parts(thirds.astype(jnp.bfloat16), mark.astype(jnp.bfloat16), ((0,), (0,)))
    lane = lax.broadcasted_iota(jnp.int32, (tall, size), 1)
    row = lax.broadcasted_iota(jnp.int32, (tall, size), 0)
    old = unpack_upper([packed_ref[tall * k : tall * k + tall] / count for k in range(3)], tall)
    for k in range(4):
        value = jnp.where(lane == size - 1, side[tall * k : tall * k + tall], old[k])
        if k == 3:
            value = jnp.where(row == tall - 1, jnp.broadcast_to(cross, value.shape), value)
        work_ref[tall * k : tall * k + tall, 0:size] = value
        work_ref[tall * k : tall * k + tall, size : 2 * size] = (lane == row + tall * k).astype(jnp.float32)

    for k in range(4):
        base = tall * k
        eliminate(work_ref, base, tall, old[0] if k == 0 else None)
        done = work_ref[base : base + tall, :]
        if k < 3:
            change = dot_stacked(done[:, 0:size], done)
            work_ref[base + tall : size, :] = work_ref[base + tall : size, :] - change[base + tall : size]
        factor_ref[base : base + tall, :] = jnp.where(lane >= row + base, done[:, 0:size], 0.0)
        if k < 2:
            continue
        begin, count_rows = (0, base + tall) if k == 2 else (base, tall)
        inverse = work_ref[begin : base + tall, size : 2 * size]
        pieces = jnp.concatenate(three_parts(inverse), axis=0)
        for c in range(comps):
            value = jnp.zeros((count_rows, points), jnp.float32)
            for n in (2, 1, 0):
                products = dot_parts(pieces[: count_rows * (3 - n)], parts_ref[n, c], ((1,), (0,)))
                for m in range(2 - n, -1, -1):
                    value = value + products[count_rows * m : count_rows * m + count_rows]
            if k == 3:
                value = value + inverse[:, size - 1 : size] * snap_ref[c]
            basis_out_ref[c, begin : base + tall, :] = value
        rows = (slice(None), pl.ds(begin, count_rows), slice(None))
        copies.append(pltpu.make_async_copy(basis_out_ref.at[rows], basis_hbm.at[rows], sems.at[k]))
        copies[-1].start()
    copies.append(pltpu.make_async_copy(factor_ref, factor_hbm, sems.at[1]))
    copies[-1].start()
    for copy in copies:
        copy.wait()


def eliminate(work_ref, base, tall, early=None):
    blocks = tall // 8
    sub = lax.broadcasted_iota(jnp.int32, (8, 128), 0)
    panel = [work_ref[base + 8 * b : base + 8 * b + 8, :] for b in range(blocks)]
    scale = [jnp.zeros((8, 128), jnp.float32) for _ in range(blocks)]
    half = tall // 2
    for low in (0, half):
        high = low + half
        rows = panel if early is None or low else [early[8 * b : 8 * b + 8] for b in range(blocks)]
        column = {
            k: {b: jnp.broadcast_to(rows[b][:, base + k : base + k + 1], (8, 128)) for b in range(k // 8, blocks)}
            for k in range(low, high)
        }
        for j in range(low, high):
            mine, at = divmod(j, 8)
            pivot = column[j][mine][at : at + 1, :]
            inverse = 1.0 / pivot
            scaled = {b: column[j][b] * inverse for b in range(mine, blocks)}
            for k in range(j + 1, high):
                other, place = divmod(k, 8)
                times = scaled[other][place : place + 1, :]
                for b in range(other, blocks):
                    column[k][b] = column[k][b] - column[j][b] * times
            scale[mine] = jnp.where(sub == at, lax.rsqrt(pivot), scale[mine])
            pivot_row = panel[mine][at : at + 1, :]
            for b in range(mine, blocks):
                times = jnp.where(sub > at, scaled[b], 0.0) if b == mine else scaled[b]
                panel[b] = panel[b] - jnp.concatenate([times, times], axis=1) * pivot_row
    for b in range(blocks):
        work_ref[base + 8 * b : base + 8 * b + 8, :] = panel[b] * jnp.concatenate([scale[b], scale[b]], axis=1)


def local(flow, basis, sample):
    fields, nx, ny, nz = flow.shape
    modes, comps, points = basis.shape
    size = modes + 1
    devices = lax.axis_size("gx") * lax.axis_size("gy") * lax.axis_size("gz")
    count = float(comps * points * devices)
    shape = functools.partial(jax.ShapeDtypeStruct, dtype=jnp.float32)
    call = functools.partial(pl.pallas_call, compiler_params=PARAMS)
    bricks = jnp.transpose(basis, (1, 0, 2))

    whole = pl.BlockSpec(memory_space=pltpu.HBM)
    flat = flow.reshape(fields, nx * ny, nz)
    quarter = size // 4
    per = -(-3 * quarter // devices)

    place = lax.axis_index("gy")
    flags = [place == 0, place == lax.axis_size("gy") - 1, place % 2 == 1]
    flags = jnp.broadcast_to(jnp.stack(flags).astype(jnp.int32)[:, None], (len(flags), nz))
    strip = shape((fields, nx * DEPTH, nz))
    strips = call(
        functools.partial(strips_kernel, nx), out_shape=(strip, strip), in_specs=[VMEM] * 2, out_specs=(VMEM, VMEM)
    )(flags, flat)
    y_even, y_odd = pairs(*strips, "gy")
    gram, basis_parts = call(
        gram_kernel,
        out_shape=(shape((devices, per + 1, size)), jax.ShapeDtypeStruct((3, comps, size, points), jnp.bfloat16)),
        in_specs=[VMEM],
        out_specs=(VMEM, VMEM),
        scratch_shapes=[pltpu.VMEM((size, size), jnp.float32), pltpu.VMEM((devices * per, size), jnp.float32)],
    )(bricks)
    y_odd, y_even, gram = lax.optimization_barrier((y_odd, y_even, gram))

    rows = ny + HALO
    face = shape((fields, DEPTH * ny + HALO, nz))
    mid, first, last = call(
        functools.partial(walls_kernel, nx),
        out_shape=(shape((fields, nx * rows, nz)), face, face),
        in_specs=[VMEM] * 4,
        out_specs=(VMEM,) * 3,
    )(flags, flat, y_odd, y_even)
    mid = mid.reshape(fields, nx, rows, nz)
    low_face, high_face = neighbours(first, last, "gx")
    parts = lax.all_to_all(gram, ALL, 0, 0)

    beside = shape((fields, DEPTH, rows, nz))
    packed, xlo, xhi = call(
        pack_kernel,
        out_shape=(shape((fields, rows, nz)), beside, beside),
        in_specs=[VMEM] * 3,
        out_specs=(VMEM,) * 3,
    )(mid, low_face, high_face)
    if lax.axis_size("gz") == 2:
        low = high = lax.ppermute(packed, "gz", [(0, 1), (1, 0)])
    else:
        low, high = neighbours(packed, packed, "gz")
    begun, cells = call(
        first_kernel,
        out_shape=(
            shape((fields, nx + 2 * DEPTH - 2, rows, nz)),
            jax.ShapeDtypeStruct((1, points), sample.dtype),
        ),
        in_specs=[VMEM, whole] + [VMEM] * 3,
        out_specs=(VMEM, VMEM),
        scratch_shapes=[pltpu.SemaphoreType.DMA],
    )(flags, sample.reshape(1, points), mid, xlo, xhi)
    flow_new, snapshot, cross = call(
        step_kernel,
        out_shape=(shape(flow.shape), shape((comps, 1, points)), shape((1, size))),
        in_specs=[VMEM] * 10,
        out_specs=(VMEM, VMEM, VMEM),
        scratch_shapes=[
            pltpu.VMEM((fields, nx + 2 * DEPTH - 2, rows, nz), jnp.float32),
            pltpu.VMEM((fields, nx + 2 * DEPTH - 4, rows, nz), jnp.float32),
        ],
    )(flags, mid, xlo, xhi, begun, packed, low, high, bricks, cells)

    send = call(
        merge_kernel, out_shape=shape((devices, per + 1, size)), in_specs=[VMEM] * 2, out_specs=VMEM
    )(parts, cross)
    got = lax.all_to_all(send, ALL, 0, 0)
    basis_next, factor, flow_next = call(
        functools.partial(final_kernel, count),
        out_shape=(shape((comps, size, points)), shape((size, size)), shape(flow.shape)),
        in_specs=[VMEM] * 4,
        out_specs=(whole,) * 3,
        scratch_shapes=[
            pltpu.VMEM((3 * quarter, size), jnp.float32),
            pltpu.VMEM((size, 2 * size), jnp.float32),
            pltpu.VMEM((comps, size, points), jnp.float32),
            pltpu.VMEM((size, size), jnp.float32),
            pltpu.SemaphoreType.DMA((4,)),
        ],
    )(got, basis_parts, snapshot, flow_new)
    return flow_next, jnp.transpose(basis_next, (1, 0, 2)), factor


def solution(mesh):
    return jax.shard_map(
        local,
        mesh=mesh,
        in_specs=(
            P(None, "gx", "gy", "gz"),
            P(None, None, ("gx", "gy", "gz")),
            P(("gx", "gy", "gz")),
        ),
        out_specs=(P(None, "gx", "gy", "gz"), P(None, None, ("gx", "gy", "gz")), P()),
        check_vma=False,
    )
```

```python
import functools

import jax
import jax.numpy as jnp
from jax import lax
from jax.experimental import pallas as pl
from jax.experimental.pallas import tpu as pltpu
from jax.sharding import PartitionSpec as P

DT_STEP = 0.35
VISCOSITY = 0.2
SOUND_SQ = 1.0
DRIVING = 0.5

ALL = ("gz", "gy", "gx")
DEPTH = 3
EXACT = lax.Precision.HIGHEST
VMEM = pl.BlockSpec(memory_space=pltpu.VMEM)
PARAMS = pltpu.CompilerParams(vmem_limit_bytes=40 * 1024 * 1024)


def dot(a, b, dims):
    return lax.dot_general(
        a, b, (dims, ((), ())), precision=EXACT, preferred_element_type=jnp.float32
    )


def three_parts(value):
    high = value.astype(jnp.bfloat16)
    rest = value - high.astype(jnp.float32)
    middle = rest.astype(jnp.bfloat16)
    return high, middle, (rest - middle.astype(jnp.float32)).astype(jnp.bfloat16)


def dot_parts(a, b, dims):
    return lax.dot_general(a, b, (dims, ((), ())), preferred_element_type=jnp.float32)


def dot_stacked(a, b):
    (a1, a2, a3), (b1, b2, b3) = three_parts(a), three_parts(b)
    first = jnp.concatenate([a1, a1, a2, a2, a1, a3], axis=0)
    second = jnp.concatenate([b1, b2, b1, b2, b3, b1], axis=0)
    return dot_parts(first, second, ((0,), (0,)))


def neighbours(block_low, block_high, axis):
    count = lax.axis_size(axis)
    forward = [(i, (i + 1) % count) for i in range(count)]
    backward = [(target, source) for source, target in forward]
    return lax.ppermute(block_high, axis, forward), lax.ppermute(block_low, axis, backward)


def pairs(block_odd, block_even, axis, other):
    count, width = lax.axis_size(axis), lax.axis_size(other)
    even = [(i, i + 1 - 2 * (i % 2)) for i in range(count)]
    odd = []
    for i in range(count):
        for k in range(width):
            to = (i, k + 1 - 2 * (k % 2)) if i in (0, count - 1) else (i - 1 + 2 * (i % 2), k)
            odd.append((i * width + k, to[0] * width + to[1]))
    from_odd = lax.ppermute(block_odd, (axis, other), odd)
    return lax.ppermute(block_even, axis, even), from_odd


LOWER_WALL, UPPER_WALL, ODD_Y = range(3)


def flag(flags_ref, which):
    return flags_ref[which : which + 1] == 1


def pack_upper(rows, tall):
    size = rows.shape[1]
    lane = lax.broadcasted_iota(jnp.int32, (tall, size), 1)
    part = [rows[tall * k : tall * k + tall] for k in range(4)]
    return [part[0], jnp.where(lane >= tall, part[1], pltpu.roll(part[3], tall, 1)), part[2]]


def unpack_upper(packed, tall):
    return [packed[0], packed[1], packed[2], pltpu.roll(packed[1], packed[1].shape[1] - tall, 1)]


def gram_kernel(basis_ref, send_ref, parts_ref, gram_ref, packed_ref):
    modes = basis_ref.shape[1]
    tall = gram_ref.shape[0] // 4
    total = jnp.zeros((modes, modes), jnp.float32)
    for c in range(basis_ref.shape[0]):
        rows = basis_ref[c]
        total = total + dot(rows, rows, ((1,), (1,)))
        filled = jnp.concatenate([rows, jnp.zeros((1, rows.shape[1]), jnp.float32)], axis=0)
        for k, part in enumerate(three_parts(filled)):
            parts_ref[k, c] = part
    gram_ref[...] = jnp.zeros_like(gram_ref)
    gram_ref[0:modes, 0:modes] = total
    packed_ref[...] = jnp.zeros_like(packed_ref)
    for k, value in enumerate(pack_upper(gram_ref[...], tall)):
        packed_ref[tall * k : tall * k + tall] = value
    per = send_ref.shape[1] - 1
    empty = jnp.zeros((1, send_ref.shape[2]), jnp.float32)
    for d in range(send_ref.shape[0]):
        send_ref[d] = jnp.concatenate([packed_ref[per * d : per * d + per], empty], axis=0)


GAP = 2
HALO = 2 * DEPTH + GAP


def strips_kernel(planes, flags_ref, flow_ref, odd_ref, even_ref):
    ny = flow_ref.shape[1] // planes
    odd = flag(flags_ref, ODD_Y)
    for f in range(flow_ref.shape[0]):
        for j in range(DEPTH):
            bottom = flow_ref[f, pl.ds(j, planes, stride=ny), :]
            top = flow_ref[f, pl.ds(ny - DEPTH + j, planes, stride=ny), :]
            even_ref[f, planes * j : planes * j + planes] = jnp.where(odd, bottom, top)
            odd_ref[f, planes * j : planes * j + planes] = jnp.where(odd, top, bottom)


def walls_kernel(planes, flags_ref, flow_ref, odd_ref, even_ref, mid_ref, first_ref, last_ref):
    fields, cells, nz = flow_ref.shape
    odd_y = flag(flags_ref, ODD_Y)
    ny = cells // planes
    rows = ny + HALO
    sub = lax.broadcasted_iota(jnp.int32, (HALO, nz), 0)
    empty = jnp.zeros((planes, nz), jnp.float32)
    for f in range(fields):
        for i in range(planes):
            mid_ref[f, rows * i : rows * i + ny] = flow_ref[f, ny * i : ny * i + ny]
        for j in range(HALO):
            k = j if j < DEPTH else j - DEPTH - GAP
            part = slice(planes * k, planes * k + planes)
            if j < DEPTH:
                value = jnp.where(odd_y, odd_ref[f, part], even_ref[f, part])
                value = jnp.where(flag(flags_ref, UPPER_WALL), 0.0, value)
            elif j < DEPTH + GAP:
                value = empty
            else:
                value = jnp.where(odd_y, even_ref[f, part], odd_ref[f, part])
                value = jnp.where(flag(flags_ref, LOWER_WALL), 0.0, value)
            mid_ref[f, pl.ds(ny + j, planes, stride=rows), :] = value
        for face_ref, begin, near, next_one in (
            (first_ref, 0, 0, 1), (last_ref, planes - DEPTH, planes - 1, planes - 2)
        ):
            for k in range(DEPTH):
                face_ref[f, ny * k : ny * k + ny] = flow_ref[f, ny * (begin + k) : ny * (begin + k) + ny]
            halos = [mid_ref[f, rows * i + ny : rows * i + rows] for i in (near, next_one)]
            face_ref[f, ny * DEPTH : ny * DEPTH + HALO] = corner_rows(*halos, sub)


def corner_rows(near, next_one, sub):
    tile = jnp.where(sub == 2, pltpu.roll(next_one, 2, 0), pltpu.roll(next_one, 6, 0))
    tile = jnp.where((sub == 2) | (sub == 5), tile, 0.0)
    return jnp.where((sub < 2) | (sub >= 6), near, tile)


def corner_planes(tile, sub):
    near = jnp.where((sub < 2) | (sub >= 6), tile, 0.0)
    next_one = jnp.where(sub == 0, pltpu.roll(tile, 6, 0), pltpu.roll(tile, 2, 0))
    return [near, jnp.where((sub == 0) | (sub == 7), next_one, 0.0), jnp.zeros_like(tile)]


def plane_of(mid_ref, xlo_ref, xhi_ref, f, i):
    nx = mid_ref.shape[1]
    if i < DEPTH:
        return xlo_ref[f, i]
    if i < DEPTH + nx:
        return mid_ref[f, i - DEPTH]
    return xhi_ref[f, i - DEPTH - nx]


GROUP = 8


def pack_kernel(mid_ref, low_ref, high_ref, packed_ref, xlo_ref, xhi_ref):
    fields, nx, rows, nz = mid_ref.shape
    ny = rows - HALO
    lane = lax.broadcasted_iota(jnp.int32, (rows, nz), 1)
    sub = lax.broadcasted_iota(jnp.int32, (HALO, nz), 0)
    for f in range(fields):
        for face_ref, out_ref, order in ((low_ref, xlo_ref, (2, 1, 0)), (high_ref, xhi_ref, (0, 1, 2))):
            face = face_ref[f]
            halo = corner_planes(face[ny * DEPTH :], sub)
            for k in range(DEPTH):
                out_ref[f, k, 0:ny] = face[ny * k : ny * k + ny]
                out_ref[f, k, ny:rows] = halo[order[k]]
        value = jnp.zeros((rows, nz), jnp.float32)
        for i in range(nx + 2 * DEPTH):
            start = GROUP * i
            moved = pltpu.roll(plane_of(mid_ref, xlo_ref, xhi_ref, f, i), (start + DEPTH) % nz, 1)
            value = jnp.where((lane >= start) & (lane < start + 2 * DEPTH), moved, value)
        packed_ref[f] = value


def step(value, by, axis):
    size = value.shape[axis]
    return pltpu.roll(value, (size - by) % size, axis)


def rates(centre, x_plus, x_minus, y_plus, y_minus, z_plus, z_minus):
    slope_x = [0.5 * (a - b) for a, b in zip(x_plus, x_minus)]
    slope_y = [0.5 * (a - b) for a, b in zip(y_plus, y_minus)]
    slope_z = [0.5 * (a - b) for a, b in zip(z_plus, z_minus)]
    pressure = [slope_x[3], slope_y[3], slope_z[3]]
    out = []
    for f in range(3):
        laplace = (
            x_plus[f] + x_minus[f] + (y_plus[f] + y_minus[f]) + (z_plus[f] + z_minus[f]) - 6.0 * centre[f]
        )
        advect = centre[0] * slope_x[f] + centre[1] * slope_y[f] + centre[2] * slope_z[f]
        value = VISCOSITY * laplace - advect - pressure[f]
        if f == 0:
            value = value + DRIVING
        out.append(value)
    out.append(-SOUND_SQ * (slope_x[0] + slope_y[1] + slope_z[2]))
    return out


def beyond_walls(flags_ref, ny, shape):
    row = lax.broadcasted_iota(jnp.int32, shape, 0)
    below = (row >= ny + DEPTH + GAP) & flag(flags_ref, LOWER_WALL)
    above = (row >= ny) & (row < ny + DEPTH) & flag(flags_ref, UPPER_WALL)
    return below | above


def plane_rates(read, i, rows, ends=None):
    every = range(4)
    centre = [read(f, i) for f in every]
    x_plus = [read(f, i + 1)[:rows] for f in every]
    x_minus = [read(f, i - 1)[:rows] for f in every]
    y_plus = [step(v, 1, 0)[:rows] for v in centre]
    y_minus = [step(v, -1, 0)[:rows] for v in centre]
    centre = [v[:rows] for v in centre]
    upward, downward = centre, centre
    if ends is not None:
        lane = lax.broadcasted_iota(jnp.int32, centre[0].shape, 1)
        upward = [jnp.where(lane == 0, e[:rows], v) for e, v in zip(ends, centre)]
        downward = [jnp.where(lane == lane.shape[1] - 1, e[:rows], v) for e, v in zip(ends, centre)]
    z_plus = [step(v, 1, 1) for v in upward]
    z_minus = [step(v, -1, 1) for v in downward]
    return centre, rates(centre, x_plus, x_minus, y_plus, y_minus, z_plus, z_minus)


def stage_one(outside, value, rate):
    return jnp.where(outside, 0.0, value + DT_STEP * rate)


def stage_two(outside, begin, value, rate):
    return jnp.where(outside, 0.0, 0.75 * begin + 0.25 * (value + DT_STEP * rate))


def first_kernel(flags_ref, sample_hbm, mid_ref, xlo_ref, xhi_ref, one_ref, sample_ref, sem):
    copy = pltpu.make_async_copy(sample_hbm, sample_ref, sem)
    copy.start()
    fields, nx, rows, nz = mid_ref.shape
    outside = beyond_walls(flags_ref, rows - HALO, (rows, nz))
    for i in range(1, nx + 2 * DEPTH - 1):
        centre, rate = plane_rates(functools.partial(plane_of, mid_ref, xlo_ref, xhi_ref), i, rows)
        for f in range(4):
            one_ref[f, i - 1] = stage_one(outside, centre[f], rate[f])
    copy.wait()


def step_kernel(
    flags_ref, mid_ref, xlo_ref, xhi_ref, first_ref, own_ref, low_ref, high_ref, basis_ref, sample_ref,
    flow_ref, snap_ref, cross_ref,
    one_ref, two_ref,
):
    fields, nx, ny, nz = flow_ref.shape
    rows = mid_ref.shape[2]
    modes = basis_ref.shape[1]
    planes = nx + 2 * DEPTH
    lane = lax.broadcasted_iota(jnp.int32, (rows, nz), 1)
    outside = beyond_walls(flags_ref, ny, (rows, nz))
    every = range(4)
    start = functools.partial(plane_of, mid_ref, xlo_ref, xhi_ref)

    left = lane % GROUP < DEPTH

    def window_rates(q):
        return rates(
            q, [step(v, GROUP, 1) for v in q], [step(v, -GROUP, 1) for v in q],
            [step(v, 1, 0) for v in q], [step(v, -1, 0) for v in q],
            [step(v, 1, 1) for v in q], [step(v, -1, 1) for v in q],
        )

    own = [own_ref[f] for f in every]
    other = [jnp.where(left, low_ref[f], high_ref[f]) for f in every]
    windows = []
    for parts in ((other, own), (own, other)):
        q0 = [jnp.where(left, a, b) for a, b in zip(*parts)]
        q1 = [stage_one(outside, v, r) for v, r in zip(q0, window_rates(q0))]
        q2 = [stage_two(outside, s, v, r) for s, v, r in zip(q0, q1, window_rates(q1))]
        windows.append((q1, q2))
    (low_one, low_two), (high_one, high_two) = windows
    ends_one = [jnp.where(left, a, b) for a, b in zip(low_one, high_one)]
    ends_two = [jnp.where(left, a, b) for a, b in zip(low_two, high_two)]
    rim_one = [jnp.where(left, b, a) for a, b in zip(low_one, high_one)]

    def at_plane(values, i):
        return [pltpu.roll(v, (2 * nz - GROUP * i - DEPTH) % nz, 1) for v in values]

    rim = (lane == 0) | (lane == nz - 1)
    for i in range(1, planes - 1):
        for f, value in enumerate(at_plane(rim_one, i)):
            one_ref[f, i - 1] = jnp.where(rim, value, first_ref[f, i - 1])
    for i in range(2, planes - 2):
        centre, rate = plane_rates(lambda f, i: one_ref[f, i - 1], i, rows, at_plane(ends_one, i))
        for f in every:
            two_ref[f, i - 2] = stage_two(outside, start(f, i), centre[f], rate[f])
    for i in range(3, planes - 3):
        centre, rate = plane_rates(lambda f, i: two_ref[f, i - 2], i, ny, at_plane(ends_two, i))
        for f in every:
            value = 1.0 / 3.0 * start(f, i)[:ny] + 2.0 / 3.0 * (centre[f] + DT_STEP * rate[f])
            flow_ref[f, i - DEPTH] = value

    points = sample_ref.shape[1]
    spot = jnp.broadcast_to(sample_ref[...], (nz, points))
    place = lax.broadcasted_iota(jnp.int32, (nx * ny, points), 0)
    in_row = (place == jnp.broadcast_to(sample_ref[...] // nz, (nx * ny, points))).astype(jnp.bfloat16)
    in_lane = lax.broadcasted_iota(jnp.int32, (nz, points), 0) == spot % nz
    product = jnp.zeros((modes + 1, points), jnp.float32)
    for c in range(3):
        field = flow_ref[c].reshape(nx * ny, nz).T
        found = sum(dot_parts(part, in_row, ((1,), (0,))) for part in three_parts(field))
        picked = jnp.sum(jnp.where(in_lane, found, 0.0), axis=0, keepdims=True)
        snap_ref[c] = picked
        product = product + jnp.concatenate([basis_ref[c], picked], axis=0) * picked
    total = jnp.sum(product, axis=1, keepdims=True)
    size = modes + 1
    diagonal = lax.broadcasted_iota(jnp.int32, (size, size), 0) == lax.broadcasted_iota(jnp.int32, (size, size), 1)
    cross_ref[...] = jnp.sum(jnp.where(diagonal, total, 0.0), axis=0, keepdims=True)


def merge_kernel(parts_ref, cross_ref, send_ref):
    total = parts_ref[0]
    for d in range(1, parts_ref.shape[0]):
        total = total + parts_ref[d]
    block = jnp.concatenate([total[: total.shape[0] - 1], cross_ref[...]], axis=0)
    for d in range(send_ref.shape[0]):
        send_ref[d] = block


def final_kernel(
    count, got_ref, parts_ref, snap_ref, flow_ref,
    basis_hbm, factor_hbm, flow_hbm,
    packed_ref, work_ref, basis_out_ref, factor_ref, sems,
):
    _, comps, size, points = parts_ref.shape
    tall = size // 4
    per = got_ref.shape[1] - 1
    copies = [pltpu.make_async_copy(flow_ref, flow_hbm, sems.at[0])]
    copies[0].start()

    total = jnp.zeros((per + 1, size), jnp.float32)
    for d in range(got_ref.shape[0]):
        block = got_ref[d]
        if per * d < packed_ref.shape[0]:
            packed_ref[per * d : per * d + per] = block[0:per]
        total = total + block
    cross = total[per : per + 1] / count
    top = lax.broadcasted_iota(jnp.int32, (16, size), 0)
    mark = (lax.broadcasted_iota(jnp.int32, (16, size), 1) == size - 1) & (top < 3)
    thirds = jnp.zeros((16, size), jnp.float32)
    for k, part in enumerate(three_parts(cross)):
        thirds = jnp.where(top == k, part.astype(jnp.float32), thirds)
    side = dot_parts(thirds.astype(jnp.bfloat16), mark.astype(jnp.bfloat16), ((0,), (0,)))
    lane = lax.broadcasted_iota(jnp.int32, (tall, size), 1)
    row = lax.broadcasted_iota(jnp.int32, (tall, size), 0)
    old = unpack_upper([packed_ref[tall * k : tall * k + tall] / count for k in range(3)], tall)
    for k in range(4):
        value = jnp.where(lane == size - 1, side[tall * k : tall * k + tall], old[k])
        if k == 3:
            value = jnp.where(row == tall - 1, jnp.broadcast_to(cross, value.shape), value)
        work_ref[tall * k : tall * k + tall, 0:size] = value
        work_ref[tall * k : tall * k + tall, size : 2 * size] = (lane == row + tall * k).astype(jnp.float32)

    for k in range(4):
        base = tall * k
        eliminate(work_ref, base, tall, old[0] if k == 0 else None)
        done = work_ref[base : base + tall, :]
        if k < 3:
            change = dot_stacked(done[:, 0:size], done)
            work_ref[base + tall : size, :] = work_ref[base + tall : size, :] - change[base + tall : size]
        factor_ref[base : base + tall, :] = jnp.where(lane >= row + base, done[:, 0:size], 0.0)
        if k < 2:
            continue
        begin, count_rows = (0, base + tall) if k == 2 else (base, tall)
        inverse = work_ref[begin : base + tall, size : 2 * size]
        pieces = jnp.concatenate(three_parts(inverse), axis=0)
        for c in range(comps):
            value = jnp.zeros((count_rows, points), jnp.float32)
            for n in (2, 1, 0):
                products = dot_parts(pieces[: count_rows * (3 - n)], parts_ref[n, c], ((1,), (0,)))
                for m in range(2 - n, -1, -1):
                    value = value + products[count_rows * m : count_rows * m + count_rows]
            if k == 3:
                value = value + inverse[:, size - 1 : size] * snap_ref[c]
            basis_out_ref[c, begin : base + tall, :] = value
        rows = (slice(None), pl.ds(begin, count_rows), slice(None))
        copies.append(pltpu.make_async_copy(basis_out_ref.at[rows], basis_hbm.at[rows], sems.at[k]))
        copies[-1].start()
    copies.append(pltpu.make_async_copy(factor_ref, factor_hbm, sems.at[1]))
    copies[-1].start()
    for copy in copies:
        copy.wait()


def eliminate(work_ref, base, tall, early=None):
    blocks = tall // 8
    sub = lax.broadcasted_iota(jnp.int32, (8, 128), 0)
    panel = [work_ref[base + 8 * b : base + 8 * b + 8, :] for b in range(blocks)]
    scale = [jnp.zeros((8, 128), jnp.float32) for _ in range(blocks)]
    half = tall // 2
    for low in (0, half):
        high = low + half
        rows = panel if early is None or low else [early[8 * b : 8 * b + 8] for b in range(blocks)]
        column = {
            k: {b: jnp.broadcast_to(rows[b][:, base + k : base + k + 1], (8, 128)) for b in range(k // 8, blocks)}
            for k in range(low, high)
        }
        for j in range(low, high):
            mine, at = divmod(j, 8)
            pivot = column[j][mine][at : at + 1, :]
            inverse = 1.0 / pivot
            scaled = {b: column[j][b] * inverse for b in range(mine, blocks)}
            for k in range(j + 1, high):
                other, place = divmod(k, 8)
                times = scaled[other][place : place + 1, :]
                for b in range(other, blocks):
                    column[k][b] = column[k][b] - column[j][b] * times
            scale[mine] = jnp.where(sub == at, lax.rsqrt(pivot), scale[mine])
            pivot_row = panel[mine][at : at + 1, :]
            for b in range(mine, blocks):
                times = jnp.where(sub > at, scaled[b], 0.0) if b == mine else scaled[b]
                panel[b] = panel[b] - jnp.concatenate([times, times], axis=1) * pivot_row
    for b in range(blocks):
        work_ref[base + 8 * b : base + 8 * b + 8, :] = panel[b] * jnp.concatenate([scale[b], scale[b]], axis=1)


def local(flow, basis, sample):
    fields, nx, ny, nz = flow.shape
    modes, comps, points = basis.shape
    size = modes + 1
    devices = lax.axis_size("gx") * lax.axis_size("gy") * lax.axis_size("gz")
    count = float(comps * points * devices)
    shape = functools.partial(jax.ShapeDtypeStruct, dtype=jnp.float32)
    call = functools.partial(pl.pallas_call, compiler_params=PARAMS)
    bricks = jnp.transpose(basis, (1, 0, 2))

    whole = pl.BlockSpec(memory_space=pltpu.HBM)
    flat = flow.reshape(fields, nx * ny, nz)
    quarter = size // 4
    per = -(-3 * quarter // devices)

    place = lax.axis_index("gy")
    flags = [place == 0, place == lax.axis_size("gy") - 1, place % 2 == 1]
    flags = jnp.broadcast_to(jnp.stack(flags).astype(jnp.int32)[:, None], (len(flags), nz))
    strip = shape((fields, nx * DEPTH, nz))
    strips = call(
        functools.partial(strips_kernel, nx), out_shape=(strip, strip), in_specs=[VMEM] * 2, out_specs=(VMEM, VMEM)
    )(flags, flat)
    y_even, y_odd = pairs(*strips, "gy", "gz")
    gram, basis_parts = call(
        gram_kernel,
        out_shape=(shape((devices, per + 1, size)), jax.ShapeDtypeStruct((3, comps, size, points), jnp.bfloat16)),
        in_specs=[VMEM],
        out_specs=(VMEM, VMEM),
        scratch_shapes=[pltpu.VMEM((size, size), jnp.float32), pltpu.VMEM((devices * per, size), jnp.float32)],
    )(bricks)
    y_odd, y_even, gram = lax.optimization_barrier((y_odd, y_even, gram))

    rows = ny + HALO
    face = shape((fields, DEPTH * ny + HALO, nz))
    mid, first, last = call(
        functools.partial(walls_kernel, nx),
        out_shape=(shape((fields, nx * rows, nz)), face, face),
        in_specs=[VMEM] * 4,
        out_specs=(VMEM,) * 3,
    )(flags, flat, y_odd, y_even)
    mid = mid.reshape(fields, nx, rows, nz)
    low_face, high_face = neighbours(first, last, "gx")
    parts = lax.all_to_all(gram, ALL, 0, 0)

    beside = shape((fields, DEPTH, rows, nz))
    packed, xlo, xhi = call(
        pack_kernel,
        out_shape=(shape((fields, rows, nz)), beside, beside),
        in_specs=[VMEM] * 3,
        out_specs=(VMEM,) * 3,
    )(mid, low_face, high_face)
    if lax.axis_size("gz") == 2:
        low = high = lax.ppermute(packed, "gz", [(0, 1), (1, 0)])
    else:
        low, high = neighbours(packed, packed, "gz")
    begun, cells = call(
        first_kernel,
        out_shape=(
            shape((fields, nx + 2 * DEPTH - 2, rows, nz)),
            jax.ShapeDtypeStruct((1, points), sample.dtype),
        ),
        in_specs=[VMEM, whole] + [VMEM] * 3,
        out_specs=(VMEM, VMEM),
        scratch_shapes=[pltpu.SemaphoreType.DMA],
    )(flags, sample.reshape(1, points), mid, xlo, xhi)
    flow_new, snapshot, cross = call(
        step_kernel,
        out_shape=(shape(flow.shape), shape((comps, 1, points)), shape((1, size))),
        in_specs=[VMEM] * 10,
        out_specs=(VMEM, VMEM, VMEM),
        scratch_shapes=[
            pltpu.VMEM((fields, nx + 2 * DEPTH - 2, rows, nz), jnp.float32),
            pltpu.VMEM((fields, nx + 2 * DEPTH - 4, rows, nz), jnp.float32),
        ],
    )(flags, mid, xlo, xhi, begun, packed, low, high, bricks, cells)

    send = call(
        merge_kernel, out_shape=shape((devices, per + 1, size)), in_specs=[VMEM] * 2, out_specs=VMEM
    )(parts, cross)
    got = lax.all_to_all(send, ALL, 0, 0)
    basis_next, factor, flow_next = call(
        functools.partial(final_kernel, count),
        out_shape=(shape((comps, size, points)), shape((size, size)), shape(flow.shape)),
        in_specs=[VMEM] * 4,
        out_specs=(whole,) * 3,
        scratch_shapes=[
            pltpu.VMEM((3 * quarter, size), jnp.float32),
            pltpu.VMEM((size, 2 * size), jnp.float32),
            pltpu.VMEM((comps, size, points), jnp.float32),
            pltpu.VMEM((size, size), jnp.float32),
            pltpu.SemaphoreType.DMA((4,)),
        ],
    )(got, basis_parts, snapshot, flow_new)
    return flow_next, jnp.transpose(basis_next, (1, 0, 2)), factor


def solution(mesh):
    return jax.shard_map(
        local,
        mesh=mesh,
        in_specs=(
            P(None, "gx", "gy", "gz"),
            P(None, None, ("gx", "gy", "gz")),
            P(("gx", "gy", "gz")),
        ),
        out_specs=(P(None, "gx", "gy", "gz"), P(None, None, ("gx", "gy", "gz")), P()),
        check_vma=False,
    )
```

```python
import functools

import jax
import jax.numpy as jnp
from jax import lax
from jax.experimental import pallas as pl
from jax.experimental.pallas import tpu as pltpu
from jax.sharding import PartitionSpec as P

DT_STEP = 0.35
VISCOSITY = 0.2
SOUND_SQ = 1.0
DRIVING = 0.5

ALL = ("gz", "gy", "gx")
DEPTH = 3
EXACT = lax.Precision.HIGHEST
VMEM = pl.BlockSpec(memory_space=pltpu.VMEM)
PARAMS = pltpu.CompilerParams(vmem_limit_bytes=40 * 1024 * 1024)


def dot(a, b, dims):
    return lax.dot_general(
        a, b, (dims, ((), ())), precision=EXACT, preferred_element_type=jnp.float32
    )


def three_parts(value):
    high = value.astype(jnp.bfloat16)
    rest = value - high.astype(jnp.float32)
    middle = rest.astype(jnp.bfloat16)
    return high, middle, (rest - middle.astype(jnp.float32)).astype(jnp.bfloat16)


def dot_parts(a, b, dims):
    return lax.dot_general(a, b, (dims, ((), ())), preferred_element_type=jnp.float32)


def dot_stacked(a, b):
    (a1, a2, a3), (b1, b2, b3) = three_parts(a), three_parts(b)
    first = jnp.concatenate([a1, a1, a2, a2, a1, a3], axis=0)
    second = jnp.concatenate([b1, b2, b1, b2, b3, b1], axis=0)
    return dot_parts(first, second, ((0,), (0,)))


def neighbours(block_low, block_high, axis):
    count = lax.axis_size(axis)
    forward = [(i, (i + 1) % count) for i in range(count)]
    backward = [(target, source) for source, target in forward]
    return lax.ppermute(block_high, axis, forward), lax.ppermute(block_low, axis, backward)


def pairs(block_odd, block_even, axis, other):
    count, width = lax.axis_size(axis), lax.axis_size(other)
    even = [(i, i + 1 - 2 * (i % 2)) for i in range(count)]
    odd = []
    for i in range(count):
        for k in range(width):
            to = (i, k + 1 - 2 * (k % 2)) if i in (0, count - 1) else (i - 1 + 2 * (i % 2), k)
            odd.append((i * width + k, to[0] * width + to[1]))
    from_odd = lax.ppermute(block_odd, (axis, other), odd)
    return lax.ppermute(block_even, axis, even), from_odd


def at_lower_wall():
    return lax.axis_index("gy") == 0


def at_upper_wall():
    return lax.axis_index("gy") == lax.axis_size("gy") - 1


def odd_place():
    return lax.axis_index("gy") % 2 == 1


def pack_upper(rows, tall):
    size = rows.shape[1]
    lane = lax.broadcasted_iota(jnp.int32, (tall, size), 1)
    part = [rows[tall * k : tall * k + tall] for k in range(4)]
    return [part[0], jnp.where(lane >= tall, part[1], pltpu.roll(part[3], tall, 1)), part[2]]


def unpack_upper(packed, tall):
    return [packed[0], packed[1], packed[2], pltpu.roll(packed[1], packed[1].shape[1] - tall, 1)]


def gram_kernel(basis_ref, send_ref, parts_ref, gram_ref, packed_ref):
    modes = basis_ref.shape[1]
    tall = gram_ref.shape[0] // 4
    total = jnp.zeros((modes, modes), jnp.float32)
    for c in range(basis_ref.shape[0]):
        rows = basis_ref[c]
        total = total + dot(rows, rows, ((1,), (1,)))
        filled = jnp.concatenate([rows, jnp.zeros((1, rows.shape[1]), jnp.float32)], axis=0)
        for k, part in enumerate(three_parts(filled)):
            parts_ref[k, c] = part
    gram_ref[...] = jnp.zeros_like(gram_ref)
    gram_ref[0:modes, 0:modes] = total
    packed_ref[...] = jnp.zeros_like(packed_ref)
    for k, value in enumerate(pack_upper(gram_ref[...], tall)):
        packed_ref[tall * k : tall * k + tall] = value
    per = send_ref.shape[1] - 1
    empty = jnp.zeros((1, send_ref.shape[2]), jnp.float32)
    for d in range(send_ref.shape[0]):
        send_ref[d] = jnp.concatenate([packed_ref[per * d : per * d + per], empty], axis=0)


GAP = 2
HALO = 2 * DEPTH + GAP


def strips_kernel(planes, flow_ref, odd_ref, even_ref):
    ny = flow_ref.shape[1] // planes
    odd = odd_place()
    for f in range(flow_ref.shape[0]):
        for j in range(DEPTH):
            bottom = flow_ref[f, pl.ds(j, planes, stride=ny), :]
            top = flow_ref[f, pl.ds(ny - DEPTH + j, planes, stride=ny), :]
            even_ref[f, planes * j : planes * j + planes] = jnp.where(odd, bottom, top)
            odd_ref[f, planes * j : planes * j + planes] = jnp.where(odd, top, bottom)


def walls_kernel(planes, flow_ref, odd_ref, even_ref, mid_ref, first_ref, last_ref):
    fields, cells, nz = flow_ref.shape
    odd_y = odd_place()
    ny = cells // planes
    rows = ny + HALO
    sub = lax.broadcasted_iota(jnp.int32, (HALO, nz), 0)
    empty = jnp.zeros((planes, nz), jnp.float32)
    for f in range(fields):
        for i in range(planes):
            mid_ref[f, rows * i : rows * i + ny] = flow_ref[f, ny * i : ny * i + ny]
        for j in range(HALO):
            k = j if j < DEPTH else j - DEPTH - GAP
            part = slice(planes * k, planes * k + planes)
            if j < DEPTH:
                value = jnp.where(odd_y, odd_ref[f, part], even_ref[f, part])
                value = jnp.where(at_upper_wall(), 0.0, value)
            elif j < DEPTH + GAP:
                value = empty
            else:
                value = jnp.where(odd_y, even_ref[f, part], odd_ref[f, part])
                value = jnp.where(at_lower_wall(), 0.0, value)
            mid_ref[f, pl.ds(ny + j, planes, stride=rows), :] = value
        for face_ref, begin, near, next_one in (
            (first_ref, 0, 0, 1), (last_ref, planes - DEPTH, planes - 1, planes - 2)
        ):
            for k in range(DEPTH):
                face_ref[f, ny * k : ny * k + ny] = flow_ref[f, ny * (begin + k) : ny * (begin + k) + ny]
            halos = [mid_ref[f, rows * i + ny : rows * i + rows] for i in (near, next_one)]
            face_ref[f, ny * DEPTH : ny * DEPTH + HALO] = corner_rows(*halos, sub)


def corner_rows(near, next_one, sub):
    tile = jnp.where(sub == 2, pltpu.roll(next_one, 2, 0), pltpu.roll(next_one, 6, 0))
    tile = jnp.where((sub == 2) | (sub == 5), tile, 0.0)
    return jnp.where((sub < 2) | (sub >= 6), near, tile)


def corner_planes(tile, sub):
    near = jnp.where((sub < 2) | (sub >= 6), tile, 0.0)
    next_one = jnp.where(sub == 0, pltpu.roll(tile, 6, 0), pltpu.roll(tile, 2, 0))
    return [near, jnp.where((sub == 0) | (sub == 7), next_one, 0.0), jnp.zeros_like(tile)]


def plane_of(mid_ref, xlo_ref, xhi_ref, f, i):
    nx = mid_ref.shape[1]
    if i < DEPTH:
        return xlo_ref[f, i]
    if i < DEPTH + nx:
        return mid_ref[f, i - DEPTH]
    return xhi_ref[f, i - DEPTH - nx]


GROUP = 8


def pack_kernel(mid_ref, low_ref, high_ref, packed_ref, xlo_ref, xhi_ref):
    fields, nx, rows, nz = mid_ref.shape
    ny = rows - HALO
    lane = lax.broadcasted_iota(jnp.int32, (rows, nz), 1)
    sub = lax.broadcasted_iota(jnp.int32, (HALO, nz), 0)
    for f in range(fields):
        for face_ref, out_ref, order in ((low_ref, xlo_ref, (2, 1, 0)), (high_ref, xhi_ref, (0, 1, 2))):
            face = face_ref[f]
            halo = corner_planes(face[ny * DEPTH :], sub)
            for k in range(DEPTH):
                out_ref[f, k, 0:ny] = face[ny * k : ny * k + ny]
                out_ref[f, k, ny:rows] = halo[order[k]]
        value = jnp.zeros((rows, nz), jnp.float32)
        for i in range(nx + 2 * DEPTH):
            start = GROUP * i
            moved = pltpu.roll(plane_of(mid_ref, xlo_ref, xhi_ref, f, i), (start + DEPTH) % nz, 1)
            value = jnp.where((lane >= start) & (lane < start + 2 * DEPTH), moved, value)
        packed_ref[f] = value


def step(value, by, axis):
    size = value.shape[axis]
    return pltpu.roll(value, (size - by) % size, axis)


def rates(centre, x_plus, x_minus, y_plus, y_minus, z_plus, z_minus):
    slope_x = [0.5 * (a - b) for a, b in zip(x_plus, x_minus)]
    slope_y = [0.5 * (a - b) for a, b in zip(y_plus, y_minus)]
    slope_z = [0.5 * (a - b) for a, b in zip(z_plus, z_minus)]
    pressure = [slope_x[3], slope_y[3], slope_z[3]]
    out = []
    for f in range(3):
        laplace = (
            x_plus[f] + x_minus[f] + (y_plus[f] + y_minus[f]) + (z_plus[f] + z_minus[f]) - 6.0 * centre[f]
        )
        advect = centre[0] * slope_x[f] + centre[1] * slope_y[f] + centre[2] * slope_z[f]
        value = VISCOSITY * laplace - advect - pressure[f]
        if f == 0:
            value = value + DRIVING
        out.append(value)
    out.append(-SOUND_SQ * (slope_x[0] + slope_y[1] + slope_z[2]))
    return out


def beyond_walls(ny, shape):
    row = lax.broadcasted_iota(jnp.int32, shape, 0)
    below = (row >= ny + DEPTH + GAP) & at_lower_wall()
    above = (row >= ny) & (row < ny + DEPTH) & at_upper_wall()
    return below | above


def plane_rates(read, i, rows, ends=None):
    every = range(4)
    centre = [read(f, i) for f in every]
    x_plus = [read(f, i + 1)[:rows] for f in every]
    x_minus = [read(f, i - 1)[:rows] for f in every]
    y_plus = [step(v, 1, 0)[:rows] for v in centre]
    y_minus = [step(v, -1, 0)[:rows] for v in centre]
    centre = [v[:rows] for v in centre]
    upward, downward = centre, centre
    if ends is not None:
        lane = lax.broadcasted_iota(jnp.int32, centre[0].shape, 1)
        upward = [jnp.where(lane == 0, e[:rows], v) for e, v in zip(ends, centre)]
        downward = [jnp.where(lane == lane.shape[1] - 1, e[:rows], v) for e, v in zip(ends, centre)]
    z_plus = [step(v, 1, 1) for v in upward]
    z_minus = [step(v, -1, 1) for v in downward]
    return centre, rates(centre, x_plus, x_minus, y_plus, y_minus, z_plus, z_minus)


def stage_one(outside, value, rate):
    return jnp.where(outside, 0.0, value + DT_STEP * rate)


def stage_two(outside, begin, value, rate):
    return jnp.where(outside, 0.0, 0.75 * begin + 0.25 * (value + DT_STEP * rate))


def first_kernel(sample_hbm, mid_ref, xlo_ref, xhi_ref, one_ref, sample_ref, sem):
    copy = pltpu.make_async_copy(sample_hbm, sample_ref, sem)
    copy.start()
    fields, nx, rows, nz = mid_ref.shape
    outside = beyond_walls(rows - HALO, (rows, nz))
    for i in range(1, nx + 2 * DEPTH - 1):
        centre, rate = plane_rates(functools.partial(plane_of, mid_ref, xlo_ref, xhi_ref), i, rows)
        for f in range(4):
            one_ref[f, i - 1] = stage_one(outside, centre[f], rate[f])
    copy.wait()


def step_kernel(
    mid_ref, xlo_ref, xhi_ref, first_ref, own_ref, low_ref, high_ref, basis_ref, sample_ref,
    flow_ref, snap_ref, cross_ref,
    one_ref, two_ref,
):
    fields, nx, ny, nz = flow_ref.shape
    rows = mid_ref.shape[2]
    modes = basis_ref.shape[1]
    planes = nx + 2 * DEPTH
    lane = lax.broadcasted_iota(jnp.int32, (rows, nz), 1)
    outside = beyond_walls(ny, (rows, nz))
    every = range(4)
    start = functools.partial(plane_of, mid_ref, xlo_ref, xhi_ref)

    left = lane % GROUP < DEPTH

    def window_rates(q):
        return rates(
            q, [step(v, GROUP, 1) for v in q], [step(v, -GROUP, 1) for v in q],
            [step(v, 1, 0) for v in q], [step(v, -1, 0) for v in q],
            [step(v, 1, 1) for v in q], [step(v, -1, 1) for v in q],
        )

    own = [own_ref[f] for f in every]
    other = [jnp.where(left, low_ref[f], high_ref[f]) for f in every]
    windows = []
    for parts in ((other, own), (own, other)):
        q0 = [jnp.where(left, a, b) for a, b in zip(*parts)]
        q1 = [stage_one(outside, v, r) for v, r in zip(q0, window_rates(q0))]
        q2 = [stage_two(outside, s, v, r) for s, v, r in zip(q0, q1, window_rates(q1))]
        windows.append((q1, q2))
    (low_one, low_two), (high_one, high_two) = windows
    ends_one = [jnp.where(left, a, b) for a, b in zip(low_one, high_one)]
    ends_two = [jnp.where(left, a, b) for a, b in zip(low_two, high_two)]
    rim_one = [jnp.where(left, b, a) for a, b in zip(low_one, high_one)]

    def at_plane(values, i):
        return [pltpu.roll(v, (2 * nz - GROUP * i - DEPTH) % nz, 1) for v in values]

    rim = (lane == 0) | (lane == nz - 1)
    for i in range(1, planes - 1):
        for f, value in enumerate(at_plane(rim_one, i)):
            one_ref[f, i - 1] = jnp.where(rim, value, first_ref[f, i - 1])
    for i in range(2, planes - 2):
        centre, rate = plane_rates(lambda f, i: one_ref[f, i - 1], i, rows, at_plane(ends_one, i))
        for f in every:
            two_ref[f, i - 2] = stage_two(outside, start(f, i), centre[f], rate[f])
    for i in range(3, planes - 3):
        centre, rate = plane_rates(lambda f, i: two_ref[f, i - 2], i, ny, at_plane(ends_two, i))
        for f in every:
            value = 1.0 / 3.0 * start(f, i)[:ny] + 2.0 / 3.0 * (centre[f] + DT_STEP * rate[f])
            flow_ref[f, i - DEPTH] = value

    points = sample_ref.shape[1]
    spot = jnp.broadcast_to(sample_ref[...], (nz, points))
    place = lax.broadcasted_iota(jnp.int32, (nx * ny, points), 0)
    in_row = (place == jnp.broadcast_to(sample_ref[...] // nz, (nx * ny, points))).astype(jnp.bfloat16)
    in_lane = lax.broadcasted_iota(jnp.int32, (nz, points), 0) == spot % nz
    product = jnp.zeros((modes + 1, points), jnp.float32)
    for c in range(3):
        field = flow_ref[c].reshape(nx * ny, nz).T
        found = sum(dot_parts(part, in_row, ((1,), (0,))) for part in three_parts(field))
        picked = jnp.sum(jnp.where(in_lane, found, 0.0), axis=0, keepdims=True)
        snap_ref[c] = picked
        product = product + jnp.concatenate([basis_ref[c], picked], axis=0) * picked
    total = jnp.sum(product, axis=1, keepdims=True)
    size = modes + 1
    diagonal = lax.broadcasted_iota(jnp.int32, (size, size), 0) == lax.broadcasted_iota(jnp.int32, (size, size), 1)
    cross_ref[...] = jnp.sum(jnp.where(diagonal, total, 0.0), axis=0, keepdims=True)


def merge_kernel(parts_ref, cross_ref, send_ref):
    total = parts_ref[0]
    for d in range(1, parts_ref.shape[0]):
        total = total + parts_ref[d]
    block = jnp.concatenate([total[: total.shape[0] - 1], cross_ref[...]], axis=0)
    for d in range(send_ref.shape[0]):
        send_ref[d] = block


def final_kernel(
    count, got_ref, parts_ref, snap_ref, flow_ref,
    basis_hbm, factor_hbm, flow_hbm,
    packed_ref, work_ref, basis_out_ref, factor_ref, sems,
):
    _, comps, size, points = parts_ref.shape
    tall = size // 4
    per = got_ref.shape[1] - 1
    copies = [pltpu.make_async_copy(flow_ref, flow_hbm, sems.at[0])]
    copies[0].start()

    total = jnp.zeros((per + 1, size), jnp.float32)
    for d in range(got_ref.shape[0]):
        block = got_ref[d]
        if per * d < packed_ref.shape[0]:
            packed_ref[per * d : per * d + per] = block[0:per]
        total = total + block
    cross = total[per : per + 1] / count
    top = lax.broadcasted_iota(jnp.int32, (16, size), 0)
    mark = (lax.broadcasted_iota(jnp.int32, (16, size), 1) == size - 1) & (top < 3)
    thirds = jnp.zeros((16, size), jnp.float32)
    for k, part in enumerate(three_parts(cross)):
        thirds = jnp.where(top == k, part.astype(jnp.float32), thirds)
    side = dot_parts(thirds.astype(jnp.bfloat16), mark.astype(jnp.bfloat16), ((0,), (0,)))
    lane = lax.broadcasted_iota(jnp.int32, (tall, size), 1)
    row = lax.broadcasted_iota(jnp.int32, (tall, size), 0)
    old = unpack_upper([packed_ref[tall * k : tall * k + tall] / count for k in range(3)], tall)
    for k in range(4):
        value = jnp.where(lane == size - 1, side[tall * k : tall * k + tall], old[k])
        if k == 3:
            value = jnp.where(row == tall - 1, jnp.broadcast_to(cross, value.shape), value)
        work_ref[tall * k : tall * k + tall, 0:size] = value
        work_ref[tall * k : tall * k + tall, size : 2 * size] = (lane == row + tall * k).astype(jnp.float32)

    for k in range(4):
        base = tall * k
        eliminate(work_ref, base, tall, old[0] if k == 0 else None)
        done = work_ref[base : base + tall, :]
        if k < 3:
            change = dot_stacked(done[:, 0:size], done)
            work_ref[base + tall : size, :] = work_ref[base + tall : size, :] - change[base + tall : size]
        factor_ref[base : base + tall, :] = jnp.where(lane >= row + base, done[:, 0:size], 0.0)
        if k < 2:
            continue
        begin, count_rows = (0, base + tall) if k == 2 else (base, tall)
        inverse = work_ref[begin : base + tall, size : 2 * size]
        pieces = jnp.concatenate(three_parts(inverse), axis=0)
        for c in range(comps):
            value = jnp.zeros((count_rows, points), jnp.float32)
            for n in (2, 1, 0):
                products = dot_parts(pieces[: count_rows * (3 - n)], parts_ref[n, c], ((1,), (0,)))
                for m in range(2 - n, -1, -1):
                    value = value + products[count_rows * m : count_rows * m + count_rows]
            if k == 3:
                value = value + inverse[:, size - 1 : size] * snap_ref[c]
            basis_out_ref[c, begin : base + tall, :] = value
        rows = (slice(None), pl.ds(begin, count_rows), slice(None))
        copies.append(pltpu.make_async_copy(basis_out_ref.at[rows], basis_hbm.at[rows], sems.at[k]))
        copies[-1].start()
    copies.append(pltpu.make_async_copy(factor_ref, factor_hbm, sems.at[1]))
    copies[-1].start()
    for copy in copies:
        copy.wait()


def eliminate(work_ref, base, tall, early=None):
    blocks = tall // 8
    sub = lax.broadcasted_iota(jnp.int32, (8, 128), 0)
    panel = [work_ref[base + 8 * b : base + 8 * b + 8, :] for b in range(blocks)]
    scale = [jnp.zeros((8, 128), jnp.float32) for _ in range(blocks)]
    half = tall // 2
    for low in (0, half):
        high = low + half
        rows = panel if early is None or low else [early[8 * b : 8 * b + 8] for b in range(blocks)]
        column = {
            k: {b: jnp.broadcast_to(rows[b][:, base + k : base + k + 1], (8, 128)) for b in range(k // 8, blocks)}
            for k in range(low, high)
        }
        for j in range(low, high):
            mine, at = divmod(j, 8)
            pivot = column[j][mine][at : at + 1, :]
            inverse = 1.0 / pivot
            scaled = {b: column[j][b] * inverse for b in range(mine, blocks)}
            for k in range(j + 1, high):
                other, place = divmod(k, 8)
                times = scaled[other][place : place + 1, :]
                for b in range(other, blocks):
                    column[k][b] = column[k][b] - column[j][b] * times
            scale[mine] = jnp.where(sub == at, lax.rsqrt(pivot), scale[mine])
            pivot_row = panel[mine][at : at + 1, :]
            for b in range(mine, blocks):
                times = jnp.where(sub > at, scaled[b], 0.0) if b == mine else scaled[b]
                panel[b] = panel[b] - jnp.concatenate([times, times], axis=1) * pivot_row
    for b in range(blocks):
        work_ref[base + 8 * b : base + 8 * b + 8, :] = panel[b] * jnp.concatenate([scale[b], scale[b]], axis=1)


def local(flow, basis, sample):
    fields, nx, ny, nz = flow.shape
    modes, comps, points = basis.shape
    size = modes + 1
    devices = lax.axis_size("gx") * lax.axis_size("gy") * lax.axis_size("gz")
    count = float(comps * points * devices)
    shape = functools.partial(jax.ShapeDtypeStruct, dtype=jnp.float32)
    call = functools.partial(pl.pallas_call, compiler_params=PARAMS)
    bricks = jnp.transpose(basis, (1, 0, 2))

    whole = pl.BlockSpec(memory_space=pltpu.HBM)
    flat = flow.reshape(fields, nx * ny, nz)
    quarter = size // 4
    per = -(-3 * quarter // devices)

    strip = shape((fields, nx * DEPTH, nz))
    strips = call(
        functools.partial(strips_kernel, nx), out_shape=(strip, strip), in_specs=[VMEM], out_specs=(VMEM, VMEM)
    )(flat)
    y_even, y_odd = pairs(*strips, "gy", "gz")
    gram, basis_parts = call(
        gram_kernel,
        out_shape=(shape((devices, per + 1, size)), jax.ShapeDtypeStruct((3, comps, size, points), jnp.bfloat16)),
        in_specs=[VMEM],
        out_specs=(VMEM, VMEM),
        scratch_shapes=[pltpu.VMEM((size, size), jnp.float32), pltpu.VMEM((devices * per, size), jnp.float32)],
    )(bricks)
    y_odd, y_even, gram = lax.optimization_barrier((y_odd, y_even, gram))

    rows = ny + HALO
    face = shape((fields, DEPTH * ny + HALO, nz))
    mid, first, last = call(
        functools.partial(walls_kernel, nx),
        out_shape=(shape((fields, nx * rows, nz)), face, face),
        in_specs=[VMEM] * 3,
        out_specs=(VMEM,) * 3,
    )(flat, y_odd, y_even)
    mid = mid.reshape(fields, nx, rows, nz)
    low_face, high_face = neighbours(first, last, "gx")
    parts = lax.all_to_all(gram, ALL, 0, 0)

    beside = shape((fields, DEPTH, rows, nz))
    packed, xlo, xhi = call(
        pack_kernel,
        out_shape=(shape((fields, rows, nz)), beside, beside),
        in_specs=[VMEM] * 3,
        out_specs=(VMEM,) * 3,
    )(mid, low_face, high_face)
    if lax.axis_size("gz") == 2:
        low = high = lax.ppermute(packed, "gz", [(0, 1), (1, 0)])
    else:
        low, high = neighbours(packed, packed, "gz")
    begun, cells = call(
        first_kernel,
        out_shape=(
            shape((fields, nx + 2 * DEPTH - 2, rows, nz)),
            jax.ShapeDtypeStruct((1, points), sample.dtype),
        ),
        in_specs=[whole] + [VMEM] * 3,
        out_specs=(VMEM, VMEM),
        scratch_shapes=[pltpu.SemaphoreType.DMA],
    )(sample.reshape(1, points), mid, xlo, xhi)
    flow_new, snapshot, cross = call(
        step_kernel,
        out_shape=(shape(flow.shape), shape((comps, 1, points)), shape((1, size))),
        in_specs=[VMEM] * 9,
        out_specs=(VMEM, VMEM, VMEM),
        scratch_shapes=[
            pltpu.VMEM((fields, nx + 2 * DEPTH - 2, rows, nz), jnp.float32),
            pltpu.VMEM((fields, nx + 2 * DEPTH - 4, rows, nz), jnp.float32),
        ],
    )(mid, xlo, xhi, begun, packed, low, high, bricks, cells)

    send = call(
        merge_kernel, out_shape=shape((devices, per + 1, size)), in_specs=[VMEM] * 2, out_specs=VMEM
    )(parts, cross)
    got = lax.all_to_all(send, ALL, 0, 0)
    basis_next, factor, flow_next = call(
        functools.partial(final_kernel, count),
        out_shape=(shape((comps, size, points)), shape((size, size)), shape(flow.shape)),
        in_specs=[VMEM] * 4,
        out_specs=(whole,) * 3,
        scratch_shapes=[
            pltpu.VMEM((3 * quarter, size), jnp.float32),
            pltpu.VMEM((size, 2 * size), jnp.float32),
            pltpu.VMEM((comps, size, points), jnp.float32),
            pltpu.VMEM((size, size), jnp.float32),
            pltpu.SemaphoreType.DMA((4,)),
        ],
    )(got, basis_parts, snapshot, flow_new)
    return flow_next, jnp.transpose(basis_next, (1, 0, 2)), factor


def solution(mesh):
    return jax.shard_map(
        local,
        mesh=mesh,
        in_specs=(
            P(None, "gx", "gy", "gz"),
            P(None, None, ("gx", "gy", "gz")),
            P(("gx", "gy", "gz")),
        ),
        out_specs=(P(None, "gx", "gy", "gz"), P(None, None, ("gx", "gy", "gz")), P()),
        check_vma=False,
    )
```

```python
import functools

import jax
import jax.numpy as jnp
from jax import lax
from jax.experimental import pallas as pl
from jax.experimental.pallas import tpu as pltpu
from jax.sharding import PartitionSpec as P

DT_STEP = 0.35
VISCOSITY = 0.2
SOUND_SQ = 1.0
DRIVING = 0.5

ALL = ("gz", "gy", "gx")
DEPTH = 3
EXACT = lax.Precision.HIGHEST
VMEM = pl.BlockSpec(memory_space=pltpu.VMEM)
PARAMS = pltpu.CompilerParams(vmem_limit_bytes=40 * 1024 * 1024)


def dot(a, b, dims):
    return lax.dot_general(
        a, b, (dims, ((), ())), precision=EXACT, preferred_element_type=jnp.float32
    )


def three_parts(value):
    high = value.astype(jnp.bfloat16)
    rest = value - high.astype(jnp.float32)
    middle = rest.astype(jnp.bfloat16)
    return high, middle, (rest - middle.astype(jnp.float32)).astype(jnp.bfloat16)


def dot_parts(a, b, dims):
    return lax.dot_general(a, b, (dims, ((), ())), preferred_element_type=jnp.float32)


def dot_stacked(a, b):
    (a1, a2, a3), (b1, b2, b3) = three_parts(a), three_parts(b)
    first = jnp.concatenate([a1, a1, a2, a2, a1, a3], axis=0)
    second = jnp.concatenate([b1, b2, b1, b2, b3, b1], axis=0)
    return dot_parts(first, second, ((0,), (0,)))


def neighbours(block_low, block_high, axis):
    count = lax.axis_size(axis)
    forward = [(i, (i + 1) % count) for i in range(count)]
    backward = [(target, source) for source, target in forward]
    return lax.ppermute(block_high, axis, forward), lax.ppermute(block_low, axis, backward)


def pairs(block_odd, block_even, axis, other):
    count, width = lax.axis_size(axis), lax.axis_size(other)
    even = [(i, i + 1 - 2 * (i % 2)) for i in range(count)]
    odd = []
    for i in range(count):
        for k in range(width):
            to = (i, k + 1 - 2 * (k % 2)) if i in (0, count - 1) else (i - 1 + 2 * (i % 2), k)
            odd.append((i * width + k, to[0] * width + to[1]))
    from_odd = lax.ppermute(block_odd, (axis, other), odd)
    return lax.ppermute(block_even, axis, even), from_odd


def at_lower_wall():
    return lax.axis_index("gy") == 0


def at_upper_wall():
    return lax.axis_index("gy") == lax.axis_size("gy") - 1


def odd_place():
    return lax.axis_index("gy") % 2 == 1


def pack_upper(rows, tall):
    size = rows.shape[1]
    lane = lax.broadcasted_iota(jnp.int32, (tall, size), 1)
    part = [rows[tall * k : tall * k + tall] for k in range(4)]
    return [part[0], jnp.where(lane >= tall, part[1], pltpu.roll(part[3], tall, 1)), part[2]]


def unpack_upper(packed, tall):
    return [packed[0], packed[1], packed[2], pltpu.roll(packed[1], packed[1].shape[1] - tall, 1)]


def gram_kernel(basis_ref, send_ref, parts_ref, gram_ref, packed_ref):
    modes = basis_ref.shape[1]
    tall = gram_ref.shape[0] // 4
    total = jnp.zeros((modes, modes), jnp.float32)
    for c in range(basis_ref.shape[0]):
        rows = basis_ref[c]
        total = total + dot(rows, rows, ((1,), (1,)))
        filled = jnp.concatenate([rows, jnp.zeros((1, rows.shape[1]), jnp.float32)], axis=0)
        for k, part in enumerate(three_parts(filled)):
            parts_ref[k, c] = part
    gram_ref[...] = jnp.zeros_like(gram_ref)
    gram_ref[0:modes, 0:modes] = total
    packed_ref[...] = jnp.zeros_like(packed_ref)
    for k, value in enumerate(pack_upper(gram_ref[...], tall)):
        packed_ref[tall * k : tall * k + tall] = value
    per = send_ref.shape[1] - 1
    empty = jnp.zeros((1, send_ref.shape[2]), jnp.float32)
    for d in range(send_ref.shape[0]):
        send_ref[d] = jnp.concatenate([packed_ref[per * d : per * d + per], empty], axis=0)


GAP = 2
HALO = 2 * DEPTH + GAP


def strips_kernel(planes, flow_ref, odd_ref, even_ref):
    ny = flow_ref.shape[1] // planes
    odd = odd_place()
    for f in range(flow_ref.shape[0]):
        for j in range(DEPTH):
            bottom = flow_ref[f, pl.ds(j, planes, stride=ny), :]
            top = flow_ref[f, pl.ds(ny - DEPTH + j, planes, stride=ny), :]
            even_ref[f, planes * j : planes * j + planes] = jnp.where(odd, bottom, top)
            odd_ref[f, planes * j : planes * j + planes] = jnp.where(odd, top, bottom)


def walls_kernel(planes, flow_ref, odd_ref, even_ref, mid_ref, first_ref, last_ref):
    fields, cells, nz = flow_ref.shape
    odd_y = odd_place()
    ny = cells // planes
    rows = ny + HALO
    sub = lax.broadcasted_iota(jnp.int32, (HALO, nz), 0)
    empty = jnp.zeros((planes, nz), jnp.float32)
    for f in range(fields):
        for i in range(planes):
            mid_ref[f, rows * i : rows * i + ny] = flow_ref[f, ny * i : ny * i + ny]
        for j in range(HALO):
            k = j if j < DEPTH else j - DEPTH - GAP
            part = slice(planes * k, planes * k + planes)
            if j < DEPTH:
                value = jnp.where(odd_y, odd_ref[f, part], even_ref[f, part])
                value = jnp.where(at_upper_wall(), 0.0, value)
            elif j < DEPTH + GAP:
                value = empty
            else:
                value = jnp.where(odd_y, even_ref[f, part], odd_ref[f, part])
                value = jnp.where(at_lower_wall(), 0.0, value)
            mid_ref[f, pl.ds(ny + j, planes, stride=rows), :] = value
        for face_ref, begin, near, next_one in (
            (first_ref, 0, 0, 1), (last_ref, planes - DEPTH, planes - 1, planes - 2)
        ):
            for k in range(DEPTH):
                face_ref[f, ny * k : ny * k + ny] = flow_ref[f, ny * (begin + k) : ny * (begin + k) + ny]
            halos = [mid_ref[f, rows * i + ny : rows * i + rows] for i in (near, next_one)]
            face_ref[f, ny * DEPTH : ny * DEPTH + HALO] = corner_rows(*halos, sub)


def corner_rows(near, next_one, sub):
    tile = jnp.where(sub == 2, pltpu.roll(next_one, 2, 0), pltpu.roll(next_one, 6, 0))
    tile = jnp.where((sub == 2) | (sub == 5), tile, 0.0)
    return jnp.where((sub < 2) | (sub >= 6), near, tile)


def corner_planes(tile, sub):
    near = jnp.where((sub < 2) | (sub >= 6), tile, 0.0)
    next_one = jnp.where(sub == 0, pltpu.roll(tile, 6, 0), pltpu.roll(tile, 2, 0))
    return [near, jnp.where((sub == 0) | (sub == 7), next_one, 0.0), jnp.zeros_like(tile)]


def plane_of(mid_ref, xlo_ref, xhi_ref, f, i):
    nx = mid_ref.shape[1]
    if i < DEPTH:
        return xlo_ref[f, i]
    if i < DEPTH + nx:
        return mid_ref[f, i - DEPTH]
    return xhi_ref[f, i - DEPTH - nx]


GROUP = 8


def pack_kernel(mid_ref, low_ref, high_ref, packed_ref, xlo_ref, xhi_ref):
    fields, nx, rows, nz = mid_ref.shape
    ny = rows - HALO
    lane = lax.broadcasted_iota(jnp.int32, (rows, nz), 1)
    sub = lax.broadcasted_iota(jnp.int32, (HALO, nz), 0)
    for f in range(fields):
        for face_ref, out_ref, order in ((low_ref, xlo_ref, (2, 1, 0)), (high_ref, xhi_ref, (0, 1, 2))):
            face = face_ref[f]
            halo = corner_planes(face[ny * DEPTH :], sub)
            for k in range(DEPTH):
                out_ref[f, k, 0:ny] = face[ny * k : ny * k + ny]
                out_ref[f, k, ny:rows] = halo[order[k]]
        value = jnp.zeros((rows, nz), jnp.float32)
        for i in range(nx + 2 * DEPTH):
            start = GROUP * i
            moved = pltpu.roll(plane_of(mid_ref, xlo_ref, xhi_ref, f, i), (start + DEPTH) % nz, 1)
            value = jnp.where((lane >= start) & (lane < start + 2 * DEPTH), moved, value)
        packed_ref[f] = value


def step(value, by, axis):
    size = value.shape[axis]
    return pltpu.roll(value, (size - by) % size, axis)


def rates(centre, x_plus, x_minus, y_plus, y_minus, z_plus, z_minus):
    slope_x = [0.5 * (a - b) for a, b in zip(x_plus, x_minus)]
    slope_y = [0.5 * (a - b) for a, b in zip(y_plus, y_minus)]
    slope_z = [0.5 * (a - b) for a, b in zip(z_plus, z_minus)]
    pressure = [slope_x[3], slope_y[3], slope_z[3]]
    out = []
    for f in range(3):
        laplace = (
            x_plus[f] + x_minus[f] + (y_plus[f] + y_minus[f]) + (z_plus[f] + z_minus[f]) - 6.0 * centre[f]
        )
        advect = centre[0] * slope_x[f] + centre[1] * slope_y[f] + centre[2] * slope_z[f]
        value = VISCOSITY * laplace - advect - pressure[f]
        if f == 0:
            value = value + DRIVING
        out.append(value)
    out.append(-SOUND_SQ * (slope_x[0] + slope_y[1] + slope_z[2]))
    return out


def beyond_walls(ny, shape):
    row = lax.broadcasted_iota(jnp.int32, shape, 0)
    below = (row >= ny + DEPTH + GAP) & at_lower_wall()
    above = (row >= ny) & (row < ny + DEPTH) & at_upper_wall()
    return below | above


def plane_rates(read, i, rows, ends=None):
    every = range(4)
    centre = [read(f, i) for f in every]
    x_plus = [read(f, i + 1)[:rows] for f in every]
    x_minus = [read(f, i - 1)[:rows] for f in every]
    y_plus = [step(v, 1, 0)[:rows] for v in centre]
    y_minus = [step(v, -1, 0)[:rows] for v in centre]
    centre = [v[:rows] for v in centre]
    upward, downward = centre, centre
    if ends is not None:
        lane = lax.broadcasted_iota(jnp.int32, centre[0].shape, 1)
        upward = [jnp.where(lane == 0, e[:rows], v) for e, v in zip(ends, centre)]
        downward = [jnp.where(lane == lane.shape[1] - 1, e[:rows], v) for e, v in zip(ends, centre)]
    z_plus = [step(v, 1, 1) for v in upward]
    z_minus = [step(v, -1, 1) for v in downward]
    return centre, rates(centre, x_plus, x_minus, y_plus, y_minus, z_plus, z_minus)


def stage_one(outside, value, rate):
    return jnp.where(outside, 0.0, value + DT_STEP * rate)


def stage_two(outside, begin, value, rate):
    return jnp.where(outside, 0.0, 0.75 * begin + 0.25 * (value + DT_STEP * rate))


def first_kernel(sample_hbm, mid_ref, xlo_ref, xhi_ref, one_ref, sample_ref, sem):
    copy = pltpu.make_async_copy(sample_hbm, sample_ref, sem)
    copy.start()
    fields, nx, rows, nz = mid_ref.shape
    outside = beyond_walls(rows - HALO, (rows, nz))
    for i in range(1, nx + 2 * DEPTH - 1):
        centre, rate = plane_rates(functools.partial(plane_of, mid_ref, xlo_ref, xhi_ref), i, rows)
        for f in range(4):
            one_ref[f, i - 1] = stage_one(outside, centre[f], rate[f])
    copy.wait()


def step_kernel(
    mid_ref, xlo_ref, xhi_ref, first_ref, own_ref, low_ref, high_ref, basis_ref, sample_ref,
    flow_ref, snap_ref, cross_ref,
    one_ref, two_ref,
):
    fields, nx, ny, nz = flow_ref.shape
    rows = mid_ref.shape[2]
    modes = basis_ref.shape[1]
    planes = nx + 2 * DEPTH
    lane = lax.broadcasted_iota(jnp.int32, (rows, nz), 1)
    outside = beyond_walls(ny, (rows, nz))
    every = range(4)
    start = functools.partial(plane_of, mid_ref, xlo_ref, xhi_ref)

    left = lane % GROUP < DEPTH

    def window_rates(q):
        return rates(
            q, [step(v, GROUP, 1) for v in q], [step(v, -GROUP, 1) for v in q],
            [step(v, 1, 0) for v in q], [step(v, -1, 0) for v in q],
            [step(v, 1, 1) for v in q], [step(v, -1, 1) for v in q],
        )

    own = [own_ref[f] for f in every]
    other = [jnp.where(left, low_ref[f], high_ref[f]) for f in every]
    windows = []
    for parts in ((other, own), (own, other)):
        q0 = [jnp.where(left, a, b) for a, b in zip(*parts)]
        q1 = [stage_one(outside, v, r) for v, r in zip(q0, window_rates(q0))]
        q2 = [stage_two(outside, s, v, r) for s, v, r in zip(q0, q1, window_rates(q1))]
        windows.append((q1, q2))
    (low_one, low_two), (high_one, high_two) = windows
    ends_one = [jnp.where(left, a, b) for a, b in zip(low_one, high_one)]
    ends_two = [jnp.where(left, a, b) for a, b in zip(low_two, high_two)]
    rim_one = [jnp.where(left, b, a) for a, b in zip(low_one, high_one)]

    def at_plane(values, i):
        return [pltpu.roll(v, (2 * nz - GROUP * i - DEPTH) % nz, 1) for v in values]

    rim = (lane == 0) | (lane == nz - 1)
    for i in range(1, planes - 1):
        for f, value in enumerate(at_plane(rim_one, i)):
            one_ref[f, i - 1] = jnp.where(rim, value, first_ref[f, i - 1])
    for i in range(2, planes - 2):
        centre, rate = plane_rates(lambda f, i: one_ref[f, i - 1], i, rows, at_plane(ends_one, i))
        for f in every:
            two_ref[f, i - 2] = stage_two(outside, start(f, i), centre[f], rate[f])
    for i in range(3, planes - 3):
        centre, rate = plane_rates(lambda f, i: two_ref[f, i - 2], i, ny, at_plane(ends_two, i))
        for f in every:
            value = 1.0 / 3.0 * start(f, i)[:ny] + 2.0 / 3.0 * (centre[f] + DT_STEP * rate[f])
            flow_ref[f, i - DEPTH] = value

    points = sample_ref.shape[1]
    spot = jnp.broadcast_to(sample_ref[...], (nz, points))
    place = lax.broadcasted_iota(jnp.int32, (nx * ny, points), 0)
    in_row = (place == jnp.broadcast_to(sample_ref[...] // nz, (nx * ny, points))).astype(jnp.bfloat16)
    in_lane = lax.broadcasted_iota(jnp.int32, (nz, points), 0) == spot % nz
    product = jnp.zeros((modes + 1, points), jnp.float32)
    for c in range(3):
        field = flow_ref[c].reshape(nx * ny, nz).T
        found = sum(dot_parts(part, in_row, ((1,), (0,))) for part in three_parts(field))
        picked = jnp.sum(jnp.where(in_lane, found, 0.0), axis=0, keepdims=True)
        snap_ref[c] = picked
        product = product + jnp.concatenate([basis_ref[c], picked], axis=0) * picked
    total = jnp.sum(product, axis=1, keepdims=True)
    size = modes + 1
    diagonal = lax.broadcasted_iota(jnp.int32, (size, size), 0) == lax.broadcasted_iota(jnp.int32, (size, size), 1)
    cross_ref[...] = jnp.sum(jnp.where(diagonal, total, 0.0), axis=0, keepdims=True)


def merge_kernel(parts_ref, cross_ref, send_ref):
    total = parts_ref[0]
    for d in range(1, parts_ref.shape[0]):
        total = total + parts_ref[d]
    block = jnp.concatenate([total[: total.shape[0] - 1], cross_ref[...]], axis=0)
    for d in range(send_ref.shape[0]):
        send_ref[d] = block


def final_kernel(
    count, got_ref, parts_ref, snap_ref, flow_ref,
    basis_hbm, factor_hbm, flow_hbm,
    packed_ref, work_ref, basis_out_ref, factor_ref, sems,
):
    _, comps, size, points = parts_ref.shape
    tall = size // 4
    per = got_ref.shape[1] - 1
    copies = [pltpu.make_async_copy(flow_ref, flow_hbm, sems.at[0])]
    copies[0].start()

    total = jnp.zeros((per + 1, size), jnp.float32)
    for d in range(got_ref.shape[0]):
        block = got_ref[d]
        if per * d < packed_ref.shape[0]:
            packed_ref[per * d : per * d + per] = block[0:per]
        total = total + block
    cross = total[per : per + 1] / count
    top = lax.broadcasted_iota(jnp.int32, (16, size), 0)
    mark = (lax.broadcasted_iota(jnp.int32, (16, size), 1) == size - 1) & (top < 3)
    thirds = jnp.zeros((16, size), jnp.float32)
    for k, part in enumerate(three_parts(cross)):
        thirds = jnp.where(top == k, part.astype(jnp.float32), thirds)
    side = dot_parts(thirds.astype(jnp.bfloat16), mark.astype(jnp.bfloat16), ((0,), (0,)))
    lane = lax.broadcasted_iota(jnp.int32, (tall, size), 1)
    row = lax.broadcasted_iota(jnp.int32, (tall, size), 0)
    old = unpack_upper([packed_ref[tall * k : tall * k + tall] / count for k in range(3)], tall)
    for k in range(4):
        value = jnp.where(lane == size - 1, side[tall * k : tall * k + tall], old[k])
        if k == 3:
            value = jnp.where(row == tall - 1, jnp.broadcast_to(cross, value.shape), value)
        work_ref[tall * k : tall * k + tall, 0:size] = value
        work_ref[tall * k : tall * k + tall, size : 2 * size] = (lane == row + tall * k).astype(jnp.float32)

    for k in range(4):
        base = tall * k
        eliminate(work_ref, base, tall, old[0] if k == 0 else None)
        done = work_ref[base : base + tall, :]
        if k < 3:
            change = dot_stacked(done[:, 0:size], done)
            work_ref[base + tall : size, :] = work_ref[base + tall : size, :] - change[base + tall : size]
        factor_ref[base : base + tall, :] = jnp.where(lane >= row + base, done[:, 0:size], 0.0)
        if k == 3:
            copies.append(pltpu.make_async_copy(factor_ref, factor_hbm, sems.at[1]))
            copies[-1].start()
        if k == 0:
            continue
        begin, count_rows = (0, base + tall) if k == 1 else (base, tall)
        inverse = work_ref[begin : base + tall, size : 2 * size]
        pieces = jnp.concatenate(three_parts(inverse), axis=0)
        for c in range(comps):
            value = jnp.zeros((count_rows, points), jnp.float32)
            for n in (2, 1, 0):
                products = dot_parts(pieces[: count_rows * (3 - n)], parts_ref[n, c], ((1,), (0,)))
                for m in range(2 - n, -1, -1):
                    value = value + products[count_rows * m : count_rows * m + count_rows]
            if k == 3:
                value = value + inverse[:, size - 1 : size] * snap_ref[c]
            basis_out_ref[c, begin : base + tall, :] = value
        rows = (slice(None), pl.ds(begin, count_rows), slice(None))
        copies.append(pltpu.make_async_copy(basis_out_ref.at[rows], basis_hbm.at[rows], sems.at[1 + k]))
        copies[-1].start()
    for copy in copies:
        copy.wait()


def eliminate(work_ref, base, tall, early=None):
    blocks = tall // 8
    sub = lax.broadcasted_iota(jnp.int32, (8, 128), 0)
    panel = [work_ref[base + 8 * b : base + 8 * b + 8, :] for b in range(blocks)]
    scale = [jnp.zeros((8, 128), jnp.float32) for _ in range(blocks)]
    half = tall // 2
    for low in (0, half):
        high = low + half
        rows = panel if early is None or low else [early[8 * b : 8 * b + 8] for b in range(blocks)]
        column = {
            k: {b: jnp.broadcast_to(rows[b][:, base + k : base + k + 1], (8, 128)) for b in range(k // 8, blocks)}
            for k in range(low, high)
        }
        for j in range(low, high):
            mine, at = divmod(j, 8)
            pivot = column[j][mine][at : at + 1, :]
            inverse = 1.0 / pivot
            scaled = {b: column[j][b] * inverse for b in range(mine, blocks)}
            for k in range(j + 1, high):
                other, place = divmod(k, 8)
                times = scaled[other][place : place + 1, :]
                for b in range(other, blocks):
                    column[k][b] = column[k][b] - column[j][b] * times
            scale[mine] = jnp.where(sub == at, lax.rsqrt(pivot), scale[mine])
            pivot_row = panel[mine][at : at + 1, :]
            for b in range(mine, blocks):
                times = jnp.where(sub > at, scaled[b], 0.0) if b == mine else scaled[b]
                panel[b] = panel[b] - jnp.concatenate([times, times], axis=1) * pivot_row
    for b in range(blocks):
        work_ref[base + 8 * b : base + 8 * b + 8, :] = panel[b] * jnp.concatenate([scale[b], scale[b]], axis=1)


def local(flow, basis, sample):
    fields, nx, ny, nz = flow.shape
    modes, comps, points = basis.shape
    size = modes + 1
    devices = lax.axis_size("gx") * lax.axis_size("gy") * lax.axis_size("gz")
    count = float(comps * points * devices)
    shape = functools.partial(jax.ShapeDtypeStruct, dtype=jnp.float32)
    call = functools.partial(pl.pallas_call, compiler_params=PARAMS)
    bricks = jnp.transpose(basis, (1, 0, 2))

    whole = pl.BlockSpec(memory_space=pltpu.HBM)
    flat = flow.reshape(fields, nx * ny, nz)
    quarter = size // 4
    per = -(-3 * quarter // devices)

    strip = shape((fields, nx * DEPTH, nz))
    strips = call(
        functools.partial(strips_kernel, nx), out_shape=(strip, strip), in_specs=[VMEM], out_specs=(VMEM, VMEM)
    )(flat)
    y_even, y_odd = pairs(*strips, "gy", "gz")
    gram, basis_parts = call(
        gram_kernel,
        out_shape=(shape((devices, per + 1, size)), jax.ShapeDtypeStruct((3, comps, size, points), jnp.bfloat16)),
        in_specs=[VMEM],
        out_specs=(VMEM, VMEM),
        scratch_shapes=[pltpu.VMEM((size, size), jnp.float32), pltpu.VMEM((devices * per, size), jnp.float32)],
    )(bricks)
    y_odd, y_even, gram = lax.optimization_barrier((y_odd, y_even, gram))

    rows = ny + HALO
    face = shape((fields, DEPTH * ny + HALO, nz))
    mid, first, last = call(
        functools.partial(walls_kernel, nx),
        out_shape=(shape((fields, nx * rows, nz)), face, face),
        in_specs=[VMEM] * 3,
        out_specs=(VMEM,) * 3,
    )(flat, y_odd, y_even)
    mid = mid.reshape(fields, nx, rows, nz)
    low_face, high_face = neighbours(first, last, "gx")
    parts = lax.all_to_all(gram, ALL, 0, 0)

    beside = shape((fields, DEPTH, rows, nz))
    packed, xlo, xhi = call(
        pack_kernel,
        out_shape=(shape((fields, rows, nz)), beside, beside),
        in_specs=[VMEM] * 3,
        out_specs=(VMEM,) * 3,
    )(mid, low_face, high_face)
    if lax.axis_size("gz") == 2:
        low = high = lax.ppermute(packed, "gz", [(0, 1), (1, 0)])
    else:
        low, high = neighbours(packed, packed, "gz")
    begun, cells = call(
        first_kernel,
        out_shape=(
            shape((fields, nx + 2 * DEPTH - 2, rows, nz)),
            jax.ShapeDtypeStruct((1, points), sample.dtype),
        ),
        in_specs=[whole] + [VMEM] * 3,
        out_specs=(VMEM, VMEM),
        scratch_shapes=[pltpu.SemaphoreType.DMA],
    )(sample.reshape(1, points), mid, xlo, xhi)
    flow_new, snapshot, cross = call(
        step_kernel,
        out_shape=(shape(flow.shape), shape((comps, 1, points)), shape((1, size))),
        in_specs=[VMEM] * 9,
        out_specs=(VMEM, VMEM, VMEM),
        scratch_shapes=[
            pltpu.VMEM((fields, nx + 2 * DEPTH - 2, rows, nz), jnp.float32),
            pltpu.VMEM((fields, nx + 2 * DEPTH - 4, rows, nz), jnp.float32),
        ],
    )(mid, xlo, xhi, begun, packed, low, high, bricks, cells)

    send = call(
        merge_kernel, out_shape=shape((devices, per + 1, size)), in_specs=[VMEM] * 2, out_specs=VMEM
    )(parts, cross)
    got = lax.all_to_all(send, ALL, 0, 0)
    basis_next, factor, flow_next = call(
        functools.partial(final_kernel, count),
        out_shape=(shape((comps, size, points)), shape((size, size)), shape(flow.shape)),
        in_specs=[VMEM] * 4,
        out_specs=(whole,) * 3,
        scratch_shapes=[
            pltpu.VMEM((3 * quarter, size), jnp.float32),
            pltpu.VMEM((size, 2 * size), jnp.float32),
            pltpu.VMEM((comps, size, points), jnp.float32),
            pltpu.VMEM((size, size), jnp.float32),
            pltpu.SemaphoreType.DMA((5,)),
        ],
    )(got, basis_parts, snapshot, flow_new)
    return flow_next, jnp.transpose(basis_next, (1, 0, 2)), factor


def solution(mesh):
    return jax.shard_map(
        local,
        mesh=mesh,
        in_specs=(
            P(None, "gx", "gy", "gz"),
            P(None, None, ("gx", "gy", "gz")),
            P(("gx", "gy", "gz")),
        ),
        out_specs=(P(None, "gx", "gy", "gz"), P(None, None, ("gx", "gy", "gz")), P()),
        check_vma=False,
    )
```

```python
import functools

import jax
import jax.numpy as jnp
from jax import lax
from jax.experimental import pallas as pl
from jax.experimental.pallas import tpu as pltpu
from jax.sharding import PartitionSpec as P

DT_STEP = 0.35
VISCOSITY = 0.2
SOUND_SQ = 1.0
DRIVING = 0.5

ALL = ("gz", "gy", "gx")
DEPTH = 3
EXACT = lax.Precision.HIGHEST
VMEM = pl.BlockSpec(memory_space=pltpu.VMEM)
PARAMS = pltpu.CompilerParams(vmem_limit_bytes=40 * 1024 * 1024)


def dot(a, b, dims):
    return lax.dot_general(
        a, b, (dims, ((), ())), precision=EXACT, preferred_element_type=jnp.float32
    )


def three_parts(value):
    high = value.astype(jnp.bfloat16)
    rest = value - high.astype(jnp.float32)
    middle = rest.astype(jnp.bfloat16)
    return high, middle, (rest - middle.astype(jnp.float32)).astype(jnp.bfloat16)


def dot_parts(a, b, dims):
    return lax.dot_general(a, b, (dims, ((), ())), preferred_element_type=jnp.float32)


def dot_stacked(a, b):
    (a1, a2, a3), (b1, b2, b3) = three_parts(a), three_parts(b)
    first = jnp.concatenate([a1, a1, a2, a2, a1, a3], axis=0)
    second = jnp.concatenate([b1, b2, b1, b2, b3, b1], axis=0)
    return dot_parts(first, second, ((0,), (0,)))


def neighbours(block_low, block_high, axis):
    count = lax.axis_size(axis)
    forward = [(i, (i + 1) % count) for i in range(count)]
    backward = [(target, source) for source, target in forward]
    return lax.ppermute(block_high, axis, forward), lax.ppermute(block_low, axis, backward)


def pairs(block_odd, block_even, axis, other):
    count, width = lax.axis_size(axis), lax.axis_size(other)
    even = [(i, i + 1 - 2 * (i % 2)) for i in range(count)]
    odd = []
    for i in range(count):
        for k in range(width):
            to = (i, k + 1 - 2 * (k % 2)) if i in (0, count - 1) else (i - 1 + 2 * (i % 2), k)
            odd.append((i * width + k, to[0] * width + to[1]))
    from_odd = lax.ppermute(block_odd, (axis, other), odd)
    return lax.ppermute(block_even, axis, even), from_odd


def at_lower_wall():
    return lax.axis_index("gy") == 0


def at_upper_wall():
    return lax.axis_index("gy") == lax.axis_size("gy") - 1


def odd_place():
    return lax.axis_index("gy") % 2 == 1


def pack_upper(rows, tall):
    size = rows.shape[1]
    lane = lax.broadcasted_iota(jnp.int32, (tall, size), 1)
    part = [rows[tall * k : tall * k + tall] for k in range(4)]
    return [part[0], jnp.where(lane >= tall, part[1], pltpu.roll(part[3], tall, 1)), part[2]]


def unpack_upper(packed, tall):
    return [packed[0], packed[1], packed[2], pltpu.roll(packed[1], packed[1].shape[1] - tall, 1)]


def gram_kernel(basis_ref, send_ref, parts_ref, gram_ref, packed_ref):
    modes = basis_ref.shape[1]
    tall = gram_ref.shape[0] // 4
    total = jnp.zeros((modes, modes), jnp.float32)
    for c in range(basis_ref.shape[0]):
        rows = basis_ref[c]
        total = total + dot(rows, rows, ((1,), (1,)))
        filled = jnp.concatenate([rows, jnp.zeros((1, rows.shape[1]), jnp.float32)], axis=0)
        for k, part in enumerate(three_parts(filled)):
            parts_ref[k, c] = part
    gram_ref[...] = jnp.zeros_like(gram_ref)
    gram_ref[0:modes, 0:modes] = total
    packed_ref[...] = jnp.zeros_like(packed_ref)
    for k, value in enumerate(pack_upper(gram_ref[...], tall)):
        packed_ref[tall * k : tall * k + tall] = value
    per = send_ref.shape[1] - 1
    empty = jnp.zeros((1, send_ref.shape[2]), jnp.float32)
    for d in range(send_ref.shape[0]):
        send_ref[d] = jnp.concatenate([packed_ref[per * d : per * d + per], empty], axis=0)


GAP = 2
HALO = 2 * DEPTH + GAP


def strips_kernel(planes, flow_hbm, odd_ref, even_ref, flow_ref, sems):
    ny = flow_ref.shape[1] // planes
    odd = odd_place()
    copies = [
        pltpu.make_async_copy(flow_hbm.at[f], flow_ref.at[f], sems.at[f]) for f in range(flow_ref.shape[0])
    ]
    for copy in copies:
        copy.start()
    for f, copy in enumerate(copies):
        copy.wait()
        for j in range(DEPTH):
            bottom = flow_ref[f, pl.ds(j, planes, stride=ny), :]
            top = flow_ref[f, pl.ds(ny - DEPTH + j, planes, stride=ny), :]
            even_ref[f, planes * j : planes * j + planes] = jnp.where(odd, bottom, top)
            odd_ref[f, planes * j : planes * j + planes] = jnp.where(odd, top, bottom)


def walls_kernel(planes, flow_ref, odd_ref, even_ref, mid_ref, first_ref, last_ref):
    fields, cells, nz = flow_ref.shape
    odd_y = odd_place()
    ny = cells // planes
    rows = ny + HALO
    sub = lax.broadcasted_iota(jnp.int32, (HALO, nz), 0)
    empty = jnp.zeros((planes, nz), jnp.float32)
    for f in range(fields):
        for i in range(planes):
            mid_ref[f, rows * i : rows * i + ny] = flow_ref[f, ny * i : ny * i + ny]
        for j in range(HALO):
            k = j if j < DEPTH else j - DEPTH - GAP
            part = slice(planes * k, planes * k + planes)
            if j < DEPTH:
                value = jnp.where(odd_y, odd_ref[f, part], even_ref[f, part])
                value = jnp.where(at_upper_wall(), 0.0, value)
            elif j < DEPTH + GAP:
                value = empty
            else:
                value = jnp.where(odd_y, even_ref[f, part], odd_ref[f, part])
                value = jnp.where(at_lower_wall(), 0.0, value)
            mid_ref[f, pl.ds(ny + j, planes, stride=rows), :] = value
        for face_ref, begin, near, next_one in (
            (first_ref, 0, 0, 1), (last_ref, planes - DEPTH, planes - 1, planes - 2)
        ):
            for k in range(DEPTH):
                face_ref[f, ny * k : ny * k + ny] = flow_ref[f, ny * (begin + k) : ny * (begin + k) + ny]
            halos = [mid_ref[f, rows * i + ny : rows * i + rows] for i in (near, next_one)]
            face_ref[f, ny * DEPTH : ny * DEPTH + HALO] = corner_rows(*halos, sub)


def corner_rows(near, next_one, sub):
    tile = jnp.where(sub == 2, pltpu.roll(next_one, 2, 0), pltpu.roll(next_one, 6, 0))
    tile = jnp.where((sub == 2) | (sub == 5), tile, 0.0)
    return jnp.where((sub < 2) | (sub >= 6), near, tile)


def corner_planes(tile, sub):
    near = jnp.where((sub < 2) | (sub >= 6), tile, 0.0)
    next_one = jnp.where(sub == 0, pltpu.roll(tile, 6, 0), pltpu.roll(tile, 2, 0))
    return [near, jnp.where((sub == 0) | (sub == 7), next_one, 0.0), jnp.zeros_like(tile)]


def plane_of(mid_ref, xlo_ref, xhi_ref, f, i):
    nx = mid_ref.shape[1]
    if i < DEPTH:
        return xlo_ref[f, i]
    if i < DEPTH + nx:
        return mid_ref[f, i - DEPTH]
    return xhi_ref[f, i - DEPTH - nx]


GROUP = 8


def pack_kernel(mid_ref, low_ref, high_ref, packed_ref, xlo_ref, xhi_ref):
    fields, nx, rows, nz = mid_ref.shape
    ny = rows - HALO
    lane = lax.broadcasted_iota(jnp.int32, (rows, nz), 1)
    sub = lax.broadcasted_iota(jnp.int32, (HALO, nz), 0)
    for f in range(fields):
        for face_ref, out_ref, order in ((low_ref, xlo_ref, (2, 1, 0)), (high_ref, xhi_ref, (0, 1, 2))):
            face = face_ref[f]
            halo = corner_planes(face[ny * DEPTH :], sub)
            for k in range(DEPTH):
                out_ref[f, k, 0:ny] = face[ny * k : ny * k + ny]
                out_ref[f, k, ny:rows] = halo[order[k]]
        value = jnp.zeros((rows, nz), jnp.float32)
        for i in range(nx + 2 * DEPTH):
            start = GROUP * i
            moved = pltpu.roll(plane_of(mid_ref, xlo_ref, xhi_ref, f, i), (start + DEPTH) % nz, 1)
            value = jnp.where((lane >= start) & (lane < start + 2 * DEPTH), moved, value)
        packed_ref[f] = value


def step(value, by, axis):
    size = value.shape[axis]
    return pltpu.roll(value, (size - by) % size, axis)


def rates(centre, x_plus, x_minus, y_plus, y_minus, z_plus, z_minus):
    slope_x = [0.5 * (a - b) for a, b in zip(x_plus, x_minus)]
    slope_y = [0.5 * (a - b) for a, b in zip(y_plus, y_minus)]
    slope_z = [0.5 * (a - b) for a, b in zip(z_plus, z_minus)]
    pressure = [slope_x[3], slope_y[3], slope_z[3]]
    out = []
    for f in range(3):
        laplace = (
            x_plus[f] + x_minus[f] + (y_plus[f] + y_minus[f]) + (z_plus[f] + z_minus[f]) - 6.0 * centre[f]
        )
        advect = centre[0] * slope_x[f] + centre[1] * slope_y[f] + centre[2] * slope_z[f]
        value = VISCOSITY * laplace - advect - pressure[f]
        if f == 0:
            value = value + DRIVING
        out.append(value)
    out.append(-SOUND_SQ * (slope_x[0] + slope_y[1] + slope_z[2]))
    return out


def beyond_walls(ny, shape):
    row = lax.broadcasted_iota(jnp.int32, shape, 0)
    below = (row >= ny + DEPTH + GAP) & at_lower_wall()
    above = (row >= ny) & (row < ny + DEPTH) & at_upper_wall()
    return below | above


def plane_rates(read, i, rows, ends=None):
    every = range(4)
    centre = [read(f, i) for f in every]
    x_plus = [read(f, i + 1)[:rows] for f in every]
    x_minus = [read(f, i - 1)[:rows] for f in every]
    y_plus = [step(v, 1, 0)[:rows] for v in centre]
    y_minus = [step(v, -1, 0)[:rows] for v in centre]
    centre = [v[:rows] for v in centre]
    upward, downward = centre, centre
    if ends is not None:
        lane = lax.broadcasted_iota(jnp.int32, centre[0].shape, 1)
        upward = [jnp.where(lane == 0, e[:rows], v) for e, v in zip(ends, centre)]
        downward = [jnp.where(lane == lane.shape[1] - 1, e[:rows], v) for e, v in zip(ends, centre)]
    z_plus = [step(v, 1, 1) for v in upward]
    z_minus = [step(v, -1, 1) for v in downward]
    return centre, rates(centre, x_plus, x_minus, y_plus, y_minus, z_plus, z_minus)


def stage_one(outside, value, rate):
    return jnp.where(outside, 0.0, value + DT_STEP * rate)


def stage_two(outside, begin, value, rate):
    return jnp.where(outside, 0.0, 0.75 * begin + 0.25 * (value + DT_STEP * rate))


def first_kernel(sample_hbm, mid_ref, xlo_ref, xhi_ref, one_ref, sample_ref, sem):
    copy = pltpu.make_async_copy(sample_hbm, sample_ref, sem)
    copy.start()
    fields, nx, rows, nz = mid_ref.shape
    outside = beyond_walls(rows - HALO, (rows, nz))
    for i in range(1, nx + 2 * DEPTH - 1):
        centre, rate = plane_rates(functools.partial(plane_of, mid_ref, xlo_ref, xhi_ref), i, rows)
        for f in range(4):
            one_ref[f, i - 1] = stage_one(outside, centre[f], rate[f])
    copy.wait()


def step_kernel(
    mid_ref, xlo_ref, xhi_ref, first_ref, own_ref, low_ref, high_ref, basis_ref, sample_ref,
    flow_ref, snap_ref, cross_ref,
    one_ref, two_ref,
):
    fields, nx, ny, nz = flow_ref.shape
    rows = mid_ref.shape[2]
    modes = basis_ref.shape[1]
    planes = nx + 2 * DEPTH
    lane = lax.broadcasted_iota(jnp.int32, (rows, nz), 1)
    outside = beyond_walls(ny, (rows, nz))
    every = range(4)
    start = functools.partial(plane_of, mid_ref, xlo_ref, xhi_ref)

    left = lane % GROUP < DEPTH

    def window_rates(q):
        return rates(
            q, [step(v, GROUP, 1) for v in q], [step(v, -GROUP, 1) for v in q],
            [step(v, 1, 0) for v in q], [step(v, -1, 0) for v in q],
            [step(v, 1, 1) for v in q], [step(v, -1, 1) for v in q],
        )

    own = [own_ref[f] for f in every]
    other = [jnp.where(left, low_ref[f], high_ref[f]) for f in every]
    windows = []
    for parts in ((other, own), (own, other)):
        q0 = [jnp.where(left, a, b) for a, b in zip(*parts)]
        q1 = [stage_one(outside, v, r) for v, r in zip(q0, window_rates(q0))]
        q2 = [stage_two(outside, s, v, r) for s, v, r in zip(q0, q1, window_rates(q1))]
        windows.append((q1, q2))
    (low_one, low_two), (high_one, high_two) = windows
    ends_one = [jnp.where(left, a, b) for a, b in zip(low_one, high_one)]
    ends_two = [jnp.where(left, a, b) for a, b in zip(low_two, high_two)]
    rim_one = [jnp.where(left, b, a) for a, b in zip(low_one, high_one)]

    def at_plane(values, i):
        return [pltpu.roll(v, (2 * nz - GROUP * i - DEPTH) % nz, 1) for v in values]

    rim = (lane == 0) | (lane == nz - 1)
    for i in range(1, planes - 1):
        for f, value in enumerate(at_plane(rim_one, i)):
            one_ref[f, i - 1] = jnp.where(rim, value, first_ref[f, i - 1])
    for i in range(2, planes - 2):
        centre, rate = plane_rates(lambda f, i: one_ref[f, i - 1], i, rows, at_plane(ends_one, i))
        for f in every:
            two_ref[f, i - 2] = stage_two(outside, start(f, i), centre[f], rate[f])
    for i in range(3, planes - 3):
        centre, rate = plane_rates(lambda f, i: two_ref[f, i - 2], i, ny, at_plane(ends_two, i))
        for f in every:
            value = 1.0 / 3.0 * start(f, i)[:ny] + 2.0 / 3.0 * (centre[f] + DT_STEP * rate[f])
            flow_ref[f, i - DEPTH] = value

    points = sample_ref.shape[1]
    spot = jnp.broadcast_to(sample_ref[...], (nz, points))
    place = lax.broadcasted_iota(jnp.int32, (nx * ny, points), 0)
    in_row = (place == jnp.broadcast_to(sample_ref[...] // nz, (nx * ny, points))).astype(jnp.bfloat16)
    in_lane = lax.broadcasted_iota(jnp.int32, (nz, points), 0) == spot % nz
    product = jnp.zeros((modes + 1, points), jnp.float32)
    for c in range(3):
        field = flow_ref[c].reshape(nx * ny, nz).T
        found = sum(dot_parts(part, in_row, ((1,), (0,))) for part in three_parts(field))
        picked = jnp.sum(jnp.where(in_lane, found, 0.0), axis=0, keepdims=True)
        snap_ref[c] = picked
        product = product + jnp.concatenate([basis_ref[c], picked], axis=0) * picked
    total = jnp.sum(product, axis=1, keepdims=True)
    size = modes + 1
    diagonal = lax.broadcasted_iota(jnp.int32, (size, size), 0) == lax.broadcasted_iota(jnp.int32, (size, size), 1)
    cross_ref[...] = jnp.sum(jnp.where(diagonal, total, 0.0), axis=0, keepdims=True)


def merge_kernel(parts_ref, cross_ref, send_ref):
    total = parts_ref[0]
    for d in range(1, parts_ref.shape[0]):
        total = total + parts_ref[d]
    block = jnp.concatenate([total[: total.shape[0] - 1], cross_ref[...]], axis=0)
    for d in range(send_ref.shape[0]):
        send_ref[d] = block


def final_kernel(
    count, got_ref, parts_ref, snap_ref, flow_ref,
    basis_hbm, factor_hbm, flow_hbm,
    packed_ref, work_ref, basis_out_ref, factor_ref, sems,
):
    _, comps, size, points = parts_ref.shape
    tall = size // 4
    per = got_ref.shape[1] - 1
    copies = [pltpu.make_async_copy(flow_ref, flow_hbm, sems.at[0])]
    copies[0].start()

    total = jnp.zeros((per + 1, size), jnp.float32)
    for d in range(got_ref.shape[0]):
        block = got_ref[d]
        if per * d < packed_ref.shape[0]:
            packed_ref[per * d : per * d + per] = block[0:per]
        total = total + block
    cross = total[per : per + 1] / count
    top = lax.broadcasted_iota(jnp.int32, (16, size), 0)
    mark = (lax.broadcasted_iota(jnp.int32, (16, size), 1) == size - 1) & (top < 3)
    thirds = jnp.zeros((16, size), jnp.float32)
    for k, part in enumerate(three_parts(cross)):
        thirds = jnp.where(top == k, part.astype(jnp.float32), thirds)
    side = dot_parts(thirds.astype(jnp.bfloat16), mark.astype(jnp.bfloat16), ((0,), (0,)))
    lane = lax.broadcasted_iota(jnp.int32, (tall, size), 1)
    row = lax.broadcasted_iota(jnp.int32, (tall, size), 0)
    old = unpack_upper([packed_ref[tall * k : tall * k + tall] / count for k in range(3)], tall)
    for k in range(4):
        value = jnp.where(lane == size - 1, side[tall * k : tall * k + tall], old[k])
        if k == 3:
            value = jnp.where(row == tall - 1, jnp.broadcast_to(cross, value.shape), value)
        work_ref[tall * k : tall * k + tall, 0:size] = value
        work_ref[tall * k : tall * k + tall, size : 2 * size] = (lane == row + tall * k).astype(jnp.float32)

    for k in range(4):
        base = tall * k
        eliminate(work_ref, base, tall, old[0] if k == 0 else None)
        done = work_ref[base : base + tall, :]
        if k < 3:
            change = dot_stacked(done[:, 0:size], done)
            work_ref[base + tall : size, :] = work_ref[base + tall : size, :] - change[base + tall : size]
        factor_ref[base : base + tall, :] = jnp.where(lane >= row + base, done[:, 0:size], 0.0)
        if k == 3:
            copies.append(pltpu.make_async_copy(factor_ref, factor_hbm, sems.at[1]))
            copies[-1].start()
        if k == 0:
            continue
        begin, count_rows = (0, base + tall) if k == 1 else (base, tall)
        inverse = work_ref[begin : base + tall, size : 2 * size]
        pieces = jnp.concatenate(three_parts(inverse), axis=0)
        for c in range(comps):
            value = jnp.zeros((count_rows, points), jnp.float32)
            for n in (2, 1, 0):
                products = dot_parts(pieces[: count_rows * (3 - n)], parts_ref[n, c], ((1,), (0,)))
                for m in range(2 - n, -1, -1):
                    value = value + products[count_rows * m : count_rows * m + count_rows]
            if k == 3:
                value = value + inverse[:, size - 1 : size] * snap_ref[c]
            basis_out_ref[c, begin : base + tall, :] = value
        rows = (slice(None), pl.ds(begin, count_rows), slice(None))
        copies.append(pltpu.make_async_copy(basis_out_ref.at[rows], basis_hbm.at[rows], sems.at[1 + k]))
        copies[-1].start()
    for copy in copies:
        copy.wait()


def eliminate(work_ref, base, tall, early=None):
    blocks = tall // 8
    sub = lax.broadcasted_iota(jnp.int32, (8, 128), 0)
    panel = [work_ref[base + 8 * b : base + 8 * b + 8, :] for b in range(blocks)]
    scale = [jnp.zeros((8, 128), jnp.float32) for _ in range(blocks)]
    half = tall // 2
    for low in (0, half):
        high = low + half
        rows = panel if early is None or low else [early[8 * b : 8 * b + 8] for b in range(blocks)]
        column = {
            k: {b: jnp.broadcast_to(rows[b][:, base + k : base + k + 1], (8, 128)) for b in range(k // 8, blocks)}
            for k in range(low, high)
        }
        for j in range(low, high):
            mine, at = divmod(j, 8)
            pivot = column[j][mine][at : at + 1, :]
            inverse = 1.0 / pivot
            scaled = {b: column[j][b] * inverse for b in range(mine, blocks)}
            for k in range(j + 1, high):
                other, place = divmod(k, 8)
                times = scaled[other][place : place + 1, :]
                for b in range(other, blocks):
                    column[k][b] = column[k][b] - column[j][b] * times
            scale[mine] = jnp.where(sub == at, lax.rsqrt(pivot), scale[mine])
            pivot_row = panel[mine][at : at + 1, :]
            for b in range(mine, blocks):
                times = jnp.where(sub > at, scaled[b], 0.0) if b == mine else scaled[b]
                panel[b] = panel[b] - jnp.concatenate([times, times], axis=1) * pivot_row
    for b in range(blocks):
        work_ref[base + 8 * b : base + 8 * b + 8, :] = panel[b] * jnp.concatenate([scale[b], scale[b]], axis=1)


def local(flow, basis, sample):
    fields, nx, ny, nz = flow.shape
    modes, comps, points = basis.shape
    size = modes + 1
    devices = lax.axis_size("gx") * lax.axis_size("gy") * lax.axis_size("gz")
    count = float(comps * points * devices)
    shape = functools.partial(jax.ShapeDtypeStruct, dtype=jnp.float32)
    call = functools.partial(pl.pallas_call, compiler_params=PARAMS)
    bricks = jnp.transpose(basis, (1, 0, 2))

    whole = pl.BlockSpec(memory_space=pltpu.HBM)
    flat = flow.reshape(fields, nx * ny, nz)
    quarter = size // 4
    per = -(-3 * quarter // devices)

    strip = shape((fields, nx * DEPTH, nz))
    strips = call(
        functools.partial(strips_kernel, nx),
        out_shape=(strip, strip),
        in_specs=[whole],
        out_specs=(VMEM, VMEM),
        scratch_shapes=[pltpu.VMEM(flat.shape, jnp.float32), pltpu.SemaphoreType.DMA((fields,))],
    )(pltpu.with_memory_space_constraint(flat, pltpu.HBM))
    y_even, y_odd = pairs(*strips, "gy", "gz")
    gram, basis_parts = call(
        gram_kernel,
        out_shape=(shape((devices, per + 1, size)), jax.ShapeDtypeStruct((3, comps, size, points), jnp.bfloat16)),
        in_specs=[VMEM],
        out_specs=(VMEM, VMEM),
        scratch_shapes=[pltpu.VMEM((size, size), jnp.float32), pltpu.VMEM((devices * per, size), jnp.float32)],
    )(bricks)
    y_odd, y_even, gram = lax.optimization_barrier((y_odd, y_even, gram))

    rows = ny + HALO
    face = shape((fields, DEPTH * ny + HALO, nz))
    mid, first, last = call(
        functools.partial(walls_kernel, nx),
        out_shape=(shape((fields, nx * rows, nz)), face, face),
        in_specs=[VMEM] * 3,
        out_specs=(VMEM,) * 3,
    )(flat, y_odd, y_even)
    mid = mid.reshape(fields, nx, rows, nz)
    low_face, high_face = neighbours(first, last, "gx")
    parts = lax.all_to_all(gram, ALL, 0, 0)

    beside = shape((fields, DEPTH, rows, nz))
    packed, xlo, xhi = call(
        pack_kernel,
        out_shape=(shape((fields, rows, nz)), beside, beside),
        in_specs=[VMEM] * 3,
        out_specs=(VMEM,) * 3,
    )(mid, low_face, high_face)
    if lax.axis_size("gz") == 2:
        low = high = lax.ppermute(packed, "gz", [(0, 1), (1, 0)])
    else:
        low, high = neighbours(packed, packed, "gz")
    begun, cells = call(
        first_kernel,
        out_shape=(
            shape((fields, nx + 2 * DEPTH - 2, rows, nz)),
            jax.ShapeDtypeStruct((1, points), sample.dtype),
        ),
        in_specs=[whole] + [VMEM] * 3,
        out_specs=(VMEM, VMEM),
        scratch_shapes=[pltpu.SemaphoreType.DMA],
    )(sample.reshape(1, points), mid, xlo, xhi)
    flow_new, snapshot, cross = call(
        step_kernel,
        out_shape=(shape(flow.shape), shape((comps, 1, points)), shape((1, size))),
        in_specs=[VMEM] * 9,
        out_specs=(VMEM, VMEM, VMEM),
        scratch_shapes=[
            pltpu.VMEM((fields, nx + 2 * DEPTH - 2, rows, nz), jnp.float32),
            pltpu.VMEM((fields, nx + 2 * DEPTH - 4, rows, nz), jnp.float32),
        ],
    )(mid, xlo, xhi, begun, packed, low, high, bricks, cells)

    send = call(
        merge_kernel, out_shape=shape((devices, per + 1, size)), in_specs=[VMEM] * 2, out_specs=VMEM
    )(parts, cross)
    got = lax.all_to_all(send, ALL, 0, 0)
    basis_next, factor, flow_next = call(
        functools.partial(final_kernel, count),
        out_shape=(shape((comps, size, points)), shape((size, size)), shape(flow.shape)),
        in_specs=[VMEM] * 4,
        out_specs=(whole,) * 3,
        scratch_shapes=[
            pltpu.VMEM((3 * quarter, size), jnp.float32),
            pltpu.VMEM((size, 2 * size), jnp.float32),
            pltpu.VMEM((comps, size, points), jnp.float32),
            pltpu.VMEM((size, size), jnp.float32),
            pltpu.SemaphoreType.DMA((5,)),
        ],
    )(got, basis_parts, snapshot, flow_new)
    return flow_next, jnp.transpose(basis_next, (1, 0, 2)), factor


def solution(mesh):
    return jax.shard_map(
        local,
        mesh=mesh,
        in_specs=(
            P(None, "gx", "gy", "gz"),
            P(None, None, ("gx", "gy", "gz")),
            P(("gx", "gy", "gz")),
        ),
        out_specs=(P(None, "gx", "gy", "gz"), P(None, None, ("gx", "gy", "gz")), P()),
        check_vma=False,
    )
```

```python
import functools

import jax
import jax.numpy as jnp
from jax import lax
from jax.experimental import pallas as pl
from jax.experimental.pallas import tpu as pltpu
from jax.sharding import PartitionSpec as P

DT_STEP = 0.35
VISCOSITY = 0.2
SOUND_SQ = 1.0
DRIVING = 0.5

ALL = ("gz", "gy", "gx")
DEPTH = 3
EXACT = lax.Precision.HIGHEST
VMEM = pl.BlockSpec(memory_space=pltpu.VMEM)
PARAMS = pltpu.CompilerParams(vmem_limit_bytes=40 * 1024 * 1024)


def dot(a, b, dims):
    return lax.dot_general(
        a, b, (dims, ((), ())), precision=EXACT, preferred_element_type=jnp.float32
    )


def three_parts(value):
    high = value.astype(jnp.bfloat16)
    rest = value - high.astype(jnp.float32)
    middle = rest.astype(jnp.bfloat16)
    return high, middle, (rest - middle.astype(jnp.float32)).astype(jnp.bfloat16)


def dot_parts(a, b, dims):
    return lax.dot_general(a, b, (dims, ((), ())), preferred_element_type=jnp.float32)


def dot_stacked(a, b):
    (a1, a2, a3), (b1, b2, b3) = three_parts(a), three_parts(b)
    first = jnp.concatenate([a1, a1, a2, a2, a1, a3], axis=0)
    second = jnp.concatenate([b1, b2, b1, b2, b3, b1], axis=0)
    return dot_parts(first, second, ((0,), (0,)))


def neighbours(block_low, block_high, axis):
    count = lax.axis_size(axis)
    forward = [(i, (i + 1) % count) for i in range(count)]
    backward = [(target, source) for source, target in forward]
    return lax.ppermute(block_high, axis, forward), lax.ppermute(block_low, axis, backward)


def pairs(block_odd, block_even, axis, other):
    count, width = lax.axis_size(axis), lax.axis_size(other)
    even = [(i, i + 1 - 2 * (i % 2)) for i in range(count)]
    odd = []
    for i in range(count):
        for k in range(width):
            to = (i, k + 1 - 2 * (k % 2)) if i in (0, count - 1) else (i - 1 + 2 * (i % 2), k)
            odd.append((i * width + k, to[0] * width + to[1]))
    from_odd = lax.ppermute(block_odd, (axis, other), odd)
    return lax.ppermute(block_even, axis, even), from_odd


def ring_pairs(block_odd, block_even, axis):
    count = lax.axis_size(axis)
    even = [(i, i + 1 - 2 * (i % 2)) for i in range(count)]
    odd = [(i, (i - 1 + 2 * (i % 2)) % count) for i in range(count)]
    from_odd = lax.ppermute(block_odd, axis, odd)
    return lax.ppermute(block_even, axis, even), from_odd


def at_lower_wall():
    return lax.axis_index("gy") == 0


def at_upper_wall():
    return lax.axis_index("gy") == lax.axis_size("gy") - 1


def odd_place(axis="gy"):
    return lax.axis_index(axis) % 2 == 1


def pack_upper(rows, tall):
    size = rows.shape[1]
    lane = lax.broadcasted_iota(jnp.int32, (tall, size), 1)
    part = [rows[tall * k : tall * k + tall] for k in range(4)]
    return [part[0], jnp.where(lane >= tall, part[1], pltpu.roll(part[3], tall, 1)), part[2]]


def unpack_upper(packed, tall):
    return [packed[0], packed[1], packed[2], pltpu.roll(packed[1], packed[1].shape[1] - tall, 1)]


def gram_kernel(basis_ref, send_ref, parts_ref, gram_ref, packed_ref):
    modes = basis_ref.shape[1]
    tall = gram_ref.shape[0] // 4
    total = jnp.zeros((modes, modes), jnp.float32)
    for c in range(basis_ref.shape[0]):
        rows = basis_ref[c]
        total = total + dot(rows, rows, ((1,), (1,)))
        filled = jnp.concatenate([rows, jnp.zeros((1, rows.shape[1]), jnp.float32)], axis=0)
        for k, part in enumerate(three_parts(filled)):
            parts_ref[k, c] = part
    gram_ref[...] = jnp.zeros_like(gram_ref)
    gram_ref[0:modes, 0:modes] = total
    packed_ref[...] = jnp.zeros_like(packed_ref)
    for k, value in enumerate(pack_upper(gram_ref[...], tall)):
        packed_ref[tall * k : tall * k + tall] = value
    per = send_ref.shape[1] - 1
    empty = jnp.zeros((1, send_ref.shape[2]), jnp.float32)
    for d in range(send_ref.shape[0]):
        send_ref[d] = jnp.concatenate([packed_ref[per * d : per * d + per], empty], axis=0)


GAP = 2
HALO = 2 * DEPTH + GAP


def strips_kernel(planes, flow_ref, odd_ref, even_ref):
    ny = flow_ref.shape[1] // planes
    odd = odd_place()
    for f in range(flow_ref.shape[0]):
        for j in range(DEPTH):
            bottom = flow_ref[f, pl.ds(j, planes, stride=ny), :]
            top = flow_ref[f, pl.ds(ny - DEPTH + j, planes, stride=ny), :]
            even_ref[f, planes * j : planes * j + planes] = jnp.where(odd, bottom, top)
            odd_ref[f, planes * j : planes * j + planes] = jnp.where(odd, top, bottom)


def walls_kernel(planes, flow_ref, odd_ref, even_ref, mid_ref, face_even_ref, face_odd_ref):
    fields, cells, nz = flow_ref.shape
    odd_y = odd_place()
    ny = cells // planes
    rows = ny + HALO
    sub = lax.broadcasted_iota(jnp.int32, (HALO, nz), 0)
    empty = jnp.zeros((planes, nz), jnp.float32)
    for f in range(fields):
        for i in range(planes):
            mid_ref[f, rows * i : rows * i + ny] = flow_ref[f, ny * i : ny * i + ny]
        for j in range(HALO):
            k = j if j < DEPTH else j - DEPTH - GAP
            part = slice(planes * k, planes * k + planes)
            if j < DEPTH:
                value = jnp.where(odd_y, odd_ref[f, part], even_ref[f, part])
                value = jnp.where(at_upper_wall(), 0.0, value)
            elif j < DEPTH + GAP:
                value = empty
            else:
                value = jnp.where(odd_y, even_ref[f, part], odd_ref[f, part])
                value = jnp.where(at_lower_wall(), 0.0, value)
            mid_ref[f, pl.ds(ny + j, planes, stride=rows), :] = value
        faces = []
        for begin, near, next_one in ((0, 0, 1), (planes - DEPTH, planes - 1, planes - 2)):
            halos = [mid_ref[f, rows * i + ny : rows * i + rows] for i in (near, next_one)]
            own = [flow_ref[f, ny * i : ny * i + ny] for i in range(begin, begin + DEPTH)]
            faces.append(own + [corner_rows(*halos, sub)])
        for k, (first, last) in enumerate(zip(*faces)):
            part = slice(ny * k, ny * k + first.shape[0])
            face_even_ref[f, part] = jnp.where(odd_place("gx"), first, last)
            face_odd_ref[f, part] = jnp.where(odd_place("gx"), last, first)


def corner_rows(near, next_one, sub):
    tile = jnp.where(sub == 2, pltpu.roll(next_one, 2, 0), pltpu.roll(next_one, 6, 0))
    tile = jnp.where((sub == 2) | (sub == 5), tile, 0.0)
    return jnp.where((sub < 2) | (sub >= 6), near, tile)


def corner_planes(tile, sub):
    near = jnp.where((sub < 2) | (sub >= 6), tile, 0.0)
    next_one = jnp.where(sub == 0, pltpu.roll(tile, 6, 0), pltpu.roll(tile, 2, 0))
    return [near, jnp.where((sub == 0) | (sub == 7), next_one, 0.0), jnp.zeros_like(tile)]


def plane_of(mid_ref, xlo_ref, xhi_ref, f, i):
    nx = mid_ref.shape[1]
    if i < DEPTH:
        return xlo_ref[f, i]
    if i < DEPTH + nx:
        return mid_ref[f, i - DEPTH]
    return xhi_ref[f, i - DEPTH - nx]


GROUP = 8


def pack_kernel(mid_ref, even_ref, odd_ref, packed_ref, xlo_ref, xhi_ref):
    fields, nx, rows, nz = mid_ref.shape
    ny = rows - HALO
    lane = lax.broadcasted_iota(jnp.int32, (rows, nz), 1)
    sub = lax.broadcasted_iota(jnp.int32, (HALO, nz), 0)
    for f in range(fields):
        for one_ref, other_ref, out_ref, order in (
            (even_ref, odd_ref, xlo_ref, (2, 1, 0)), (odd_ref, even_ref, xhi_ref, (0, 1, 2))
        ):
            face = jnp.where(odd_place("gx"), one_ref[f], other_ref[f])
            halo = corner_planes(face[ny * DEPTH :], sub)
            for k in range(DEPTH):
                out_ref[f, k, 0:ny] = face[ny * k : ny * k + ny]
                out_ref[f, k, ny:rows] = halo[order[k]]
        value = jnp.zeros((rows, nz), jnp.float32)
        for i in range(nx + 2 * DEPTH):
            start = GROUP * i
            moved = pltpu.roll(plane_of(mid_ref, xlo_ref, xhi_ref, f, i), (start + DEPTH) % nz, 1)
            value = jnp.where((lane >= start) & (lane < start + 2 * DEPTH), moved, value)
        packed_ref[f] = value


def step(value, by, axis):
    size = value.shape[axis]
    return pltpu.roll(value, (size - by) % size, axis)


def rates(centre, x_plus, x_minus, y_plus, y_minus, z_plus, z_minus):
    slope_x = [0.5 * (a - b) for a, b in zip(x_plus, x_minus)]
    slope_y = [0.5 * (a - b) for a, b in zip(y_plus, y_minus)]
    slope_z = [0.5 * (a - b) for a, b in zip(z_plus, z_minus)]
    pressure = [slope_x[3], slope_y[3], slope_z[3]]
    out = []
    for f in range(3):
        laplace = (
            x_plus[f] + x_minus[f] + (y_plus[f] + y_minus[f]) + (z_plus[f] + z_minus[f]) - 6.0 * centre[f]
        )
        advect = centre[0] * slope_x[f] + centre[1] * slope_y[f] + centre[2] * slope_z[f]
        value = VISCOSITY * laplace - advect - pressure[f]
        if f == 0:
            value = value + DRIVING
        out.append(value)
    out.append(-SOUND_SQ * (slope_x[0] + slope_y[1] + slope_z[2]))
    return out


def beyond_walls(ny, shape):
    row = lax.broadcasted_iota(jnp.int32, shape, 0)
    below = (row >= ny + DEPTH + GAP) & at_lower_wall()
    above = (row >= ny) & (row < ny + DEPTH) & at_upper_wall()
    return below | above


def plane_rates(read, i, rows, ends=None):
    every = range(4)
    centre = [read(f, i) for f in every]
    x_plus = [read(f, i + 1)[:rows] for f in every]
    x_minus = [read(f, i - 1)[:rows] for f in every]
    y_plus = [step(v, 1, 0)[:rows] for v in centre]
    y_minus = [step(v, -1, 0)[:rows] for v in centre]
    centre = [v[:rows] for v in centre]
    upward, downward = centre, centre
    if ends is not None:
        lane = lax.broadcasted_iota(jnp.int32, centre[0].shape, 1)
        upward = [jnp.where(lane == 0, e[:rows], v) for e, v in zip(ends, centre)]
        downward = [jnp.where(lane == lane.shape[1] - 1, e[:rows], v) for e, v in zip(ends, centre)]
    z_plus = [step(v, 1, 1) for v in upward]
    z_minus = [step(v, -1, 1) for v in downward]
    return centre, rates(centre, x_plus, x_minus, y_plus, y_minus, z_plus, z_minus)


def stage_one(outside, value, rate):
    return jnp.where(outside, 0.0, value + DT_STEP * rate)


def stage_two(outside, begin, value, rate):
    return jnp.where(outside, 0.0, 0.75 * begin + 0.25 * (value + DT_STEP * rate))


def first_kernel(sample_hbm, mid_ref, xlo_ref, xhi_ref, one_ref, sample_ref, sem):
    copy = pltpu.make_async_copy(sample_hbm, sample_ref, sem)
    copy.start()
    fields, nx, rows, nz = mid_ref.shape
    outside = beyond_walls(rows - HALO, (rows, nz))
    for i in range(1, nx + 2 * DEPTH - 1):
        centre, rate = plane_rates(functools.partial(plane_of, mid_ref, xlo_ref, xhi_ref), i, rows)
        for f in range(4):
            one_ref[f, i - 1] = stage_one(outside, centre[f], rate[f])
    copy.wait()


def step_kernel(
    mid_ref, xlo_ref, xhi_ref, first_ref, own_ref, low_ref, high_ref, basis_ref, sample_ref,
    flow_ref, snap_ref, cross_ref,
    one_ref, two_ref,
):
    fields, nx, ny, nz = flow_ref.shape
    rows = mid_ref.shape[2]
    modes = basis_ref.shape[1]
    planes = nx + 2 * DEPTH
    lane = lax.broadcasted_iota(jnp.int32, (rows, nz), 1)
    outside = beyond_walls(ny, (rows, nz))
    every = range(4)
    start = functools.partial(plane_of, mid_ref, xlo_ref, xhi_ref)

    left = lane % GROUP < DEPTH

    def window_rates(q):
        return rates(
            q, [step(v, GROUP, 1) for v in q], [step(v, -GROUP, 1) for v in q],
            [step(v, 1, 0) for v in q], [step(v, -1, 0) for v in q],
            [step(v, 1, 1) for v in q], [step(v, -1, 1) for v in q],
        )

    own = [own_ref[f] for f in every]
    other = [jnp.where(left, low_ref[f], high_ref[f]) for f in every]
    windows = []
    for parts in ((other, own), (own, other)):
        q0 = [jnp.where(left, a, b) for a, b in zip(*parts)]
        q1 = [stage_one(outside, v, r) for v, r in zip(q0, window_rates(q0))]
        q2 = [stage_two(outside, s, v, r) for s, v, r in zip(q0, q1, window_rates(q1))]
        windows.append((q1, q2))
    (low_one, low_two), (high_one, high_two) = windows
    ends_one = [jnp.where(left, a, b) for a, b in zip(low_one, high_one)]
    ends_two = [jnp.where(left, a, b) for a, b in zip(low_two, high_two)]
    rim_one = [jnp.where(left, b, a) for a, b in zip(low_one, high_one)]

    def at_plane(values, i):
        return [pltpu.roll(v, (2 * nz - GROUP * i - DEPTH) % nz, 1) for v in values]

    rim = (lane == 0) | (lane == nz - 1)
    for i in range(1, planes - 1):
        for f, value in enumerate(at_plane(rim_one, i)):
            one_ref[f, i - 1] = jnp.where(rim, value, first_ref[f, i - 1])
    for i in range(2, planes - 2):
        centre, rate = plane_rates(lambda f, i: one_ref[f, i - 1], i, rows, at_plane(ends_one, i))
        for f in every:
            two_ref[f, i - 2] = stage_two(outside, start(f, i), centre[f], rate[f])
    for i in range(3, planes - 3):
        centre, rate = plane_rates(lambda f, i: two_ref[f, i - 2], i, ny, at_plane(ends_two, i))
        for f in every:
            value = 1.0 / 3.0 * start(f, i)[:ny] + 2.0 / 3.0 * (centre[f] + DT_STEP * rate[f])
            flow_ref[f, i - DEPTH] = value

    points = sample_ref.shape[1]
    spot = jnp.broadcast_to(sample_ref[...], (nz, points))
    place = lax.broadcasted_iota(jnp.int32, (nx * ny, points), 0)
    in_row = (place == jnp.broadcast_to(sample_ref[...] // nz, (nx * ny, points))).astype(jnp.bfloat16)
    in_lane = lax.broadcasted_iota(jnp.int32, (nz, points), 0) == spot % nz
    product = jnp.zeros((modes + 1, points), jnp.float32)
    for c in range(3):
        field = flow_ref[c].reshape(nx * ny, nz).T
        found = sum(dot_parts(part, in_row, ((1,), (0,))) for part in three_parts(field))
        picked = jnp.sum(jnp.where(in_lane, found, 0.0), axis=0, keepdims=True)
        snap_ref[c] = picked
        product = product + jnp.concatenate([basis_ref[c], picked], axis=0) * picked
    total = jnp.sum(product, axis=1, keepdims=True)
    size = modes + 1
    diagonal = lax.broadcasted_iota(jnp.int32, (size, size), 0) == lax.broadcasted_iota(jnp.int32, (size, size), 1)
    cross_ref[...] = jnp.sum(jnp.where(diagonal, total, 0.0), axis=0, keepdims=True)


def merge_kernel(parts_ref, cross_ref, send_ref):
    total = parts_ref[0]
    for d in range(1, parts_ref.shape[0]):
        total = total + parts_ref[d]
    block = jnp.concatenate([total[: total.shape[0] - 1], cross_ref[...]], axis=0)
    for d in range(send_ref.shape[0]):
        send_ref[d] = block


def final_kernel(
    count, got_ref, parts_ref, snap_ref, flow_ref,
    basis_hbm, factor_hbm, flow_hbm,
    packed_ref, work_ref, basis_out_ref, factor_ref, sems,
):
    _, comps, size, points = parts_ref.shape
    tall = size // 4
    per = got_ref.shape[1] - 1
    copies = [pltpu.make_async_copy(flow_ref, flow_hbm, sems.at[0])]
    copies[0].start()

    total = jnp.zeros((per + 1, size), jnp.float32)
    for d in range(got_ref.shape[0]):
        block = got_ref[d]
        if per * d < packed_ref.shape[0]:
            packed_ref[per * d : per * d + per] = block[0:per]
        total = total + block
    cross = total[per : per + 1] / count
    top = lax.broadcasted_iota(jnp.int32, (16, size), 0)
    mark = (lax.broadcasted_iota(jnp.int32, (16, size), 1) == size - 1) & (top < 3)
    thirds = jnp.zeros((16, size), jnp.float32)
    for k, part in enumerate(three_parts(cross)):
        thirds = jnp.where(top == k, part.astype(jnp.float32), thirds)
    side = dot_parts(thirds.astype(jnp.bfloat16), mark.astype(jnp.bfloat16), ((0,), (0,)))
    lane = lax.broadcasted_iota(jnp.int32, (tall, size), 1)
    row = lax.broadcasted_iota(jnp.int32, (tall, size), 0)
    old = unpack_upper([packed_ref[tall * k : tall * k + tall] / count for k in range(3)], tall)
    for k in range(4):
        value = jnp.where(lane == size - 1, side[tall * k : tall * k + tall], old[k])
        if k == 3:
            value = jnp.where(row == tall - 1, jnp.broadcast_to(cross, value.shape), value)
        work_ref[tall * k : tall * k + tall, 0:size] = value
        work_ref[tall * k : tall * k + tall, size : 2 * size] = (lane == row + tall * k).astype(jnp.float32)

    for k in range(4):
        base = tall * k
        eliminate(work_ref, base, tall, old[0] if k == 0 else None)
        done = work_ref[base : base + tall, :]
        if k < 3:
            change = dot_stacked(done[:, 0:size], done)
            work_ref[base + tall : size, :] = work_ref[base + tall : size, :] - change[base + tall : size]
        factor_ref[base : base + tall, :] = jnp.where(lane >= row + base, done[:, 0:size], 0.0)
        if k == 3:
            copies.append(pltpu.make_async_copy(factor_ref, factor_hbm, sems.at[1]))
            copies[-1].start()
        if k == 0:
            continue
        begin, count_rows = (0, base + tall) if k == 1 else (base, tall)
        inverse = work_ref[begin : base + tall, size : 2 * size]
        pieces = jnp.concatenate(three_parts(inverse), axis=0)
        for c in range(comps):
            value = jnp.zeros((count_rows, points), jnp.float32)
            for n in (2, 1, 0):
                products = dot_parts(pieces[: count_rows * (3 - n)], parts_ref[n, c], ((1,), (0,)))
                for m in range(2 - n, -1, -1):
                    value = value + products[count_rows * m : count_rows * m + count_rows]
            if k == 3:
                value = value + inverse[:, size - 1 : size] * snap_ref[c]
            basis_out_ref[c, begin : base + tall, :] = value
        rows = (slice(None), pl.ds(begin, count_rows), slice(None))
        copies.append(pltpu.make_async_copy(basis_out_ref.at[rows], basis_hbm.at[rows], sems.at[1 + k]))
        copies[-1].start()
    for copy in copies:
        copy.wait()


def eliminate(work_ref, base, tall, early=None):
    blocks = tall // 8
    sub = lax.broadcasted_iota(jnp.int32, (8, 128), 0)
    panel = [work_ref[base + 8 * b : base + 8 * b + 8, :] for b in range(blocks)]
    scale = [jnp.zeros((8, 128), jnp.float32) for _ in range(blocks)]
    half = tall // 2
    for low in (0, half):
        high = low + half
        rows = panel if early is None or low else [early[8 * b : 8 * b + 8] for b in range(blocks)]
        column = {
            k: {b: jnp.broadcast_to(rows[b][:, base + k : base + k + 1], (8, 128)) for b in range(k // 8, blocks)}
            for k in range(low, high)
        }
        for j in range(low, high):
            mine, at = divmod(j, 8)
            pivot = column[j][mine][at : at + 1, :]
            inverse = 1.0 / pivot
            scaled = {b: column[j][b] * inverse for b in range(mine, blocks)}
            for k in range(j + 1, high):
                other, place = divmod(k, 8)
                times = scaled[other][place : place + 1, :]
                for b in range(other, blocks):
                    column[k][b] = column[k][b] - column[j][b] * times
            scale[mine] = jnp.where(sub == at, lax.rsqrt(pivot), scale[mine])
            pivot_row = panel[mine][at : at + 1, :]
            for b in range(mine, blocks):
                times = jnp.where(sub > at, scaled[b], 0.0) if b == mine else scaled[b]
                panel[b] = panel[b] - jnp.concatenate([times, times], axis=1) * pivot_row
    for b in range(blocks):
        work_ref[base + 8 * b : base + 8 * b + 8, :] = panel[b] * jnp.concatenate([scale[b], scale[b]], axis=1)


def local(flow, basis, sample):
    fields, nx, ny, nz = flow.shape
    modes, comps, points = basis.shape
    size = modes + 1
    devices = lax.axis_size("gx") * lax.axis_size("gy") * lax.axis_size("gz")
    count = float(comps * points * devices)
    shape = functools.partial(jax.ShapeDtypeStruct, dtype=jnp.float32)
    call = functools.partial(pl.pallas_call, compiler_params=PARAMS)
    bricks = jnp.transpose(basis, (1, 0, 2))

    whole = pl.BlockSpec(memory_space=pltpu.HBM)
    flat = flow.reshape(fields, nx * ny, nz)
    quarter = size // 4
    per = -(-3 * quarter // devices)

    strip = shape((fields, nx * DEPTH, nz))
    strips = call(
        functools.partial(strips_kernel, nx), out_shape=(strip, strip), in_specs=[VMEM], out_specs=(VMEM, VMEM)
    )(flat)
    y_even, y_odd = pairs(*strips, "gy", "gz")
    gram, basis_parts = call(
        gram_kernel,
        out_shape=(shape((devices, per + 1, size)), jax.ShapeDtypeStruct((3, comps, size, points), jnp.bfloat16)),
        in_specs=[VMEM],
        out_specs=(VMEM, VMEM),
        scratch_shapes=[pltpu.VMEM((size, size), jnp.float32), pltpu.VMEM((devices * per, size), jnp.float32)],
    )(bricks)
    y_odd, y_even, gram = lax.optimization_barrier((y_odd, y_even, gram))

    rows = ny + HALO
    face = shape((fields, DEPTH * ny + HALO, nz))
    mid, face_even, face_odd = call(
        functools.partial(walls_kernel, nx),
        out_shape=(shape((fields, nx * rows, nz)), face, face),
        in_specs=[VMEM] * 3,
        out_specs=(VMEM,) * 3,
    )(flat, y_odd, y_even)
    mid = mid.reshape(fields, nx, rows, nz)
    x_even, x_odd = ring_pairs(face_odd, face_even, "gx")
    parts = lax.all_to_all(gram, ALL, 0, 0)

    beside = shape((fields, DEPTH, rows, nz))
    packed, xlo, xhi = call(
        pack_kernel,
        out_shape=(shape((fields, rows, nz)), beside, beside),
        in_specs=[VMEM] * 3,
        out_specs=(VMEM,) * 3,
    )(mid, x_even, x_odd)
    if lax.axis_size("gz") == 2:
        low = high = lax.ppermute(packed, "gz", [(0, 1), (1, 0)])
    else:
        low, high = neighbours(packed, packed, "gz")
    begun, cells = call(
        first_kernel,
        out_shape=(
            shape((fields, nx + 2 * DEPTH - 2, rows, nz)),
            jax.ShapeDtypeStruct((1, points), sample.dtype),
        ),
        in_specs=[whole] + [VMEM] * 3,
        out_specs=(VMEM, VMEM),
        scratch_shapes=[pltpu.SemaphoreType.DMA],
    )(sample.reshape(1, points), mid, xlo, xhi)
    flow_new, snapshot, cross = call(
        step_kernel,
        out_shape=(shape(flow.shape), shape((comps, 1, points)), shape((1, size))),
        in_specs=[VMEM] * 9,
        out_specs=(VMEM, VMEM, VMEM),
        scratch_shapes=[
            pltpu.VMEM((fields, nx + 2 * DEPTH - 2, rows, nz), jnp.float32),
            pltpu.VMEM((fields, nx + 2 * DEPTH - 4, rows, nz), jnp.float32),
        ],
    )(mid, xlo, xhi, begun, packed, low, high, bricks, cells)

    send = call(
        merge_kernel, out_shape=shape((devices, per + 1, size)), in_specs=[VMEM] * 2, out_specs=VMEM
    )(parts, cross)
    got = lax.all_to_all(send, ALL, 0, 0)
    basis_next, factor, flow_next = call(
        functools.partial(final_kernel, count),
        out_shape=(shape((comps, size, points)), shape((size, size)), shape(flow.shape)),
        in_specs=[VMEM] * 4,
        out_specs=(whole,) * 3,
        scratch_shapes=[
            pltpu.VMEM((3 * quarter, size), jnp.float32),
            pltpu.VMEM((size, 2 * size), jnp.float32),
            pltpu.VMEM((comps, size, points), jnp.float32),
            pltpu.VMEM((size, size), jnp.float32),
            pltpu.SemaphoreType.DMA((5,)),
        ],
    )(got, basis_parts, snapshot, flow_new)
    return flow_next, jnp.transpose(basis_next, (1, 0, 2)), factor


def solution(mesh):
    return jax.shard_map(
        local,
        mesh=mesh,
        in_specs=(
            P(None, "gx", "gy", "gz"),
            P(None, None, ("gx", "gy", "gz")),
            P(("gx", "gy", "gz")),
        ),
        out_specs=(P(None, "gx", "gy", "gz"), P(None, None, ("gx", "gy", "gz")), P()),
        check_vma=False,
    )
```

```python
import functools

import jax
import jax.numpy as jnp
from jax import lax
from jax.experimental import pallas as pl
from jax.experimental.pallas import tpu as pltpu
from jax.sharding import PartitionSpec as P

DT_STEP = 0.35
VISCOSITY = 0.2
SOUND_SQ = 1.0
DRIVING = 0.5

ALL = ("gz", "gy", "gx")
DEPTH = 3
EXACT = lax.Precision.HIGHEST
VMEM = pl.BlockSpec(memory_space=pltpu.VMEM)
PARAMS = pltpu.CompilerParams(vmem_limit_bytes=40 * 1024 * 1024)


def dot(a, b, dims):
    return lax.dot_general(
        a, b, (dims, ((), ())), precision=EXACT, preferred_element_type=jnp.float32
    )


def three_parts(value):
    high = value.astype(jnp.bfloat16)
    rest = value - high.astype(jnp.float32)
    middle = rest.astype(jnp.bfloat16)
    return high, middle, (rest - middle.astype(jnp.float32)).astype(jnp.bfloat16)


def dot_parts(a, b, dims):
    return lax.dot_general(a, b, (dims, ((), ())), preferred_element_type=jnp.float32)


def dot_stacked(a, b):
    (a1, a2, a3), (b1, b2, b3) = three_parts(a), three_parts(b)
    first = jnp.concatenate([a1, a1, a2, a2, a1, a3], axis=0)
    second = jnp.concatenate([b1, b2, b1, b2, b3, b1], axis=0)
    return dot_parts(first, second, ((0,), (0,)))


def neighbours(block_low, block_high, axis):
    count = lax.axis_size(axis)
    forward = [(i, (i + 1) % count) for i in range(count)]
    backward = [(target, source) for source, target in forward]
    return lax.ppermute(block_high, axis, forward), lax.ppermute(block_low, axis, backward)


def pairs(block_odd, block_even, axis, other):
    count, width = lax.axis_size(axis), lax.axis_size(other)
    even = [(i, i + 1 - 2 * (i % 2)) for i in range(count)]
    odd = []
    for i in range(count):
        for k in range(width):
            to = (i, k + 1 - 2 * (k % 2)) if i in (0, count - 1) else (i - 1 + 2 * (i % 2), k)
            odd.append((i * width + k, to[0] * width + to[1]))
    from_odd = lax.ppermute(block_odd, (axis, other), odd)
    return lax.ppermute(block_even, axis, even), from_odd


def ring_pairs(block_odd, block_even, axis):
    count = lax.axis_size(axis)
    even = [(i, i + 1 - 2 * (i % 2)) for i in range(count)]
    odd = [(i, (i - 1 + 2 * (i % 2)) % count) for i in range(count)]
    from_odd = lax.ppermute(block_odd, axis, odd)
    return lax.ppermute(block_even, axis, even), from_odd


def at_lower_wall():
    return lax.axis_index("gy") == 0


def at_upper_wall():
    return lax.axis_index("gy") == lax.axis_size("gy") - 1


def odd_place(axis="gy"):
    return lax.axis_index(axis) % 2 == 1


def pack_upper(rows, tall):
    size = rows.shape[1]
    lane = lax.broadcasted_iota(jnp.int32, (tall, size), 1)
    part = [rows[tall * k : tall * k + tall] for k in range(4)]
    return [part[0], jnp.where(lane >= tall, part[1], pltpu.roll(part[3], tall, 1)), part[2]]


def unpack_upper(packed, tall):
    return [packed[0], packed[1], packed[2], pltpu.roll(packed[1], packed[1].shape[1] - tall, 1)]


def gram_kernel(basis_hbm, send_ref, parts_ref, gram_ref, packed_ref, basis_ref, sems):
    modes = basis_ref.shape[1]
    copies = [
        pltpu.make_async_copy(basis_hbm.at[c], basis_ref.at[c], sems.at[c]) for c in range(basis_ref.shape[0])
    ]
    for copy in copies:
        copy.start()
    tall = gram_ref.shape[0] // 4
    total = jnp.zeros((modes, modes), jnp.float32)
    for c in range(basis_ref.shape[0]):
        copies[c].wait()
        rows = basis_ref[c]
        total = total + dot(rows, rows, ((1,), (1,)))
        filled = jnp.concatenate([rows, jnp.zeros((1, rows.shape[1]), jnp.float32)], axis=0)
        for k, part in enumerate(three_parts(filled)):
            parts_ref[k, c] = part
    gram_ref[...] = jnp.zeros_like(gram_ref)
    gram_ref[0:modes, 0:modes] = total
    packed_ref[...] = jnp.zeros_like(packed_ref)
    for k, value in enumerate(pack_upper(gram_ref[...], tall)):
        packed_ref[tall * k : tall * k + tall] = value
    per = send_ref.shape[1] - 1
    empty = jnp.zeros((1, send_ref.shape[2]), jnp.float32)
    for d in range(send_ref.shape[0]):
        send_ref[d] = jnp.concatenate([packed_ref[per * d : per * d + per], empty], axis=0)


GAP = 2
HALO = 2 * DEPTH + GAP


def strips_kernel(planes, flow_ref, odd_ref, even_ref):
    ny = flow_ref.shape[1] // planes
    odd = odd_place()
    for f in range(flow_ref.shape[0]):
        for j in range(DEPTH):
            bottom = flow_ref[f, pl.ds(j, planes, stride=ny), :]
            top = flow_ref[f, pl.ds(ny - DEPTH + j, planes, stride=ny), :]
            even_ref[f, planes * j : planes * j + planes] = jnp.where(odd, bottom, top)
            odd_ref[f, planes * j : planes * j + planes] = jnp.where(odd, top, bottom)


def walls_kernel(planes, flow_ref, odd_ref, even_ref, mid_ref, face_even_ref, face_odd_ref):
    fields, cells, nz = flow_ref.shape
    odd_y = odd_place()
    ny = cells // planes
    rows = ny + HALO
    sub = lax.broadcasted_iota(jnp.int32, (HALO, nz), 0)
    empty = jnp.zeros((planes, nz), jnp.float32)
    for f in range(fields):
        for i in range(planes):
            mid_ref[f, rows * i : rows * i + ny] = flow_ref[f, ny * i : ny * i + ny]
        for j in range(HALO):
            k = j if j < DEPTH else j - DEPTH - GAP
            part = slice(planes * k, planes * k + planes)
            if j < DEPTH:
                value = jnp.where(odd_y, odd_ref[f, part], even_ref[f, part])
                value = jnp.where(at_upper_wall(), 0.0, value)
            elif j < DEPTH + GAP:
                value = empty
            else:
                value = jnp.where(odd_y, even_ref[f, part], odd_ref[f, part])
                value = jnp.where(at_lower_wall(), 0.0, value)
            mid_ref[f, pl.ds(ny + j, planes, stride=rows), :] = value
        faces = []
        for begin, near, next_one in ((0, 0, 1), (planes - DEPTH, planes - 1, planes - 2)):
            halos = [mid_ref[f, rows * i + ny : rows * i + rows] for i in (near, next_one)]
            own = [flow_ref[f, ny * i : ny * i + ny] for i in range(begin, begin + DEPTH)]
            faces.append(own + [corner_rows(*halos, sub)])
        for k, (first, last) in enumerate(zip(*faces)):
            part = slice(ny * k, ny * k + first.shape[0])
            face_even_ref[f, part] = jnp.where(odd_place("gx"), first, last)
            face_odd_ref[f, part] = jnp.where(odd_place("gx"), last, first)


def corner_rows(near, next_one, sub):
    tile = jnp.where(sub == 2, pltpu.roll(next_one, 2, 0), pltpu.roll(next_one, 6, 0))
    tile = jnp.where((sub == 2) | (sub == 5), tile, 0.0)
    return jnp.where((sub < 2) | (sub >= 6), near, tile)


def corner_planes(tile, sub):
    near = jnp.where((sub < 2) | (sub >= 6), tile, 0.0)
    next_one = jnp.where(sub == 0, pltpu.roll(tile, 6, 0), pltpu.roll(tile, 2, 0))
    return [near, jnp.where((sub == 0) | (sub == 7), next_one, 0.0), jnp.zeros_like(tile)]


def plane_of(mid_ref, xlo_ref, xhi_ref, f, i):
    nx = mid_ref.shape[1]
    if i < DEPTH:
        return xlo_ref[f, i]
    if i < DEPTH + nx:
        return mid_ref[f, i - DEPTH]
    return xhi_ref[f, i - DEPTH - nx]


GROUP = 8


def pack_kernel(mid_ref, even_ref, odd_ref, packed_ref, xlo_ref, xhi_ref):
    fields, nx, rows, nz = mid_ref.shape
    ny = rows - HALO
    lane = lax.broadcasted_iota(jnp.int32, (rows, nz), 1)
    sub = lax.broadcasted_iota(jnp.int32, (HALO, nz), 0)
    for f in range(fields):
        for one_ref, other_ref, out_ref, order in (
            (even_ref, odd_ref, xlo_ref, (2, 1, 0)), (odd_ref, even_ref, xhi_ref, (0, 1, 2))
        ):
            face = jnp.where(odd_place("gx"), one_ref[f], other_ref[f])
            halo = corner_planes(face[ny * DEPTH :], sub)
            for k in range(DEPTH):
                out_ref[f, k, 0:ny] = face[ny * k : ny * k + ny]
                out_ref[f, k, ny:rows] = halo[order[k]]
        value = jnp.zeros((rows, nz), jnp.float32)
        for i in range(nx + 2 * DEPTH):
            start = GROUP * i
            moved = pltpu.roll(plane_of(mid_ref, xlo_ref, xhi_ref, f, i), (start + DEPTH) % nz, 1)
            value = jnp.where((lane >= start) & (lane < start + 2 * DEPTH), moved, value)
        packed_ref[f] = value


def step(value, by, axis):
    size = value.shape[axis]
    return pltpu.roll(value, (size - by) % size, axis)


def rates(centre, x_plus, x_minus, y_plus, y_minus, z_plus, z_minus):
    slope_x = [0.5 * (a - b) for a, b in zip(x_plus, x_minus)]
    slope_y = [0.5 * (a - b) for a, b in zip(y_plus, y_minus)]
    slope_z = [0.5 * (a - b) for a, b in zip(z_plus, z_minus)]
    pressure = [slope_x[3], slope_y[3], slope_z[3]]
    out = []
    for f in range(3):
        laplace = (
            x_plus[f] + x_minus[f] + (y_plus[f] + y_minus[f]) + (z_plus[f] + z_minus[f]) - 6.0 * centre[f]
        )
        advect = centre[0] * slope_x[f] + centre[1] * slope_y[f] + centre[2] * slope_z[f]
        value = VISCOSITY * laplace - advect - pressure[f]
        if f == 0:
            value = value + DRIVING
        out.append(value)
    out.append(-SOUND_SQ * (slope_x[0] + slope_y[1] + slope_z[2]))
    return out


def beyond_walls(ny, shape):
    row = lax.broadcasted_iota(jnp.int32, shape, 0)
    below = (row >= ny + DEPTH + GAP) & at_lower_wall()
    above = (row >= ny) & (row < ny + DEPTH) & at_upper_wall()
    return below | above


def plane_rates(read, i, rows, ends=None):
    every = range(4)
    centre = [read(f, i) for f in every]
    x_plus = [read(f, i + 1)[:rows] for f in every]
    x_minus = [read(f, i - 1)[:rows] for f in every]
    y_plus = [step(v, 1, 0)[:rows] for v in centre]
    y_minus = [step(v, -1, 0)[:rows] for v in centre]
    centre = [v[:rows] for v in centre]
    upward, downward = centre, centre
    if ends is not None:
        lane = lax.broadcasted_iota(jnp.int32, centre[0].shape, 1)
        upward = [jnp.where(lane == 0, e[:rows], v) for e, v in zip(ends, centre)]
        downward = [jnp.where(lane == lane.shape[1] - 1, e[:rows], v) for e, v in zip(ends, centre)]
    z_plus = [step(v, 1, 1) for v in upward]
    z_minus = [step(v, -1, 1) for v in downward]
    return centre, rates(centre, x_plus, x_minus, y_plus, y_minus, z_plus, z_minus)


def stage_one(outside, value, rate):
    return jnp.where(outside, 0.0, value + DT_STEP * rate)


def stage_two(outside, begin, value, rate):
    return jnp.where(outside, 0.0, 0.75 * begin + 0.25 * (value + DT_STEP * rate))


def first_kernel(sample_hbm, mid_ref, xlo_ref, xhi_ref, one_ref, sample_ref, sem):
    copy = pltpu.make_async_copy(sample_hbm, sample_ref, sem)
    copy.start()
    fields, nx, rows, nz = mid_ref.shape
    outside = beyond_walls(rows - HALO, (rows, nz))
    for i in range(1, nx + 2 * DEPTH - 1):
        centre, rate = plane_rates(functools.partial(plane_of, mid_ref, xlo_ref, xhi_ref), i, rows)
        for f in range(4):
            one_ref[f, i - 1] = stage_one(outside, centre[f], rate[f])
    copy.wait()


def step_kernel(
    mid_ref, xlo_ref, xhi_ref, first_ref, own_ref, low_ref, high_ref, basis_ref, sample_ref,
    flow_ref, snap_ref, cross_ref,
    one_ref, two_ref,
):
    fields, nx, ny, nz = flow_ref.shape
    rows = mid_ref.shape[2]
    modes = basis_ref.shape[1]
    planes = nx + 2 * DEPTH
    lane = lax.broadcasted_iota(jnp.int32, (rows, nz), 1)
    outside = beyond_walls(ny, (rows, nz))
    every = range(4)
    start = functools.partial(plane_of, mid_ref, xlo_ref, xhi_ref)

    left = lane % GROUP < DEPTH

    def window_rates(q):
        return rates(
            q, [step(v, GROUP, 1) for v in q], [step(v, -GROUP, 1) for v in q],
            [step(v, 1, 0) for v in q], [step(v, -1, 0) for v in q],
            [step(v, 1, 1) for v in q], [step(v, -1, 1) for v in q],
        )

    own = [own_ref[f] for f in every]
    other = [jnp.where(left, low_ref[f], high_ref[f]) for f in every]
    windows = []
    for parts in ((other, own), (own, other)):
        q0 = [jnp.where(left, a, b) for a, b in zip(*parts)]
        q1 = [stage_one(outside, v, r) for v, r in zip(q0, window_rates(q0))]
        q2 = [stage_two(outside, s, v, r) for s, v, r in zip(q0, q1, window_rates(q1))]
        windows.append((q1, q2))
    (low_one, low_two), (high_one, high_two) = windows
    ends_one = [jnp.where(left, a, b) for a, b in zip(low_one, high_one)]
    ends_two = [jnp.where(left, a, b) for a, b in zip(low_two, high_two)]
    rim_one = [jnp.where(left, b, a) for a, b in zip(low_one, high_one)]

    def at_plane(values, i):
        return [pltpu.roll(v, (2 * nz - GROUP * i - DEPTH) % nz, 1) for v in values]

    rim = (lane == 0) | (lane == nz - 1)
    for i in range(1, planes - 1):
        for f, value in enumerate(at_plane(rim_one, i)):
            one_ref[f, i - 1] = jnp.where(rim, value, first_ref[f, i - 1])
    for i in range(2, planes - 2):
        centre, rate = plane_rates(lambda f, i: one_ref[f, i - 1], i, rows, at_plane(ends_one, i))
        for f in every:
            two_ref[f, i - 2] = stage_two(outside, start(f, i), centre[f], rate[f])
    for i in range(3, planes - 3):
        centre, rate = plane_rates(lambda f, i: two_ref[f, i - 2], i, ny, at_plane(ends_two, i))
        for f in every:
            value = 1.0 / 3.0 * start(f, i)[:ny] + 2.0 / 3.0 * (centre[f] + DT_STEP * rate[f])
            flow_ref[f, i - DEPTH] = value

    points = sample_ref.shape[1]
    spot = jnp.broadcast_to(sample_ref[...], (nz, points))
    place = lax.broadcasted_iota(jnp.int32, (nx * ny, points), 0)
    in_row = (place == jnp.broadcast_to(sample_ref[...] // nz, (nx * ny, points))).astype(jnp.bfloat16)
    in_lane = lax.broadcasted_iota(jnp.int32, (nz, points), 0) == spot % nz
    product = jnp.zeros((modes + 1, points), jnp.float32)
    for c in range(3):
        field = flow_ref[c].reshape(nx * ny, nz).T
        found = sum(dot_parts(part, in_row, ((1,), (0,))) for part in three_parts(field))
        picked = jnp.sum(jnp.where(in_lane, found, 0.0), axis=0, keepdims=True)
        snap_ref[c] = picked
        product = product + jnp.concatenate([basis_ref[c], picked], axis=0) * picked
    total = jnp.sum(product, axis=1, keepdims=True)
    size = modes + 1
    diagonal = lax.broadcasted_iota(jnp.int32, (size, size), 0) == lax.broadcasted_iota(jnp.int32, (size, size), 1)
    cross_ref[...] = jnp.sum(jnp.where(diagonal, total, 0.0), axis=0, keepdims=True)


def merge_kernel(parts_ref, cross_ref, send_ref):
    total = parts_ref[0]
    for d in range(1, parts_ref.shape[0]):
        total = total + parts_ref[d]
    block = jnp.concatenate([total[: total.shape[0] - 1], cross_ref[...]], axis=0)
    for d in range(send_ref.shape[0]):
        send_ref[d] = block


def final_kernel(
    count, got_ref, parts_ref, snap_ref, flow_ref,
    basis_hbm, factor_hbm, flow_hbm,
    packed_ref, work_ref, basis_out_ref, factor_ref, sems,
):
    _, comps, size, points = parts_ref.shape
    tall = size // 4
    per = got_ref.shape[1] - 1
    copies = [pltpu.make_async_copy(flow_ref, flow_hbm, sems.at[0])]
    copies[0].start()

    total = jnp.zeros((per + 1, size), jnp.float32)
    for d in range(got_ref.shape[0]):
        block = got_ref[d]
        if per * d < packed_ref.shape[0]:
            packed_ref[per * d : per * d + per] = block[0:per]
        total = total + block
    cross = total[per : per + 1] / count
    top = lax.broadcasted_iota(jnp.int32, (16, size), 0)
    mark = (lax.broadcasted_iota(jnp.int32, (16, size), 1) == size - 1) & (top < 3)
    thirds = jnp.zeros((16, size), jnp.float32)
    for k, part in enumerate(three_parts(cross)):
        thirds = jnp.where(top == k, part.astype(jnp.float32), thirds)
    side = dot_parts(thirds.astype(jnp.bfloat16), mark.astype(jnp.bfloat16), ((0,), (0,)))
    lane = lax.broadcasted_iota(jnp.int32, (tall, size), 1)
    row = lax.broadcasted_iota(jnp.int32, (tall, size), 0)
    old = unpack_upper([packed_ref[tall * k : tall * k + tall] / count for k in range(3)], tall)
    for k in range(4):
        value = jnp.where(lane == size - 1, side[tall * k : tall * k + tall], old[k])
        if k == 3:
            value = jnp.where(row == tall - 1, jnp.broadcast_to(cross, value.shape), value)
        work_ref[tall * k : tall * k + tall, 0:size] = value
        work_ref[tall * k : tall * k + tall, size : 2 * size] = (lane == row + tall * k).astype(jnp.float32)

    for k in range(4):
        base = tall * k
        eliminate(work_ref, base, tall, old[0] if k == 0 else None)
        done = work_ref[base : base + tall, :]
        if k < 3:
            change = dot_stacked(done[:, 0:size], done)
            work_ref[base + tall : size, :] = work_ref[base + tall : size, :] - change[base + tall : size]
        factor_ref[base : base + tall, :] = jnp.where(lane >= row + base, done[:, 0:size], 0.0)
        if k == 3:
            copies.append(pltpu.make_async_copy(factor_ref, factor_hbm, sems.at[1]))
            copies[-1].start()
        if k == 0:
            continue
        begin, count_rows = (0, base + tall) if k == 1 else (base, tall)
        inverse = work_ref[begin : base + tall, size : 2 * size]
        pieces = jnp.concatenate(three_parts(inverse), axis=0)
        for c in range(comps):
            value = jnp.zeros((count_rows, points), jnp.float32)
            for n in (2, 1, 0):
                products = dot_parts(pieces[: count_rows * (3 - n)], parts_ref[n, c], ((1,), (0,)))
                for m in range(2 - n, -1, -1):
                    value = value + products[count_rows * m : count_rows * m + count_rows]
            if k == 3:
                value = value + inverse[:, size - 1 : size] * snap_ref[c]
            basis_out_ref[c, begin : base + tall, :] = value
        rows = (slice(None), pl.ds(begin, count_rows), slice(None))
        copies.append(pltpu.make_async_copy(basis_out_ref.at[rows], basis_hbm.at[rows], sems.at[1 + k]))
        copies[-1].start()
    for copy in copies:
        copy.wait()


def eliminate(work_ref, base, tall, early=None):
    blocks = tall // 8
    sub = lax.broadcasted_iota(jnp.int32, (8, 128), 0)
    panel = [work_ref[base + 8 * b : base + 8 * b + 8, :] for b in range(blocks)]
    scale = [jnp.zeros((8, 128), jnp.float32) for _ in range(blocks)]
    half = tall // 2
    for low in (0, half):
        high = low + half
        rows = panel if early is None or low else [early[8 * b : 8 * b + 8] for b in range(blocks)]
        column = {
            k: {b: jnp.broadcast_to(rows[b][:, base + k : base + k + 1], (8, 128)) for b in range(k // 8, blocks)}
            for k in range(low, high)
        }
        for j in range(low, high):
            mine, at = divmod(j, 8)
            pivot = column[j][mine][at : at + 1, :]
            inverse = 1.0 / pivot
            scaled = {b: column[j][b] * inverse for b in range(mine, blocks)}
            for k in range(j + 1, high):
                other, place = divmod(k, 8)
                times = scaled[other][place : place + 1, :]
                for b in range(other, blocks):
                    column[k][b] = column[k][b] - column[j][b] * times
            scale[mine] = jnp.where(sub == at, lax.rsqrt(pivot), scale[mine])
            pivot_row = panel[mine][at : at + 1, :]
            for b in range(mine, blocks):
                times = jnp.where(sub > at, scaled[b], 0.0) if b == mine else scaled[b]
                panel[b] = panel[b] - jnp.concatenate([times, times], axis=1) * pivot_row
    for b in range(blocks):
        work_ref[base + 8 * b : base + 8 * b + 8, :] = panel[b] * jnp.concatenate([scale[b], scale[b]], axis=1)


def local(flow, basis, sample):
    fields, nx, ny, nz = flow.shape
    modes, comps, points = basis.shape
    size = modes + 1
    devices = lax.axis_size("gx") * lax.axis_size("gy") * lax.axis_size("gz")
    count = float(comps * points * devices)
    shape = functools.partial(jax.ShapeDtypeStruct, dtype=jnp.float32)
    call = functools.partial(pl.pallas_call, compiler_params=PARAMS)
    bricks = jnp.transpose(basis, (1, 0, 2))

    whole = pl.BlockSpec(memory_space=pltpu.HBM)
    flat = flow.reshape(fields, nx * ny, nz)
    quarter = size // 4
    per = -(-3 * quarter // devices)

    strip = shape((fields, nx * DEPTH, nz))
    strips = call(
        functools.partial(strips_kernel, nx), out_shape=(strip, strip), in_specs=[VMEM], out_specs=(VMEM, VMEM)
    )(flat)
    y_even, y_odd = pairs(*strips, "gy", "gz")
    gram, basis_parts = call(
        gram_kernel,
        out_shape=(shape((devices, per + 1, size)), jax.ShapeDtypeStruct((3, comps, size, points), jnp.bfloat16)),
        in_specs=[whole],
        out_specs=(VMEM, VMEM),
        scratch_shapes=[pltpu.VMEM((size, size), jnp.float32), pltpu.VMEM((devices * per, size), jnp.float32),
            pltpu.VMEM(bricks.shape, jnp.float32),
            pltpu.SemaphoreType.DMA((comps,)),
        ],
    )(pltpu.with_memory_space_constraint(bricks, pltpu.HBM))
    y_odd, y_even, gram = lax.optimization_barrier((y_odd, y_even, gram))

    rows = ny + HALO
    face = shape((fields, DEPTH * ny + HALO, nz))
    mid, face_even, face_odd = call(
        functools.partial(walls_kernel, nx),
        out_shape=(shape((fields, nx * rows, nz)), face, face),
        in_specs=[VMEM] * 3,
        out_specs=(VMEM,) * 3,
    )(flat, y_odd, y_even)
    mid = mid.reshape(fields, nx, rows, nz)
    x_even, x_odd = ring_pairs(face_odd, face_even, "gx")
    parts = lax.all_to_all(gram, ALL, 0, 0)

    beside = shape((fields, DEPTH, rows, nz))
    packed, xlo, xhi = call(
        pack_kernel,
        out_shape=(shape((fields, rows, nz)), beside, beside),
        in_specs=[VMEM] * 3,
        out_specs=(VMEM,) * 3,
    )(mid, x_even, x_odd)
    if lax.axis_size("gz") == 2:
        low = high = lax.ppermute(packed, "gz", [(0, 1), (1, 0)])
    else:
        low, high = neighbours(packed, packed, "gz")
    begun, cells = call(
        first_kernel,
        out_shape=(
            shape((fields, nx + 2 * DEPTH - 2, rows, nz)),
            jax.ShapeDtypeStruct((1, points), sample.dtype),
        ),
        in_specs=[whole] + [VMEM] * 3,
        out_specs=(VMEM, VMEM),
        scratch_shapes=[pltpu.SemaphoreType.DMA],
    )(sample.reshape(1, points), mid, xlo, xhi)
    flow_new, snapshot, cross = call(
        step_kernel,
        out_shape=(shape(flow.shape), shape((comps, 1, points)), shape((1, size))),
        in_specs=[VMEM] * 9,
        out_specs=(VMEM, VMEM, VMEM),
        scratch_shapes=[
            pltpu.VMEM((fields, nx + 2 * DEPTH - 2, rows, nz), jnp.float32),
            pltpu.VMEM((fields, nx + 2 * DEPTH - 4, rows, nz), jnp.float32),
        ],
    )(mid, xlo, xhi, begun, packed, low, high, bricks, cells)

    send = call(
        merge_kernel, out_shape=shape((devices, per + 1, size)), in_specs=[VMEM] * 2, out_specs=VMEM
    )(parts, cross)
    got = lax.all_to_all(send, ALL, 0, 0)
    basis_next, factor, flow_next = call(
        functools.partial(final_kernel, count),
        out_shape=(shape((comps, size, points)), shape((size, size)), shape(flow.shape)),
        in_specs=[VMEM] * 4,
        out_specs=(whole,) * 3,
        scratch_shapes=[
            pltpu.VMEM((3 * quarter, size), jnp.float32),
            pltpu.VMEM((size, 2 * size), jnp.float32),
            pltpu.VMEM((comps, size, points), jnp.float32),
            pltpu.VMEM((size, size), jnp.float32),
            pltpu.SemaphoreType.DMA((5,)),
        ],
    )(got, basis_parts, snapshot, flow_new)
    return flow_next, jnp.transpose(basis_next, (1, 0, 2)), factor


def solution(mesh):
    return jax.shard_map(
        local,
        mesh=mesh,
        in_specs=(
            P(None, "gx", "gy", "gz"),
            P(None, None, ("gx", "gy", "gz")),
            P(("gx", "gy", "gz")),
        ),
        out_specs=(P(None, "gx", "gy", "gz"), P(None, None, ("gx", "gy", "gz")), P()),
        check_vma=False,
    )
```
